32 devices in a mesh: grp: 4 (over y, core), dev: 8 (over z, x).
Axes of the slice: x: 2, y: 2, z: 4, core: 2. Of those that a mesh axis runs over, the one named last changes fastest.
Arguments:
- conc_old: float32 [128, 256, 256], P('grp', 'dev'), may hold values from 0.5 to 2
- phi_old: float32 [128, 256, 256], P('grp', 'dev'), may hold values from -6 to 6
- solid_pot: float32 [128, 256, 256], P('grp', 'dev'), may hold values from -4.5 to 6
- phase_label: int32 [128, 256, 256], P('grp', 'dev'), may hold values from 0 to 2
- iface_block: int32 [4, 2048], P('grp', 'dev'), may hold values from 0 to 2047
- iface_owner: int32 [4, 2048, 1], P('grp', 'dev'), may hold values from 0 to 7; in each aligned block of 256 rows (0 to 255, 256 to 511, ..., all dimensions but the last counted through in order) at most 64 rows name the same one
Outputs:
- concentration: float32 [128, 256, 256], P('grp', 'dev')
- flux: float32 [128, 256, 256], P('grp', 'dev')
- potential: float32 [128, 256, 256], P('grp', 'dev')
The draws below stay inside these ranges and needn't reach their ends.
Inputs may be any that keep to these rules, and one draw needn't show every extreme that they name: `iface_owner`: among the 256 entries of one index of dev, no owner is named more than 64 times, a bound that some block reaches.
All inputs are finite; a program needn't handle non-finite values.
Results may differ from the reference program's by a relative error of at most 0.0005.
Values sent between devices are 32-bit elements; how exact they have to be, the bound alone decides.
No kernel may reach another device: no remote copies, remote signals or barrier semaphores. Data moves between devices by JAX's collectives and lax.ppermute only.
A program may use at most 64 MiB of HBM per device.

```python
import math
import jax
import jax.numpy as jnp
import numpy as np

CX = 32
CY = 32
CZ = 256
LIST_DEV = 256
SWEEPS = 4
SMOOTH = 2
COARSE_SWEEPS = 8
GROUPS = 4
NX = 128
NY = 256
BLK_DEV = 2048
CAP = 64
LIST = 2048
N_DEV = 8


def brick_offsets(key):
    table_key = jax.random.fold_in(key, 7301)
    table_off = jax.random.uniform(table_key, (NX // CX, NY // CY), jnp.float32, -4.0, 4.0)
    spread_off = jnp.repeat(jnp.repeat(table_off, CX, axis=0), CY, axis=1)
    return spread_off[:, :, None]


def draw_phi_old(key, part):
    rough_key = jax.random.fold_in(key, 4111)
    rough = jnp.clip(jax.random.normal(rough_key, (NX, NY, CZ), jnp.float32), -2.0, 2.0)
    return (brick_offsets(key) + rough).astype(jnp.float32)


def draw_solid_pot(key, part):
    rough_key = jax.random.fold_in(key, 5923)
    unit = jax.random.uniform(rough_key, (NX, NY, CZ), jnp.float32, 0.0, 1.0)
    rough = -0.5 + 2.5 * unit
    return (brick_offsets(key) + rough).astype(jnp.float32)


def with_ends(values, stream_key, smallest, top_value):
    longest = values.shape.index(max(values.shape))
    spots = []
    for shift in (0, 1):
        where = [jax.random.randint(jax.random.fold_in(stream_key, axis), (), 0, length) for axis, length in enumerate(values.shape)]
        where[longest] = (where[longest] + shift) % values.shape[longest]
        spots.append(tuple(where))
    return values.at[spots[0]].set(smallest).at[spots[1]].set(top_value)


def level_of(rng, shape, split, low, top_value):
    def one(dim, shards_of):
        draws = jax.random.uniform(jax.random.fold_in(jax.random.fold_in(rng, 6), dim), (shards_of,), jnp.float32, low / len(split), top_value / len(split))
        return jnp.repeat(jnp.exp(draws), shape[dim] // shards_of).reshape((-1,) + (1,) * (len(shape) - dim - 1))

    level = one(*split[0])
    for cut in split[1:]:
        level = level * one(*cut)
    return level


def deal_out(own_key, own, number, rows, count, top, reach, skew):
    sequence = jax.random.permutation(own_key, count)
    crowded, common = portions_of(count, rows * top, reach, skew, True), portions_of(count, rows * top, reach, skew, False)
    places = jnp.arange(count)

    def named(lengths, offset_by):
        used = int((lengths > 0).sum())
        fixed = max(1, used // 4)
        moved = fixed + (places - fixed + offset_by * (used - fixed)) % max(1, count - fixed)
        return jnp.zeros((count,), jnp.int32).at[sequence[jnp.where(places < fixed, places, moved)]].set(jnp.asarray(lengths, jnp.int32))

    lengths = jnp.where(number % 4 == 0, named(crowded, number // 4), named(common, number - number // 4 - 1))
    mixed = jax.random.permutation(jax.random.fold_in(own, 3), count)
    source_of, taker = mixed[0:count // 2 * 2:2], mixed[1:count // 2 * 2:2]
    room = jnp.minimum(lengths[source_of] - 1, reach - lengths[taker]) // 2
    room = jnp.where((source_of == sequence[0]) | (taker == sequence[0]) | (lengths[taker] == 0), 0, jnp.maximum(room, 0))
    moved = jax.random.randint(jax.random.fold_in(own, 4), (count // 2,), 0, 1 << 20) % (room + 1)
    lengths = lengths.at[source_of].add(-moved).at[taker].add(moved)
    items = jnp.searchsorted(jnp.cumsum(lengths), jnp.arange(rows * top), side="right").astype(jnp.int32)
    grid = items.reshape(top, rows).T
    grid = grid[jax.random.permutation(jax.random.fold_in(own, 1), rows)]
    offset_by = jax.random.randint(jax.random.fold_in(own, 2), (rows, 1), 0, top)
    return jnp.take_along_axis(grid, (jnp.arange(top)[None, :] + offset_by) % top, axis=1)


def portions_of(count, total, bound, skew, full):
    portions = [(1 << 20) // math.isqrt(grade ** skew) + 1 for grade in range(1, count + 1)]
    largest = bound if full else min(bound, max(-(-total // count), total * portions[0] // sum(portions)))
    least = 1 if total - largest >= count - 1 else 0
    counts, rest = [largest] + [least] * (count - 1), total - largest - least * (count - 1)
    while rest > 0:
        candidates = [i for i in range(1, count) if counts[i] < largest] or [i for i in range(1, count) if counts[i] < bound]
        pool, remaining = sum([portions[i] for i in candidates]), rest
        for i in candidates:
            addition = min(bound - counts[i], max(1, remaining * portions[i] // pool), rest)
            counts[i] = counts[i] + addition
            rest = rest - addition
    return np.array(counts)


def setup_inputs(seed: int = 0) -> dict:
    key_list = jax.random.split(jax.random.key(seed), 7)
    conc_old = jnp.clip(jnp.exp(math.log(2.0) - 1.3862944 * jax.random.uniform(key_list[0], (NX, NY, CZ), jnp.float32) ** level_of(key_list[0], (NX, NY, CZ), ((0, 4), (1, 8)), -0.2, 0.2)), 0.5, 2.0)
    phi_old = draw_phi_old(jax.random.fold_in(key_list[6], 71), 0)
    solid_pot = draw_solid_pot(jax.random.fold_in(key_list[6], 71), 0)
    phase_label = with_ends(jax.random.randint(key_list[3], (NX, NY, CZ), 0, 3), jax.random.fold_in(key_list[3], 1), 0, 2).astype(jnp.int32)
    iface_block = with_ends(jax.random.randint(key_list[4], (GROUPS, LIST), 0, BLK_DEV), jax.random.fold_in(key_list[4], 1), 0, BLK_DEV - 1).astype(jnp.int32)
    iface_owner_keys = jax.random.split(jax.random.fold_in(key_list[5], 1), GROUPS * LIST // LIST_DEV)
    iface_owner_turns = jax.random.permutation(jax.random.fold_in(key_list[5], 3), GROUPS * LIST // LIST_DEV)
    iface_owner = jax.vmap(lambda own, number: deal_out(jax.random.fold_in(key_list[5], 2), own, number, LIST_DEV, N_DEV, 1, CAP, 2))(iface_owner_keys, iface_owner_turns).reshape((GROUPS, LIST, 1))
    return {"conc_old": conc_old, "phi_old": phi_old, "solid_pot": solid_pot, "phase_label": phase_label, "iface_block": iface_block, "iface_owner": iface_owner}


MASS = 0.05
OMEGA = 0.8
DIFFUSION_TABLE = (1.5, 0.1, 0.4)
CONDUCT_TABLE = (1.0, 0.3, 0.6)
KINETIC_TABLE = (0.2, 1.0, 0.5)

def lookup(phase_label, table_vals):
    return jnp.where(phase_label == 0, table_vals[0], jnp.where(phase_label == 1, table_vals[1], table_vals[2])).astype(jnp.float32)

def split_parts(padded):
    middle = padded[1:-1, 1:-1, 1:-1]
    in_plane = padded[2:, 1:-1, 1:-1] + padded[:-2, 1:-1, 1:-1] + padded[1:-1, 2:, 1:-1] + padded[1:-1, :-2, 1:-1]
    along_z = padded[1:-1, 1:-1, 2:] + padded[1:-1, 1:-1, :-2]
    return (middle, in_plane, along_z)

def apply_level(padded, conduct, weight):
    middle, in_plane, along_z = split_parts(padded)
    return MASS * middle + conduct * (weight * (4.0 * middle - in_plane) + 2.0 * middle - along_z)

def zero_padded(field_in):
    return jnp.pad(field_in, 1)

def smooth(current, source, conduct, weight, padder):
    diagonal = MASS + conduct * (4.0 * weight + 2.0)
    return current + OMEGA * (source - apply_level(padder(current), conduct, weight)) / diagonal

def residual_of(current, source, conduct, weight, padder):
    return source - apply_level(padder(current), conduct, weight)

def restrict(field_in):
    extent_x, extent_y, extent_z = field_in.shape
    return field_in.reshape(extent_x // 2, 2, extent_y // 2, 2, extent_z).mean(axis=(1, 3))

def inject(field_in):
    return jnp.repeat(jnp.repeat(field_in, 2, axis=0), 2, axis=1)

def butler_volmer(concentration, phi_old, solid_pot, kinetic):
    over_pot = solid_pot - phi_old - 0.2 * jnp.log(concentration)
    return 2.0 * kinetic * jnp.sqrt(concentration) * jnp.sinh(0.5 * over_pot)

def coarse_solve(source, conduct):
    current = jnp.zeros_like(source)
    for _ in range(COARSE_SWEEPS):
        current = smooth(current, source, conduct, 0.0625, zero_padded)
    resid_coarse = residual_of(current, source, conduct, 0.0625, zero_padded)
    load = apply_level(zero_padded(jnp.ones_like(source)), conduct, 0.0625)
    return current + jnp.sum(resid_coarse) / jnp.sum(load)

def reference(conc_old, phi_old, solid_pot, phase_label, iface_block, iface_owner):
    diffusion = lookup(phase_label, DIFFUSION_TABLE)
    concentration = conc_old
    for _ in range(SWEEPS):
        middle, in_plane, along_z = split_parts(zero_padded(concentration))
        concentration = (conc_old + diffusion * (in_plane + along_z)) / (1.0 + 6.0 * diffusion)
    kinetic = lookup(phase_label, KINETIC_TABLE)
    flux_all = butler_volmer(concentration, phi_old, solid_pot, kinetic)
    owners = iface_owner[:, :, 0]
    group_ids = jnp.broadcast_to(jnp.arange(GROUPS, dtype=jnp.int32)[:, None], owners.shape)
    listed = jnp.zeros((GROUPS, N_DEV, BLK_DEV), jnp.float32).at[group_ids, owners, iface_block].set(1.0)
    listed = listed.reshape(GROUPS, N_DEV, CX, CY, CZ // 128).transpose(0, 2, 1, 3, 4).reshape(NX, NY, CZ // 128)
    flux = (flux_all.reshape(NX, NY, CZ // 128, 128) * listed[..., None]).reshape(NX, NY, CZ)
    conduct = lookup(phase_label, CONDUCT_TABLE) * conc_old
    source_fine = MASS * phi_old + flux
    potential = phi_old
    for _ in range(SMOOTH):
        potential = smooth(potential, source_fine, conduct, 1.0, zero_padded)
    resid_fine = residual_of(potential, source_fine, conduct, 1.0, zero_padded)
    conduct_mid = restrict(conduct)
    source_mid = restrict(resid_fine)
    error_mid = jnp.zeros_like(source_mid)
    for _ in range(SMOOTH):
        error_mid = smooth(error_mid, source_mid, conduct_mid, 0.25, zero_padded)
    resid_mid = residual_of(error_mid, source_mid, conduct_mid, 0.25, zero_padded)
    conduct_coarse = restrict(conduct_mid).reshape(GROUPS, CX // 4, NY // 4, CZ)
    source_coarse = restrict(resid_mid).reshape(GROUPS, CX // 4, NY // 4, CZ)
    error_coarse = jax.vmap(coarse_solve)(source_coarse, conduct_coarse)
    error_coarse = error_coarse.reshape(NX // 4, NY // 4, CZ)
    error_mid = error_mid + inject(error_coarse)
    for _ in range(SMOOTH):
        error_mid = smooth(error_mid, source_mid, conduct_mid, 0.25, zero_padded)
    potential = potential + inject(error_mid)
    for _ in range(SMOOTH):
        potential = smooth(potential, source_fine, conduct, 1.0, zero_padded)
    return (concentration, flux, potential)
```

```python
import jax
import jax.numpy as jnp
from jax import lax
from jax.experimental import pallas as pl
from jax.experimental.pallas import tpu as pltpu
from jax.sharding import PartitionSpec as P


F32 = jnp.float32
MASS = 0.05
OMEGA = 0.8
DIFFUSION_TABLE = (1.5, 0.1, 0.4)
CONDUCT_TABLE = (1.0, 0.3, 0.6)
KINETIC_TABLE = (0.2, 1.0, 0.5)
SWEEPS = 4
COARSE_SWEEPS = 8
HALO = 4
ZHALO = 16
LANES = 128
VMEM_LIMIT = 40 * 1024 * 1024


def shaped(*shape):
    return jax.ShapeDtypeStruct(shape, F32)


def call(kernel, outs, args, scratch=(), in_specs=None, flops=10**6, name=None):
    whole = pl.BlockSpec(memory_space=pltpu.VMEM)
    size = sum(4 * a.size for a in args) + sum(4 * o.size for o in outs)
    return pl.pallas_call(
        kernel,
        out_shape=tuple(outs),
        grid=(1,) if in_specs else (),
        in_specs=in_specs or [whole] * len(args),
        out_specs=tuple([whole] * len(outs)),
        scratch_shapes=list(scratch),
        compiler_params=pltpu.CompilerParams(vmem_limit_bytes=VMEM_LIMIT),
        cost_estimate=pl.CostEstimate(flops=flops, bytes_accessed=size, transcendentals=0),
        name=name,
    )(*args)


def vmem(*shape):
    return pltpu.VMEM(shape, F32)


def iota(shape, dim):
    return lax.broadcasted_iota(jnp.int32, shape, dim)


def pick(label, table):
    return jnp.where(label == 0, table[0], jnp.where(label == 1, table[1], table[2])).astype(F32)


def loop(low, high, body, unroll=1):
    lax.fori_loop(low, high, lambda i, c: (body(i), c)[1], 0, unroll=unroll)


def even(axis):
    return lax.rem(lax.axis_index(axis), 2) == 0


def along_y(v):
    return pltpu.roll(v, 1, 0) + pltpu.roll(v, v.shape[0] - 1, 0)


def along_z(v):
    n = v.shape[1]
    lane = iota(v.shape, 1)
    left = jnp.where(lane == 0, 0.0, pltpu.roll(v, 1, 1))
    right = jnp.where(lane == n - 1, 0.0, pltpu.roll(v, n - 1, 1))
    return left + right


def upper(shape=(8, 256)):
    return iota(shape, 0) < HALO


def pack_first(a, b):
    return jnp.where(upper(), a, pltpu.roll(b, HALO, 0))


def pack_last(a, b):
    return jnp.where(upper(), pltpu.roll(b, HALO, 0), a)


def halo_one(after, before):
    return jnp.where(upper(), after, before)


def halo_two(after, before):
    return pltpu.roll(jnp.where(upper(), before, after), HALO, 0)


def twice(tile, scratch):
    for h in range(2):
        part = tile[:, h * LANES : (h + 1) * LANES]
        scratch[h, pl.ds(0, 8, stride=2), :] = part
        scratch[h, pl.ds(1, 8, stride=2), :] = part
    return jnp.concatenate([scratch[0], scratch[1]], axis=1)


def pair_rows(v, scratch):
    half = v.shape[0] // 2
    parts = []
    for h in range(2):
        scratch[h] = v[:, h * LANES : (h + 1) * LANES]
        parts.append(scratch[h, pl.ds(0, half, stride=2), :] + scratch[h, pl.ds(1, half, stride=2), :])
    return jnp.concatenate(parts, axis=1)


def z_chunk(low, high, j, width):
    start = j * width - ZHALO
    size = low.shape[1]
    a = pltpu.roll(low, (-start) % size, 1)[:, :LANES]
    b = pltpu.roll(high, (64 - start) % size, 1)[:, :LANES]
    lane = iota((8, LANES), 1)
    z = start + lax.rem(lane, 64)
    return jnp.where((z >= 0) & (z < size), jnp.where(lane < 64, a, b), 0.0)


def first_pack_kernel(conc, label, phi, pay_a, pay_b, mid, pairs):
    nx = conc.shape[0]
    is_even = even("dev")

    def put(index, first, last):
        pay_a[index] = jnp.where(is_even, last, first)
        pay_b[index] = jnp.where(is_even, first, last)

    def edges(i):
        a, b = conc[i, 0:8, :], label[i, 0:8, :].astype(F32)
        c, d = conc[i, 24:32, :], label[i, 24:32, :].astype(F32)
        put(i, pack_first(a, b), pack_last(c, d))

    loop(0, nx, edges, 4)

    def phi_edges(i):
        put(
            nx + i,
            pack_first(phi[i, 0:8, :], phi[i + nx // 2, 0:8, :]),
            pack_last(phi[i, 24:32, :], phi[i + nx // 2, 24:32, :]),
        )

    loop(0, nx // 2, phi_edges, 4)

    def coarsen(i):
        total = conc[2 * i] * pick(label[2 * i], CONDUCT_TABLE) + conc[2 * i + 1] * pick(label[2 * i + 1], CONDUCT_TABLE)
        mid[i] = 0.25 * pair_rows(total, pairs.at[i])

    loop(0, nx // 2, coarsen, 2)

    def mid_edges(i):
        put(
            nx + nx // 2 + i,
            pack_first(mid[i, 0:8, :], mid[i + nx // 4, 0:8, :]),
            pack_last(mid[i, 8:16, :], mid[i + nx // 4, 8:16, :]),
        )

    loop(0, nx // 4, mid_edges, 4)


def list_kernel(owner, block, mid, post, pairs, coarse):
    peers = post.shape[0]
    entries = owner.shape[1]
    row = owner[...] * 32 + lax.div(block[...], 64)
    column = lax.rem(block[...], 64)
    hit_row = (iota((peers * 32, entries), 0) == row).astype(jnp.bfloat16)
    hit_column = (iota((LANES, entries), 0) == column).astype(jnp.bfloat16)
    named = lax.dot_general(hit_row, hit_column, (((1,), (1,)), ((), ())), preferred_element_type=F32)
    for j in range(peers):
        for r in range(4):
            post[j, r] = named[j * 32 + r * 8 : j * 32 + r * 8 + 8, :]
    for i in range(8):
        coarse[i] = 0.25 * pair_rows(mid[2 * i] + mid[2 * i + 1], pairs.at[i])
    for j in range(peers):
        for i in range(4):
            post[j, 4 + i] = z_chunk(coarse[i], coarse[i + 4], j, 256 // peers)


def first_pack_x_kernel(conc_f, conc_l, label_f, label_l, phi_f, phi_l, mid_f, mid_l, r_a, r_b, pay_a, pay_b):
    is_even_d, is_even_g = even("dev"), even("grp")
    nx = 32

    def halos(index):
        a, b = r_a[index], r_b[index]
        return jnp.where(is_even_d, a, b), jnp.where(is_even_d, b, a)

    def side(pay, conc, label, phi, mid, x0):
        for k in range(HALO):
            x = x0 + k
            after, before = halos(x)
            for t in range(4):
                rows = slice(8 * t, 8 * t + 8)
                pay[5 * k + t] = conc[k, rows, :]
                pay[20 + 5 * k + t] = label[k, rows, :].astype(F32)
                pay[40 + 5 * k + t] = phi[k, rows, :]
            pay[5 * k + 4] = halo_one(after, before)
            pay[20 + 5 * k + 4] = halo_two(after, before)
            after, before = halos(nx + x % (nx // 2))
            pay[40 + 5 * k + 4] = (halo_one if x < nx // 2 else halo_two)(after, before)
            m = (0 if x0 == 0 else nx // 2 - HALO) + k
            for t in range(2):
                pay[60 + 3 * k + t] = mid[k, 8 * t : 8 * t + 8, :]
            after, before = halos(nx + nx // 2 + m % (nx // 4))
            pay[60 + 3 * k + 2] = (halo_one if m < nx // 4 else halo_two)(after, before)

    def write(pay, first):
        if first:
            side(pay, conc_f, label_f, phi_f, mid_f, 0)
        else:
            side(pay, conc_l, label_l, phi_l, mid_l, nx - HALO)

    @pl.when(is_even_g)
    def _():
        write(pay_a, False)
        write(pay_b, True)

    @pl.when(jnp.logical_not(is_even_g))
    def _():
        write(pay_a, True)
        write(pay_b, False)


def y_sides(r_a, r_b, index):
    is_even = even("dev")
    a, b = r_a[index], r_b[index]
    return jnp.where(is_even, a, b), jnp.where(is_even, b, a)


def x_sides(r_a, r_b, index):
    is_even = even("grp")
    a, b = r_a[index], r_b[index]
    return jnp.where(is_even, a, b), jnp.where(is_even, b, a)


def conc_kernel(conc, label, phi, solid, y_a, y_b, x_a, x_b, lists, out, flux, pay_a, pay_b, one, two, gain, base, marked):
    nx = conc.shape[0]
    ratio = tuple(d / (1.0 + 6.0 * d) for d in DIFFUSION_TABLE)
    inverse = tuple(1.0 / (1.0 + 6.0 * d) for d in DIFFUSION_TABLE)

    def put(x, rows, c, lab):
        one[x, rows, :] = c
        gain[x, rows, :] = jnp.where(c > 0.0, pick(lab, ratio), 0.0)
        base[x, rows, :] = c * pick(lab, inverse)

    def own(i):
        put(HALO + i, slice(0, 32), conc[i], label[i])
        after, before = y_sides(y_a, y_b, i)
        put(HALO + i, slice(32, 40), halo_one(after, before), halo_two(after, before))

    loop(0, nx, own, 2)
    for k in range(HALO):
        for t in range(5):
            rows = slice(8 * t, 8 * t + 8)
            c_after, c_before = x_sides(x_a, x_b, 5 * k + t)
            l_after, l_before = x_sides(x_a, x_b, 20 + 5 * k + t)
            put(k, rows, c_before, l_before)
            put(HALO + nx + k, rows, c_after, l_after)

    def stencil(old, x):
        mid = old[x]
        return base[x] + gain[x] * ((old[x - 1] + old[x + 1]) + (along_y(mid) + along_z(mid)))

    fields = (one, two)
    for s in range(1, SWEEPS):
        old, new = fields[(s - 1) % 2], fields[s % 2]

        def sweep(x, old=old, new=new):
            new[x] = stencil(old, x)

        loop(s, nx + 2 * HALO - s, sweep, 4 if s % 2 == 0 else 2)

    old = fields[(SWEEPS - 1) % 2]
    row = iota((32, LANES), 0)
    col = iota((32, LANES), 1)
    is_row = lax.div(col, 2) == row
    spread = (lax.rem(iota((LANES, 256), 0), 2) == lax.div(iota((LANES, 256), 1), LANES)).astype(jnp.bfloat16)
    named = jnp.sum(lists[:, 0:4], axis=0).reshape(32, LANES)
    for i in range(32):
        marked[i] = jnp.broadcast_to(named[i : i + 1, :], (8, LANES))

    def last(i):
        c = stencil(old, HALO + i)[0:32, :]
        out[i] = c
        marks = jnp.where(is_row, jnp.concatenate([marked[i]] * 4, axis=0), 0.0).astype(jnp.bfloat16)
        listed = jnp.dot(marks, spread, preferred_element_type=F32) > 0.5
        drive = 0.5 * (solid[i] - phi[i])
        logc = jnp.log(c)
        value = jnp.exp(drive + 0.4 * logc) - jnp.exp(0.6 * logc - drive)
        flux[i] = jnp.where(listed, pick(label[i], KINETIC_TABLE) * value, 0.0)

    loop(0, nx, last, 2)
    is_even = even("dev")

    def edges(i):
        first = pack_first(flux[i, 0:8, :], flux[i + nx // 2, 0:8, :])
        final = pack_last(flux[i, 24:32, :], flux[i + nx // 2, 24:32, :])
        pay_a[i] = jnp.where(is_even, final, first)
        pay_b[i] = jnp.where(is_even, first, final)

    loop(0, nx // 2, edges, 4)


def ready_kernel(conc, label, phi, y_a, y_b, x_a, x_b, weight, scale, share, start, field):
    nx = conc.shape[0]

    def put(x, rows, c, lab, p):
        conduct = c * pick(lab, CONDUCT_TABLE)
        factor = OMEGA / (MASS + 6.0 * conduct)
        weight[x, rows, :] = conduct * factor
        scale[x, rows, :] = factor
        share[x, rows, :] = MASS * p * factor
        field[x, rows, :] = p

    def own(i):
        put(HALO + i, slice(0, 32), conc[i], label[i], phi[i])

    loop(0, nx, own, 2)

    def sides(half, first, second):
        def body(i):
            after, before = y_sides(y_a, y_b, nx + i)
            p = second(after, before)
            after, before = y_sides(y_a, y_b, half * (nx // 2) + i)
            put(HALO + half * (nx // 2) + i, slice(32, 40), halo_one(after, before), halo_two(after, before), p)

        loop(0, nx // 2, body, 2)

    sides(0, halo_one, halo_one)
    sides(1, halo_one, halo_two)
    for k in range(HALO):
        for t in range(5):
            rows = slice(8 * t, 8 * t + 8)
            c_after, c_before = x_sides(x_a, x_b, 5 * k + t)
            l_after, l_before = x_sides(x_a, x_b, 20 + 5 * k + t)
            p_after, p_before = x_sides(x_a, x_b, 40 + 5 * k + t)
            put(k, rows, c_before, l_before, p_before)
            put(HALO + nx + k, rows, c_after, l_after, p_after)

    def sweep(x):
        p = field[x]
        around = (field[x - 1] + field[x + 1]) + (along_y(p) + along_z(p))
        start[x] = 0.2 * p + share[x] + weight[x] * around

    loop(1, nx + 2 * HALO - 1, sweep, 2)


def flux_pack_x_kernel(flux_f, flux_l, r_a, r_b, pay_a, pay_b):
    is_even = even("grp")
    nx = 32
    for k in range(HALO):
        for t in range(4):
            rows = slice(8 * t, 8 * t + 8)
            first, last = flux_f[k, rows, :], flux_l[k, rows, :]
            pay_a[5 * k + t] = jnp.where(is_even, last, first)
            pay_b[5 * k + t] = jnp.where(is_even, first, last)
        first = halo_one(*y_sides(r_a, r_b, k))
        last = halo_two(*y_sides(r_a, r_b, nx // 2 - HALO + k))
        pay_a[5 * k + 4] = jnp.where(is_even, last, first)
        pay_b[5 * k + 4] = jnp.where(is_even, first, last)


def potential_kernel(
    flux, y_a, y_b, x_a, x_b, weight, scale, share, start, after_two, source, source_mid, pay_a, pay_b, field, pairs
):
    nx = flux.shape[0]

    def put(x, rows, f):
        part = scale[x, rows, :] * f
        source[x, rows, :] = share[x, rows, :] + part
        field[x, rows, :] = start[x, rows, :] + part

    def own(i):
        put(HALO + i, slice(0, 32), flux[i])

    loop(0, nx, own, 2)

    def low(i):
        put(HALO + i, slice(32, 40), halo_one(*y_sides(y_a, y_b, i)))

    loop(0, nx // 2, low, 4)

    def high(i):
        put(HALO + nx // 2 + i, slice(32, 40), halo_two(*y_sides(y_a, y_b, i)))

    loop(0, nx // 2, high, 4)
    for k in range(1, HALO):
        for t in range(5):
            rows = slice(8 * t, 8 * t + 8)
            put(k, rows, x_sides(x_a, x_b, 5 * k + t)[1])
    for k in range(HALO - 1):
        for t in range(5):
            rows = slice(8 * t, 8 * t + 8)
            put(HALO + nx + k, rows, x_sides(x_a, x_b, 5 * k + t)[0])

    def around(values, x):
        v = values[x]
        return v, weight[x] * ((values[x - 1] + values[x + 1]) + (along_y(v) + along_z(v)))

    def sweep(x):
        v, near = around(field, x)
        after_two[x] = 0.2 * v + (source[x] + near)

    loop(2, nx + 2 * HALO - 2, sweep, 2)

    def remainder(x):
        v, near = around(after_two, x)
        return ((source[x] - OMEGA * v) + near)[0:32, :] / scale[x, 0:32, :]

    def coarsen(i):
        x = HALO + 2 * i
        source_mid[i] = 0.25 * pair_rows(remainder(x) + remainder(x + 1), pairs.at[i])

    loop(0, nx // 2, coarsen, 1)
    mid_edges(source_mid, pay_a, pay_b)


def mid_edges(field, pay_a, pay_b):
    is_even = even("dev")
    n = field.shape[0]
    for i in range(n // 2):
        first = pack_first(field[i, 0:8, :], field[i + n // 2, 0:8, :])
        final = pack_last(field[i, 8:16, :], field[i + n // 2, 8:16, :])
        pay_a[i] = jnp.where(is_even, final, first)
        pay_b[i] = jnp.where(is_even, first, final)


def mid_pack_x_kernel(field, r_a, r_b, pay_a, pay_b):
    is_even = even("grp")
    n = field.shape[0]
    for k in range(HALO):
        for t in range(2):
            rows = slice(8 * t, 8 * t + 8)
            first, last = field[k, rows, :], field[n - HALO + k, rows, :]
            pay_a[3 * k + t] = jnp.where(is_even, last, first)
            pay_b[3 * k + t] = jnp.where(is_even, first, last)
        first = halo_one(*y_sides(r_a, r_b, k))
        last = halo_two(*y_sides(r_a, r_b, n // 2 - HALO + k))
        pay_a[3 * k + 2] = jnp.where(is_even, last, first)
        pay_b[3 * k + 2] = jnp.where(is_even, first, last)


def mid_kernel(
    source_own, conduct_own, f_a, f_b, fx_a, fx_b, y_a, y_b, x_a, x_b, after_two, source, weight, post, scale, field,
    pairs, pairs_2, coarse
):
    n = source_own.shape[0]

    def put(x, rows, b, conduct):
        factor = OMEGA / (MASS + 3.0 * conduct)
        weight[x, rows, :] = conduct * factor
        scale[x, rows, :] = factor
        source[x, rows, :] = factor * b

    for i in range(n):
        put(HALO + i, slice(0, 16), source_own[i], conduct_own[i])
        halo = halo_one if i < n // 2 else halo_two
        put(
            HALO + i,
            slice(16, 24),
            halo(*y_sides(y_a, y_b, i % (n // 2))),
            halo(*y_sides(f_a, f_b, 48 + i % (n // 2))),
        )
    for k in range(HALO):
        for t in range(3):
            rows = slice(8 * t, 8 * t + 8)
            b_after, b_before = x_sides(x_a, x_b, 3 * k + t)
            c_after, c_before = x_sides(fx_a, fx_b, 60 + 3 * k + t)
            put(k, rows, b_before, c_before)
            put(HALO + n + k, rows, b_after, c_after)

    def around(values, x):
        v = values[x]
        return v, weight[x] * (0.25 * ((values[x - 1] + values[x + 1]) + along_y(v)) + along_z(v))

    def sweep(x):
        v, near = around(source, x)
        after_two[x] = 0.2 * v + (source[x] + near)

    loop(1, n + 2 * HALO - 1, sweep, 2)

    def remainder(x):
        v, near = around(after_two, x)
        return ((source[x] - OMEGA * v) + near)[0:16, :] / scale[x, 0:16, :]

    for i in range(n // 2):
        x = HALO + 2 * i
        coarse[i] = 0.25 * pair_rows(remainder(x) + remainder(x + 1), pairs.at[i])
    peers = post.shape[0]
    for j in range(peers):
        for i in range(4):
            post[j, i] = z_chunk(coarse[i], coarse[i + 4], j, 256 // peers)


def coarse_kernel(recv, conduct, post, source, weight, scale, one, two):
    peers = recv.shape[0]
    ny = 8 * peers
    width = 256 // peers
    w = 0.0625
    lane = iota((ny, LANES), 1)
    row = iota((ny, LANES), 0)
    right_half = lane >= 64
    l64 = lax.rem(lane, 64)
    z = lax.axis_index("dev") * width - ZHALO + l64
    valid = (l64 >= ZHALO) & (l64 < ZHALO + width)
    no_z = ((z == 0) | (z == 255)).astype(F32)
    no_y = ((row == 0) | (row == ny - 1)).astype(F32)
    load_sum = jnp.zeros((ny, LANES), F32)
    for i in range(4):
        k = jnp.concatenate([conduct[s, 4 + i] for s in range(peers)], axis=0)
        b = jnp.concatenate([recv[s, i] for s in range(peers)], axis=0)
        factor = OMEGA / (MASS + 2.25 * k)
        weight[i] = k * factor
        scale[i] = factor
        source[i] = factor * b
        no_x = 0.0
        if i == 0:
            no_x = 1.0 - right_half.astype(F32)
        if i == 3:
            no_x = right_half.astype(F32)
        load_sum += jnp.where(valid, MASS + k * (w * (no_x + no_y) + no_z), 0.0)

    def around(values, i):
        v = values[i]
        if i == 0:
            back = jnp.where(right_half, pltpu.roll(values[3], 64, 1), 0.0)
        else:
            back = values[i - 1]
        if i == 3:
            front = jnp.where(right_half, 0.0, pltpu.roll(values[0], 64, 1))
        else:
            front = values[i + 1]
        up = jnp.where(row == 0, 0.0, pltpu.roll(v, 1, 0))
        down = jnp.where(row == ny - 1, 0.0, pltpu.roll(v, ny - 1, 0))
        sides = pltpu.roll(v, 1, 1) + pltpu.roll(v, LANES - 1, 1)
        return v, weight[i] * (w * ((back + front) + (up + down)) + sides)

    old = source
    for s in range(1, COARSE_SWEEPS):
        new = one if s % 2 else two
        for i in range(4):
            v, near = around(old, i)
            new[i] = 0.2 * v + (source[i] + near)
        old = new
    resid_sum = jnp.zeros((ny, LANES), F32)
    for i in range(4):
        v, near = around(old, i)
        resid_sum += jnp.where(valid, ((source[i] - OMEGA * v) + near) / scale[i], 0.0)
    resid_tile = jnp.sum(resid_sum.reshape(peers, 8, LANES), axis=0)
    load_tile = jnp.sum(load_sum.reshape(peers, 8, LANES), axis=0)
    per = LANES // width
    vregs = 16 // per
    tile_lane = iota((8, LANES), 1)
    zero = jnp.zeros((8, LANES), F32)
    for d in range(peers):
        for q in range(vregs):
            total = zero
            for g in range(per):
                x, t = divmod(q * per + g, 2)
                at = 64 * (x // 4) + ZHALO
                tile = lambda s: old[x % 4, 8 * s : 8 * s + 8, :] if 0 <= s < peers else zero
                value = tile(d) if t == 0 else jnp.where(upper((8, LANES)), tile(d + 1), tile(d - 1))
                shift = (g * width - at) % LANES
                if shift:
                    value = pltpu.roll(value, shift, 1)
                mine = (tile_lane >= g * width) & (tile_lane < (g + 1) * width)
                total = jnp.where(mine, value, total)
            post[d, q] = total
        post[d, vregs] = resid_tile
        post[d, vregs + 1] = load_tile


def spread_kernel(recv, error, pay_a, pay_b):
    peers = recv.shape[0]
    width = 256 // peers
    per = LANES // width
    vregs = 16 // per
    resid = jnp.sum(jnp.sum(recv[:, vregs], axis=0))
    load = jnp.sum(jnp.sum(recv[:, vregs + 1], axis=0))
    shift_c = (jnp.full((8, LANES), resid, F32) / jnp.full((8, LANES), load, F32))
    tile_lane = iota((8, LANES), 1)
    for x in range(8):
        for t in range(2):
            q, g = divmod(2 * x + t, per)
            for h in range(2):
                total = jnp.zeros((8, LANES), F32)
                for j in range(peers // 2):
                    shift = ((j - g) * width) % LANES
                    value = recv[h * (peers // 2) + j, q]
                    if shift:
                        value = pltpu.roll(value, shift, 1)
                    mine = (tile_lane >= j * width) & (tile_lane < (j + 1) * width)
                    total = jnp.where(mine, value, total)
                error[x, 8 * t : 8 * t + 8, h * LANES : (h + 1) * LANES] = total + shift_c
    is_even = even("grp")
    for k in range(2):
        pay_a[k] = jnp.where(is_even, error[6 + k], error[k])
        pay_b[k] = jnp.where(is_even, error[k], error[6 + k])


def finish_kernel(
    error, x_a, x_b, mid_two, mid_source, mid_weight, fine_two, fine_source, fine_weight, out, one, two, fine_one, fine_last, dup
):
    n = mid_two.shape[0]
    nf = fine_two.shape[0]

    def squeeze(tile):
        return jnp.where(iota((8, 256), 0) < 2, tile, pltpu.roll(tile, 4, 0))

    after, before = x_sides(x_a, x_b, slice(0, 2))
    for c in range(-2, 10):
        plane = before[c + 2] if c < 0 else (after[c - 8] if c >= 8 else error[c])
        spread = jnp.concatenate([twice(plane[0:8], dup.at[0]), twice(squeeze(plane[8:16]), dup.at[1])[0:8]], axis=0)
        for x in (2 * c + HALO, 2 * c + 1 + HALO):
            one[x] = jnp.where(mid_weight[x] > 0.0, mid_two[x] + spread, 0.0)

    def around(values, weights, x, w):
        v = values[x]
        inner = (values[x - 1] + values[x + 1]) + along_y(v)
        return 0.2 * v + weights[x] * (w * inner + along_z(v))

    for s, (old, new) in ((2, (one, two)), (3, (two, one))):

        def sweep(x, old=old, new=new):
            new[x] = mid_source[x] + around(old, mid_weight, x, 0.25)

        loop(s, n - s, sweep, 2)

    def lift(m):
        plane = one[m]
        spread = jnp.concatenate(
            [twice(plane[0:8], dup.at[0]), twice(plane[8:16], dup.at[1]), twice(squeeze(plane[16:24]), dup.at[2])[0:8]],
            axis=0,
        )
        x = 2 * m - HALO
        fine_one[x] = fine_two[x] + spread
        fine_one[x + 1] = fine_two[x + 1] + spread

    loop(3, n - 3, lift, 1)

    def sweep_one(x):
        fine_last[x] = fine_source[x] + around(fine_one, fine_weight, x, 1.0)

    loop(3, nf - 3, sweep_one, 2)

    def sweep_two(i):
        x = HALO + i
        out[i] = (fine_source[x] + around(fine_last, fine_weight, x, 1.0))[0:32, :]

    loop(0, out.shape[0], sweep_two, 2)


def swap(pay_a, pay_b, axis):
    size = lax.axis_size(axis)
    pairs_a = [(i, i + 1) for i in range(0, size - 1, 2)]
    pairs_b = [(i, i + 1) for i in range(1, size - 1, 2)]
    both = lambda pairs: pairs + [(j, i) for i, j in pairs]
    return lax.ppermute(pay_a, axis, both(pairs_a)), lax.ppermute(pay_b, axis, both(pairs_b))


def edge_specs(width, length):
    shape = lambda n: (HALO,) + n
    first = pl.BlockSpec(shape((length, 256)), lambda i: (0, 0, 0))
    last = pl.BlockSpec(shape((length, 256)), lambda i: (width // HALO - 1, 0, 0))
    return [first, last]


def body(conc_old, phi_old, solid_pot, phase_label, iface_block, iface_owner):
    peers = lax.axis_size("dev")
    nx = conc_old.shape[0]
    half = nx // 2
    whole = pl.BlockSpec(memory_space=pltpu.VMEM)
    ext = (nx + 2 * HALO, nx + 2 * HALO, 256)
    ext_mid = (half + 2 * HALO, half + 2 * HALO, 256)

    pay_y = nx + half + half // 2
    pay_a, pay_b, conduct_mid = call(
        first_pack_kernel,
        [shaped(pay_y, 8, 256), shaped(pay_y, 8, 256), shaped(half, half, 256)],
        [conc_old, phase_label, phi_old],
        [vmem(half, 2, nx, LANES)],
        name="first_pack",
    )
    y_a, y_b = swap(pay_a, pay_b, "dev")
    (named,) = call(
        list_kernel,
        [shaped(peers, 8, 8, LANES)],
        [iface_owner.reshape(1, -1), iface_block, conduct_mid],
        [vmem(8, 2, half, LANES), vmem(8, 8, 256)],
        name="list_pack",
    )
    named = lax.all_to_all(named, "dev", split_axis=0, concat_axis=0, tiled=True)
    pay_x = HALO * 18
    pay_a, pay_b = call(
        first_pack_x_kernel,
        [shaped(pay_x, 8, 256)] * 2,
        [conc_old, conc_old, phase_label, phase_label, phi_old, phi_old, conduct_mid, conduct_mid, y_a, y_b],
        in_specs=edge_specs(nx, nx) * 3 + edge_specs(half, half) + [whole] * 2,
        name="first_pack_x",
    )
    x_a, x_b = swap(pay_a, pay_b, "grp")

    concentration, flux, pay_a, pay_b = call(
        conc_kernel,
        [shaped(nx, nx, 256), shaped(nx, nx, 256), shaped(half, 8, 256), shaped(half, 8, 256)],
        [conc_old, phase_label, phi_old, solid_pot, y_a, y_b, x_a, x_b, named],
        [vmem(*ext)] * 4 + [vmem(32, 8, LANES)],
        name="electrolyte",
    )
    f_a, f_b = swap(pay_a, pay_b, "dev")
    weight, scale, share, start = call(
        ready_kernel,
        [shaped(*ext)] * 4,
        [conc_old, phase_label, phi_old, y_a, y_b, x_a, x_b],
        [vmem(*ext)],
        name="ready",
    )
    pay_a, pay_b = call(
        flux_pack_x_kernel,
        [shaped(5 * HALO, 8, 256)] * 2,
        [flux, flux, f_a, f_b],
        in_specs=edge_specs(nx, nx) + [whole] * 2,
        name="flux_pack_x",
    )
    fx_a, fx_b = swap(pay_a, pay_b, "grp")
    fine_two, fine_source, source_mid, pay_a, pay_b = call(
        potential_kernel,
        [shaped(*ext), shaped(*ext), shaped(half, half, 256), shaped(half // 2, 8, 256), shaped(half // 2, 8, 256)],
        [flux, f_a, f_b, fx_a, fx_b, weight, scale, share, start],
        [vmem(*ext), vmem(half, 2, nx, LANES)],
        name="potential",
    )
    m_a, m_b = swap(pay_a, pay_b, "dev")
    pay_a, pay_b = call(mid_pack_x_kernel, [shaped(3 * HALO, 8, 256)] * 2, [source_mid, m_a, m_b], name="mid_pack_x")
    mx_a, mx_b = swap(pay_a, pay_b, "grp")
    mid_two, mid_source, mid_weight, post = call(
        mid_kernel,
        [shaped(*ext_mid)] * 3 + [shaped(peers, 4, 8, LANES)],
        [source_mid, conduct_mid, y_a, y_b, x_a, x_b, m_a, m_b, mx_a, mx_b],
        [vmem(*ext_mid), vmem(*ext_mid), vmem(8, 2, half, LANES), vmem(8, 2, half, LANES), vmem(8, 8, 256)],
        name="middle",
    )
    post = lax.all_to_all(post, "dev", split_axis=0, concat_axis=0, tiled=True)
    tiles = 16 * (256 // peers) // LANES + 2
    slab = [vmem(4, 8 * peers, LANES)]
    (post,) = call(coarse_kernel, [shaped(peers, tiles, 8, LANES)], [post, named], slab * 5, name="coarse")
    post = lax.all_to_all(post, "dev", split_axis=0, concat_axis=0, tiled=True)
    error, pay_a, pay_b = call(
        spread_kernel, [shaped(8, 16, 256), shaped(2, 16, 256), shaped(2, 16, 256)], [post], name="spread"
    )
    e_a, e_b = swap(pay_a, pay_b, "grp")
    (potential,) = call(
        finish_kernel,
        [shaped(nx, nx, 256)],
        [error, e_a, e_b, mid_two, mid_source, mid_weight, fine_two, fine_source, weight],
        [vmem(*ext_mid), vmem(*ext_mid), vmem(*ext), vmem(*ext), vmem(3, 2, 16, LANES)],
        name="finish",
    )
    return (concentration, flux, potential)


def solution(mesh):
    brick = P("grp", "dev", None)
    return jax.shard_map(
        body,
        mesh=mesh,
        in_specs=(brick, brick, brick, brick, P("grp", "dev"), brick),
        out_specs=(brick, brick, brick),
        check_vma=False,
    )
```

```python
import jax
import jax.numpy as jnp
from jax import lax
from jax.experimental import pallas as pl
from jax.experimental.pallas import tpu as pltpu
from jax.sharding import PartitionSpec as P


F32 = jnp.float32
MASS = 0.05
OMEGA = 0.8
DIFFUSION_TABLE = (1.5, 0.1, 0.4)
CONDUCT_TABLE = (1.0, 0.3, 0.6)
KINETIC_TABLE = (0.2, 1.0, 0.5)
SWEEPS = 4
COARSE_SWEEPS = 8
COARSE_NEAR = 8
HALO = 4
LANES = 128
VMEM_LIMIT = 28 * 1024 * 1024


def shaped(*shape):
    return jax.ShapeDtypeStruct(shape, F32)


WHOLE = pl.BlockSpec(memory_space=pltpu.VMEM)
FAR = pl.BlockSpec(memory_space=pltpu.HBM)


def call(kernel, outs, args, scratch=(), in_specs=None, out_specs=None, flops=10**6, name=None):
    size = sum(4 * a.size for a in args) + sum(4 * o.size for o in outs)
    return pl.pallas_call(
        kernel,
        out_shape=tuple(outs),
        in_specs=in_specs or [WHOLE] * len(args),
        out_specs=tuple(out_specs or [WHOLE] * len(outs)),
        scratch_shapes=list(scratch),
        compiler_params=pltpu.CompilerParams(vmem_limit_bytes=VMEM_LIMIT),
        cost_estimate=pl.CostEstimate(flops=flops, bytes_accessed=size, transcendentals=0),
        name=name,
    )(*args)


def vmem(*shape):
    return pltpu.VMEM(shape, F32)


def iota(shape, dim):
    return lax.broadcasted_iota(jnp.int32, shape, dim)


def pick(label, table):
    return jnp.where(label == 0, table[0], jnp.where(label == 1, table[1], table[2])).astype(F32)


def loop(low, high, body, unroll=8):
    steps = (high - low) // unroll

    def step(i, carry):
        for u in range(unroll):
            body(low + i * unroll + u)
        return carry

    if steps > 1:
        lax.fori_loop(0, steps, step, 0)
    else:
        steps = 0
    for x in range(low + steps * unroll, high):
        body(x)


def even(axis):
    return lax.rem(lax.axis_index(axis), 2) == 0


def along_y(v):
    return pltpu.roll(v, 1, 0) + pltpu.roll(v, v.shape[0] - 1, 0)


def along_z(v):
    low, high = v[:, :LANES], v[:, LANES:]
    lane = iota(low.shape, 1)
    first, last = lane == 0, lane == LANES - 1
    low_up, high_up = pltpu.roll(low, 1, 1), pltpu.roll(high, 1, 1)
    low_down, high_down = pltpu.roll(low, LANES - 1, 1), pltpu.roll(high, LANES - 1, 1)
    low_sum = jnp.where(first, 0.0, low_up) + jnp.where(last, high_down, low_down)
    high_sum = jnp.where(first, low_up, high_up) + jnp.where(last, 0.0, high_down)
    return jnp.concatenate([low_sum, high_sum], axis=1)


def upper(shape=(8, 256)):
    return iota(shape, 0) < HALO


def twice(tile, scratch):
    for h in range(2):
        part = tile[:, h * LANES : (h + 1) * LANES]
        scratch[h, pl.ds(0, 8, stride=2), :] = part
        scratch[h, pl.ds(1, 8, stride=2), :] = part
    return jnp.concatenate([scratch[0], scratch[1]], axis=1)


def pair_rows(v, scratch):
    half = v.shape[0] // 2
    parts = []
    for h in range(2):
        scratch[h] = v[:, h * LANES : (h + 1) * LANES]
        parts.append(scratch[h, pl.ds(0, half, stride=2), :] + scratch[h, pl.ds(1, half, stride=2), :])
    return jnp.concatenate(parts, axis=1)


def either(flag, if_true, if_false):
    return jnp.where(flag, if_true, if_false)


def y_sides(r_a, r_b, at, count):
    flag = even("dev")
    a, b = r_a[at : at + count, :], r_b[at : at + count, :]
    return either(flag, a, b), either(flag, b, a)


def x_sides(r_a, r_b, index):
    flag = even("grp")
    a, b = r_a[index], r_b[index]
    return either(flag, a, b), either(flag, b, a)


def send_y(pay_a, pay_b, at, first, last):
    flag = even("dev")
    n = first.shape[0]
    pay_a[at : at + n, :] = either(flag, last, first)
    pay_b[at : at + n, :] = either(flag, first, last)


def send_x(pay_a, pay_b, index, first, last):
    flag = even("grp")
    pay_a[index] = either(flag, last, first)
    pay_b[index] = either(flag, first, last)


def halo_tile(after, before):
    parts = [after]
    if after.shape[0] < HALO:
        parts.append(jnp.zeros((2 * HALO - 2 * after.shape[0], after.shape[1]), F32))
    return jnp.concatenate(parts + [before], axis=0)


def first_pack_kernel(conc, label, owner, block, pay_a, pay_b, c_first, c_last, l_first, l_last, sems):
    nx = conc.shape[0]
    copies = []
    for i, (ref, at, to) in enumerate(((conc, 0, c_first), (conc, 24, c_last), (label, 0, l_first), (label, 24, l_last))):
        copies.append(pltpu.make_async_copy(ref.at[:, pl.ds(at, 8), :], to, sems.at[i]))
        copies[-1].start()
    named = jnp.concatenate([owner[...], block[...], jnp.zeros((6, 256), jnp.int32)], axis=0).astype(F32)
    pay_a[7 * nx : 7 * nx + 8, :] = named
    pay_b[7 * nx : 7 * nx + 8, :] = named
    for c in copies:
        c.wait()
    for x in range(nx):
        send_y(pay_a, pay_b, 7 * x, c_first[x, 0:4, :], c_last[x, 4:8, :])
        send_y(pay_a, pay_b, 7 * x + 4, l_first[x, 0:3, :].astype(F32), l_last[x, 5:8, :].astype(F32))


def own_kernel(conc, label, phi, mid, coarse, pay_a, pay_b, pairs, pairs_2):
    nx = conc.shape[0]
    half = nx // 2

    def coarsen(i):
        total = conc[2 * i] * pick(label[2 * i], CONDUCT_TABLE) + conc[2 * i + 1] * pick(label[2 * i + 1], CONDUCT_TABLE)
        mid[i] = 0.25 * pair_rows(total, pairs.at[i])

    loop(0, half, coarsen, 4)
    for i in range(half // 2):
        coarse[i] = 0.25 * pair_rows(mid[2 * i] + mid[2 * i + 1], pairs_2.at[i])
    for k in range(HALO):
        for t in range(4):
            rows = slice(8 * t, 8 * t + 8)
            send_x(pay_a, pay_b, 4 * k + t, phi[k, rows, :], phi[nx - HALO + k, rows, :])
        for t in range(2):
            rows = slice(8 * t, 8 * t + 8)
            send_x(pay_a, pay_b, 16 + 2 * k + t, mid[k, rows, :], mid[half - HALO + k, rows, :])


def first_pack_x_kernel(conc, label, r_a, r_b, token, pay_a, pay_b):
    nx = conc.shape[0]

    def plane(ref, k, t, offset, count):
        if t < 4:
            return ref[k, 8 * t : 8 * t + 8, :].astype(F32)
        return halo_tile(*y_sides(r_a, r_b, 7 * k + offset, count))

    for t in range(5):
        for k in range(HALO):
            send_x(pay_a, pay_b, 5 * k + t, plane(conc, k, t, 0, 4), plane(conc, nx - HALO + k, t, 0, 4))
        for k in range(3):
            send_x(pay_a, pay_b, 20 + 5 * k + t, plane(label, k, t, 4, 3), plane(label, nx - 3 + k, t, 4, 3))


def second_pack_kernel(phi, mid, coarse, x_a, x_b, pay_a, pay_b, pay_c, pay_d):
    nx = phi.shape[0]
    half = nx // 2
    for x in range(nx):
        send_y(pay_a, pay_b, 4 * (HALO + x), phi[x, 0:4, :], phi[x, 28:32, :])
    for k in range(HALO):
        for t, at in ((0, slice(0, 4)), (3, slice(4, 8))):
            after, before = x_sides(x_a, x_b, 4 * k + t)
            if t == 0:
                first_after, first_before = after[at], before[at]
            else:
                last_after, last_before = after[at], before[at]
        send_y(pay_a, pay_b, 4 * k, first_before, last_before)
        send_y(pay_a, pay_b, 4 * (HALO + nx + k), first_after, last_after)
    base = 4 * (nx + 2 * HALO)
    for x in range(half):
        send_y(pay_a, pay_b, base + 4 * (HALO + x), mid[x, 0:4, :], mid[x, 12:16, :])
    for k in range(HALO):
        first_after, first_before = (v[0:4] for v in x_sides(x_a, x_b, 16 + 2 * k))
        last_after, last_before = (v[4:8] for v in x_sides(x_a, x_b, 16 + 2 * k + 1))
        send_y(pay_a, pay_b, base + 4 * k, first_before, last_before)
        send_y(pay_a, pay_b, base + 4 * (HALO + half + k), first_after, last_after)
    base += 4 * (half + 2 * HALO)
    for x in range(8):
        pay_a[base + 8 * x : base + 8 * x + 8, :] = coarse[x]
        pay_b[base + 8 * x : base + 8 * x + 8, :] = coarse[x]
    far_edges(coarse, pay_c, pay_d)


def far_edges(field, pay_c, pay_d):
    flag = low_pair()
    for x in range(8):
        first, last = field[x, 0:1, :], field[x, 7:8, :]
        pay_c[x : x + 1, :] = either(flag, last, first)
        pay_d[x : x + 1, :] = either(flag, first, last)


def low_pair():
    return lax.rem(lax.axis_index("dev"), 4) < 2


def wide_plane(own, r_a, r_b, r_c, r_d, base, x):
    flag = low_pair()
    c, d = r_c[x : x + 1, :], r_d[x : x + 1, :]
    after, before = y_sides(r_a, r_b, base + 8 * x, 8)
    gap = jnp.zeros((6, 256), F32)
    return jnp.concatenate([own[x], after, either(flag, c, d), gap, either(flag, d, c), before], axis=0)


def sweeps_kernel(conc, label, y_a, y_b, x_a, x_b, out, one, two, gain, base):
    nx = conc.shape[0]
    ratio = tuple(d / (1.0 + 6.0 * d) for d in DIFFUSION_TABLE)
    inverse = tuple(1.0 / (1.0 + 6.0 * d) for d in DIFFUSION_TABLE)

    def put(x, rows, c, lab):
        one[x, rows, :] = c
        gain[x, rows, :] = jnp.where(c > 0.0, pick(lab, ratio), 0.0)
        base[x, rows, :] = c * pick(lab, inverse)

    def own(i):
        put(HALO + i, slice(0, 32), conc[i], label[i])

    loop(0, nx, own)
    for i in range(nx):
        c = halo_tile(*y_sides(y_a, y_b, 7 * i, 4))
        lab = halo_tile(*y_sides(y_a, y_b, 7 * i + 4, 3))
        put(HALO + i, slice(32, 40), c, lab)
    for t in range(5):
        rows = slice(8 * t, 8 * t + 8)
        for k in range(HALO):
            c_after, c_before = x_sides(x_a, x_b, 5 * k + t)
            l_after = x_sides(x_a, x_b, 20 + 5 * min(k, 2) + t)[0]
            l_before = x_sides(x_a, x_b, 20 + 5 * max(k - 1, 0) + t)[1]
            put(k, rows, c_before, l_before)
            put(HALO + nx + k, rows, c_after, l_after)

    def stencil(old, x):
        mid = old[x]
        return base[x] + gain[x] * ((old[x - 1] + old[x + 1]) + (along_y(mid) + along_z(mid)))

    fields = (one, two)
    for s in range(1, SWEEPS):
        old, new = fields[(s - 1) % 2], fields[s % 2]

        def sweep(x, old=old, new=new):
            new[x] = stencil(old, x)

        loop(s, nx + 2 * HALO - s, sweep)

    old = fields[(SWEEPS - 1) % 2]

    def last(i):
        out[i] = stencil(old, HALO + i)[0:32, :]

    loop(0, nx, last)


def flux_kernel(conc, label, phi, solid, lists, flux, pay_a, pay_b, marked):
    nx = conc.shape[0]
    entries = lists.shape[0] // 2 * 256
    owner = jnp.concatenate([lists[2 * i : 2 * i + 1, :] for i in range(entries // 256)], axis=1)
    block = jnp.concatenate([lists[2 * i + 1 : 2 * i + 2, :] for i in range(entries // 256)], axis=1)
    here = lax.axis_index("dev")
    block = jnp.where(owner.astype(jnp.int32) == here, block.astype(jnp.int32), -1)
    hit_row = (iota((32, entries), 0) == lax.shift_right_arithmetic(block, 6)).astype(jnp.bfloat16)
    hit_column = (iota((LANES, entries), 0) == lax.rem(block, 64)).astype(jnp.bfloat16)
    named = lax.dot_general(hit_row, hit_column, (((1,), (1,)), ((), ())), preferred_element_type=F32)
    for i in range(32):
        marked[i] = jnp.broadcast_to(named[i : i + 1, :], (8, LANES))
    is_row = lax.div(iota((32, LANES), 1), 2) == iota((32, LANES), 0)
    spread = (lax.rem(iota((LANES, 256), 0), 2) == lax.div(iota((LANES, 256), 1), LANES)).astype(jnp.bfloat16)

    def plane(i):
        marks = jnp.where(is_row, jnp.concatenate([marked[i]] * 4, axis=0), 0.0).astype(jnp.bfloat16)
        listed = jnp.dot(marks, spread, preferred_element_type=F32) > 0.5
        drive = 0.5 * (solid[i] - phi[i])
        logc = jnp.log(conc[i])
        value = jnp.exp(drive + 0.4 * logc) - jnp.exp(0.6 * logc - drive)
        flux[i] = jnp.where(listed, pick(label[i], KINETIC_TABLE) * value, 0.0)

    loop(0, nx, plane, 4)
    for x in range(nx):
        send_y(pay_a, pay_b, 3 * x, flux[x, 0:3, :], flux[x, 29:32, :])


def store_kernel(conc, flux, conc_out, flux_out, token, sems):
    copies = []
    for i, (ref, to) in enumerate(((conc, conc_out), (flux, flux_out))):
        for j in range(4):
            rows = pl.ds(8 * j, 8)
            copies.append(pltpu.make_async_copy(ref.at[rows], to.at[rows], sems.at[4 * i + j]))
            copies[-1].start()
    token[...] = jnp.zeros(token.shape, F32)
    for c in copies:
        c.wait()


def ready_kernel(conc, label, phi, y_a, y_b, x_a, x_b, yy_a, yy_b, xx_a, xx_b, weight, scale, share, start, token, field):
    nx = conc.shape[0]
    token[...] = jnp.zeros(token.shape, F32)

    def put(x, rows, c, lab, p):
        conduct = c * pick(lab, CONDUCT_TABLE)
        factor = OMEGA / (MASS + 6.0 * conduct)
        weight[x, rows, :] = conduct * factor
        scale[x, rows, :] = factor
        share[x, rows, :] = MASS * p * factor
        field[x, rows, :] = p

    def own(i):
        put(HALO + i, slice(0, 32), conc[i], label[i], phi[i])

    loop(0, nx, own, 4)
    low = slice(32, 40)
    for i in range(nx):
        c = halo_tile(*y_sides(y_a, y_b, 7 * i, 4))
        lab = halo_tile(*y_sides(y_a, y_b, 7 * i + 4, 3))
        put(HALO + i, low, c, lab, halo_tile(*y_sides(yy_a, yy_b, 4 * (HALO + i), 4)))
    for t in range(5):
        rows = slice(8 * t, 8 * t + 8)
        for k in range(HALO):
            c_after, c_before = x_sides(x_a, x_b, 5 * k + t)
            l_after = x_sides(x_a, x_b, 20 + 5 * min(k, 2) + t)[0]
            l_before = x_sides(x_a, x_b, 20 + 5 * max(k - 1, 0) + t)[1]
            if t < 4:
                p_after, p_before = x_sides(xx_a, xx_b, 4 * k + t)
            else:
                p_after = halo_tile(*y_sides(yy_a, yy_b, 4 * (HALO + nx + k), 4))
                p_before = halo_tile(*y_sides(yy_a, yy_b, 4 * k, 4))
            put(k, rows, c_before, l_before, p_before)
            put(HALO + nx + k, rows, c_after, l_after, p_after)

    def sweep(x):
        p = field[x]
        around = (field[x - 1] + field[x + 1]) + (along_y(p) + along_z(p))
        start[x] = 0.2 * p + share[x] + weight[x] * around

    loop(1, nx + 2 * HALO - 1, sweep)


def flux_pack_x_kernel(flux, r_a, r_b, token, token_2, pay_a, pay_b):
    nx = flux.shape[0]

    def tile(x, t):
        if t < 4:
            return flux[x, 8 * t : 8 * t + 8, :]
        return halo_tile(*y_sides(r_a, r_b, 3 * x, 3))

    for k in range(3):
        for t in range(5):
            send_x(pay_a, pay_b, 5 * k + t, tile(k, t), tile(nx - 3 + k, t))


def potential_kernel(
    flux, y_a, y_b, x_a, x_b, weight, scale, share, start, after_two, source, source_mid, pay_a, pay_b, field, pairs
):
    nx = flux.shape[0]
    half = nx // 2

    def put(x, rows, f):
        part = scale[x, rows, :] * f
        source[x, rows, :] = share[x, rows, :] + part
        field[x, rows, :] = start[x, rows, :] + part

    def own(i):
        put(HALO + i, slice(0, 32), flux[i])

    loop(0, nx, own)
    for i in range(nx):
        put(HALO + i, slice(32, 40), halo_tile(*y_sides(y_a, y_b, 3 * i, 3)))
    for k in range(3):
        for t in range(5):
            rows = slice(8 * t, 8 * t + 8)
            after, before = x_sides(x_a, x_b, 5 * k + t)
            put(1 + k, rows, before)
            put(HALO + nx + k, rows, after)

    def around(values, x):
        v = values[x]
        return v, weight[x] * ((values[x - 1] + values[x + 1]) + (along_y(v) + along_z(v)))

    def sweep(x):
        v, near = around(field, x)
        after_two[x] = 0.2 * v + (source[x] + near)

    loop(2, nx + 2 * HALO - 2, sweep)

    def remainder(x):
        v, near = around(after_two, x)
        return ((source[x] - OMEGA * v) + near)[0:32, :] / scale[x, 0:32, :]

    def coarsen(i):
        x = HALO + 2 * i
        source_mid[i] = 0.25 * pair_rows(remainder(x) + remainder(x + 1), pairs.at[i])

    loop(0, half, coarsen, 4)
    for x in range(half):
        send_y(pay_a, pay_b, 4 * x, source_mid[x, 0:4, :], source_mid[x, 12:16, :])


def mid_pack_x_kernel(field, r_a, r_b, token, pay_a, pay_b):
    n = field.shape[0]

    def tile(x, t):
        if t < 2:
            return field[x, 8 * t : 8 * t + 8, :]
        return halo_tile(*y_sides(r_a, r_b, 4 * x, 4))

    for k in range(HALO):
        for t in range(3):
            send_x(pay_a, pay_b, 3 * k + t, tile(k, t), tile(n - HALO + k, t))


def mid_kernel(
    source_own, conduct_own, yy_a, yy_b, xx_a, xx_b, y_a, y_b, x_a, x_b, rho, load,
    after_two, source, weight, coarse, pay_a, pay_b, pay_c, pay_d, part, scale, pairs, pairs_2,
):
    n = source_own.shape[0]
    base = 4 * (2 * n + 2 * HALO)

    def put(x, rows, b, conduct):
        factor = OMEGA / (MASS + 3.0 * conduct)
        weight[x, rows, :] = conduct * factor
        scale[x, rows, :] = factor
        source[x, rows, :] = factor * b

    def far(x):
        return halo_tile(*y_sides(yy_a, yy_b, base + 4 * x, 4))

    for i in range(n):
        put(HALO + i, slice(0, 16), source_own[i], conduct_own[i])
        put(HALO + i, slice(16, 24), halo_tile(*y_sides(y_a, y_b, 4 * i, 4)), far(HALO + i))
    for k in range(HALO):
        for t in range(3):
            rows = slice(8 * t, 8 * t + 8)
            b_after, b_before = x_sides(x_a, x_b, 3 * k + t)
            if t < 2:
                c_after, c_before = x_sides(xx_a, xx_b, 16 + 2 * k + t)
            else:
                c_after, c_before = far(HALO + n + k), far(k)
            put(k, rows, b_before, c_before)
            put(HALO + n + k, rows, b_after, c_after)

    def around(values, x):
        v = values[x]
        return v, weight[x] * (0.25 * ((values[x - 1] + values[x + 1]) + along_y(v)) + along_z(v))

    def sweep(x):
        v, near = around(source, x)
        after_two[x] = 0.2 * v + (source[x] + near)

    loop(1, n + 2 * HALO - 1, sweep, 11)

    def remainder(x):
        v, near = around(after_two, x)
        return ((source[x] - OMEGA * v) + near)[0:16, :] / scale[x, 0:16, :]

    total = jnp.zeros((8, 256), F32)
    for i in range(n // 2):
        x = HALO + 2 * i
        value = 0.25 * pair_rows(remainder(x) + remainder(x + 1), pairs.at[i])
        coarse[i] = value
        pay_a[8 * i : 8 * i + 8, :] = value
        pay_b[8 * i : 8 * i + 8, :] = value
        total += rho[i] * value
    sums = jnp.concatenate([total[:, :LANES] + total[:, LANES:], load[...]], axis=1)
    pay_a[64:72, :] = sums
    pay_b[64:72, :] = sums
    part[...] = sums
    far_edges(coarse, pay_c, pay_d)


COARSE_W = 0.0625


def coarse_sum(values, x):
    v = values[x]
    inner = along_y(v)
    if x > 0:
        inner = inner + values[x - 1]
    if x < len(values) - 1:
        inner = inner + values[x + 1]
    return COARSE_W * inner + along_z(v)


def coarse_ready_kernel(own, r_a, r_b, r_c, r_d, weight, scale, rho, load, token, one, two, conduct):
    token[...] = jnp.zeros(token.shape, F32)
    base = r_a.shape[0] - 64
    for x in range(8):
        k = wide_plane(own, r_a, r_b, r_c, r_d, base, x)
        factor = OMEGA / (MASS + 2.25 * k)
        conduct[x] = k
        weight[x] = k * factor
        scale[x] = factor
        one[x] = jnp.ones(k.shape, F32)
    fields = (one, two)
    for s in range(COARSE_SWEEPS):
        old, new = fields[s % 2], fields[(s + 1) % 2]
        for x in range(8):
            near = [conduct[i] * old[i] if 0 <= i < 8 else None for i in (x - 1, x, x + 1)]
            inner = along_y(near[1])
            for other in (near[0], near[2]):
                if other is not None:
                    inner = inner + other
            new[x] = 0.2 * old[x] + scale[x] * (COARSE_W * inner + along_z(near[1]))
    last = fields[COARSE_SWEEPS % 2]
    peer, peers = lax.axis_index("dev"), lax.axis_size("dev")
    row, z = iota((8, 256), 0), iota((8, 256), 1)
    edge_y = ((row == 0) & (peer == 0)) | ((row == 7) & (peer == peers - 1))
    edge = edge_y.astype(F32) * COARSE_W + ((z == 0) | (z == 255)).astype(F32)
    total = jnp.zeros((8, 256), F32)
    for x in range(8):
        rho[x] = last[x, 0:8, :]
        total += MASS + own[x] * (edge + (COARSE_W if x in (0, 7) else 0.0))
    load[...] = total[:, :LANES] + total[:, LANES:]


def coarse_kernel(own, r_a, r_b, r_c, r_d, weight, scale, error, source, one, two):
    for x in range(8):
        source[x] = scale[x] * wide_plane(own, r_a, r_b, r_c, r_d, 0, x)
    old = source
    for s in range(1, COARSE_SWEEPS):
        new = one if s % 2 else two
        planes = [old.at[x] for x in range(8)]
        for x in range(8):
            v = old[x]
            inner = along_y(v)
            if x > 0:
                inner = inner + old[x - 1]
            if x < 7:
                inner = inner + old[x + 1]
            new[x] = 0.2 * v + (source[x] + weight[x] * (COARSE_W * inner + along_z(v)))
        old = new
    for x in range(8):
        error[x, 0:8, :] = old[x, 0:8, :]
        error[x, 8:16, :] = jnp.where(upper(), old[x, 8:16, :], old[x, 24:32, :])


def shift_kernel(error, sums, out, pay_a, pay_b):
    resid = jnp.sum(sums[:, :LANES])
    load = jnp.sum(sums[:, LANES:])
    shift_c = jnp.full((16, 256), resid, F32) / jnp.full((16, 256), load, F32)
    for x in range(8):
        out[x] = error[x] + shift_c
    for k in range(2):
        send_x(pay_a, pay_b, k, out[k], out[6 + k])


def finish_kernel(
    error, x_a, x_b, mid_two, mid_source, mid_weight, fine_two, fine_source, fine_weight,
    out, one, two, fine_one, fine_last, dup, dup_2, result, sems,
):
    n = mid_two.shape[0]
    nf = fine_two.shape[0]
    nx = out.shape[0]

    def squeeze(tile):
        return jnp.where(iota((8, 256), 0) < 2, tile, pltpu.roll(tile, 4, 0))

    after, before = x_sides(x_a, x_b, slice(0, 2))
    for c in range(-2, 10):
        plane = before[c + 2] if c < 0 else (after[c - 8] if c >= 8 else error[c])
        room = dup.at[c + 2]
        spread = jnp.concatenate([twice(plane[0:8], room.at[0]), twice(squeeze(plane[8:16]), room.at[1])[0:8]], axis=0)
        for x in (2 * c + HALO, 2 * c + 1 + HALO):
            one[x] = jnp.where(mid_weight[x] > 0.0, mid_two[x] + spread, 0.0)

    def around(values, weights, x, w):
        v = values[x]
        inner = (values[x - 1] + values[x + 1]) + along_y(v)
        return 0.2 * v + weights[x] * (w * inner + along_z(v))

    for s, (old, new) in ((2, (one, two)), (3, (two, one))):

        def sweep(x, old=old, new=new):
            new[x] = mid_source[x] + around(old, mid_weight, x, 0.25)

        loop(s, n - s, sweep, 10)

    def lift(m):
        plane = one[m]
        room = dup_2.at[m]
        spread = jnp.concatenate(
            [twice(plane[0:8], room.at[0]), twice(plane[8:16], room.at[1]), twice(squeeze(plane[16:24]), room.at[2])[0:8]],
            axis=0,
        )
        x = 2 * m - HALO
        fine_one[x] = fine_two[x] + spread
        fine_one[x + 1] = fine_two[x + 1] + spread

    loop(3, n - 3, lift, 6)

    def sweep_one(x):
        fine_last[x] = fine_source[x] + around(fine_one, fine_weight, x, 1.0)

    loop(3, nf - 3, sweep_one)
    copies = []
    for j in range(nx // 8):

        def sweep_two(i):
            x = HALO + i
            result[i] = (fine_source[x] + around(fine_last, fine_weight, x, 1.0))[0:32, :]

        for i in range(8 * j, 8 * j + 8):
            sweep_two(i)
        rows = pl.ds(8 * j, 8)
        copies.append(pltpu.make_async_copy(result.at[rows], out.at[rows], sems.at[j]))
        copies[-1].start()
    for c in copies:
        c.wait()


def both_ways(pairs):
    return pairs + [(j, i) for i, j in pairs]


def swap(pay_a, pay_b, axis):
    size = lax.axis_size(axis)
    pairs_a = [(i, i + 1) for i in range(0, size - 1, 2)]
    pairs_b = [(i, i + 1) for i in range(1, size - 1, 2)]
    return lax.ppermute(pay_a, axis, both_ways(pairs_a)), lax.ppermute(pay_b, axis, both_ways(pairs_b))


def swap_far(pay_c, pay_d):
    size = lax.axis_size("dev")
    pairs_c = [(i, i + 2) for i in range(size - 2) if i % 4 < 2]
    pairs_d = [(i, i + 2) for i in range(size - 2) if i % 4 >= 2]
    return lax.ppermute(pay_c, "dev", both_ways(pairs_c)), lax.ppermute(pay_d, "dev", both_ways(pairs_d))


def exchange(value, distance):
    return lax.ppermute(value, "dev", [(i, i ^ distance) for i in range(lax.axis_size("dev"))])


def body(conc_old, phi_old, solid_pot, phase_label, iface_block, iface_owner):
    peers = lax.axis_size("dev")
    nx = conc_old.shape[0]
    half = nx // 2
    quarter = nx // 4
    ext = (nx + 2 * HALO, nx + 2 * HALO, 256)
    ext_mid = (half + 2 * HALO, half + 2 * HALO, 256)
    token_shape = shaped(8, LANES)

    pay_a, pay_b = call(
        first_pack_kernel,
        [shaped(7 * nx + 8, 256)] * 2,
        [conc_old, phase_label, iface_owner.reshape(1, -1), iface_block],
        [vmem(nx, 8, 256)] * 2 + [pltpu.VMEM((nx, 8, 256), jnp.int32)] * 2 + [pltpu.SemaphoreType.DMA((4,))],
        in_specs=[FAR, FAR, WHOLE, WHOLE],
        name="first_pack",
    )
    own_lists = pay_a[7 * nx : 7 * nx + 2]
    y_a, y_b = swap(pay_a, pay_b, "dev")
    conduct_mid, conduct_coarse, pay_a, pay_b = call(
        own_kernel,
        [shaped(half, half, 256), shaped(quarter, quarter, 256), shaped(24, 8, 256), shaped(24, 8, 256)],
        [conc_old, phase_label, phi_old],
        [vmem(half, 2, nx, LANES), vmem(quarter, 2, half, LANES)],
        name="own",
    )
    xx_a, xx_b = swap(pay_a, pay_b, "grp")
    pay_a, pay_b = call(
        first_pack_x_kernel,
        [shaped(35, 8, 256)] * 2,
        [conc_old, phase_label, y_a, y_b, conduct_coarse],
        name="first_pack_x",
    )
    x_a, x_b = swap(pay_a, pay_b, "grp")
    lists = jnp.concatenate([own_lists, y_a[7 * nx : 7 * nx + 2]], axis=0)
    distance = 2
    while distance < peers:
        lists = jnp.concatenate([lists, exchange(lists, distance)], axis=0)
        distance *= 2
    wide_rows = 4 * (nx + half + 4 * HALO) + 64
    pay_a, pay_b, pay_c, pay_d = call(
        second_pack_kernel,
        [shaped(wide_rows, 256)] * 2 + [shaped(8, 256)] * 2,
        [phi_old, conduct_mid, conduct_coarse, xx_a, xx_b],
        name="second_pack",
    )
    yy_a, yy_b = swap(pay_a, pay_b, "dev")
    yy_c, yy_d = swap_far(pay_c, pay_d)

    (conc_new,) = call(
        sweeps_kernel,
        [shaped(nx, nx, 256)],
        [conc_old, phase_label, y_a, y_b, x_a, x_b],
        [vmem(*ext)] * 4,
        name="sweeps",
    )
    flux_own, pay_a, pay_b = call(
        flux_kernel,
        [shaped(nx, nx, 256), shaped(3 * nx, 256), shaped(3 * nx, 256)],
        [conc_new, phase_label, phi_old, solid_pot, lists],
        [vmem(32, 8, LANES)],
        name="flux",
    )
    f_a, f_b = swap(pay_a, pay_b, "dev")
    concentration, flux, stored = call(
        store_kernel,
        [shaped(nx, nx, 256), shaped(nx, nx, 256), token_shape],
        [conc_new, flux_own],
        [pltpu.SemaphoreType.DMA((8,))],
        out_specs=[FAR, FAR, WHOLE],
        name="store",
    )
    weight, scale, share, start, made = call(
        ready_kernel,
        [shaped(*ext)] * 4 + [token_shape],
        [conc_old, phase_label, phi_old, y_a, y_b, x_a, x_b, yy_a, yy_b, xx_a, xx_b],
        [vmem(*ext)],
        name="ready",
    )
    pay_a, pay_b = call(
        flux_pack_x_kernel, [shaped(15, 8, 256)] * 2, [flux_own, f_a, f_b, stored, made], name="flux_pack_x"
    )
    fx_a, fx_b = swap(pay_a, pay_b, "grp")
    fine_two, fine_source, source_mid, pay_a, pay_b = call(
        potential_kernel,
        [shaped(*ext), shaped(*ext), shaped(half, half, 256), shaped(4 * half, 256), shaped(4 * half, 256)],
        [flux_own, f_a, f_b, fx_a, fx_b, weight, scale, share, start],
        [vmem(*ext), vmem(half, 2, nx, LANES)],
        name="potential",
    )
    m_a, m_b = swap(pay_a, pay_b, "dev")
    wide = (quarter, 32, 256)
    weight_coarse, scale_coarse, rho, load, made = call(
        coarse_ready_kernel,
        [shaped(*wide), shaped(*wide), shaped(quarter, quarter, 256), shaped(8, LANES), token_shape],
        [conduct_coarse, yy_a, yy_b, yy_c, yy_d],
        [vmem(*wide)] * 3,
        name="coarse_ready",
    )
    pay_a, pay_b = call(
        mid_pack_x_kernel, [shaped(3 * HALO, 8, 256)] * 2, [source_mid, m_a, m_b, made], name="mid_pack_x"
    )
    mx_a, mx_b = swap(pay_a, pay_b, "grp")
    mid_two, mid_source, mid_weight, source_coarse, pay_a, pay_b, pay_c, pay_d, sums = call(
        mid_kernel,
        [shaped(*ext_mid)] * 3
        + [shaped(quarter, quarter, 256), shaped(72, 256), shaped(72, 256)]
        + [shaped(8, 256)] * 3,
        [source_mid, conduct_mid, yy_a, yy_b, xx_a, xx_b, m_a, m_b, mx_a, mx_b, rho, load],
        [vmem(*ext_mid), vmem(8, 2, half, LANES), vmem(8, 2, half, LANES)],
        name="middle",
    )
    c_a, c_b = swap(pay_a, pay_b, "dev")
    c_c, c_d = swap_far(pay_c, pay_d)
    (error,) = call(
        coarse_kernel,
        [shaped(8, 16, 256)],
        [source_coarse, c_a, c_b, c_c, c_d, weight_coarse, scale_coarse],
        [vmem(*wide)] * 3,
        name="coarse",
    )
    sums = sums + c_a[64:72]
    distance = 2
    while distance < peers:
        sums = sums + exchange(sums, distance)
        distance *= 2
    error, pay_a, pay_b = call(
        shift_kernel, [shaped(8, 16, 256), shaped(2, 16, 256), shaped(2, 16, 256)], [error, sums], name="shift"
    )
    e_a, e_b = swap(pay_a, pay_b, "grp")
    (potential,) = call(
        finish_kernel,
        [shaped(nx, nx, 256)],
        [error, e_a, e_b, mid_two, mid_source, mid_weight, fine_two, fine_source, weight],
        [vmem(*ext_mid)] * 2
        + [vmem(*ext)] * 2
        + [vmem(12, 2, 2, 16, LANES), vmem(half + 2 * HALO, 3, 2, 16, LANES), vmem(nx, nx, 256)]
        + [pltpu.SemaphoreType.DMA((4,))],
        out_specs=[FAR],
        name="finish",
    )
    return (concentration, flux, potential)


def solution(mesh):
    brick = P("grp", "dev", None)
    return jax.shard_map(
        body,
        mesh=mesh,
        in_specs=(brick, brick, brick, brick, P("grp", "dev"), brick),
        out_specs=(brick, brick, brick),
        check_vma=False,
    )
```

```python
import jax
import jax.numpy as jnp
from jax import lax
from jax.experimental import pallas as pl
from jax.experimental.pallas import tpu as pltpu
from jax.sharding import PartitionSpec as P


F32 = jnp.float32
MASS = 0.05
OMEGA = 0.8
DIFFUSION_TABLE = (1.5, 0.1, 0.4)
CONDUCT_TABLE = (1.0, 0.3, 0.6)
KINETIC_TABLE = (0.2, 1.0, 0.5)
SWEEPS = 4
COARSE_SWEEPS = 8
COARSE_NEAR = 8
HALO = 4
LANES = 128
VMEM_LIMIT = 28 * 1024 * 1024
VMEM_MOST = 58 * 1024 * 1024


def shaped(*shape):
    return jax.ShapeDtypeStruct(shape, F32)


WHOLE = pl.BlockSpec(memory_space=pltpu.VMEM)
FAR = pl.BlockSpec(memory_space=pltpu.HBM)


def call(kernel, outs, args, scratch=(), in_specs=None, out_specs=None, limit=VMEM_LIMIT, flops=10**6, name=None):
    size = sum(4 * a.size for a in args) + sum(4 * o.size for o in outs)
    return pl.pallas_call(
        kernel,
        out_shape=tuple(outs),
        in_specs=in_specs or [WHOLE] * len(args),
        out_specs=tuple(out_specs or [WHOLE] * len(outs)),
        scratch_shapes=list(scratch),
        compiler_params=pltpu.CompilerParams(vmem_limit_bytes=limit),
        cost_estimate=pl.CostEstimate(flops=flops, bytes_accessed=size, transcendentals=0),
        name=name,
    )(*args)


def vmem(*shape):
    return pltpu.VMEM(shape, F32)


def iota(shape, dim):
    return lax.broadcasted_iota(jnp.int32, shape, dim)


def pick(label, table):
    return jnp.where(label == 0, table[0], jnp.where(label == 1, table[1], table[2])).astype(F32)


def loop(low, high, body, unroll=8):
    steps = (high - low) // unroll

    def step(i, carry):
        for u in range(unroll):
            body(low + i * unroll + u)
        return carry

    if steps > 1:
        lax.fori_loop(0, steps, step, 0)
    else:
        steps = 0
    for x in range(low + steps * unroll, high):
        body(x)


def even(axis):
    return lax.rem(lax.axis_index(axis), 2) == 0


def along_y(v):
    return pltpu.roll(v, 1, 0) + pltpu.roll(v, v.shape[0] - 1, 0)


def along_z(v):
    low, high = v[:, :LANES], v[:, LANES:]
    lane = iota(low.shape, 1)
    first, last = lane == 0, lane == LANES - 1
    low_up, high_up = pltpu.roll(low, 1, 1), pltpu.roll(high, 1, 1)
    low_down, high_down = pltpu.roll(low, LANES - 1, 1), pltpu.roll(high, LANES - 1, 1)
    low_sum = jnp.where(first, 0.0, low_up) + jnp.where(last, high_down, low_down)
    high_sum = jnp.where(first, low_up, high_up) + jnp.where(last, 0.0, high_down)
    return jnp.concatenate([low_sum, high_sum], axis=1)


def upper(shape=(8, 256)):
    return iota(shape, 0) < HALO


def twice(tile, scratch):
    for h in range(2):
        part = tile[:, h * LANES : (h + 1) * LANES]
        scratch[h, pl.ds(0, 8, stride=2), :] = part
        scratch[h, pl.ds(1, 8, stride=2), :] = part
    return jnp.concatenate([scratch[0], scratch[1]], axis=1)


def pair_rows(v, scratch):
    half = v.shape[0] // 2
    parts = []
    for h in range(2):
        scratch[h] = v[:, h * LANES : (h + 1) * LANES]
        parts.append(scratch[h, pl.ds(0, half, stride=2), :] + scratch[h, pl.ds(1, half, stride=2), :])
    return jnp.concatenate(parts, axis=1)


def either(flag, if_true, if_false):
    return jnp.where(flag, if_true, if_false)


def y_sides(r_a, r_b, at, count):
    flag = even("dev")
    a, b = r_a[at : at + count, :], r_b[at : at + count, :]
    return either(flag, a, b), either(flag, b, a)


def x_sides(r_a, r_b, index):
    flag = even("grp")
    a, b = r_a[index], r_b[index]
    return either(flag, a, b), either(flag, b, a)


def send_y(pay_a, pay_b, at, first, last):
    flag = even("dev")
    n = first.shape[0]
    pay_a[at : at + n, :] = either(flag, last, first)
    pay_b[at : at + n, :] = either(flag, first, last)


def send_x(pay_a, pay_b, index, first, last):
    flag = even("grp")
    pay_a[index] = either(flag, last, first)
    pay_b[index] = either(flag, first, last)


def halo_tile(after, before):
    parts = [after]
    if after.shape[0] < HALO:
        parts.append(jnp.zeros((2 * HALO - 2 * after.shape[0], after.shape[1]), F32))
    return jnp.concatenate(parts + [before], axis=0)


def first_pack_kernel(
    conc, label, owner, block, pay_a, pay_b, own_lists, c_first, c_last, l_first, l_last, own_owner, own_block, sems
):
    nx = conc.shape[0]
    copies = [pltpu.make_async_copy(owner, own_owner, sems.at[4]), pltpu.make_async_copy(block, own_block, sems.at[5])]
    for i, (ref, at, to) in enumerate(((conc, 0, c_first), (conc, 24, c_last), (label, 0, l_first), (label, 24, l_last))):
        copies.append(pltpu.make_async_copy(ref.at[:, pl.ds(at, 8), :], to, sems.at[i]))
    for c in copies:
        c.start()
    for c in copies:
        c.wait()
    named = jnp.concatenate([own_owner[...], own_block[...], jnp.zeros((6, 256), jnp.int32)], axis=0).astype(F32)
    own_lists[...] = named
    pay_a[7 * nx : 7 * nx + 8, :] = named
    pay_b[7 * nx : 7 * nx + 8, :] = named
    for x in range(nx):
        send_y(pay_a, pay_b, 7 * x, c_first[x, 0:4, :], c_last[x, 4:8, :])
        send_y(pay_a, pay_b, 7 * x + 4, l_first[x, 0:3, :].astype(F32), l_last[x, 5:8, :].astype(F32))


def own_kernel(conc, label, phi, mid, coarse, pay_a, pay_b, pairs, pairs_2):
    nx = conc.shape[0]
    half = nx // 2

    def coarsen(i):
        total = conc[2 * i] * pick(label[2 * i], CONDUCT_TABLE) + conc[2 * i + 1] * pick(label[2 * i + 1], CONDUCT_TABLE)
        mid[i] = 0.25 * pair_rows(total, pairs.at[i])

    loop(0, half, coarsen, 4)
    for i in range(half // 2):
        coarse[i] = 0.25 * pair_rows(mid[2 * i] + mid[2 * i + 1], pairs_2.at[i])
    for k in range(HALO):
        for t in range(4):
            rows = slice(8 * t, 8 * t + 8)
            send_x(pay_a, pay_b, 4 * k + t, phi[k, rows, :], phi[nx - HALO + k, rows, :])
        for t in range(2):
            rows = slice(8 * t, 8 * t + 8)
            send_x(pay_a, pay_b, 16 + 2 * k + t, mid[k, rows, :], mid[half - HALO + k, rows, :])


def first_pack_x_kernel(conc, label, r_a, r_b, token, pay_a, pay_b):
    nx = conc.shape[0]

    def plane(ref, k, t, offset, count):
        if t < 4:
            return ref[k, 8 * t : 8 * t + 8, :].astype(F32)
        return halo_tile(*y_sides(r_a, r_b, 7 * k + offset, count))

    for t in range(5):
        for k in range(HALO):
            send_x(pay_a, pay_b, 5 * k + t, plane(conc, k, t, 0, 4), plane(conc, nx - HALO + k, t, 0, 4))
        for k in range(3):
            send_x(pay_a, pay_b, 20 + 5 * k + t, plane(label, k, t, 4, 3), plane(label, nx - 3 + k, t, 4, 3))


def second_pack_kernel(phi, mid, coarse, x_a, x_b, token, pay_a, pay_b):
    nx = phi.shape[0]
    half = nx // 2
    for x in range(nx):
        send_y(pay_a, pay_b, 4 * (HALO + x), phi[x, 0:4, :], phi[x, 28:32, :])
    for k in range(HALO):
        for t, at in ((0, slice(0, 4)), (3, slice(4, 8))):
            after, before = x_sides(x_a, x_b, 4 * k + t)
            if t == 0:
                first_after, first_before = after[at], before[at]
            else:
                last_after, last_before = after[at], before[at]
        send_y(pay_a, pay_b, 4 * k, first_before, last_before)
        send_y(pay_a, pay_b, 4 * (HALO + nx + k), first_after, last_after)
    base = 4 * (nx + 2 * HALO)
    for x in range(half):
        send_y(pay_a, pay_b, base + 4 * (HALO + x), mid[x, 0:4, :], mid[x, 12:16, :])
    for k in range(HALO):
        first_after, first_before = (v[0:4] for v in x_sides(x_a, x_b, 16 + 2 * k))
        last_after, last_before = (v[4:8] for v in x_sides(x_a, x_b, 16 + 2 * k + 1))
        send_y(pay_a, pay_b, base + 4 * k, first_before, last_before)
        send_y(pay_a, pay_b, base + 4 * (HALO + half + k), first_after, last_after)
    base += 4 * (half + 2 * HALO)
    for x in range(8):
        pay_a[base + 8 * x : base + 8 * x + 8, :] = coarse[x]
        pay_b[base + 8 * x : base + 8 * x + 8, :] = coarse[x]


def wide_rows(own, after_own, before_own, after, before):
    gap = jnp.zeros((6, 256), F32)
    return jnp.concatenate([own, after_own, after, gap, before, before_own], axis=0)


def sweeps_kernel(conc, label, y_a, y_b, x_a, x_b, out, one, two, gain, base):
    nx = conc.shape[0]
    ratio = tuple(d / (1.0 + 6.0 * d) for d in DIFFUSION_TABLE)
    inverse = tuple(1.0 / (1.0 + 6.0 * d) for d in DIFFUSION_TABLE)

    def put(x, rows, c, lab):
        one[x, rows, :] = c
        gain[x, rows, :] = jnp.where(c > 0.0, pick(lab, ratio), 0.0)
        base[x, rows, :] = c * pick(lab, inverse)

    def own(i):
        put(HALO + i, slice(0, 32), conc[i], label[i])

    loop(0, nx, own)
    for i in range(nx):
        c = halo_tile(*y_sides(y_a, y_b, 7 * i, 4))
        lab = halo_tile(*y_sides(y_a, y_b, 7 * i + 4, 3))
        put(HALO + i, slice(32, 40), c, lab)
    for t in range(5):
        rows = slice(8 * t, 8 * t + 8)
        for k in range(HALO):
            c_after, c_before = x_sides(x_a, x_b, 5 * k + t)
            l_after = x_sides(x_a, x_b, 20 + 5 * min(k, 2) + t)[0]
            l_before = x_sides(x_a, x_b, 20 + 5 * max(k - 1, 0) + t)[1]
            put(k, rows, c_before, l_before)
            put(HALO + nx + k, rows, c_after, l_after)

    def stencil(old, x):
        mid = old[x]
        return base[x] + gain[x] * ((old[x - 1] + old[x + 1]) + (along_y(mid) + along_z(mid)))

    fields = (one, two)
    for s in range(1, SWEEPS):
        old, new = fields[(s - 1) % 2], fields[s % 2]

        def sweep(x, old=old, new=new):
            new[x] = stencil(old, x)

        loop(s, nx + 2 * HALO - s, sweep)

    old = fields[(SWEEPS - 1) % 2]

    def last(i):
        out[i] = stencil(old, HALO + i)[0:32, :]

    loop(0, nx, last)


def flux_kernel(conc, label, phi, solid, *rest):
    lists_refs, (flux, pay_a, pay_b, marked) = rest[:-4], rest[-4:]
    lists = jnp.concatenate([r[...] for r in lists_refs], axis=0)
    nx = conc.shape[0]
    entries = lists.shape[0] // 2 * 256
    owner = jnp.concatenate([lists[2 * i : 2 * i + 1, :] for i in range(entries // 256)], axis=1)
    block = jnp.concatenate([lists[2 * i + 1 : 2 * i + 2, :] for i in range(entries // 256)], axis=1)
    here = lax.axis_index("dev")
    block = jnp.where(owner.astype(jnp.int32) == here, block.astype(jnp.int32), -1)
    hit_row = (iota((32, entries), 0) == lax.shift_right_arithmetic(block, 6)).astype(jnp.bfloat16)
    hit_column = (iota((LANES, entries), 0) == lax.rem(block, 64)).astype(jnp.bfloat16)
    named = lax.dot_general(hit_row, hit_column, (((1,), (1,)), ((), ())), preferred_element_type=F32)
    for i in range(32):
        marked[i] = jnp.broadcast_to(named[i : i + 1, :], (8, LANES))
    is_row = lax.div(iota((32, LANES), 1), 2) == iota((32, LANES), 0)
    spread = (lax.rem(iota((LANES, 256), 0), 2) == lax.div(iota((LANES, 256), 1), LANES)).astype(jnp.bfloat16)

    def plane(i):
        marks = jnp.where(is_row, jnp.concatenate([marked[i]] * 4, axis=0), 0.0).astype(jnp.bfloat16)
        listed = jnp.dot(marks, spread, preferred_element_type=F32) > 0.5
        drive = 0.5 * (solid[i] - phi[i])
        logc = jnp.log(conc[i])
        value = jnp.exp(drive + 0.4 * logc) - jnp.exp(0.6 * logc - drive)
        flux[i] = jnp.where(listed, pick(label[i], KINETIC_TABLE) * value, 0.0)

    loop(0, nx, plane, 4)
    for x in range(nx):
        send_y(pay_a, pay_b, 3 * x, flux[x, 0:3, :], flux[x, 29:32, :])


def store_kernel(conc, flux, conc_out, flux_out, token, sems):
    copies = []
    for i, (ref, to) in enumerate(((conc, conc_out), (flux, flux_out))):
        for j in range(4):
            rows = pl.ds(8 * j, 8)
            copies.append(pltpu.make_async_copy(ref.at[rows], to.at[rows], sems.at[4 * i + j]))
            copies[-1].start()
    token[...] = jnp.zeros(token.shape, F32)
    for c in copies:
        c.wait()


def ready_kernel(conc, label, phi, y_a, y_b, x_a, x_b, yy_a, yy_b, xx_a, xx_b, weight, scale, share, start, token, field):
    nx = conc.shape[0]
    token[...] = jnp.zeros(token.shape, F32)

    def put(x, rows, c, lab, p):
        conduct = c * pick(lab, CONDUCT_TABLE)
        factor = OMEGA / (MASS + 6.0 * conduct)
        weight[x, rows, :] = conduct * factor
        scale[x, rows, :] = factor
        share[x, rows, :] = MASS * p * factor
        field[x, rows, :] = p

    def own(i):
        put(HALO + i, slice(0, 32), conc[i], label[i], phi[i])

    loop(0, nx, own, 4)
    low = slice(32, 40)
    for i in range(nx):
        c = halo_tile(*y_sides(y_a, y_b, 7 * i, 4))
        lab = halo_tile(*y_sides(y_a, y_b, 7 * i + 4, 3))
        put(HALO + i, low, c, lab, halo_tile(*y_sides(yy_a, yy_b, 4 * (HALO + i), 4)))
    for t in range(5):
        rows = slice(8 * t, 8 * t + 8)
        for k in range(HALO):
            c_after, c_before = x_sides(x_a, x_b, 5 * k + t)
            l_after = x_sides(x_a, x_b, 20 + 5 * min(k, 2) + t)[0]
            l_before = x_sides(x_a, x_b, 20 + 5 * max(k - 1, 0) + t)[1]
            if t < 4:
                p_after, p_before = x_sides(xx_a, xx_b, 4 * k + t)
            else:
                p_after = halo_tile(*y_sides(yy_a, yy_b, 4 * (HALO + nx + k), 4))
                p_before = halo_tile(*y_sides(yy_a, yy_b, 4 * k, 4))
            put(k, rows, c_before, l_before, p_before)
            put(HALO + nx + k, rows, c_after, l_after, p_after)

    def sweep(x):
        p = field[x]
        around = (field[x - 1] + field[x + 1]) + (along_y(p) + along_z(p))
        start[x] = 0.2 * p + share[x] + weight[x] * around

    loop(1, nx + 2 * HALO - 1, sweep)


def flux_pack_x_kernel(flux, r_a, r_b, token, token_2, pay_a, pay_b):
    nx = flux.shape[0]

    def tile(x, t):
        if t < 4:
            return flux[x, 8 * t : 8 * t + 8, :]
        return halo_tile(*y_sides(r_a, r_b, 3 * x, 3))

    for k in range(3):
        for t in range(5):
            send_x(pay_a, pay_b, 5 * k + t, tile(k, t), tile(nx - 3 + k, t))


def potential_kernel(
    flux, y_a, y_b, x_a, x_b, weight, scale, share, start, after_two, source, source_mid, pay_a, pay_b, field, pairs
):
    nx = flux.shape[0]
    half = nx // 2

    def put(x, rows, f):
        part = scale[x, rows, :] * f
        source[x, rows, :] = share[x, rows, :] + part
        field[x, rows, :] = start[x, rows, :] + part

    def own(i):
        put(HALO + i, slice(0, 32), flux[i])

    loop(0, nx, own)
    for i in range(nx):
        put(HALO + i, slice(32, 40), halo_tile(*y_sides(y_a, y_b, 3 * i, 3)))
    for k in range(3):
        for t in range(5):
            rows = slice(8 * t, 8 * t + 8)
            after, before = x_sides(x_a, x_b, 5 * k + t)
            put(1 + k, rows, before)
            put(HALO + nx + k, rows, after)

    def around(values, x):
        v = values[x]
        return v, weight[x] * ((values[x - 1] + values[x + 1]) + (along_y(v) + along_z(v)))

    def sweep(x):
        v, near = around(field, x)
        after_two[x] = 0.2 * v + (source[x] + near)

    loop(2, nx + 2 * HALO - 2, sweep)

    def remainder(x):
        v, near = around(after_two, x)
        return ((source[x] - OMEGA * v) + near)[0:32, :] / scale[x, 0:32, :]

    def coarsen(i):
        x = HALO + 2 * i
        source_mid[i] = 0.25 * pair_rows(remainder(x) + remainder(x + 1), pairs.at[i])

    loop(0, half, coarsen, 4)
    for x in range(half):
        send_y(pay_a, pay_b, 4 * x, source_mid[x, 0:4, :], source_mid[x, 12:16, :])


def mid_pack_x_kernel(field, r_a, r_b, token, pay_a, pay_b):
    n = field.shape[0]

    def tile(x, t):
        if t < 2:
            return field[x, 8 * t : 8 * t + 8, :]
        return halo_tile(*y_sides(r_a, r_b, 4 * x, 4))

    for k in range(HALO):
        for t in range(3):
            send_x(pay_a, pay_b, 3 * k + t, tile(k, t), tile(n - HALO + k, t))


def mid_kernel(
    source_own, conduct_own, yy_a, yy_b, xx_a, xx_b, y_a, y_b, x_a, x_b, rho, load,
    after_two, source, weight, coarse, conduct, pay_a, pay_b, part, scale, mid_conduct, pairs, pairs_2,
):
    n = source_own.shape[0]
    base = 4 * (2 * n + 2 * HALO)

    def put(x, rows, b, k):
        factor = OMEGA / (MASS + 3.0 * k)
        weight[x, rows, :] = k * factor
        scale[x, rows, :] = factor
        source[x, rows, :] = factor * b
        mid_conduct[x, rows, :] = k

    def far(x):
        return halo_tile(*y_sides(yy_a, yy_b, base + 4 * x, 4))

    for i in range(n):
        put(HALO + i, slice(0, 16), source_own[i], conduct_own[i])
        put(HALO + i, slice(16, 24), halo_tile(*y_sides(y_a, y_b, 4 * i, 4)), far(HALO + i))
    for k in range(HALO):
        for t in range(3):
            rows = slice(8 * t, 8 * t + 8)
            b_after, b_before = x_sides(x_a, x_b, 3 * k + t)
            if t < 2:
                c_after, c_before = x_sides(xx_a, xx_b, 16 + 2 * k + t)
            else:
                c_after, c_before = far(HALO + n + k), far(k)
            put(k, rows, b_before, c_before)
            put(HALO + n + k, rows, b_after, c_after)

    def around(values, x):
        v = values[x]
        return v, weight[x] * (0.25 * ((values[x - 1] + values[x + 1]) + along_y(v)) + along_z(v))

    def sweep(x):
        v, near = around(source, x)
        after_two[x] = 0.2 * v + (source[x] + near)

    loop(1, n + 2 * HALO - 1, sweep, 11)

    def remainder(x):
        v, near = around(after_two, x)
        return ((source[x] - OMEGA * v) + near) / scale[x]

    total = jnp.zeros((8, 256), F32)
    for i in range(n // 2):
        x = HALO + 2 * i
        value = 0.25 * pair_rows(remainder(x) + remainder(x + 1), pairs.at[i])
        k = 0.25 * pair_rows(mid_conduct[x] + mid_conduct[x + 1], pairs_2.at[i])
        coarse[i] = value
        conduct[i] = k
        send_y(pay_a, pay_b, 9 * i, value[1:9], jnp.concatenate([value[11:12], value[0:7]], axis=0))
        send_y(pay_a, pay_b, 9 * i + 8, k[8:9], k[11:12])
        total += rho[i] * value[0:8]
    sums = jnp.concatenate([total[:, :LANES] + total[:, LANES:], load[...]], axis=1)
    pay_a[72:80, :] = sums
    pay_b[72:80, :] = sums
    part[...] = sums


COARSE_W = 0.0625


def coarse_ready_kernel(own, r_a, r_b, rho, load, token, one, two, conduct, scale):
    token[...] = jnp.zeros(token.shape, F32)
    base = r_a.shape[0] - 64
    for x in range(8):
        after, before = y_sides(r_a, r_b, base + 8 * x, 8)
        k = jnp.concatenate([own[x], after, jnp.zeros((8, 256), F32), before], axis=0)
        conduct[x] = k
        scale[x] = OMEGA / (MASS + 2.25 * k)
        one[x] = jnp.ones(k.shape, F32)
    fields = (one, two)
    for s in range(COARSE_SWEEPS):
        old, new = fields[s % 2], fields[(s + 1) % 2]
        for x in range(8):
            near = [conduct[i] * old[i] if 0 <= i < 8 else None for i in (x - 1, x, x + 1)]
            inner = along_y(near[1])
            for other in (near[0], near[2]):
                if other is not None:
                    inner = inner + other
            new[x] = 0.2 * old[x] + scale[x] * (COARSE_W * inner + along_z(near[1]))
    last = fields[COARSE_SWEEPS % 2]
    peer, peers = lax.axis_index("dev"), lax.axis_size("dev")
    row, z = iota((8, 256), 0), iota((8, 256), 1)
    edge_y = ((row == 0) & (peer == 0)) | ((row == 7) & (peer == peers - 1))
    edge = edge_y.astype(F32) * COARSE_W + ((z == 0) | (z == 255)).astype(F32)
    total = jnp.zeros((8, 256), F32)
    for x in range(8):
        rho[x] = last[x, 0:8, :]
        total += MASS + own[x] * (edge + (COARSE_W if x in (0, 7) else 0.0))
    load[...] = total[:, :LANES] + total[:, LANES:]


def coarse_kernel(own, conduct, far_a, far_b, r_a, r_b, error, source, weight, one, two):
    base = far_a.shape[0] - 64
    for x in range(8):
        after, before = y_sides(r_a, r_b, 9 * x, 8)
        b = wide_rows(own[x, 0:8, :], own[x, 8:9, :], own[x, 11:12, :], after, before)
        last_after, last_before = y_sides(r_a, r_b, 9 * x + 8, 1)
        after, before = y_sides(far_a, far_b, base + 8 * x, 8)
        after = jnp.concatenate([after[1:8], last_after], axis=0)
        before = jnp.concatenate([last_before, before[0:7]], axis=0)
        k = wide_rows(conduct[x, 0:8, :], conduct[x, 8:9, :], conduct[x, 11:12, :], after, before)
        factor = OMEGA / (MASS + 2.25 * k)
        weight[x] = k * factor
        source[x] = factor * b
    old = source
    for s in range(1, COARSE_SWEEPS):
        new = one if s % 2 else two
        for x in range(8):
            v = old[x]
            inner = along_y(v)
            if x > 0:
                inner = inner + old[x - 1]
            if x < 7:
                inner = inner + old[x + 1]
            new[x] = 0.2 * v + (source[x] + weight[x] * (COARSE_W * inner + along_z(v)))
        old = new
    for x in range(8):
        error[x, 0:8, :] = old[x, 0:8, :]
        error[x, 8:16, :] = jnp.where(upper(), old[x, 8:16, :], old[x, 24:32, :])


def shift_kernel(error, sums, out, pay_a, pay_b):
    resid = jnp.sum(sums[:, :LANES])
    load = jnp.sum(sums[:, LANES:])
    shift_c = jnp.full((16, 256), resid, F32) / jnp.full((16, 256), load, F32)
    for x in range(8):
        out[x] = error[x] + shift_c
    for k in range(2):
        send_x(pay_a, pay_b, k, out[k], out[6 + k])


def finish_kernel(
    error, x_a, x_b, mid_two, mid_source, mid_weight, fine_two, fine_source, fine_weight,
    out, one, two, fine_one, fine_last, dup, dup_2, result, sems,
):
    n = mid_two.shape[0]
    nf = fine_two.shape[0]
    nx = out.shape[0]

    def squeeze(tile):
        return jnp.where(iota((8, 256), 0) < 2, tile, pltpu.roll(tile, 4, 0))

    after, before = x_sides(x_a, x_b, slice(0, 2))
    for c in range(-2, 10):
        plane = before[c + 2] if c < 0 else (after[c - 8] if c >= 8 else error[c])
        room = dup.at[c + 2]
        spread = jnp.concatenate([twice(plane[0:8], room.at[0]), twice(squeeze(plane[8:16]), room.at[1])[0:8]], axis=0)
        for x in (2 * c + HALO, 2 * c + 1 + HALO):
            one[x] = jnp.where(mid_weight[x] > 0.0, mid_two[x] + spread, 0.0)

    def around(values, weights, x, w):
        v = values[x]
        inner = (values[x - 1] + values[x + 1]) + along_y(v)
        return 0.2 * v + weights[x] * (w * inner + along_z(v))

    for s, (old, new) in ((2, (one, two)), (3, (two, one))):

        def sweep(x, old=old, new=new):
            new[x] = mid_source[x] + around(old, mid_weight, x, 0.25)

        loop(s, n - s, sweep, 10)

    def lift(m):
        plane = one[m]
        room = dup_2.at[m]
        spread = jnp.concatenate(
            [twice(plane[0:8], room.at[0]), twice(plane[8:16], room.at[1]), twice(squeeze(plane[16:24]), room.at[2])[0:8]],
            axis=0,
        )
        x = 2 * m - HALO
        fine_one[x] = fine_two[x] + spread
        fine_one[x + 1] = fine_two[x + 1] + spread

    loop(3, n - 3, lift, 6)

    def sweep_one(x):
        fine_last[x] = fine_source[x] + around(fine_one, fine_weight, x, 1.0)

    loop(3, nf - 3, sweep_one)
    copies = []
    for j in range(nx // 8):

        def sweep_two(i):
            x = HALO + i
            result[i] = (fine_source[x] + around(fine_last, fine_weight, x, 1.0))[0:32, :]

        for i in range(8 * j, 8 * j + 8):
            sweep_two(i)
        rows = pl.ds(8 * j, 8)
        copies.append(pltpu.make_async_copy(result.at[rows], out.at[rows], sems.at[j]))
        copies[-1].start()
    for c in copies:
        c.wait()


def both_ways(pairs):
    return pairs + [(j, i) for i, j in pairs]


def swap(pay_a, pay_b, axis):
    size = lax.axis_size(axis)
    pairs_a = [(i, i + 1) for i in range(0, size - 1, 2)]
    pairs_b = [(i, i + 1) for i in range(1, size - 1, 2)]
    from_b = lax.ppermute(pay_b, axis, both_ways(pairs_b))
    return lax.ppermute(pay_a, axis, both_ways(pairs_a)), from_b


def exchange(value, distance):
    return lax.ppermute(value, "dev", [(i, i ^ distance) for i in range(lax.axis_size("dev"))])


def body(conc_old, phi_old, solid_pot, phase_label, iface_block, iface_owner):
    peers = lax.axis_size("dev")
    nx = conc_old.shape[0]
    half = nx // 2
    quarter = nx // 4
    ext = (nx + 2 * HALO, nx + 2 * HALO, 256)
    ext_mid = (half + 2 * HALO, half + 2 * HALO, 256)
    token_shape = shaped(8, LANES)

    pay_a, pay_b, own_lists = call(
        first_pack_kernel,
        [shaped(7 * nx + 8, 256)] * 2 + [shaped(8, 256)],
        [conc_old, phase_label, iface_owner.reshape(1, -1), iface_block],
        [vmem(nx, 8, 256)] * 2
        + [pltpu.VMEM((nx, 8, 256), jnp.int32)] * 2
        + [pltpu.VMEM((1, 256), jnp.int32)] * 2
        + [pltpu.SemaphoreType.DMA((6,))],
        in_specs=[FAR] * 4,
        limit=VMEM_MOST,
        name="first_pack",
    )
    y_a, y_b = swap(pay_a, pay_b, "dev")
    conduct_mid, conduct_coarse, pay_a, pay_b = call(
        own_kernel,
        [shaped(half, half, 256), shaped(quarter, quarter, 256), shaped(24, 8, 256), shaped(24, 8, 256)],
        [conc_old, phase_label, phi_old],
        [vmem(half, 2, nx, LANES), vmem(quarter, 2, half, LANES)],
        name="own",
    )
    xx_a, xx_b = swap(pay_a, pay_b, "grp")
    pay_a, pay_b = call(
        first_pack_x_kernel,
        [shaped(35, 8, 256)] * 2,
        [conc_old, phase_label, y_a, y_b, conduct_coarse],
        name="first_pack_x",
    )
    x_a, x_b = swap(pay_a, pay_b, "grp")
    lists = jnp.concatenate([own_lists[0:2], y_a[7 * nx : 7 * nx + 2]], axis=0)
    pieces = [lists]
    distance = 2
    while distance < peers:
        if distance > 2:
            lists = jnp.concatenate(pieces, axis=0)
        pieces.append(exchange(lists, distance))
        distance *= 2
    far_rows = 4 * (nx + half + 4 * HALO) + 64
    pay_a, pay_b = call(
        second_pack_kernel,
        [shaped(far_rows, 256)] * 2,
        [phi_old, conduct_mid, conduct_coarse, xx_a, xx_b, lists],
        name="second_pack",
    )
    yy_a, yy_b = swap(pay_a, pay_b, "dev")

    (conc_new,) = call(
        sweeps_kernel,
        [shaped(nx, nx, 256)],
        [conc_old, phase_label, y_a, y_b, x_a, x_b],
        [vmem(*ext)] * 4,
        name="sweeps",
    )
    flux_own, pay_a, pay_b = call(
        flux_kernel,
        [shaped(nx, nx, 256), shaped(3 * nx, 256), shaped(3 * nx, 256)],
        [conc_new, phase_label, phi_old, solid_pot] + pieces,
        [vmem(32, 8, LANES)],
        name="flux",
    )
    f_a, f_b = swap(pay_a, pay_b, "dev")
    concentration, flux, stored = call(
        store_kernel,
        [shaped(nx, nx, 256), shaped(nx, nx, 256), token_shape],
        [conc_new, flux_own],
        [pltpu.SemaphoreType.DMA((8,))],
        out_specs=[FAR, FAR, WHOLE],
        name="store",
    )
    weight, scale, share, start, made = call(
        ready_kernel,
        [shaped(*ext)] * 4 + [token_shape],
        [conc_old, phase_label, phi_old, y_a, y_b, x_a, x_b, yy_a, yy_b, xx_a, xx_b],
        [vmem(*ext)],
        name="ready",
    )
    pay_a, pay_b = call(
        flux_pack_x_kernel, [shaped(15, 8, 256)] * 2, [flux_own, f_a, f_b, stored, made], name="flux_pack_x"
    )
    fx_a, fx_b = swap(pay_a, pay_b, "grp")
    fine_two, fine_source, source_mid, pay_a, pay_b = call(
        potential_kernel,
        [shaped(*ext), shaped(*ext), shaped(half, half, 256), shaped(4 * half, 256), shaped(4 * half, 256)],
        [flux_own, f_a, f_b, fx_a, fx_b, weight, scale, share, start],
        [vmem(*ext), vmem(half, 2, nx, LANES)],
        name="potential",
    )
    m_a, m_b = swap(pay_a, pay_b, "dev")
    wide = (quarter, 32, 256)
    rho, load, made = call(
        coarse_ready_kernel,
        [shaped(quarter, quarter, 256), shaped(8, LANES), token_shape],
        [conduct_coarse, yy_a, yy_b],
        [vmem(*wide)] * 4,
        name="coarse_ready",
    )
    pay_a, pay_b = call(
        mid_pack_x_kernel, [shaped(3 * HALO, 8, 256)] * 2, [source_mid, m_a, m_b, made], name="mid_pack_x"
    )
    mx_a, mx_b = swap(pay_a, pay_b, "grp")
    mid_two, mid_source, mid_weight, source_coarse, wide_coarse, pay_a, pay_b, sums = call(
        mid_kernel,
        [shaped(*ext_mid)] * 3
        + [shaped(quarter, 12, 256), shaped(quarter, 12, 256), shaped(80, 256), shaped(80, 256), shaped(8, 256)],
        [source_mid, conduct_mid, yy_a, yy_b, xx_a, xx_b, m_a, m_b, mx_a, mx_b, rho, load],
        [vmem(*ext_mid)] * 2 + [vmem(8, 2, half + 2 * HALO, LANES)] * 2,
        name="middle",
    )
    c_a, c_b = swap(pay_a, pay_b, "dev")
    (error,) = call(
        coarse_kernel,
        [shaped(8, 16, 256)],
        [source_coarse, wide_coarse, yy_a, yy_b, c_a, c_b],
        [vmem(*wide)] * 4,
        name="coarse",
    )
    sums = sums + c_a[72:80]
    distance = 2
    while distance < peers:
        sums = sums + exchange(sums, distance)
        distance *= 2
    error, pay_a, pay_b = call(
        shift_kernel, [shaped(8, 16, 256), shaped(2, 16, 256), shaped(2, 16, 256)], [error, sums], name="shift"
    )
    e_a, e_b = swap(pay_a, pay_b, "grp")
    (potential,) = call(
        finish_kernel,
        [shaped(nx, nx, 256)],
        [error, e_a, e_b, mid_two, mid_source, mid_weight, fine_two, fine_source, weight],
        [vmem(*ext_mid)] * 2
        + [vmem(*ext)] * 2
        + [vmem(12, 2, 2, 16, LANES), vmem(half + 2 * HALO, 3, 2, 16, LANES), vmem(nx, nx, 256)]
        + [pltpu.SemaphoreType.DMA((4,))],
        out_specs=[FAR],
        name="finish",
    )
    return (concentration, flux, potential)


def solution(mesh):
    brick = P("grp", "dev", None)
    return jax.shard_map(
        body,
        mesh=mesh,
        in_specs=(brick, brick, brick, brick, P("grp", "dev"), brick),
        out_specs=(brick, brick, brick),
        check_vma=False,
    )
```

```python
import jax
import jax.numpy as jnp
from jax import lax
from jax.experimental import pallas as pl
from jax.experimental.pallas import tpu as pltpu
from jax.sharding import PartitionSpec as P


F32 = jnp.float32
MASS = 0.05
OMEGA = 0.8
DIFFUSION_TABLE = (1.5, 0.1, 0.4)
CONDUCT_TABLE = (1.0, 0.3, 0.6)
KINETIC_TABLE = (0.2, 1.0, 0.5)
SWEEPS = 4
COARSE_SWEEPS = 8
COARSE_NEAR = 8
HALO = 4
LANES = 128
VMEM_LIMIT = 28 * 1024 * 1024
VMEM_MOST = 58 * 1024 * 1024


def shaped(*shape):
    return jax.ShapeDtypeStruct(shape, F32)


WHOLE = pl.BlockSpec(memory_space=pltpu.VMEM)
FAR = pl.BlockSpec(memory_space=pltpu.HBM)


def call(kernel, outs, args, scratch=(), in_specs=None, out_specs=None, limit=VMEM_LIMIT, aliases=None, flops=10**6, name=None):
    size = sum(4 * a.size for a in args) + sum(4 * o.size for o in outs)
    return pl.pallas_call(
        kernel,
        out_shape=tuple(outs),
        in_specs=in_specs or [WHOLE] * len(args),
        out_specs=tuple(out_specs or [WHOLE] * len(outs)),
        scratch_shapes=list(scratch),
        input_output_aliases=aliases or {},
        compiler_params=pltpu.CompilerParams(vmem_limit_bytes=limit),
        cost_estimate=pl.CostEstimate(flops=flops, bytes_accessed=size, transcendentals=0),
        name=name,
    )(*args)


def vmem(*shape):
    return pltpu.VMEM(shape, F32)


def iota(shape, dim):
    return lax.broadcasted_iota(jnp.int32, shape, dim)


def pick(label, table):
    return jnp.where(label == 0, table[0], jnp.where(label == 1, table[1], table[2])).astype(F32)


def loop(low, high, body, unroll=8):
    steps = (high - low) // unroll

    def step(i, carry):
        for u in range(unroll):
            body(low + i * unroll + u)
        return carry

    if steps > 1:
        lax.fori_loop(0, steps, step, 0)
    else:
        steps = 0
    for x in range(low + steps * unroll, high):
        body(x)


def odd(axis):
    return lax.rem(lax.axis_index(axis), 2) == 1


def along_y(v):
    return pltpu.roll(v, 1, 0) + pltpu.roll(v, v.shape[0] - 1, 0)


def along_z(v):
    low, high = v[:, :LANES], v[:, LANES:]
    lane = iota(low.shape, 1)
    first, last = lane == 0, lane == LANES - 1
    low_up, high_up = pltpu.roll(low, 1, 1), pltpu.roll(high, 1, 1)
    low_down, high_down = pltpu.roll(low, LANES - 1, 1), pltpu.roll(high, LANES - 1, 1)
    low_sum = jnp.where(first, 0.0, low_up) + jnp.where(last, high_down, low_down)
    high_sum = jnp.where(first, low_up, high_up) + jnp.where(last, 0.0, high_down)
    return jnp.concatenate([low_sum, high_sum], axis=1)


def upper(shape=(8, 256)):
    return iota(shape, 0) < HALO


def twice(tile, scratch):
    for h in range(2):
        part = tile[:, h * LANES : (h + 1) * LANES]
        scratch[h, pl.ds(0, 8, stride=2), :] = part
        scratch[h, pl.ds(1, 8, stride=2), :] = part
    return jnp.concatenate([scratch[0], scratch[1]], axis=1)


def pair_rows(v, scratch):
    half = v.shape[0] // 2
    parts = []
    for h in range(2):
        scratch[h] = v[:, h * LANES : (h + 1) * LANES]
        parts.append(scratch[h, pl.ds(0, half, stride=2), :] + scratch[h, pl.ds(1, half, stride=2), :])
    return jnp.concatenate(parts, axis=1)


def either(flag, if_true, if_false):
    return jnp.where(flag, if_true, if_false)


def y_sides(r_a, r_b, at, count):
    flag = odd("dev")
    a, b = r_a[at : at + count, :], r_b[at : at + count, :]
    return either(flag, a, b), either(flag, b, a)


def x_sides(r_a, r_b, index):
    flag = odd("grp")
    a, b = r_a[index], r_b[index]
    return either(flag, a, b), either(flag, b, a)


def send_y(pay_a, pay_b, at, first, last):
    flag = odd("dev")
    n = first.shape[0]
    pay_a[at : at + n, :] = either(flag, last, first)
    pay_b[at : at + n, :] = either(flag, first, last)


def send_x(pay_a, pay_b, index, first, last):
    flag = odd("grp")
    pay_a[index] = either(flag, last, first)
    pay_b[index] = either(flag, first, last)


def halo_tile(after, before):
    parts = [after]
    if after.shape[0] < HALO:
        parts.append(jnp.zeros((2 * HALO - 2 * after.shape[0], after.shape[1]), F32))
    return jnp.concatenate(parts + [before], axis=0)


def first_pack_kernel(
    conc, label, owner, block, pay_a, pay_b, own_lists, c_first, c_last, l_first, l_last, own_owner, own_block, sems
):
    nx = conc.shape[0]
    copies = [pltpu.make_async_copy(owner, own_owner, sems.at[4]), pltpu.make_async_copy(block, own_block, sems.at[5])]
    for i, (ref, at, to) in enumerate(((conc, 0, c_first), (conc, 24, c_last), (label, 0, l_first), (label, 24, l_last))):
        copies.append(pltpu.make_async_copy(ref.at[:, pl.ds(at, 8), :], to, sems.at[i]))
    for c in copies:
        c.start()
    for c in copies:
        c.wait()
    named = jnp.concatenate([own_owner[...], own_block[...], jnp.zeros((6, 256), jnp.int32)], axis=0).astype(F32)
    for j in range(own_lists.shape[0]):
        own_lists[j] = named
    for x in range(nx):
        send_y(pay_a, pay_b, 7 * x, c_first[x, 0:4, :], c_last[x, 4:8, :])
        send_y(pay_a, pay_b, 7 * x + 4, l_first[x, 0:3, :].astype(F32), l_last[x, 5:8, :].astype(F32))


def own_kernel(conc, label, phi, mid, coarse, pay_a, pay_b, pairs, pairs_2):
    nx = conc.shape[0]
    half = nx // 2

    def coarsen(i):
        total = conc[2 * i] * pick(label[2 * i], CONDUCT_TABLE) + conc[2 * i + 1] * pick(label[2 * i + 1], CONDUCT_TABLE)
        mid[i] = 0.25 * pair_rows(total, pairs.at[i])

    loop(0, half, coarsen, 4)
    for i in range(half // 2):
        coarse[i] = 0.25 * pair_rows(mid[2 * i] + mid[2 * i + 1], pairs_2.at[i])
    for k in range(HALO):
        for t in range(4):
            rows = slice(8 * t, 8 * t + 8)
            send_x(pay_a, pay_b, 4 * k + t, phi[k, rows, :], phi[nx - HALO + k, rows, :])
        for t in range(2):
            rows = slice(8 * t, 8 * t + 8)
            send_x(pay_a, pay_b, 16 + 2 * k + t, mid[k, rows, :], mid[half - HALO + k, rows, :])


def first_pack_x_kernel(conc, label, r_a, r_b, token, pay_a, pay_b):
    nx = conc.shape[0]

    def plane(ref, k, t, offset, count):
        if t < 4:
            return ref[k, 8 * t : 8 * t + 8, :].astype(F32)
        return halo_tile(*y_sides(r_a, r_b, 7 * k + offset, count))

    for t in range(5):
        for k in range(HALO):
            send_x(pay_a, pay_b, 5 * k + t, plane(conc, k, t, 0, 4), plane(conc, nx - HALO + k, t, 0, 4))
        for k in range(3):
            send_x(pay_a, pay_b, 20 + 5 * k + t, plane(label, k, t, 4, 3), plane(label, nx - 3 + k, t, 4, 3))


def second_pack_kernel(phi, mid, coarse, x_a, x_b, pay_a, pay_b):
    nx = phi.shape[0]
    half = nx // 2
    for x in range(nx):
        send_y(pay_a, pay_b, 4 * (HALO + x), phi[x, 0:4, :], phi[x, 28:32, :])
    for k in range(HALO):
        for t, at in ((0, slice(0, 4)), (3, slice(4, 8))):
            after, before = x_sides(x_a, x_b, 4 * k + t)
            if t == 0:
                first_after, first_before = after[at], before[at]
            else:
                last_after, last_before = after[at], before[at]
        send_y(pay_a, pay_b, 4 * k, first_before, last_before)
        send_y(pay_a, pay_b, 4 * (HALO + nx + k), first_after, last_after)
    base = 4 * (nx + 2 * HALO)
    for x in range(half):
        send_y(pay_a, pay_b, base + 4 * (HALO + x), mid[x, 0:4, :], mid[x, 12:16, :])
    for k in range(HALO):
        first_after, first_before = (v[0:4] for v in x_sides(x_a, x_b, 16 + 2 * k))
        last_after, last_before = (v[4:8] for v in x_sides(x_a, x_b, 16 + 2 * k + 1))
        send_y(pay_a, pay_b, base + 4 * k, first_before, last_before)
        send_y(pay_a, pay_b, base + 4 * (HALO + half + k), first_after, last_after)
    base += 4 * (half + 2 * HALO)
    for x in range(8):
        pay_a[base + 8 * x : base + 8 * x + 8, :] = coarse[x]
        pay_b[base + 8 * x : base + 8 * x + 8, :] = coarse[x]


def wide_rows(own, after_own, before_own, after, before):
    gap = jnp.zeros((6, 256), F32)
    return jnp.concatenate([own, after_own, after, gap, before, before_own], axis=0)


def sweeps_kernel(conc, label, y_a, y_b, x_a, x_b, out, one, two, gain, base):
    nx = conc.shape[0]
    ratio = tuple(d / (1.0 + 6.0 * d) for d in DIFFUSION_TABLE)
    inverse = tuple(1.0 / (1.0 + 6.0 * d) for d in DIFFUSION_TABLE)

    def put(x, rows, c, lab):
        one[x, rows, :] = c
        gain[x, rows, :] = jnp.where(c > 0.0, pick(lab, ratio), 0.0)
        base[x, rows, :] = c * pick(lab, inverse)

    def own(i):
        put(HALO + i, slice(0, 32), conc[i], label[i])

    loop(0, nx, own)
    for i in range(nx):
        c = halo_tile(*y_sides(y_a, y_b, 7 * i, 4))
        lab = halo_tile(*y_sides(y_a, y_b, 7 * i + 4, 3))
        put(HALO + i, slice(32, 40), c, lab)
    for t in range(5):
        rows = slice(8 * t, 8 * t + 8)
        for k in range(HALO):
            c_after, c_before = x_sides(x_a, x_b, 5 * k + t)
            l_after = x_sides(x_a, x_b, 20 + 5 * min(k, 2) + t)[0]
            l_before = x_sides(x_a, x_b, 20 + 5 * max(k - 1, 0) + t)[1]
            put(k, rows, c_before, l_before)
            put(HALO + nx + k, rows, c_after, l_after)

    def stencil(old, x):
        mid = old[x]
        return base[x] + gain[x] * ((old[x - 1] + old[x + 1]) + (along_y(mid) + along_z(mid)))

    fields = (one, two)
    for s in range(1, SWEEPS):
        old, new = fields[(s - 1) % 2], fields[s % 2]

        def sweep(x, old=old, new=new):
            new[x] = stencil(old, x)

        loop(s, nx + 2 * HALO - s, sweep)

    old = fields[(SWEEPS - 1) % 2]

    def last(i):
        out[i] = stencil(old, HALO + i)[0:32, :]

    loop(0, nx, last)


def flux_kernel(conc, label, phi, solid, lists, flux, pay_a, pay_b, marked):
    nx = conc.shape[0]
    entries = lists.shape[0] * 256
    owner = jnp.concatenate([lists[i, 0:1, :] for i in range(lists.shape[0])], axis=1)
    block = jnp.concatenate([lists[i, 1:2, :] for i in range(lists.shape[0])], axis=1)
    here = lax.axis_index("dev")
    block = jnp.where(owner.astype(jnp.int32) == here, block.astype(jnp.int32), -1)
    hit_row = (iota((32, entries), 0) == lax.shift_right_arithmetic(block, 6)).astype(jnp.bfloat16)
    hit_column = (iota((LANES, entries), 0) == lax.rem(block, 64)).astype(jnp.bfloat16)
    named = lax.dot_general(hit_row, hit_column, (((1,), (1,)), ((), ())), preferred_element_type=F32)
    for i in range(32):
        marked[i] = jnp.broadcast_to(named[i : i + 1, :], (8, LANES))
    is_row = lax.div(iota((32, LANES), 1), 2) == iota((32, LANES), 0)
    spread = (lax.rem(iota((LANES, 256), 0), 2) == lax.div(iota((LANES, 256), 1), LANES)).astype(jnp.bfloat16)

    def plane(i):
        marks = jnp.where(is_row, jnp.concatenate([marked[i]] * 4, axis=0), 0.0).astype(jnp.bfloat16)
        listed = jnp.dot(marks, spread, preferred_element_type=F32) > 0.5
        drive = 0.5 * (solid[i] - phi[i])
        logc = jnp.log(conc[i])
        value = jnp.exp(drive + 0.4 * logc) - jnp.exp(0.6 * logc - drive)
        flux[i] = jnp.where(listed, pick(label[i], KINETIC_TABLE) * value, 0.0)

    loop(0, nx, plane, 4)
    for x in range(nx):
        send_y(pay_a, pay_b, 3 * x, flux[x, 0:3, :], flux[x, 29:32, :])


def store_kernel(conc, flux, conc_out, flux_out, token, sems):
    copies = []
    for i, (ref, to) in enumerate(((conc, conc_out), (flux, flux_out))):
        for j in range(4):
            rows = pl.ds(8 * j, 8)
            copies.append(pltpu.make_async_copy(ref.at[rows], to.at[rows], sems.at[4 * i + j]))
            copies[-1].start()
    token[...] = jnp.zeros(token.shape, F32)
    for c in copies:
        c.wait()


def ready_kernel(conc, label, phi, y_a, y_b, x_a, x_b, yy_a, yy_b, xx_a, xx_b, weight, scale, share, start, token, field):
    nx = conc.shape[0]
    token[...] = jnp.zeros(token.shape, F32)

    def put(x, rows, c, lab, p):
        conduct = c * pick(lab, CONDUCT_TABLE)
        factor = OMEGA / (MASS + 6.0 * conduct)
        weight[x, rows, :] = conduct * factor
        scale[x, rows, :] = factor
        share[x, rows, :] = MASS * p * factor
        field[x, rows, :] = p

    def own(i):
        put(HALO + i, slice(0, 32), conc[i], label[i], phi[i])

    loop(0, nx, own, 4)
    low = slice(32, 40)
    for i in range(nx):
        c = halo_tile(*y_sides(y_a, y_b, 7 * i, 4))
        lab = halo_tile(*y_sides(y_a, y_b, 7 * i + 4, 3))
        put(HALO + i, low, c, lab, halo_tile(*y_sides(yy_a, yy_b, 4 * (HALO + i), 4)))
    for t in range(5):
        rows = slice(8 * t, 8 * t + 8)
        for k in range(HALO):
            c_after, c_before = x_sides(x_a, x_b, 5 * k + t)
            l_after = x_sides(x_a, x_b, 20 + 5 * min(k, 2) + t)[0]
            l_before = x_sides(x_a, x_b, 20 + 5 * max(k - 1, 0) + t)[1]
            if t < 4:
                p_after, p_before = x_sides(xx_a, xx_b, 4 * k + t)
            else:
                p_after = halo_tile(*y_sides(yy_a, yy_b, 4 * (HALO + nx + k), 4))
                p_before = halo_tile(*y_sides(yy_a, yy_b, 4 * k, 4))
            put(k, rows, c_before, l_before, p_before)
            put(HALO + nx + k, rows, c_after, l_after, p_after)

    def sweep(x):
        p = field[x]
        around = (field[x - 1] + field[x + 1]) + (along_y(p) + along_z(p))
        start[x] = 0.2 * p + share[x] + weight[x] * around

    loop(1, nx + 2 * HALO - 1, sweep)


def flux_pack_x_kernel(flux, r_a, r_b, token, token_2, pay_a, pay_b):
    nx = flux.shape[0]

    def tile(x, t):
        if t < 4:
            return flux[x, 8 * t : 8 * t + 8, :]
        return halo_tile(*y_sides(r_a, r_b, 3 * x, 3))

    for k in range(3):
        for t in range(5):
            send_x(pay_a, pay_b, 5 * k + t, tile(k, t), tile(nx - 3 + k, t))


def potential_inner_kernel(flux, y_a, y_b, weight, scale, share, start, after_two, source, first, source_mid, pairs):
    nx = flux.shape[0]

    def put(x, rows, f):
        part = scale[x, rows, :] * f
        source[x, rows, :] = share[x, rows, :] + part
        first[x, rows, :] = start[x, rows, :] + part

    def own(i):
        put(HALO + i, slice(0, 32), flux[i])

    loop(0, nx, own)
    for i in range(nx):
        put(HALO + i, slice(32, 40), halo_tile(*y_sides(y_a, y_b, 3 * i, 3)))

    def around(values, x):
        v = values[x]
        return v, weight[x] * ((values[x - 1] + values[x + 1]) + (along_y(v) + along_z(v)))

    def sweep(x):
        v, near = around(first, x)
        after_two[x] = 0.2 * v + (source[x] + near)

    loop(HALO + 1, HALO + nx - 1, sweep)

    def remainder(x):
        v, near = around(after_two, x)
        return ((source[x] - OMEGA * v) + near)[0:32, :] / scale[x, 0:32, :]

    def coarsen(i):
        x = HALO + 2 * i
        source_mid[i] = 0.25 * pair_rows(remainder(x) + remainder(x + 1), pairs.at[i])

    loop(1, nx // 2 - 1, coarsen, 4)


def potential_edge_kernel(
    x_a, x_b, weight, scale, share, start, inner_two, inner_source, inner_first, inner_mid,
    edge_two, edge_source, source_mid, pay_a, pay_b, first, pairs,
):
    half = source_mid.shape[0]
    nx = 2 * half
    for side, face in ((0, HALO), (1, HALO + nx)):
        base = 8 * side + HALO - face
        for k in range(3):
            x = face - 3 + k if side == 0 else face + k
            for t in range(5):
                rows = slice(8 * t, 8 * t + 8)
                part = scale[x, rows, :] * x_sides(x_a, x_b, 5 * k + t)[1 - side]
                edge_source[base + x, rows, :] = share[x, rows, :] + part
                first[base + x, rows, :] = start[x, rows, :] + part

        def first_of(x, base=base):
            return inner_first[x] if HALO <= x < HALO + nx else first[base + x]

        def source_of(x, base=base):
            return inner_source[x] if HALO <= x < HALO + nx else edge_source[base + x]

        def two_of(x, base=base):
            return inner_two[x] if HALO < x < HALO + nx - 1 else edge_two[base + x]

        for x in range(face - 2, face + 1) if side == 0 else range(face - 1, face + 2):
            v = first_of(x)
            near = weight[x] * ((first_of(x - 1) + first_of(x + 1)) + (along_y(v) + along_z(v)))
            edge_two[base + x] = 0.2 * v + (source_of(x) + near)
        total = 0.0
        at = face if side == 0 else face - 2
        for x in (at, at + 1):
            v = two_of(x)
            near = weight[x] * ((two_of(x - 1) + two_of(x + 1)) + (along_y(v) + along_z(v)))
            total = total + ((source_of(x) - OMEGA * v) + near)[0:32, :] / scale[x, 0:32, :]
        source_mid[0 if side == 0 else half - 1] = 0.25 * pair_rows(total, pairs.at[side])
    for x in range(1, half - 1):
        source_mid[x] = inner_mid[x]
    for x in range(half):
        send_y(pay_a, pay_b, 4 * x, source_mid[x, 0:4, :], source_mid[x, 12:16, :])


def mid_pack_x_kernel(field, r_a, r_b, token, pay_a, pay_b):
    n = field.shape[0]

    def tile(x, t):
        if t < 2:
            return field[x, 8 * t : 8 * t + 8, :]
        return halo_tile(*y_sides(r_a, r_b, 4 * x, 4))

    for k in range(HALO):
        for t in range(3):
            send_x(pay_a, pay_b, 3 * k + t, tile(k, t), tile(n - HALO + k, t))


def mid_kernel(
    source_own, conduct_own, yy_a, yy_b, xx_a, xx_b, y_a, y_b, x_a, x_b, rho, load,
    after_two, source, weight, coarse, conduct, pay_a, pay_b, part, scale, mid_conduct, pairs, pairs_2,
):
    n = source_own.shape[0]
    base = 4 * (2 * n + 2 * HALO)

    def put(x, rows, b, k):
        factor = OMEGA / (MASS + 3.0 * k)
        weight[x, rows, :] = k * factor
        scale[x, rows, :] = factor
        source[x, rows, :] = factor * b
        mid_conduct[x, rows, :] = k

    def far(x):
        return halo_tile(*y_sides(yy_a, yy_b, base + 4 * x, 4))

    for i in range(n):
        put(HALO + i, slice(0, 16), source_own[i], conduct_own[i])
        put(HALO + i, slice(16, 24), halo_tile(*y_sides(y_a, y_b, 4 * i, 4)), far(HALO + i))
    for k in range(HALO):
        for t in range(3):
            rows = slice(8 * t, 8 * t + 8)
            b_after, b_before = x_sides(x_a, x_b, 3 * k + t)
            if t < 2:
                c_after, c_before = x_sides(xx_a, xx_b, 16 + 2 * k + t)
            else:
                c_after, c_before = far(HALO + n + k), far(k)
            put(k, rows, b_before, c_before)
            put(HALO + n + k, rows, b_after, c_after)

    def around(values, x):
        v = values[x]
        return v, weight[x] * (0.25 * ((values[x - 1] + values[x + 1]) + along_y(v)) + along_z(v))

    def sweep(x):
        v, near = around(source, x)
        after_two[x] = 0.2 * v + (source[x] + near)

    loop(1, n + 2 * HALO - 1, sweep, 11)

    def remainder(x):
        v, near = around(after_two, x)
        return ((source[x] - OMEGA * v) + near) / scale[x]

    total = jnp.zeros((8, 256), F32)
    for i in range(n // 2):
        x = HALO + 2 * i
        value = 0.25 * pair_rows(remainder(x) + remainder(x + 1), pairs.at[i])
        k = 0.25 * pair_rows(mid_conduct[x] + mid_conduct[x + 1], pairs_2.at[i])
        coarse[i] = value
        conduct[i] = k
        send_y(pay_a, pay_b, 9 * i, value[1:9], jnp.concatenate([value[11:12], value[0:7]], axis=0))
        send_y(pay_a, pay_b, 9 * i + 8, k[8:9], k[11:12])
        total += rho[i] * value[0:8]
    sums = jnp.concatenate([total[:, :LANES] + total[:, LANES:], load[...]], axis=1)
    pay_a[72:80, :] = sums
    pay_b[72:80, :] = sums
    part[...] = sums


COARSE_W = 0.0625


def coarse_ready_kernel(own, r_a, r_b, rho, load, token, one, two, conduct, scale):
    token[...] = jnp.zeros(token.shape, F32)
    base = r_a.shape[0] - 64
    for x in range(8):
        after, before = y_sides(r_a, r_b, base + 8 * x, 8)
        k = jnp.concatenate([own[x], after, jnp.zeros((8, 256), F32), before], axis=0)
        conduct[x] = k
        scale[x] = OMEGA / (MASS + 2.25 * k)
        one[x] = jnp.ones(k.shape, F32)
    fields = (one, two)
    for s in range(COARSE_SWEEPS):
        old, new = fields[s % 2], fields[(s + 1) % 2]
        for x in range(8):
            near = [conduct[i] * old[i] if 0 <= i < 8 else None for i in (x - 1, x, x + 1)]
            inner = along_y(near[1])
            for other in (near[0], near[2]):
                if other is not None:
                    inner = inner + other
            new[x] = 0.2 * old[x] + scale[x] * (COARSE_W * inner + along_z(near[1]))
    last = fields[COARSE_SWEEPS % 2]
    peer, peers = lax.axis_index("dev"), lax.axis_size("dev")
    row, z = iota((8, 256), 0), iota((8, 256), 1)
    edge_y = ((row == 0) & (peer == 0)) | ((row == 7) & (peer == peers - 1))
    edge = edge_y.astype(F32) * COARSE_W + ((z == 0) | (z == 255)).astype(F32)
    total = jnp.zeros((8, 256), F32)
    for x in range(8):
        rho[x] = last[x, 0:8, :]
        total += MASS + own[x] * (edge + (COARSE_W if x in (0, 7) else 0.0))
    load[...] = total[:, :LANES] + total[:, LANES:]


def coarse_kernel(own, conduct, far_a, far_b, r_a, r_b, error, source, weight, one, two):
    base = far_a.shape[0] - 64
    for x in range(8):
        after, before = y_sides(r_a, r_b, 9 * x, 8)
        b = wide_rows(own[x, 0:8, :], own[x, 8:9, :], own[x, 11:12, :], after, before)
        last_after, last_before = y_sides(r_a, r_b, 9 * x + 8, 1)
        after, before = y_sides(far_a, far_b, base + 8 * x, 8)
        after = jnp.concatenate([after[1:8], last_after], axis=0)
        before = jnp.concatenate([last_before, before[0:7]], axis=0)
        k = wide_rows(conduct[x, 0:8, :], conduct[x, 8:9, :], conduct[x, 11:12, :], after, before)
        factor = OMEGA / (MASS + 2.25 * k)
        weight[x] = k * factor
        source[x] = factor * b
    old = source
    for s in range(1, COARSE_SWEEPS):
        new = one if s % 2 else two
        for x in range(8):
            v = old[x]
            inner = along_y(v)
            if x > 0:
                inner = inner + old[x - 1]
            if x < 7:
                inner = inner + old[x + 1]
            new[x] = 0.2 * v + (source[x] + weight[x] * (COARSE_W * inner + along_z(v)))
        old = new
    for x in range(8):
        error[x, 0:8, :] = old[x, 0:8, :]
        error[x, 8:16, :] = jnp.where(upper(), old[x, 8:16, :], old[x, 24:32, :])


def shift_kernel(error, sums, out, pay_a, pay_b):
    resid = jnp.sum(sums[:, :LANES])
    load = jnp.sum(sums[:, LANES:])
    shift_c = jnp.full((16, 256), resid, F32) / jnp.full((16, 256), load, F32)
    for x in range(8):
        out[x] = error[x] + shift_c
    for k in range(2):
        send_x(pay_a, pay_b, k, out[k], out[6 + k])


def squeeze(tile):
    return jnp.where(iota((8, 256), 0) < 2, tile, pltpu.roll(tile, 4, 0))


def spread_coarse(plane, room):
    return jnp.concatenate([twice(plane[0:8], room.at[0]), twice(squeeze(plane[8:16]), room.at[1])[0:8]], axis=0)


def spread_mid(plane, room):
    parts = [twice(plane[0:8], room.at[0]), twice(plane[8:16], room.at[1]), twice(squeeze(plane[16:24]), room.at[2])[0:8]]
    return jnp.concatenate(parts, axis=0)


def smoothed(before, v, after, weight, source, w):
    inner = (before + after) + along_y(v)
    return source + (0.2 * v + weight * (w * inner + along_z(v)))


def finish_inner_kernel(
    error, mid_two, mid_source, mid_weight, fine_two, fine_source, fine_weight,
    out, zero, one, fine_one, fine_last, two, dup, dup_2, result, sems,
):
    n = mid_two.shape[0]
    nf = fine_two.shape[0]
    for c in range(8):
        spread = spread_coarse(error[c], dup.at[c])
        for x in (2 * c + HALO, 2 * c + 1 + HALO):
            zero[x] = jnp.where(mid_weight[x] > 0.0, mid_two[x] + spread, 0.0)

    def sweep_mid(x, old, new):
        new[x] = smoothed(old[x - 1], old[x], old[x + 1], mid_weight[x], mid_source[x], 0.25)

    for x in range(HALO + 1, n - HALO - 1):
        sweep_mid(x, zero, one)
    for x in range(HALO + 2, n - HALO - 2):
        sweep_mid(x, one, two)

    def lift(m):
        spread = spread_mid(two[m], dup_2.at[m])
        x = 2 * m - HALO
        fine_one[x] = fine_two[x] + spread
        fine_one[x + 1] = fine_two[x + 1] + spread

    loop(HALO + 2, n - HALO - 2, lift, 6)

    def sweep_one(x):
        fine_last[x] = smoothed(fine_one[x - 1], fine_one[x], fine_one[x + 1], fine_weight[x], fine_source[x], 1.0)

    low, high = 2 * HALO + 1, nf - 2 * HALO - 1
    loop(low, high, sweep_one, 11)
    copies = []
    low, high = low + 1, high - 1
    for j in range(2):
        mid = low + (high - low) // 2
        for x in range(low, mid) if j == 0 else range(mid, high):
            v = smoothed(fine_last[x - 1], fine_last[x], fine_last[x + 1], fine_weight[x], fine_source[x], 1.0)
            result[x - HALO] = v[0:32, :]
        rows = pl.ds(low - HALO, mid - low) if j == 0 else pl.ds(mid - HALO, high - mid)
        copies.append(pltpu.make_async_copy(result.at[rows], out.at[rows], sems.at[j]))
        copies[-1].start()
    for c in copies:
        c.wait()


def finish_edge_kernel(
    x_a, x_b, mid_two, mid_source, mid_weight, fine_two, edge_two, fine_source, edge_source, fine_weight,
    zero, one, fine_one, fine_last, begun, out, zero_edge, one_edge, fine_edge, last_edge, dup, dup_2, result, sems,
):
    n = mid_two.shape[0]
    nf = fine_two.shape[0]
    nx = nf - 2 * HALO
    copies = []
    planes = x_sides(x_a, x_b, slice(0, 2))
    for side in (0, 1):
        sign = 1 if side == 0 else -1
        at = lambda k, side=side: HALO + k if side == 0 else n - HALO - 1 - k
        fine = lambda k, side=side: HALO + k if side == 0 else nf - HALO - 1 - k
        base = 8 * side + (0 if side == 0 else HALO - HALO - nx)
        for c in range(2):
            plane = planes[1 - side][c]
            spread = spread_coarse(plane, dup.at[2 * side + c])
            first = 2 * c if side == 0 else n - HALO + 2 * c
            for x in (first, first + 1):
                zero_edge[x] = jnp.where(mid_weight[x] > 0.0, mid_two[x] + spread, 0.0)

        def zero_of(k):
            return zero[at(k)] if k >= 0 else zero_edge[at(k)]

        def one_of(k):
            return one[at(k)] if k >= 1 else one_edge[at(k)]

        for k in range(-2, 1):
            x = at(k)
            one_edge[x] = smoothed(zero_of(k - 1), zero_of(k), zero_of(k + 1), mid_weight[x], mid_source[x], 0.25)
        for k in range(-1, 2):
            x = at(k)
            value = smoothed(one_of(k - 1), one_of(k), one_of(k + 1), mid_weight[x], mid_source[x], 0.25)
            spread = spread_mid(value, dup_2.at[3 * side + k + 1])
            for f in (fine(2 * k), fine(2 * k + 1)):
                inside = HALO < f < nf - HALO - 1
                before = fine_two[f] if inside else edge_two[base + f]
                fine_edge[f] = before + spread

        def fine_of(k):
            return fine_one[fine(k)] if k >= 4 else fine_edge[fine(k)]

        def last_of(k):
            return fine_last[fine(k)] if k >= 5 else last_edge[fine(k)]

        for k in range(-1, 5):
            f = fine(k)
            source = fine_source[f] if HALO <= f < nf - HALO else edge_source[base + f]
            last_edge[f] = smoothed(fine_of(k - 1), fine_of(k), fine_of(k + 1), fine_weight[f], source, 1.0)
        for k in range(6):
            f = fine(k)
            v = smoothed(last_of(k - 1), last_of(k), last_of(k + 1), fine_weight[f], fine_source[f], 1.0)
            result[f - HALO] = v[0:32, :]
        rows = pl.ds(0, 6) if side == 0 else pl.ds(nx - 6, 6)
        copies.append(pltpu.make_async_copy(result.at[rows], out.at[rows], sems.at[side]))
        copies[-1].start()
    for c in copies:
        c.wait()


def both_ways(pairs):
    return pairs + [(j, i) for i, j in pairs]


def swap(pay_a, pay_b, axis):
    size = lax.axis_size(axis)
    pairs_a = [(i, i + 1) for i in range(1, size - 1, 2)]
    pairs_b = [(i, i + 1) for i in range(0, size - 1, 2)]
    return lax.ppermute(pay_a, axis, both_ways(pairs_a)), lax.ppermute(pay_b, axis, both_ways(pairs_b))


def exchange(value, distance):
    return lax.ppermute(value, "dev", [(i, i ^ distance) for i in range(lax.axis_size("dev"))])


def body(conc_old, phi_old, solid_pot, phase_label, iface_block, iface_owner):
    peers = lax.axis_size("dev")
    nx = conc_old.shape[0]
    half = nx // 2
    quarter = nx // 4
    ext = (nx + 2 * HALO, nx + 2 * HALO, 256)
    ext_mid = (half + 2 * HALO, half + 2 * HALO, 256)
    token_shape = shaped(8, LANES)

    pay_a, pay_b, own_lists = call(
        first_pack_kernel,
        [shaped(7 * nx, 256)] * 2 + [shaped(peers, 8, 256)],
        [conc_old, phase_label, iface_owner.reshape(1, -1), iface_block],
        [vmem(nx, 8, 256)] * 2
        + [pltpu.VMEM((nx, 8, 256), jnp.int32)] * 2
        + [pltpu.VMEM((1, 256), jnp.int32)] * 2
        + [pltpu.SemaphoreType.DMA((6,))],
        in_specs=[FAR] * 4,
        limit=VMEM_MOST,
        name="first_pack",
    )
    y_a, y_b = swap(pay_a, pay_b, "dev")
    conduct_mid, conduct_coarse, pay_a, pay_b = call(
        own_kernel,
        [shaped(half, half, 256), shaped(quarter, quarter, 256), shaped(24, 8, 256), shaped(24, 8, 256)],
        [conc_old, phase_label, phi_old],
        [vmem(half, 2, nx, LANES), vmem(quarter, 2, half, LANES)],
        name="own",
    )
    xx_a, xx_b = swap(pay_a, pay_b, "grp")
    lists = lax.all_to_all(own_lists, "dev", split_axis=0, concat_axis=0, tiled=True)
    pay_a, pay_b = call(
        first_pack_x_kernel,
        [shaped(35, 8, 256)] * 2,
        [conc_old, phase_label, y_a, y_b, lists],
        name="first_pack_x",
    )
    x_a, x_b = swap(pay_a, pay_b, "grp")
    far_rows = 4 * (nx + half + 4 * HALO) + 64
    pay_a, pay_b = call(
        second_pack_kernel,
        [shaped(far_rows, 256)] * 2,
        [phi_old, conduct_mid, conduct_coarse, xx_a, xx_b],
        name="second_pack",
    )
    yy_a, yy_b = swap(pay_a, pay_b, "dev")

    (conc_new,) = call(
        sweeps_kernel,
        [shaped(nx, nx, 256)],
        [conc_old, phase_label, y_a, y_b, x_a, x_b],
        [vmem(*ext)] * 4,
        name="sweeps",
    )
    flux_own, pay_a, pay_b = call(
        flux_kernel,
        [shaped(nx, nx, 256), shaped(3 * nx, 256), shaped(3 * nx, 256)],
        [conc_new, phase_label, phi_old, solid_pot, lists],
        [vmem(32, 8, LANES)],
        name="flux",
    )
    f_a, f_b = swap(pay_a, pay_b, "dev")
    concentration, flux, stored = call(
        store_kernel,
        [shaped(nx, nx, 256), shaped(nx, nx, 256), token_shape],
        [conc_new, flux_own],
        [pltpu.SemaphoreType.DMA((8,))],
        out_specs=[FAR, FAR, WHOLE],
        name="store",
    )
    weight, scale, share, start, made = call(
        ready_kernel,
        [shaped(*ext)] * 4 + [token_shape],
        [conc_old, phase_label, phi_old, y_a, y_b, x_a, x_b, yy_a, yy_b, xx_a, xx_b],
        [vmem(*ext)],
        name="ready",
    )
    pay_a, pay_b = call(
        flux_pack_x_kernel, [shaped(15, 8, 256)] * 2, [flux_own, f_a, f_b, stored, made], name="flux_pack_x"
    )
    fx_a, fx_b = swap(pay_a, pay_b, "grp")
    fine_two, fine_source, fine_first, inner_mid = call(
        potential_inner_kernel,
        [shaped(*ext)] * 3 + [shaped(half, half, 256)],
        [flux_own, f_a, f_b, weight, scale, share, start],
        [vmem(half, 2, nx, LANES)],
        name="potential_inner",
    )
    edge = (16, nx + 2 * HALO, 256)
    edge_two, edge_source, source_mid, pay_a, pay_b = call(
        potential_edge_kernel,
        [shaped(*edge), shaped(*edge), shaped(half, half, 256), shaped(4 * half, 256), shaped(4 * half, 256)],
        [fx_a, fx_b, weight, scale, share, start, fine_two, fine_source, fine_first, inner_mid],
        [vmem(*edge), vmem(2, 2, nx, LANES)],
        name="potential_edge",
    )
    m_a, m_b = swap(pay_a, pay_b, "dev")
    wide = (quarter, 32, 256)
    rho, load, made = call(
        coarse_ready_kernel,
        [shaped(quarter, quarter, 256), shaped(8, LANES), token_shape],
        [conduct_coarse, yy_a, yy_b],
        [vmem(*wide)] * 4,
        name="coarse_ready",
    )
    pay_a, pay_b = call(
        mid_pack_x_kernel, [shaped(3 * HALO, 8, 256)] * 2, [source_mid, m_a, m_b, made], name="mid_pack_x"
    )
    mx_a, mx_b = swap(pay_a, pay_b, "grp")
    mid_two, mid_source, mid_weight, source_coarse, wide_coarse, pay_a, pay_b, sums = call(
        mid_kernel,
        [shaped(*ext_mid)] * 3
        + [shaped(quarter, 12, 256), shaped(quarter, 12, 256), shaped(80, 256), shaped(80, 256), shaped(8, 256)],
        [source_mid, conduct_mid, yy_a, yy_b, xx_a, xx_b, m_a, m_b, mx_a, mx_b, rho, load],
        [vmem(*ext_mid)] * 2 + [vmem(8, 2, half + 2 * HALO, LANES)] * 2,
        name="middle",
    )
    c_a, c_b = swap(pay_a, pay_b, "dev")
    (error,) = call(
        coarse_kernel,
        [shaped(8, 16, 256)],
        [source_coarse, wide_coarse, yy_a, yy_b, c_a, c_b],
        [vmem(*wide)] * 4,
        name="coarse",
    )
    sums = sums + c_b[72:80]
    distance = 2
    while distance < peers:
        sums = sums + exchange(sums, distance)
        distance *= 2
    error, pay_a, pay_b = call(
        shift_kernel, [shaped(8, 16, 256), shaped(2, 16, 256), shaped(2, 16, 256)], [error, sums], name="shift"
    )
    e_a, e_b = swap(pay_a, pay_b, "grp")
    begun, zero, one, fine_one, fine_last = call(
        finish_inner_kernel,
        [shaped(nx, nx, 256), shaped(*ext_mid), shaped(*ext_mid), shaped(*ext), shaped(*ext)],
        [error, mid_two, mid_source, mid_weight, fine_two, fine_source, weight],
        [vmem(*ext_mid), vmem(8, 2, 2, 16, LANES), vmem(half + 2 * HALO, 3, 2, 16, LANES), vmem(nx, nx, 256)]
        + [pltpu.SemaphoreType.DMA((2,))],
        out_specs=[FAR] + [WHOLE] * 4,
        name="finish_inner",
    )
    finish_args = [e_a, e_b, mid_two, mid_source, mid_weight, fine_two, edge_two, fine_source, edge_source, weight]
    finish_args += [zero, one, fine_one, fine_last, begun]
    (potential,) = call(
        finish_edge_kernel,
        [shaped(nx, nx, 256)],
        finish_args,
        [vmem(*ext_mid), vmem(*ext_mid), vmem(*ext), vmem(*ext)]
        + [vmem(4, 2, 2, 16, LANES), vmem(6, 3, 2, 16, LANES), vmem(nx, nx, 256)]
        + [pltpu.SemaphoreType.DMA((2,))],
        in_specs=[WHOLE] * (len(finish_args) - 1) + [FAR],
        out_specs=[FAR],
        aliases={len(finish_args) - 1: 0},
        name="finish_edge",
    )
    return (concentration, flux, potential)


def solution(mesh):
    brick = P("grp", "dev", None)
    return jax.shard_map(
        body,
        mesh=mesh,
        in_specs=(brick, brick, brick, brick, P("grp", "dev"), brick),
        out_specs=(brick, brick, brick),
        check_vma=False,
    )
```

```python
import jax
import jax.numpy as jnp
from jax import lax
from jax.experimental import pallas as pl
from jax.experimental.pallas import tpu as pltpu
from jax.sharding import PartitionSpec as P


F32 = jnp.float32
MASS = 0.05
OMEGA = 0.8
DIFFUSION_TABLE = (1.5, 0.1, 0.4)
CONDUCT_TABLE = (1.0, 0.3, 0.6)
KINETIC_TABLE = (0.2, 1.0, 0.5)
SWEEPS = 4
COARSE_SWEEPS = 8
COARSE_NEAR = 8
HALO = 4
LANES = 128
VMEM_LIMIT = 28 * 1024 * 1024
VMEM_MOST = 58 * 1024 * 1024


def shaped(*shape):
    return jax.ShapeDtypeStruct(shape, F32)


WHOLE = pl.BlockSpec(memory_space=pltpu.VMEM)
FAR = pl.BlockSpec(memory_space=pltpu.HBM)


def call(kernel, outs, args, scratch=(), in_specs=None, out_specs=None, limit=VMEM_LIMIT, aliases=None, flops=10**6, name=None):
    size = sum(4 * a.size for a in args) + sum(4 * o.size for o in outs)
    return pl.pallas_call(
        kernel,
        out_shape=tuple(outs),
        in_specs=in_specs or [WHOLE] * len(args),
        out_specs=tuple(out_specs or [WHOLE] * len(outs)),
        scratch_shapes=list(scratch),
        input_output_aliases=aliases or {},
        compiler_params=pltpu.CompilerParams(vmem_limit_bytes=limit),
        cost_estimate=pl.CostEstimate(flops=flops, bytes_accessed=size, transcendentals=0),
        name=name,
    )(*args)


def vmem(*shape):
    return pltpu.VMEM(shape, F32)


def iota(shape, dim):
    return lax.broadcasted_iota(jnp.int32, shape, dim)


def pick(label, table):
    return jnp.where(label == 0, table[0], jnp.where(label == 1, table[1], table[2])).astype(F32)


def loop(low, high, body, unroll=8):
    steps = (high - low) // unroll

    def step(i, carry):
        for u in range(unroll):
            body(low + i * unroll + u)
        return carry

    if steps > 1:
        lax.fori_loop(0, steps, step, 0)
    else:
        steps = 0
    for x in range(low + steps * unroll, high):
        body(x)


def odd(axis):
    return lax.rem(lax.axis_index(axis), 2) == 1


def along_y(v):
    return pltpu.roll(v, 1, 0) + pltpu.roll(v, v.shape[0] - 1, 0)


def along_z(v):
    low, high = v[:, :LANES], v[:, LANES:]
    lane = iota(low.shape, 1)
    first, last = lane == 0, lane == LANES - 1
    low_up, high_up = pltpu.roll(low, 1, 1), pltpu.roll(high, 1, 1)
    low_down, high_down = pltpu.roll(low, LANES - 1, 1), pltpu.roll(high, LANES - 1, 1)
    low_sum = jnp.where(first, 0.0, low_up) + jnp.where(last, high_down, low_down)
    high_sum = jnp.where(first, low_up, high_up) + jnp.where(last, 0.0, high_down)
    return jnp.concatenate([low_sum, high_sum], axis=1)


def upper(shape=(8, 256)):
    return iota(shape, 0) < HALO


def twice(tile, scratch):
    for h in range(2):
        part = tile[:, h * LANES : (h + 1) * LANES]
        scratch[h, pl.ds(0, 8, stride=2), :] = part
        scratch[h, pl.ds(1, 8, stride=2), :] = part
    return jnp.concatenate([scratch[0], scratch[1]], axis=1)


def pair_rows(v, scratch):
    half = v.shape[0] // 2
    parts = []
    for h in range(2):
        scratch[h] = v[:, h * LANES : (h + 1) * LANES]
        parts.append(scratch[h, pl.ds(0, half, stride=2), :] + scratch[h, pl.ds(1, half, stride=2), :])
    return jnp.concatenate(parts, axis=1)


def either(flag, if_true, if_false):
    return jnp.where(flag, if_true, if_false)


def y_sides(r_a, r_b, at, count):
    flag = odd("dev")
    a, b = r_a[at : at + count, :], r_b[at : at + count, :]
    return either(flag, a, b), either(flag, b, a)


def x_sides(r_a, r_b, index):
    flag = odd("grp")
    a, b = r_a[index], r_b[index]
    return either(flag, a, b), either(flag, b, a)


def send_y(pay_a, pay_b, at, first, last):
    flag = odd("dev")
    n = first.shape[0]
    pay_a[at : at + n, :] = either(flag, last, first)
    pay_b[at : at + n, :] = either(flag, first, last)


def send_x(pay_a, pay_b, index, first, last):
    flag = odd("grp")
    pay_a[index] = either(flag, last, first)
    pay_b[index] = either(flag, first, last)


def halo_tile(after, before):
    parts = [after]
    if after.shape[0] < HALO:
        parts.append(jnp.zeros((2 * HALO - 2 * after.shape[0], after.shape[1]), F32))
    return jnp.concatenate(parts + [before], axis=0)


def first_pack_kernel(
    conc, label, owner, block, pay_a, pay_b, own_lists, c_first, c_last, l_first, l_last, own_owner, own_block, sems
):
    nx = conc.shape[0]
    copies = [pltpu.make_async_copy(owner, own_owner, sems.at[4]), pltpu.make_async_copy(block, own_block, sems.at[5])]
    for i, (ref, at, to) in enumerate(((conc, 0, c_first), (conc, 28, c_last), (label, 0, l_first), (label, 28, l_last))):
        copies.append(pltpu.make_async_copy(ref.at[:, pl.ds(at, 4), :], to, sems.at[i]))
    for c in copies:
        c.start()
    for c in copies:
        c.wait()
    named = jnp.concatenate([own_owner[...], own_block[...], jnp.zeros((6, 256), jnp.int32)], axis=0).astype(F32)
    own_lists[...] = named
    for x in range(nx):
        send_y(pay_a, pay_b, 7 * x, c_first[x], c_last[x])
        send_y(pay_a, pay_b, 7 * x + 4, l_first[x, 0:3, :].astype(F32), l_last[x, 1:4, :].astype(F32))


def own_kernel(conc, label, phi, mid, coarse, pay_a, pay_b, pairs, pairs_2):
    nx = conc.shape[0]
    half = nx // 2

    def coarsen(i):
        total = conc[2 * i] * pick(label[2 * i], CONDUCT_TABLE) + conc[2 * i + 1] * pick(label[2 * i + 1], CONDUCT_TABLE)
        mid[i] = 0.25 * pair_rows(total, pairs.at[i])

    loop(0, half, coarsen, 4)
    for i in range(half // 2):
        coarse[i] = 0.25 * pair_rows(mid[2 * i] + mid[2 * i + 1], pairs_2.at[i])
    for k in range(HALO):
        for t in range(4):
            rows = slice(8 * t, 8 * t + 8)
            send_x(pay_a, pay_b, 4 * k + t, phi[k, rows, :], phi[nx - HALO + k, rows, :])
        for t in range(2):
            rows = slice(8 * t, 8 * t + 8)
            send_x(pay_a, pay_b, 16 + 2 * k + t, mid[k, rows, :], mid[half - HALO + k, rows, :])


def first_pack_x_kernel(conc, label, r_a, r_b, token, pay_a, pay_b):
    nx = conc.shape[0]

    def plane(ref, k, t, offset, count):
        if t < 4:
            return ref[k, 8 * t : 8 * t + 8, :].astype(F32)
        return halo_tile(*y_sides(r_a, r_b, 7 * k + offset, count))

    for t in range(5):
        for k in range(HALO):
            send_x(pay_a, pay_b, 5 * k + t, plane(conc, k, t, 0, 4), plane(conc, nx - HALO + k, t, 0, 4))
        for k in range(3):
            send_x(pay_a, pay_b, 20 + 5 * k + t, plane(label, k, t, 4, 3), plane(label, nx - 3 + k, t, 4, 3))


def corner_rows(n, reach):
    counts = [min(HALO, k + reach) for k in range(HALO)]
    counts = counts + [HALO] * n + counts[::-1]
    return counts, [sum(counts[:i]) for i in range(len(counts))]


def second_rows(nx):
    phi, mid = (sum(corner_rows(n, reach)[0]) for n, reach in ((nx, 0), (nx // 2, 1)))
    return phi, phi + mid, phi + mid + 64


def second_pack_kernel(phi, mid, coarse, lists, x_a, x_b, pay_a, pay_b, token):
    nx = phi.shape[0]
    starts = second_rows(nx)

    def put(own, n, reach, index, base):
        counts, at = corner_rows(n, reach)
        tiles = own.shape[1] // 8
        for x in range(n):
            send_y(pay_a, pay_b, base + at[HALO + x], own[x, 0:4, :], own[x, 8 * tiles - 4 : 8 * tiles, :])
        for k in range(HALO):
            first_after, first_before = x_sides(x_a, x_b, index + tiles * k)
            last_after, last_before = x_sides(x_a, x_b, index + tiles * k + tiles - 1)
            for x, first, last in ((k, first_before, last_before), (HALO + n + k, first_after, last_after)):
                if counts[x]:
                    send_y(pay_a, pay_b, base + at[x], first[0 : counts[x]], last[8 - counts[x] : 8])

    put(phi, nx, 0, 0, 0)
    put(mid, nx // 2, 1, 16, starts[0])
    base = starts[1]
    for x in range(8):
        pay_a[base + 8 * x : base + 8 * x + 8, :] = coarse[x]
        pay_b[base + 8 * x : base + 8 * x + 8, :] = coarse[x]
    base = starts[2]
    pay_b[base : base + lists.shape[0], :] = lists[...]
    token[...] = jnp.zeros(token.shape, F32)


def second_halo(r_a, r_b, n, reach, x, base):
    counts, at = corner_rows(n, reach)
    if not counts[x]:
        return jnp.zeros((8, 256), F32)
    return halo_tile(*y_sides(r_a, r_b, base + at[x], counts[x]))


def wide_rows(own, after_own, before_own, after, before):
    gap = jnp.zeros((6, 256), F32)
    return jnp.concatenate([own, after_own, after, gap, before, before_own], axis=0)


def sweeps_kernel(conc, label, y_a, y_b, x_a, x_b, out, one, two, gain, base):
    nx = conc.shape[0]
    ratio = tuple(d / (1.0 + 6.0 * d) for d in DIFFUSION_TABLE)
    inverse = tuple(1.0 / (1.0 + 6.0 * d) for d in DIFFUSION_TABLE)

    def put(x, rows, c, lab):
        one[x, rows, :] = c
        gain[x, rows, :] = jnp.where(c > 0.0, pick(lab, ratio), 0.0)
        base[x, rows, :] = c * pick(lab, inverse)

    def own(i):
        put(HALO + i, slice(0, 32), conc[i], label[i])

    loop(0, nx, own)
    for i in range(nx):
        c = halo_tile(*y_sides(y_a, y_b, 7 * i, 4))
        lab = halo_tile(*y_sides(y_a, y_b, 7 * i + 4, 3))
        put(HALO + i, slice(32, 40), c, lab)
    for t in range(5):
        rows = slice(8 * t, 8 * t + 8)
        for k in range(HALO):
            c_after, c_before = x_sides(x_a, x_b, 5 * k + t)
            l_after = x_sides(x_a, x_b, 20 + 5 * min(k, 2) + t)[0]
            l_before = x_sides(x_a, x_b, 20 + 5 * max(k - 1, 0) + t)[1]
            put(k, rows, c_before, l_before)
            put(HALO + nx + k, rows, c_after, l_after)

    def stencil(old, x):
        mid = old[x]
        return base[x] + gain[x] * ((old[x - 1] + old[x + 1]) + (along_y(mid) + along_z(mid)))

    fields = (one, two)
    for s in range(1, SWEEPS):
        old, new = fields[(s - 1) % 2], fields[s % 2]

        def sweep(x, old=old, new=new):
            new[x] = stencil(old, x)

        loop(s, nx + 2 * HALO - s, sweep)

    old = fields[(SWEEPS - 1) % 2]

    def last(i):
        out[i] = stencil(old, HALO + i)[0:32, :]

    loop(0, nx, last)


def flux_kernel(conc, label, phi, solid, flux, pay_a, pay_b):
    nx = conc.shape[0]

    def plane(i):
        drive = 0.5 * (solid[i] - phi[i])
        logc = jnp.log(conc[i])
        value = jnp.exp(drive + 0.4 * logc) - jnp.exp(0.6 * logc - drive)
        flux[i] = pick(label[i], KINETIC_TABLE) * value

    loop(0, nx, plane, 4)
    for x in range(nx):
        send_y(pay_a, pay_b, 3 * x, flux[x, 0:3, :], flux[x, 29:32, :])


def store_kernel(conc, flux_all, lists, far, conc_out, flux_out, flux, halo_mask, marked, sems):
    nx = conc.shape[0]
    copies = [pltpu.make_async_copy(conc, conc_out, sems.at[4])]
    copies[0].start()
    rows = lists.shape[0]
    pieces = [lists[i : i + 1, :] for i in range(rows)] + [far[i : i + 1, :] for i in range(far.shape[0] - rows, far.shape[0])]
    owner = jnp.concatenate(pieces[0::2], axis=1).astype(jnp.int32)
    block = jnp.concatenate(pieces[1::2], axis=1).astype(jnp.int32)
    entries = owner.shape[1]
    hit_column = (iota((LANES, entries), 0) == lax.rem(block, 64)).astype(jnp.bfloat16)
    at_row = lax.shift_right_arithmetic(block, 6)
    here = lax.axis_index("dev")
    for j in range(3):
        mine = jnp.where(owner == here + j - 1, at_row, -1)
        hit_row = (iota((nx, entries), 0) == mine).astype(jnp.bfloat16)
        named = lax.dot_general(hit_row, hit_column, (((1,), (1,)), ((), ())), preferred_element_type=F32)
        for i in range(nx):
            marked[j, i] = jnp.broadcast_to(named[i : i + 1, :], (8, LANES))
    is_row = lax.div(iota((32, LANES), 1), 2) == iota((32, LANES), 0)
    row, pair = iota((8, LANES), 0), lax.div(iota((8, LANES), 1), 2)
    is_after = (row < 3) & (pair == row)
    is_before = (row >= 5) & (pair == row + 24)
    spread = (lax.rem(iota((LANES, 256), 0), 2) == lax.div(iota((LANES, 256), 1), LANES)).astype(jnp.bfloat16)

    def plane(i):
        marks = jnp.where(is_row, jnp.concatenate([marked[1, i]] * 4, axis=0), 0.0)
        beyond = jnp.where(is_after, marked[2, i], jnp.where(is_before, marked[0, i], 0.0))
        marks = jnp.concatenate([marks, beyond], axis=0).astype(jnp.bfloat16)
        listed = jnp.dot(marks, spread, preferred_element_type=F32) > 0.5
        flux[i] = jnp.where(listed[0:32], flux_all[i], 0.0)
        halo_mask[i] = jnp.where(listed[32:40], 1.0, 0.0)

    for j in range(4):
        part = nx // 4
        loop(part * j, part * (j + 1), plane, 4)
        rows = pl.ds(part * j, part)
        copies.append(pltpu.make_async_copy(flux.at[rows], flux_out.at[rows], sems.at[j]))
        copies[-1].start()
    for c in copies:
        c.wait()


def ready_kernel(conc, label, phi, y_a, y_b, x_a, x_b, yy_a, yy_b, xx_a, xx_b, weight, scale, share, start, token, field):
    nx = conc.shape[0]
    token[...] = jnp.zeros(token.shape, F32)

    def put(x, rows, c, lab, p):
        conduct = c * pick(lab, CONDUCT_TABLE)
        factor = OMEGA / (MASS + 6.0 * conduct)
        weight[x, rows, :] = conduct * factor
        scale[x, rows, :] = factor
        share[x, rows, :] = MASS * p * factor
        field[x, rows, :] = p

    def own(i):
        put(HALO + i, slice(0, 32), conc[i], label[i], phi[i])

    loop(0, nx, own, 4)
    low = slice(32, 40)
    for i in range(nx):
        c = halo_tile(*y_sides(y_a, y_b, 7 * i, 4))
        lab = halo_tile(*y_sides(y_a, y_b, 7 * i + 4, 3))
        put(HALO + i, low, c, lab, second_halo(yy_a, yy_b, nx, 0, HALO + i, 0))
    for t in range(5):
        rows = slice(8 * t, 8 * t + 8)
        for k in range(HALO):
            c_after, c_before = x_sides(x_a, x_b, 5 * k + t)
            l_after = x_sides(x_a, x_b, 20 + 5 * min(k, 2) + t)[0]
            l_before = x_sides(x_a, x_b, 20 + 5 * max(k - 1, 0) + t)[1]
            if t < 4:
                p_after, p_before = x_sides(xx_a, xx_b, 4 * k + t)
            else:
                p_after = second_halo(yy_a, yy_b, nx, 0, HALO + nx + k, 0)
                p_before = second_halo(yy_a, yy_b, nx, 0, k, 0)
            put(k, rows, c_before, l_before, p_before)
            put(HALO + nx + k, rows, c_after, l_after, p_after)

    def sweep(x):
        p = field[x]
        around = (field[x - 1] + field[x + 1]) + (along_y(p) + along_z(p))
        start[x] = 0.2 * p + share[x] + weight[x] * around

    loop(1, nx + 2 * HALO - 1, sweep)


def flux_pack_x_kernel(flux, r_a, r_b, mask, token, pay_a, pay_b):
    nx = flux.shape[0]

    def tile(x, t):
        if t < 4:
            return flux[x, 8 * t : 8 * t + 8, :]
        return mask[x] * halo_tile(*y_sides(r_a, r_b, 3 * x, 3))

    for k in range(3):
        for t in range(5):
            send_x(pay_a, pay_b, 5 * k + t, tile(k, t), tile(nx - 3 + k, t))


def potential_inner_kernel(flux, mask, y_a, y_b, weight, scale, share, start, after_two, source, first, source_mid, pairs):
    nx = flux.shape[0]

    def put(x, rows, f):
        part = scale[x, rows, :] * f
        source[x, rows, :] = share[x, rows, :] + part
        first[x, rows, :] = start[x, rows, :] + part

    def own(i):
        put(HALO + i, slice(0, 32), flux[i])

    loop(0, nx, own)
    for i in range(nx):
        put(HALO + i, slice(32, 40), mask[i] * halo_tile(*y_sides(y_a, y_b, 3 * i, 3)))

    def around(values, x):
        v = values[x]
        return v, weight[x] * ((values[x - 1] + values[x + 1]) + (along_y(v) + along_z(v)))

    def sweep(x):
        v, near = around(first, x)
        after_two[x] = 0.2 * v + (source[x] + near)

    loop(HALO + 1, HALO + nx - 1, sweep)

    def remainder(x):
        v, near = around(after_two, x)
        return ((source[x] - OMEGA * v) + near)[0:32, :] / scale[x, 0:32, :]

    def coarsen(i):
        x = HALO + 2 * i
        source_mid[i] = 0.25 * pair_rows(remainder(x) + remainder(x + 1), pairs.at[i])

    loop(1, nx // 2 - 1, coarsen, 4)


def potential_edge_kernel(
    x_a, x_b, weight, scale, share, start, inner_two, inner_source, inner_first, inner_mid,
    edge_two, edge_source, source_mid, pay_a, pay_b, first, pairs,
):
    half = source_mid.shape[0]
    nx = 2 * half
    for side, face in ((0, HALO), (1, HALO + nx)):
        base = 8 * side + HALO - face
        for k in range(3):
            x = face - 3 + k if side == 0 else face + k
            for t in range(5):
                rows = slice(8 * t, 8 * t + 8)
                part = scale[x, rows, :] * x_sides(x_a, x_b, 5 * k + t)[1 - side]
                edge_source[base + x, rows, :] = share[x, rows, :] + part
                first[base + x, rows, :] = start[x, rows, :] + part

        def first_of(x, base=base):
            return inner_first[x] if HALO <= x < HALO + nx else first[base + x]

        def source_of(x, base=base):
            return inner_source[x] if HALO <= x < HALO + nx else edge_source[base + x]

        def two_of(x, base=base):
            return inner_two[x] if HALO < x < HALO + nx - 1 else edge_two[base + x]

        for x in range(face - 2, face + 1) if side == 0 else range(face - 1, face + 2):
            v = first_of(x)
            near = weight[x] * ((first_of(x - 1) + first_of(x + 1)) + (along_y(v) + along_z(v)))
            edge_two[base + x] = 0.2 * v + (source_of(x) + near)
        total = 0.0
        at = face if side == 0 else face - 2
        for x in (at, at + 1):
            v = two_of(x)
            near = weight[x] * ((two_of(x - 1) + two_of(x + 1)) + (along_y(v) + along_z(v)))
            total = total + ((source_of(x) - OMEGA * v) + near)[0:32, :] / scale[x, 0:32, :]
        source_mid[0 if side == 0 else half - 1] = 0.25 * pair_rows(total, pairs.at[side])
    for x in range(1, half - 1):
        source_mid[x] = inner_mid[x]
    for x in range(half):
        send_y(pay_a, pay_b, 4 * x, source_mid[x, 0:4, :], source_mid[x, 12:16, :])


def mid_pack_x_kernel(field, r_a, r_b, token, pay_a, pay_b):
    n = field.shape[0]

    def tile(x, t):
        if t < 2:
            return field[x, 8 * t : 8 * t + 8, :]
        return halo_tile(*y_sides(r_a, r_b, 4 * x, 4))

    for k in range(HALO):
        for t in range(3):
            send_x(pay_a, pay_b, 3 * k + t, tile(k, t), tile(n - HALO + k, t))


def mid_kernel(
    source_own, conduct_own, yy_a, yy_b, xx_a, xx_b, y_a, y_b, x_a, x_b, rho, load,
    after_two, source, weight, coarse, conduct, pay_a, pay_b, part, scale, mid_conduct, pairs, pairs_2,
):
    n = source_own.shape[0]
    base = second_rows(2 * n)[0]

    def put(x, rows, b, k):
        factor = OMEGA / (MASS + 3.0 * k)
        weight[x, rows, :] = k * factor
        scale[x, rows, :] = factor
        source[x, rows, :] = factor * b
        mid_conduct[x, rows, :] = k

    def far(x):
        return second_halo(yy_a, yy_b, n, 1, x, base)

    for i in range(n):
        put(HALO + i, slice(0, 16), source_own[i], conduct_own[i])
        put(HALO + i, slice(16, 24), halo_tile(*y_sides(y_a, y_b, 4 * i, 4)), far(HALO + i))
    for k in range(HALO):
        for t in range(3):
            rows = slice(8 * t, 8 * t + 8)
            b_after, b_before = x_sides(x_a, x_b, 3 * k + t)
            if t < 2:
                c_after, c_before = x_sides(xx_a, xx_b, 16 + 2 * k + t)
            else:
                c_after, c_before = far(HALO + n + k), far(k)
            put(k, rows, b_before, c_before)
            put(HALO + n + k, rows, b_after, c_after)

    def around(values, x):
        v = values[x]
        return v, weight[x] * (0.25 * ((values[x - 1] + values[x + 1]) + along_y(v)) + along_z(v))

    def sweep(x):
        v, near = around(source, x)
        after_two[x] = 0.2 * v + (source[x] + near)

    loop(1, n + 2 * HALO - 1, sweep, 11)

    def remainder(x):
        v, near = around(after_two, x)
        return ((source[x] - OMEGA * v) + near) / scale[x]

    total = jnp.zeros((8, 256), F32)
    for i in range(n // 2):
        x = HALO + 2 * i
        value = 0.25 * pair_rows(remainder(x) + remainder(x + 1), pairs.at[i])
        k = 0.25 * pair_rows(mid_conduct[x] + mid_conduct[x + 1], pairs_2.at[i])
        coarse[i] = value
        conduct[i] = k
        send_y(pay_a, pay_b, 9 * i, value[1:9], jnp.concatenate([value[11:12], value[0:7]], axis=0))
        send_y(pay_a, pay_b, 9 * i + 8, k[8:9], k[11:12])
        total += rho[i] * value[0:8]
    part[...] = jnp.concatenate([total[:, :LANES] + total[:, LANES:], load[...]], axis=1)


COARSE_W = 0.0625


def coarse_ready_kernel(own, r_a, r_b, rho, load, token, one, two, conduct, scale):
    token[...] = jnp.zeros(token.shape, F32)
    base = r_a.shape[0] - 64
    for x in range(8):
        after, before = y_sides(r_a, r_b, base + 8 * x, 8)
        k = jnp.concatenate([own[x], after, jnp.zeros((8, 256), F32), before], axis=0)
        conduct[x] = k
        scale[x] = OMEGA / (MASS + 2.25 * k)
        one[x] = jnp.ones(k.shape, F32)
    fields = (one, two)
    for s in range(COARSE_SWEEPS):
        old, new = fields[s % 2], fields[(s + 1) % 2]
        for x in range(8):
            near = [conduct[i] * old[i] if 0 <= i < 8 else None for i in (x - 1, x, x + 1)]
            inner = along_y(near[1])
            for other in (near[0], near[2]):
                if other is not None:
                    inner = inner + other
            new[x] = 0.2 * old[x] + scale[x] * (COARSE_W * inner + along_z(near[1]))
    last = fields[COARSE_SWEEPS % 2]
    peer, peers = lax.axis_index("dev"), lax.axis_size("dev")
    row, z = iota((8, 256), 0), iota((8, 256), 1)
    edge_y = ((row == 0) & (peer == 0)) | ((row == 7) & (peer == peers - 1))
    edge = edge_y.astype(F32) * COARSE_W + ((z == 0) | (z == 255)).astype(F32)
    total = jnp.zeros((8, 256), F32)
    for x in range(8):
        rho[x] = last[x, 0:8, :]
        total += MASS + own[x] * (edge + (COARSE_W if x in (0, 7) else 0.0))
    load[...] = total[:, :LANES] + total[:, LANES:]


def late_kernel(pay, token, out):
    out[...] = pay[...]


def coarse_kernel(own, conduct, far_a, far_b, r_a, r_b, error, source, weight, one, two):
    base = far_a.shape[0] - 64
    for x in range(8):
        after, before = y_sides(r_a, r_b, 9 * x, 8)
        b = wide_rows(own[x, 0:8, :], own[x, 8:9, :], own[x, 11:12, :], after, before)
        last_after, last_before = y_sides(r_a, r_b, 9 * x + 8, 1)
        after, before = y_sides(far_a, far_b, base + 8 * x, 8)
        after = jnp.concatenate([after[1:8], last_after], axis=0)
        before = jnp.concatenate([last_before, before[0:7]], axis=0)
        k = wide_rows(conduct[x, 0:8, :], conduct[x, 8:9, :], conduct[x, 11:12, :], after, before)
        factor = OMEGA / (MASS + 2.25 * k)
        weight[x] = k * factor
        source[x] = factor * b
    old = source
    for s in range(1, COARSE_SWEEPS):
        new = one if s % 2 else two
        for x in range(8):
            v = old[x]
            inner = along_y(v)
            if x > 0:
                inner = inner + old[x - 1]
            if x < 7:
                inner = inner + old[x + 1]
            new[x] = 0.2 * v + (source[x] + weight[x] * (COARSE_W * inner + along_z(v)))
        old = new
    for x in range(8):
        error[x, 0:8, :] = old[x, 0:8, :]
        error[x, 8:16, :] = jnp.where(upper(), old[x, 8:16, :], old[x, 24:32, :])


def shift_kernel(error, sums, out, pay_a, pay_b):
    resid = jnp.sum(sums[:, :LANES])
    load = jnp.sum(sums[:, LANES:])
    shift_c = jnp.full((16, 256), resid, F32) / jnp.full((16, 256), load, F32)
    for x in range(8):
        out[x] = error[x] + shift_c
    for k in range(2):
        send_x(pay_a, pay_b, k, out[k], out[6 + k])


def squeeze(tile):
    return jnp.where(iota((8, 256), 0) < 2, tile, pltpu.roll(tile, 4, 0))


def spread_coarse(plane, room):
    return jnp.concatenate([twice(plane[0:8], room.at[0]), twice(squeeze(plane[8:16]), room.at[1])[0:8]], axis=0)


def spread_mid(plane, room):
    parts = [twice(plane[0:8], room.at[0]), twice(plane[8:16], room.at[1]), twice(squeeze(plane[16:24]), room.at[2])[0:8]]
    return jnp.concatenate(parts, axis=0)


def smoothed(before, v, after, weight, source, w):
    inner = (before + after) + along_y(v)
    return source + (0.2 * v + weight * (w * inner + along_z(v)))


def finish_inner_kernel(
    error, mid_two, mid_source, mid_weight, fine_two, fine_source, fine_weight,
    out, zero, one, fine_one, fine_last, two, dup, dup_2, result, sems,
):
    n = mid_two.shape[0]
    nf = fine_two.shape[0]
    for c in range(8):
        spread = spread_coarse(error[c], dup.at[c])
        for x in (2 * c + HALO, 2 * c + 1 + HALO):
            zero[x] = jnp.where(mid_weight[x] > 0.0, mid_two[x] + spread, 0.0)

    def sweep_mid(x, old, new):
        new[x] = smoothed(old[x - 1], old[x], old[x + 1], mid_weight[x], mid_source[x], 0.25)

    for x in range(HALO + 1, n - HALO - 1):
        sweep_mid(x, zero, one)
    for x in range(HALO + 2, n - HALO - 2):
        sweep_mid(x, one, two)

    def lift(m):
        spread = spread_mid(two[m], dup_2.at[m])
        x = 2 * m - HALO
        fine_one[x] = fine_two[x] + spread
        fine_one[x + 1] = fine_two[x + 1] + spread

    loop(HALO + 2, n - HALO - 2, lift, 6)

    def sweep_one(x):
        fine_last[x] = smoothed(fine_one[x - 1], fine_one[x], fine_one[x + 1], fine_weight[x], fine_source[x], 1.0)

    low, high = 2 * HALO + 1, nf - 2 * HALO - 1
    loop(low, high, sweep_one, 11)
    copies = []
    low, high = low + 1, high - 1
    for j in range(2):
        mid = low + (high - low) // 2
        for x in range(low, mid) if j == 0 else range(mid, high):
            v = smoothed(fine_last[x - 1], fine_last[x], fine_last[x + 1], fine_weight[x], fine_source[x], 1.0)
            result[x - HALO] = v[0:32, :]
        rows = pl.ds(low - HALO, mid - low) if j == 0 else pl.ds(mid - HALO, high - mid)
        copies.append(pltpu.make_async_copy(result.at[rows], out.at[rows], sems.at[j]))
        copies[-1].start()
    for c in copies:
        c.wait()


def finish_edge_kernel(
    x_a, x_b, mid_two, mid_source, mid_weight, fine_two, edge_two, fine_source, edge_source, fine_weight,
    zero, one, fine_one, fine_last, begun, out, zero_edge, one_edge, fine_edge, last_edge, dup, dup_2, result, sems,
):
    n = mid_two.shape[0]
    nf = fine_two.shape[0]
    nx = nf - 2 * HALO
    copies = []
    planes = x_sides(x_a, x_b, slice(0, 2))
    for side in (0, 1):
        sign = 1 if side == 0 else -1
        at = lambda k, side=side: HALO + k if side == 0 else n - HALO - 1 - k
        fine = lambda k, side=side: HALO + k if side == 0 else nf - HALO - 1 - k
        base = 8 * side + (0 if side == 0 else HALO - HALO - nx)
        for c in range(2):
            plane = planes[1 - side][c]
            spread = spread_coarse(plane, dup.at[2 * side + c])
            first = 2 * c if side == 0 else n - HALO + 2 * c
            for x in (first, first + 1):
                zero_edge[x] = jnp.where(mid_weight[x] > 0.0, mid_two[x] + spread, 0.0)

        def zero_of(k):
            return zero[at(k)] if k >= 0 else zero_edge[at(k)]

        def one_of(k):
            return one[at(k)] if k >= 1 else one_edge[at(k)]

        for k in range(-2, 1):
            x = at(k)
            one_edge[x] = smoothed(zero_of(k - 1), zero_of(k), zero_of(k + 1), mid_weight[x], mid_source[x], 0.25)
        for k in range(-1, 2):
            x = at(k)
            value = smoothed(one_of(k - 1), one_of(k), one_of(k + 1), mid_weight[x], mid_source[x], 0.25)
            spread = spread_mid(value, dup_2.at[3 * side + k + 1])
            for f in (fine(2 * k), fine(2 * k + 1)):
                inside = HALO < f < nf - HALO - 1
                before = fine_two[f] if inside else edge_two[base + f]
                fine_edge[f] = before + spread

        def fine_of(k):
            return fine_one[fine(k)] if k >= 4 else fine_edge[fine(k)]

        def last_of(k):
            return fine_last[fine(k)] if k >= 5 else last_edge[fine(k)]

        for k in range(-1, 5):
            f = fine(k)
            source = fine_source[f] if HALO <= f < nf - HALO else edge_source[base + f]
            last_edge[f] = smoothed(fine_of(k - 1), fine_of(k), fine_of(k + 1), fine_weight[f], source, 1.0)
        for k in range(6):
            f = fine(k)
            v = smoothed(last_of(k - 1), last_of(k), last_of(k + 1), fine_weight[f], fine_source[f], 1.0)
            result[f - HALO] = v[0:32, :]
        rows = pl.ds(0, 6) if side == 0 else pl.ds(nx - 6, 6)
        copies.append(pltpu.make_async_copy(result.at[rows], out.at[rows], sems.at[side]))
        copies[-1].start()
    for c in copies:
        c.wait()


def both_ways(pairs):
    return pairs + [(j, i) for i, j in pairs]


def swap(pay_a, pay_b, axis):
    size = lax.axis_size(axis)
    pairs_a = [(i, i + 1) for i in range(1, size - 1, 2)]
    pairs_b = [(i, i + 1) for i in range(0, size - 1, 2)]
    return lax.ppermute(pay_a, axis, both_ways(pairs_a)), lax.ppermute(pay_b, axis, both_ways(pairs_b))


def exchange(value, distance):
    return lax.ppermute(value, "dev", [(i, i ^ distance) for i in range(lax.axis_size("dev"))])


def body(conc_old, phi_old, solid_pot, phase_label, iface_block, iface_owner):
    peers = lax.axis_size("dev")
    nx = conc_old.shape[0]
    half = nx // 2
    quarter = nx // 4
    ext = (nx + 2 * HALO, nx + 2 * HALO, 256)
    ext_mid = (half + 2 * HALO, half + 2 * HALO, 256)
    token_shape = shaped(8, LANES)

    pay_a, pay_b, own_lists = call(
        first_pack_kernel,
        [shaped(7 * nx, 256)] * 2 + [shaped(8, 256)],
        [conc_old, phase_label, iface_owner.reshape(1, -1), iface_block],
        [vmem(nx, HALO, 256)] * 2
        + [pltpu.VMEM((nx, HALO, 256), jnp.int32)] * 2
        + [pltpu.VMEM((1, 256), jnp.int32)] * 2
        + [pltpu.SemaphoreType.DMA((6,))],
        in_specs=[FAR] * 4,
        limit=VMEM_MOST,
        name="first_pack",
    )
    y_a, y_b = swap(pay_a, pay_b, "dev")
    conduct_mid, conduct_coarse, pay_a, pay_b = call(
        own_kernel,
        [shaped(half, half, 256), shaped(quarter, quarter, 256), shaped(24, 8, 256), shaped(24, 8, 256)],
        [conc_old, phase_label, phi_old],
        [vmem(half, 2, nx, LANES), vmem(quarter, 2, half, LANES)],
        name="own",
    )
    xx_a, xx_b = swap(pay_a, pay_b, "grp")
    lists = own_lists[0:2]
    distance = peers // 2
    while distance > 1:
        lists = jnp.concatenate([lists, exchange(lists, distance)], axis=0)
        distance //= 2
    far_rows = second_rows(nx)[2]
    pay_a, pay_b, sent = call(
        second_pack_kernel,
        [shaped(far_rows, 256), shaped(far_rows + peers, 256), token_shape],
        [phi_old, conduct_mid, conduct_coarse, lists, xx_a, xx_b],
        name="second_pack",
    )
    yy_a, yy_b = swap(pay_a, pay_b, "dev")
    pay_a, pay_b = call(
        first_pack_x_kernel,
        [shaped(35, 8, 256)] * 2,
        [conc_old, phase_label, y_a, y_b, sent],
        name="first_pack_x",
    )
    x_a, x_b = swap(pay_a, pay_b, "grp")

    (conc_new,) = call(
        sweeps_kernel,
        [shaped(nx, nx, 256)],
        [conc_old, phase_label, y_a, y_b, x_a, x_b],
        [vmem(*ext)] * 4,
        name="sweeps",
    )
    flux_all, pay_a, pay_b = call(
        flux_kernel,
        [shaped(nx, nx, 256), shaped(3 * nx, 256), shaped(3 * nx, 256)],
        [conc_new, phase_label, phi_old, solid_pot],
        name="flux",
    )
    f_a, f_b = swap(pay_a, pay_b, "dev")
    concentration, flux, flux_own, halo_mask = call(
        store_kernel,
        [shaped(nx, nx, 256), shaped(nx, nx, 256), shaped(nx, nx, 256), shaped(nx, 8, 256)],
        [conc_new, flux_all, lists, yy_b],
        [vmem(3, nx, 8, LANES), pltpu.SemaphoreType.DMA((5,))],
        out_specs=[FAR, FAR, WHOLE, WHOLE],
        name="store",
    )
    weight, scale, share, start, made = call(
        ready_kernel,
        [shaped(*ext)] * 4 + [token_shape],
        [conc_old, phase_label, phi_old, y_a, y_b, x_a, x_b, yy_a, yy_b, xx_a, xx_b],
        [vmem(*ext)],
        name="ready",
    )
    pay_a, pay_b = call(
        flux_pack_x_kernel, [shaped(15, 8, 256)] * 2, [flux_own, f_a, f_b, halo_mask, made], name="flux_pack_x"
    )
    fx_a, fx_b = swap(pay_a, pay_b, "grp")
    fine_two, fine_source, fine_first, inner_mid = call(
        potential_inner_kernel,
        [shaped(*ext)] * 3 + [shaped(half, half, 256)],
        [flux_own, halo_mask, f_a, f_b, weight, scale, share, start],
        [vmem(half, 2, nx, LANES)],
        name="potential_inner",
    )
    edge = (16, nx + 2 * HALO, 256)
    edge_two, edge_source, source_mid, pay_a, pay_b = call(
        potential_edge_kernel,
        [shaped(*edge), shaped(*edge), shaped(half, half, 256), shaped(4 * half, 256), shaped(4 * half, 256)],
        [fx_a, fx_b, weight, scale, share, start, fine_two, fine_source, fine_first, inner_mid],
        [vmem(*edge), vmem(2, 2, nx, LANES)],
        name="potential_edge",
    )
    m_a, m_b = swap(pay_a, pay_b, "dev")
    wide = (quarter, 32, 256)
    rho, load, made = call(
        coarse_ready_kernel,
        [shaped(quarter, quarter, 256), shaped(8, LANES), token_shape],
        [conduct_coarse, yy_a, yy_b],
        [vmem(*wide)] * 4,
        name="coarse_ready",
    )
    pay_a, pay_b = call(
        mid_pack_x_kernel, [shaped(3 * HALO, 8, 256)] * 2, [source_mid, m_a, m_b, made], name="mid_pack_x"
    )
    mx_a, mx_b = swap(pay_a, pay_b, "grp")
    mid_two, mid_source, mid_weight, source_coarse, wide_coarse, pay_a, pay_b, sums = call(
        mid_kernel,
        [shaped(*ext_mid)] * 3
        + [shaped(quarter, 12, 256), shaped(quarter, 12, 256), shaped(72, 256), shaped(72, 256), shaped(8, 256)],
        [source_mid, conduct_mid, yy_a, yy_b, xx_a, xx_b, m_a, m_b, mx_a, mx_b, rho, load],
        [vmem(*ext_mid)] * 2 + [vmem(8, 2, half + 2 * HALO, LANES)] * 2,
        name="middle",
    )
    early = sums = sums + exchange(sums, 1)
    distance = 2
    while distance < peers:
        sums = sums + exchange(sums, distance)
        distance *= 2
    (pay_b,) = call(late_kernel, [shaped(72, 256)], [pay_b, early], name="late")
    c_a, c_b = swap(pay_a, pay_b, "dev")
    (error,) = call(
        coarse_kernel,
        [shaped(8, 16, 256)],
        [source_coarse, wide_coarse, yy_a, yy_b, c_a, c_b],
        [vmem(*wide)] * 4,
        name="coarse",
    )
    error, pay_a, pay_b = call(
        shift_kernel, [shaped(8, 16, 256), shaped(2, 16, 256), shaped(2, 16, 256)], [error, sums], name="shift"
    )
    e_a, e_b = swap(pay_a, pay_b, "grp")
    begun, zero, one, fine_one, fine_last = call(
        finish_inner_kernel,
        [shaped(nx, nx, 256), shaped(*ext_mid), shaped(*ext_mid), shaped(*ext), shaped(*ext)],
        [error, mid_two, mid_source, mid_weight, fine_two, fine_source, weight],
        [vmem(*ext_mid), vmem(8, 2, 2, 16, LANES), vmem(half + 2 * HALO, 3, 2, 16, LANES), vmem(nx, nx, 256)]
        + [pltpu.SemaphoreType.DMA((2,))],
        out_specs=[FAR] + [WHOLE] * 4,
        name="finish_inner",
    )
    finish_args = [e_a, e_b, mid_two, mid_source, mid_weight, fine_two, edge_two, fine_source, edge_source, weight]
    finish_args += [zero, one, fine_one, fine_last, begun]
    (potential,) = call(
        finish_edge_kernel,
        [shaped(nx, nx, 256)],
        finish_args,
        [vmem(*ext_mid), vmem(*ext_mid), vmem(*ext), vmem(*ext)]
        + [vmem(4, 2, 2, 16, LANES), vmem(6, 3, 2, 16, LANES), vmem(nx, nx, 256)]
        + [pltpu.SemaphoreType.DMA((2,))],
        in_specs=[WHOLE] * (len(finish_args) - 1) + [FAR],
        out_specs=[FAR],
        aliases={len(finish_args) - 1: 0},
        name="finish_edge",
    )
    return (concentration, flux, potential)


def solution(mesh):
    brick = P("grp", "dev", None)
    return jax.shard_map(
        body,
        mesh=mesh,
        in_specs=(brick, brick, brick, brick, P("grp", "dev"), brick),
        out_specs=(brick, brick, brick),
        check_vma=False,
    )
```

```python
import jax
import jax.numpy as jnp
from jax import lax
from jax.experimental import pallas as pl
from jax.experimental.pallas import tpu as pltpu
from jax.sharding import PartitionSpec as P


F32 = jnp.float32
MASS = 0.05
OMEGA = 0.8
DIFFUSION_TABLE = (1.5, 0.1, 0.4)
RATIO_TABLE = tuple(d / (1.0 + 6.0 * d) for d in DIFFUSION_TABLE)
INVERSE_TABLE = tuple(1.0 / (1.0 + 6.0 * d) for d in DIFFUSION_TABLE)
CONDUCT_TABLE = (1.0, 0.3, 0.6)
KINETIC_TABLE = (0.2, 1.0, 0.5)
SWEEPS = 4
COARSE_SWEEPS = 8
COARSE_NEAR = 8
HALO = 4
LANES = 128
VMEM_LIMIT = 28 * 1024 * 1024
VMEM_MOST = 58 * 1024 * 1024


def shaped(*shape):
    return jax.ShapeDtypeStruct(shape, F32)


WHOLE = pl.BlockSpec(memory_space=pltpu.VMEM)
FAR = pl.BlockSpec(memory_space=pltpu.HBM)


def call(kernel, outs, args, scratch=(), in_specs=None, out_specs=None, limit=VMEM_LIMIT, aliases=None, flops=10**6, name=None):
    size = sum(4 * a.size for a in args) + sum(4 * o.size for o in outs)
    return pl.pallas_call(
        kernel,
        out_shape=tuple(outs),
        in_specs=in_specs or [WHOLE] * len(args),
        out_specs=tuple(out_specs or [WHOLE] * len(outs)),
        scratch_shapes=list(scratch),
        input_output_aliases=aliases or {},
        compiler_params=pltpu.CompilerParams(vmem_limit_bytes=limit),
        cost_estimate=pl.CostEstimate(flops=flops, bytes_accessed=size, transcendentals=0),
        name=name,
    )(*args)


def vmem(*shape):
    return pltpu.VMEM(shape, F32)


def iota(shape, dim):
    return lax.broadcasted_iota(jnp.int32, shape, dim)


def pick(label, table):
    return jnp.where(label == 0, table[0], jnp.where(label == 1, table[1], table[2])).astype(F32)


def loop(low, high, body, unroll=8):
    steps = (high - low) // unroll

    def step(i, carry):
        for u in range(unroll):
            body(low + i * unroll + u)
        return carry

    if steps > 1:
        lax.fori_loop(0, steps, step, 0)
    else:
        steps = 0
    for x in range(low + steps * unroll, high):
        body(x)


def odd(axis):
    return lax.rem(lax.axis_index(axis), 2) == 1


def along_y(v):
    return pltpu.roll(v, 1, 0) + pltpu.roll(v, v.shape[0] - 1, 0)


def along_z(v):
    low, high = v[:, :LANES], v[:, LANES:]
    lane = iota(low.shape, 1)
    first, last = lane == 0, lane == LANES - 1
    low_up, high_up = pltpu.roll(low, 1, 1), pltpu.roll(high, 1, 1)
    low_down, high_down = pltpu.roll(low, LANES - 1, 1), pltpu.roll(high, LANES - 1, 1)
    low_sum = jnp.where(first, 0.0, low_up) + jnp.where(last, high_down, low_down)
    high_sum = jnp.where(first, low_up, high_up) + jnp.where(last, 0.0, high_down)
    return jnp.concatenate([low_sum, high_sum], axis=1)


def upper(shape=(8, 256)):
    return iota(shape, 0) < HALO


def twice(tile, scratch):
    for h in range(2):
        part = tile[:, h * LANES : (h + 1) * LANES]
        scratch[h, pl.ds(0, 8, stride=2), :] = part
        scratch[h, pl.ds(1, 8, stride=2), :] = part
    return jnp.concatenate([scratch[0], scratch[1]], axis=1)


def pair_rows(v, scratch):
    half = v.shape[0] // 2
    parts = []
    for h in range(2):
        scratch[h] = v[:, h * LANES : (h + 1) * LANES]
        parts.append(scratch[h, pl.ds(0, half, stride=2), :] + scratch[h, pl.ds(1, half, stride=2), :])
    return jnp.concatenate(parts, axis=1)


def either(flag, if_true, if_false):
    return jnp.where(flag, if_true, if_false)


def y_sides(r_a, r_b, at, count):
    flag = odd("dev")
    a, b = r_a[at : at + count, :], r_b[at : at + count, :]
    return either(flag, a, b), either(flag, b, a)


def x_sides(r_a, r_b, index):
    flag = odd("grp")
    a, b = r_a[index], r_b[index]
    return either(flag, a, b), either(flag, b, a)


def send_y(pay_a, pay_b, at, first, last):
    flag = odd("dev")
    n = first.shape[0]
    pay_a[at : at + n, :] = either(flag, last, first)
    pay_b[at : at + n, :] = either(flag, first, last)


def send_x(pay_a, pay_b, index, first, last):
    flag = odd("grp")
    pay_a[index] = either(flag, last, first)
    pay_b[index] = either(flag, first, last)


def halo_tile(after, before):
    parts = [after]
    if after.shape[0] < HALO:
        parts.append(jnp.zeros((2 * HALO - 2 * after.shape[0], after.shape[1]), F32))
    return jnp.concatenate(parts + [before], axis=0)


def first_pack_kernel(
    conc, label, owner, block, pay_a, pay_b, own_lists, c_first, c_last, l_first, l_last, own_owner, own_block, sems
):
    nx = conc.shape[0]
    copies = [pltpu.make_async_copy(owner, own_owner, sems.at[4]), pltpu.make_async_copy(block, own_block, sems.at[5])]
    for i, (ref, at, to) in enumerate(((conc, 0, c_first), (conc, 28, c_last), (label, 0, l_first), (label, 28, l_last))):
        copies.append(pltpu.make_async_copy(ref.at[:, pl.ds(at, 4), :], to, sems.at[i]))
    for c in copies:
        c.start()
    for c in copies:
        c.wait()
    named = jnp.concatenate([own_owner[...], own_block[...], jnp.zeros((6, 256), jnp.int32)], axis=0).astype(F32)
    own_lists[...] = named
    for x in range(nx):
        send_y(pay_a, pay_b, 7 * x, c_first[x], c_last[x])
        send_y(pay_a, pay_b, 7 * x + 4, l_first[x, 0:3, :].astype(F32), l_last[x, 1:4, :].astype(F32))


def own_kernel(conc, label, phi, named, mid, coarse, pay_a, pay_b, lists, gain, base, pairs, pairs_2):
    nx = conc.shape[0]
    half = nx // 2
    lists[...] = named[0:2, :]

    def coefficients(i):
        gain[i] = pick(label[i], RATIO_TABLE)
        base[i] = conc[i] * pick(label[i], INVERSE_TABLE)

    loop(0, nx, coefficients, 4)

    def coarsen(i):
        total = conc[2 * i] * pick(label[2 * i], CONDUCT_TABLE) + conc[2 * i + 1] * pick(label[2 * i + 1], CONDUCT_TABLE)
        mid[i] = 0.25 * pair_rows(total, pairs.at[i])

    loop(0, half, coarsen, 4)
    for i in range(half // 2):
        coarse[i] = 0.25 * pair_rows(mid[2 * i] + mid[2 * i + 1], pairs_2.at[i])
    for k in range(HALO):
        for t in range(4):
            rows = slice(8 * t, 8 * t + 8)
            send_x(pay_a, pay_b, 4 * k + t, phi[k, rows, :], phi[nx - HALO + k, rows, :])
        for t in range(2):
            rows = slice(8 * t, 8 * t + 8)
            send_x(pay_a, pay_b, 16 + 2 * k + t, mid[k, rows, :], mid[half - HALO + k, rows, :])


def first_pack_x_kernel(conc, label, r_a, r_b, token, pay_a, pay_b):
    nx = conc.shape[0]

    def plane(ref, k, t, offset, count):
        if t < 4:
            return ref[k, 8 * t : 8 * t + 8, :].astype(F32)
        return halo_tile(*y_sides(r_a, r_b, 7 * k + offset, count))

    for t in range(5):
        for k in range(HALO):
            send_x(pay_a, pay_b, 5 * k + t, plane(conc, k, t, 0, 4), plane(conc, nx - HALO + k, t, 0, 4))
        for k in range(3):
            send_x(pay_a, pay_b, 20 + 5 * k + t, plane(label, k, t, 4, 3), plane(label, nx - 3 + k, t, 4, 3))


def corner_rows(n, reach):
    counts = [min(HALO, k + reach) for k in range(HALO)]
    counts = counts + [HALO] * n + counts[::-1]
    return counts, [sum(counts[:i]) for i in range(len(counts))]


def second_rows(nx):
    phi, mid = (sum(corner_rows(n, reach)[0]) for n, reach in ((nx, 0), (nx // 2, 1)))
    return phi, phi + mid, phi + mid + 64


def second_pack_kernel(phi, mid, coarse, lists, x_a, x_b, pay_a, pay_b):
    nx = phi.shape[0]
    starts = second_rows(nx)

    def put(own, n, reach, index, base):
        counts, at = corner_rows(n, reach)
        tiles = own.shape[1] // 8
        for x in range(n):
            send_y(pay_a, pay_b, base + at[HALO + x], own[x, 0:4, :], own[x, 8 * tiles - 4 : 8 * tiles, :])
        for k in range(HALO):
            first_after, first_before = x_sides(x_a, x_b, index + tiles * k)
            last_after, last_before = x_sides(x_a, x_b, index + tiles * k + tiles - 1)
            for x, first, last in ((k, first_before, last_before), (HALO + n + k, first_after, last_after)):
                if counts[x]:
                    send_y(pay_a, pay_b, base + at[x], first[0 : counts[x]], last[8 - counts[x] : 8])

    put(phi, nx, 0, 0, 0)
    put(mid, nx // 2, 1, 16, starts[0])
    base = starts[1]
    for x in range(8):
        pay_a[base + 8 * x : base + 8 * x + 8, :] = coarse[x]
        pay_b[base + 8 * x : base + 8 * x + 8, :] = coarse[x]
    base = starts[2]
    pay_b[base : base + lists.shape[0], :] = lists[...]


def second_halo(r_a, r_b, n, reach, x, base):
    counts, at = corner_rows(n, reach)
    if not counts[x]:
        return jnp.zeros((8, 256), F32)
    return halo_tile(*y_sides(r_a, r_b, base + at[x], counts[x]))


def wide_rows(own, after_own, before_own, after, before):
    gap = jnp.zeros((6, 256), F32)
    return jnp.concatenate([own, after_own, after, gap, before, before_own], axis=0)


def sweeps_kernel(conc, label, gain_own, base_own, y_a, y_b, x_a, x_b, out, one, two, gain_far, base_far, gain_x, base_x):
    nx = conc.shape[0]

    def own(i):
        one[HALO + i, 0:32, :] = conc[i]

    loop(0, nx, own)
    for i in range(nx):
        c = halo_tile(*y_sides(y_a, y_b, 7 * i, 4))
        lab = halo_tile(*y_sides(y_a, y_b, 7 * i + 4, 3))
        one[HALO + i, 32:40, :] = c
        gain_far[i] = jnp.where(c > 0.0, pick(lab, RATIO_TABLE), 0.0)
        base_far[i] = c * pick(lab, INVERSE_TABLE)

    def put(x, rows, c, lab):
        one[x, rows, :] = c
        at = x if x < HALO else x - nx
        gain_x[at, rows, :] = jnp.where(c > 0.0, pick(lab, RATIO_TABLE), 0.0)
        base_x[at, rows, :] = c * pick(lab, INVERSE_TABLE)

    for t in range(5):
        rows = slice(8 * t, 8 * t + 8)
        for k in range(HALO):
            c_after, c_before = x_sides(x_a, x_b, 5 * k + t)
            l_after = x_sides(x_a, x_b, 20 + 5 * min(k, 2) + t)[0]
            l_before = x_sides(x_a, x_b, 20 + 5 * max(k - 1, 0) + t)[1]
            put(k, rows, c_before, l_before)
            put(HALO + nx + k, rows, c_after, l_after)

    def neighbours(old, x):
        mid = old[x]
        return (old[x - 1] + old[x + 1]) + (along_y(mid) + along_z(mid))

    fields = (one, two)
    for s in range(1, SWEEPS):
        old, new = fields[(s - 1) % 2], fields[s % 2]

        def sweep(i, old=old, new=new):
            gain = jnp.concatenate([gain_own[i], gain_far[i]], axis=0)
            base = jnp.concatenate([base_own[i], base_far[i]], axis=0)
            new[HALO + i] = base + gain * neighbours(old, HALO + i)

        loop(0, nx, sweep)
        for k in range(s, HALO):
            for x, at in ((k, k), (2 * HALO + nx - 1 - k, 2 * HALO - 1 - k)):
                new[x] = base_x[at] + gain_x[at] * neighbours(old, x)

    old = fields[(SWEEPS - 1) % 2]

    def last(i):
        out[i] = base_own[i] + gain_own[i] * neighbours(old, HALO + i)[0:32, :]

    loop(0, nx, last)


def flux_kernel(conc, label, phi, solid, flux, pay_a, pay_b):
    nx = conc.shape[0]

    def plane(i):
        drive = 0.5 * (solid[i] - phi[i])
        logc = jnp.log(conc[i])
        value = jnp.exp(drive + 0.4 * logc) - jnp.exp(0.6 * logc - drive)
        flux[i] = pick(label[i], KINETIC_TABLE) * value

    loop(0, nx, plane, 4)
    for x in range(nx):
        send_y(pay_a, pay_b, 3 * x, flux[x, 0:3, :], flux[x, 29:32, :])


def mask_kernel(flux_all, lists, far, flux, halo_mask, marked):
    nx = flux_all.shape[0]
    rows = lists.shape[0]
    pieces = [lists[i : i + 1, :] for i in range(rows)] + [far[i : i + 1, :] for i in range(far.shape[0] - rows, far.shape[0])]
    owner = jnp.concatenate(pieces[0::2], axis=1).astype(jnp.int32)
    block = jnp.concatenate(pieces[1::2], axis=1).astype(jnp.int32)
    entries = owner.shape[1]
    hit_column = (iota((LANES, entries), 0) == lax.rem(block, 64)).astype(jnp.bfloat16)
    at_row = lax.shift_right_arithmetic(block, 6)
    here = lax.axis_index("dev")
    for j in range(3):
        mine = jnp.where(owner == here + j - 1, at_row, -1)
        hit_row = (iota((nx, entries), 0) == mine).astype(jnp.bfloat16)
        named = lax.dot_general(hit_row, hit_column, (((1,), (1,)), ((), ())), preferred_element_type=F32)
        for i in range(nx):
            marked[j, i] = jnp.broadcast_to(named[i : i + 1, :], (8, LANES))
    is_row = lax.div(iota((32, LANES), 1), 2) == iota((32, LANES), 0)
    row, pair = iota((8, LANES), 0), lax.div(iota((8, LANES), 1), 2)
    is_after = (row < 3) & (pair == row)
    is_before = (row >= 5) & (pair == row + 24)
    spread = (lax.rem(iota((LANES, 256), 0), 2) == lax.div(iota((LANES, 256), 1), LANES)).astype(jnp.bfloat16)

    def plane(i):
        marks = jnp.where(is_row, jnp.concatenate([marked[1, i]] * 4, axis=0), 0.0)
        beyond = jnp.where(is_after, marked[2, i], jnp.where(is_before, marked[0, i], 0.0))
        marks = jnp.concatenate([marks, beyond], axis=0).astype(jnp.bfloat16)
        listed = jnp.dot(marks, spread, preferred_element_type=F32) > 0.5
        flux[i] = jnp.where(listed[0:32], flux_all[i], 0.0)
        halo_mask[i] = jnp.where(listed[32:40], 1.0, 0.0)

    loop(0, nx, plane, 4)


def store_kernel(conc, flux, conc_out, flux_out, token, sems):
    copies = []
    for i, (ref, to) in enumerate(((conc, conc_out), (flux, flux_out))):
        for j in range(4):
            rows = pl.ds(8 * j, 8)
            copies.append(pltpu.make_async_copy(ref.at[rows], to.at[rows], sems.at[4 * i + j]))
            copies[-1].start()
    token[...] = jnp.zeros(token.shape, F32)
    for c in copies:
        c.wait()


def ready_kernel(conc, label, phi, y_a, y_b, x_a, x_b, yy_a, yy_b, xx_a, xx_b, weight, scale, field, token):
    nx = conc.shape[0]
    token[...] = jnp.zeros(token.shape, F32)

    def put(x, rows, c, lab, p):
        conduct = c * pick(lab, CONDUCT_TABLE)
        factor = OMEGA / (MASS + 6.0 * conduct)
        weight[x, rows, :] = conduct * factor
        scale[x, rows, :] = factor
        field[x, rows, :] = p

    def own(i):
        put(HALO + i, slice(0, 32), conc[i], label[i], phi[i])

    loop(0, nx, own, 4)
    low = slice(32, 40)
    for i in range(nx):
        c = halo_tile(*y_sides(y_a, y_b, 7 * i, 4))
        lab = halo_tile(*y_sides(y_a, y_b, 7 * i + 4, 3))
        put(HALO + i, low, c, lab, second_halo(yy_a, yy_b, nx, 0, HALO + i, 0))
    for t in range(5):
        rows = slice(8 * t, 8 * t + 8)
        for k in range(HALO):
            c_after, c_before = x_sides(x_a, x_b, 5 * k + t)
            l_after = x_sides(x_a, x_b, 20 + 5 * min(k, 2) + t)[0]
            l_before = x_sides(x_a, x_b, 20 + 5 * max(k - 1, 0) + t)[1]
            if t < 4:
                p_after, p_before = x_sides(xx_a, xx_b, 4 * k + t)
            else:
                p_after = second_halo(yy_a, yy_b, nx, 0, HALO + nx + k, 0)
                p_before = second_halo(yy_a, yy_b, nx, 0, k, 0)
            put(k, rows, c_before, l_before, p_before)
            put(HALO + nx + k, rows, c_after, l_after, p_after)


def flux_pack_x_kernel(flux, r_a, r_b, mask, token, pay_a, pay_b):
    nx = flux.shape[0]

    def tile(x, t):
        if t < 4:
            return flux[x, 8 * t : 8 * t + 8, :]
        return mask[x] * halo_tile(*y_sides(r_a, r_b, 3 * x, 3))

    for k in range(3):
        for t in range(5):
            send_x(pay_a, pay_b, 5 * k + t, tile(k, t), tile(nx - 3 + k, t))


def first_sweep(field, weight, scale, x, rows, flux):
    p = field[x]
    near = (field[x - 1] + field[x + 1]) + (along_y(p) + along_z(p))
    b = scale[x, rows, :] * (MASS * p[rows, :] + flux)
    return b, 0.2 * p[rows, :] + weight[x, rows, :] * near[rows, :] + b


def potential_inner_kernel(flux, mask, y_a, y_b, weight, scale, field, after_two, source, first, source_mid, far, pairs):
    nx = flux.shape[0]
    for i in range(nx):
        far[i] = mask[i] * halo_tile(*y_sides(y_a, y_b, 3 * i, 3))

    def own(i):
        x = HALO + i
        f = jnp.concatenate([flux[i], far[i]], axis=0)
        source[x], first[x] = first_sweep(field, weight, scale, x, slice(0, 40), f)

    loop(0, nx, own)

    def around(values, x):
        v = values[x]
        return v, weight[x] * ((values[x - 1] + values[x + 1]) + (along_y(v) + along_z(v)))

    def sweep(x):
        v, near = around(first, x)
        after_two[x] = 0.2 * v + (source[x] + near)

    loop(HALO + 1, HALO + nx - 1, sweep)

    def remainder(x):
        v, near = around(after_two, x)
        return ((source[x] - OMEGA * v) + near)[0:32, :] / scale[x, 0:32, :]

    def coarsen(i):
        x = HALO + 2 * i
        source_mid[i] = 0.25 * pair_rows(remainder(x) + remainder(x + 1), pairs.at[i])

    loop(1, nx // 2 - 1, coarsen, 4)


def potential_edge_kernel(
    x_a, x_b, weight, scale, field, inner_two, inner_source, inner_first, inner_mid,
    edge_two, edge_source, source_mid, pay_a, pay_b, first, pairs,
):
    half = source_mid.shape[0]
    nx = 2 * half
    for side, face in ((0, HALO), (1, HALO + nx)):
        base = 8 * side + HALO - face
        for k in range(3):
            x = face - 3 + k if side == 0 else face + k
            f = jnp.concatenate([x_sides(x_a, x_b, 5 * k + t)[1 - side] for t in range(5)], axis=0)
            edge_source[base + x], first[base + x] = first_sweep(field, weight, scale, x, slice(0, 40), f)

        def first_of(x, base=base):
            return inner_first[x] if HALO <= x < HALO + nx else first[base + x]

        def source_of(x, base=base):
            return inner_source[x] if HALO <= x < HALO + nx else edge_source[base + x]

        def two_of(x, base=base):
            return inner_two[x] if HALO < x < HALO + nx - 1 else edge_two[base + x]

        for x in range(face - 2, face + 1) if side == 0 else range(face - 1, face + 2):
            v = first_of(x)
            near = weight[x] * ((first_of(x - 1) + first_of(x + 1)) + (along_y(v) + along_z(v)))
            edge_two[base + x] = 0.2 * v + (source_of(x) + near)
        total = 0.0
        at = face if side == 0 else face - 2
        for x in (at, at + 1):
            v = two_of(x)
            near = weight[x] * ((two_of(x - 1) + two_of(x + 1)) + (along_y(v) + along_z(v)))
            total = total + ((source_of(x) - OMEGA * v) + near)[0:32, :] / scale[x, 0:32, :]
        source_mid[0 if side == 0 else half - 1] = 0.25 * pair_rows(total, pairs.at[side])
    for x in range(1, half - 1):
        source_mid[x] = inner_mid[x]
    for x in range(half):
        send_y(pay_a, pay_b, 4 * x, source_mid[x, 0:4, :], source_mid[x, 12:16, :])


def mid_pack_x_kernel(field, r_a, r_b, token, token_2, pay_a, pay_b):
    n = field.shape[0]

    def tile(x, t):
        if t < 2:
            return field[x, 8 * t : 8 * t + 8, :]
        return halo_tile(*y_sides(r_a, r_b, 4 * x, 4))

    for k in range(HALO):
        for t in range(3):
            send_x(pay_a, pay_b, 3 * k + t, tile(k, t), tile(n - HALO + k, t))


def mid_kernel(
    source_own, conduct_own, yy_a, yy_b, xx_a, xx_b, y_a, y_b, x_a, x_b, rho, load,
    after_two, source, weight, coarse, conduct, pay_a, pay_b, part, scale, mid_conduct, pairs, pairs_2,
):
    n = source_own.shape[0]
    base = second_rows(2 * n)[0]

    def put(x, rows, b, k):
        factor = OMEGA / (MASS + 3.0 * k)
        weight[x, rows, :] = k * factor
        scale[x, rows, :] = factor
        source[x, rows, :] = factor * b
        mid_conduct[x, rows, :] = k

    def far(x):
        return second_halo(yy_a, yy_b, n, 1, x, base)

    for i in range(n):
        put(HALO + i, slice(0, 16), source_own[i], conduct_own[i])
        put(HALO + i, slice(16, 24), halo_tile(*y_sides(y_a, y_b, 4 * i, 4)), far(HALO + i))
    for k in range(HALO):
        for t in range(3):
            rows = slice(8 * t, 8 * t + 8)
            b_after, b_before = x_sides(x_a, x_b, 3 * k + t)
            if t < 2:
                c_after, c_before = x_sides(xx_a, xx_b, 16 + 2 * k + t)
            else:
                c_after, c_before = far(HALO + n + k), far(k)
            put(k, rows, b_before, c_before)
            put(HALO + n + k, rows, b_after, c_after)

    def around(values, x):
        v = values[x]
        return v, weight[x] * (0.25 * ((values[x - 1] + values[x + 1]) + along_y(v)) + along_z(v))

    def sweep(x):
        v, near = around(source, x)
        after_two[x] = 0.2 * v + (source[x] + near)

    loop(1, n + 2 * HALO - 1, sweep, 11)

    def remainder(x):
        v, near = around(after_two, x)
        return ((source[x] - OMEGA * v) + near) / scale[x]

    total = jnp.zeros((8, 256), F32)
    for i in range(n // 2):
        x = HALO + 2 * i
        value = 0.25 * pair_rows(remainder(x) + remainder(x + 1), pairs.at[i])
        k = 0.25 * pair_rows(mid_conduct[x] + mid_conduct[x + 1], pairs_2.at[i])
        coarse[i] = value
        conduct[i] = k
        send_y(pay_a, pay_b, 9 * i, value[1:9], jnp.concatenate([value[11:12], value[0:7]], axis=0))
        send_y(pay_a, pay_b, 9 * i + 8, k[8:9], k[11:12])
        total += rho[i] * value[0:8]
    sums = jnp.concatenate([total[:, :LANES] + total[:, LANES:], load[...]], axis=1)
    pay_b[72:80, :] = sums
    part[...] = sums


COARSE_W = 0.0625


def coarse_ready_kernel(own, r_a, r_b, rho, load, token, one, two, conduct, scale):
    token[...] = jnp.zeros(token.shape, F32)
    base = r_a.shape[0] - 64
    for x in range(8):
        after, before = y_sides(r_a, r_b, base + 8 * x, 8)
        k = jnp.concatenate([own[x], after, jnp.zeros((8, 256), F32), before], axis=0)
        conduct[x] = k
        scale[x] = OMEGA / (MASS + 2.25 * k)
        one[x] = jnp.ones(k.shape, F32)
    fields = (one, two)
    for s in range(COARSE_SWEEPS):
        old, new = fields[s % 2], fields[(s + 1) % 2]
        for x in range(8):
            near = [conduct[i] * old[i] if 0 <= i < 8 else None for i in (x - 1, x, x + 1)]
            inner = along_y(near[1])
            for other in (near[0], near[2]):
                if other is not None:
                    inner = inner + other
            new[x] = 0.2 * old[x] + scale[x] * (COARSE_W * inner + along_z(near[1]))
    last = fields[COARSE_SWEEPS % 2]
    peer, peers = lax.axis_index("dev"), lax.axis_size("dev")
    row, z = iota((8, 256), 0), iota((8, 256), 1)
    edge_y = ((row == 0) & (peer == 0)) | ((row == 7) & (peer == peers - 1))
    edge = edge_y.astype(F32) * COARSE_W + ((z == 0) | (z == 255)).astype(F32)
    total = jnp.zeros((8, 256), F32)
    for x in range(8):
        rho[x] = last[x, 0:8, :]
        total += MASS + own[x] * (edge + (COARSE_W if x in (0, 7) else 0.0))
    load[...] = total[:, :LANES] + total[:, LANES:]


def coarse_kernel(own, conduct, far_a, far_b, r_a, r_b, error, source, weight, one, two):
    base = far_a.shape[0] - 64
    for x in range(8):
        after, before = y_sides(r_a, r_b, 9 * x, 8)
        b = wide_rows(own[x, 0:8, :], own[x, 8:9, :], own[x, 11:12, :], after, before)
        last_after, last_before = y_sides(r_a, r_b, 9 * x + 8, 1)
        after, before = y_sides(far_a, far_b, base + 8 * x, 8)
        after = jnp.concatenate([after[1:8], last_after], axis=0)
        before = jnp.concatenate([last_before, before[0:7]], axis=0)
        k = wide_rows(conduct[x, 0:8, :], conduct[x, 8:9, :], conduct[x, 11:12, :], after, before)
        factor = OMEGA / (MASS + 2.25 * k)
        weight[x] = k * factor
        source[x] = factor * b
    old = source
    for s in range(1, COARSE_SWEEPS):
        new = one if s % 2 else two
        for x in range(8):
            v = old[x]
            inner = along_y(v)
            if x > 0:
                inner = inner + old[x - 1]
            if x < 7:
                inner = inner + old[x + 1]
            new[x] = 0.2 * v + (source[x] + weight[x] * (COARSE_W * inner + along_z(v)))
        old = new
    for x in range(8):
        error[x, 0:8, :] = old[x, 0:8, :]
        error[x, 8:16, :] = jnp.where(upper(), old[x, 8:16, :], old[x, 24:32, :])


def shift_kernel(error, sums, out, pay_a, pay_b):
    resid = jnp.sum(sums[:, :LANES])
    load = jnp.sum(sums[:, LANES:])
    shift_c = jnp.full((16, 256), resid, F32) / jnp.full((16, 256), load, F32)
    for x in range(8):
        out[x] = error[x] + shift_c
    for k in range(2):
        send_x(pay_a, pay_b, k, out[k], out[6 + k])


def squeeze(tile):
    return jnp.where(iota((8, 256), 0) < 2, tile, pltpu.roll(tile, 4, 0))


def spread_coarse(plane, room):
    return jnp.concatenate([twice(plane[0:8], room.at[0]), twice(squeeze(plane[8:16]), room.at[1])[0:8]], axis=0)


def spread_mid(plane, room):
    parts = [twice(plane[0:8], room.at[0]), twice(plane[8:16], room.at[1]), twice(squeeze(plane[16:24]), room.at[2])[0:8]]
    return jnp.concatenate(parts, axis=0)


def smoothed(before, v, after, weight, source, w):
    inner = (before + after) + along_y(v)
    return source + (0.2 * v + weight * (w * inner + along_z(v)))


def finish_inner_kernel(
    error, mid_two, mid_source, mid_weight, fine_two, fine_source, fine_weight,
    out, zero, one, fine_one, fine_last, two, dup, dup_2, result, sems,
):
    n = mid_two.shape[0]
    nf = fine_two.shape[0]
    for c in range(8):
        spread = spread_coarse(error[c], dup.at[c])
        for x in (2 * c + HALO, 2 * c + 1 + HALO):
            zero[x] = jnp.where(mid_weight[x] > 0.0, mid_two[x] + spread, 0.0)

    def sweep_mid(x, old, new):
        new[x] = smoothed(old[x - 1], old[x], old[x + 1], mid_weight[x], mid_source[x], 0.25)

    for x in range(HALO + 1, n - HALO - 1):
        sweep_mid(x, zero, one)
    for x in range(HALO + 2, n - HALO - 2):
        sweep_mid(x, one, two)

    def lift(m):
        spread = spread_mid(two[m], dup_2.at[m])
        x = 2 * m - HALO
        fine_one[x] = fine_two[x] + spread
        fine_one[x + 1] = fine_two[x + 1] + spread

    loop(HALO + 2, n - HALO - 2, lift, 6)

    def sweep_one(x):
        fine_last[x] = smoothed(fine_one[x - 1], fine_one[x], fine_one[x + 1], fine_weight[x], fine_source[x], 1.0)

    low, high = 2 * HALO + 1, nf - 2 * HALO - 1
    loop(low, high, sweep_one, 11)
    copies = []
    low, high = low + 1, high - 1
    for j in range(2):
        mid = low + (high - low) // 2
        for x in range(low, mid) if j == 0 else range(mid, high):
            v = smoothed(fine_last[x - 1], fine_last[x], fine_last[x + 1], fine_weight[x], fine_source[x], 1.0)
            result[x - HALO] = v[0:32, :]
        rows = pl.ds(low - HALO, mid - low) if j == 0 else pl.ds(mid - HALO, high - mid)
        copies.append(pltpu.make_async_copy(result.at[rows], out.at[rows], sems.at[j]))
        copies[-1].start()
    for c in copies:
        c.wait()


def finish_edge_kernel(
    x_a, x_b, mid_two, mid_source, mid_weight, fine_two, edge_two, fine_source, edge_source, fine_weight,
    zero, one, fine_one, fine_last, begun, out, zero_edge, one_edge, fine_edge, last_edge, dup, dup_2, result, sems,
):
    n = mid_two.shape[0]
    nf = fine_two.shape[0]
    nx = nf - 2 * HALO
    copies = []
    planes = x_sides(x_a, x_b, slice(0, 2))
    for side in (0, 1):
        sign = 1 if side == 0 else -1
        at = lambda k, side=side: HALO + k if side == 0 else n - HALO - 1 - k
        fine = lambda k, side=side: HALO + k if side == 0 else nf - HALO - 1 - k
        base = 8 * side + (0 if side == 0 else HALO - HALO - nx)
        for c in range(2):
            plane = planes[1 - side][c]
            spread = spread_coarse(plane, dup.at[2 * side + c])
            first = 2 * c if side == 0 else n - HALO + 2 * c
            for x in (first, first + 1):
                zero_edge[x] = jnp.where(mid_weight[x] > 0.0, mid_two[x] + spread, 0.0)

        def zero_of(k):
            return zero[at(k)] if k >= 0 else zero_edge[at(k)]

        def one_of(k):
            return one[at(k)] if k >= 1 else one_edge[at(k)]

        for k in range(-2, 1):
            x = at(k)
            one_edge[x] = smoothed(zero_of(k - 1), zero_of(k), zero_of(k + 1), mid_weight[x], mid_source[x], 0.25)
        for k in range(-1, 2):
            x = at(k)
            value = smoothed(one_of(k - 1), one_of(k), one_of(k + 1), mid_weight[x], mid_source[x], 0.25)
            spread = spread_mid(value, dup_2.at[3 * side + k + 1])
            for f in (fine(2 * k), fine(2 * k + 1)):
                inside = HALO < f < nf - HALO - 1
                before = fine_two[f] if inside else edge_two[base + f]
                fine_edge[f] = before + spread

        def fine_of(k):
            return fine_one[fine(k)] if k >= 4 else fine_edge[fine(k)]

        def last_of(k):
            return fine_last[fine(k)] if k >= 5 else last_edge[fine(k)]

        for k in range(-1, 5):
            f = fine(k)
            source = fine_source[f] if HALO <= f < nf - HALO else edge_source[base + f]
            last_edge[f] = smoothed(fine_of(k - 1), fine_of(k), fine_of(k + 1), fine_weight[f], source, 1.0)
        for k in range(6):
            f = fine(k)
            v = smoothed(last_of(k - 1), last_of(k), last_of(k + 1), fine_weight[f], fine_source[f], 1.0)
            result[f - HALO] = v[0:32, :]
        rows = pl.ds(0, 6) if side == 0 else pl.ds(nx - 6, 6)
        copies.append(pltpu.make_async_copy(result.at[rows], out.at[rows], sems.at[side]))
        copies[-1].start()
    for c in copies:
        c.wait()


def both_ways(pairs):
    return pairs + [(j, i) for i, j in pairs]


def swap(pay_a, pay_b, axis):
    size = lax.axis_size(axis)
    pairs_a = [(i, i + 1) for i in range(1, size - 1, 2)]
    pairs_b = [(i, i + 1) for i in range(0, size - 1, 2)]
    return lax.ppermute(pay_a, axis, both_ways(pairs_a)), lax.ppermute(pay_b, axis, both_ways(pairs_b))


def exchange(value, distance):
    return lax.ppermute(value, "dev", [(i, i ^ distance) for i in range(lax.axis_size("dev"))])


def body(conc_old, phi_old, solid_pot, phase_label, iface_block, iface_owner):
    peers = lax.axis_size("dev")
    nx = conc_old.shape[0]
    half = nx // 2
    quarter = nx // 4
    ext = (nx + 2 * HALO, nx + 2 * HALO, 256)
    ext_mid = (half + 2 * HALO, half + 2 * HALO, 256)
    token_shape = shaped(8, LANES)

    pay_a, pay_b, own_lists = call(
        first_pack_kernel,
        [shaped(7 * nx, 256)] * 2 + [shaped(8, 256)],
        [conc_old, phase_label, iface_owner.reshape(1, -1), iface_block],
        [vmem(nx, HALO, 256)] * 2
        + [pltpu.VMEM((nx, HALO, 256), jnp.int32)] * 2
        + [pltpu.VMEM((1, 256), jnp.int32)] * 2
        + [pltpu.SemaphoreType.DMA((6,))],
        in_specs=[FAR] * 4,
        limit=VMEM_MOST,
        name="first_pack",
    )
    y_a, y_b = swap(pay_a, pay_b, "dev")
    conduct_mid, conduct_coarse, pay_a, pay_b, lists, gain, base = call(
        own_kernel,
        [shaped(half, half, 256), shaped(quarter, quarter, 256), shaped(24, 8, 256), shaped(24, 8, 256)]
        + [shaped(2, 256), shaped(nx, nx, 256), shaped(nx, nx, 256)],
        [conc_old, phase_label, phi_old, own_lists],
        [vmem(half, 2, nx, LANES), vmem(quarter, 2, half, LANES)],
        name="own",
    )
    xx_a, xx_b = swap(pay_a, pay_b, "grp")
    distance = peers // 2
    while distance > 1:
        lists = jnp.concatenate([lists, exchange(lists, distance)], axis=0)
        distance //= 2
    far_rows = second_rows(nx)[2]
    far_pay = call(
        second_pack_kernel,
        [shaped(far_rows, 256), shaped(far_rows + peers, 256)],
        [phi_old, conduct_mid, conduct_coarse, lists, xx_a, xx_b],
        name="second_pack",
    )
    yy_a, yy_b = swap(*far_pay, "dev")
    pay_a, pay_b = call(
        first_pack_x_kernel,
        [shaped(35, 8, 256)] * 2,
        [conc_old, phase_label, y_a, y_b, conduct_coarse],
        name="first_pack_x",
    )
    x_a, x_b = swap(pay_a, pay_b, "grp")

    (conc_new,) = call(
        sweeps_kernel,
        [shaped(nx, nx, 256)],
        [conc_old, phase_label, gain, base, y_a, y_b, x_a, x_b],
        [vmem(*ext)] * 2 + [vmem(nx, 8, 256)] * 2 + [vmem(2 * HALO, nx + 2 * HALO, 256)] * 2,
        name="sweeps",
    )
    flux_all, pay_a, pay_b = call(
        flux_kernel,
        [shaped(nx, nx, 256), shaped(3 * nx, 256), shaped(3 * nx, 256)],
        [conc_new, phase_label, phi_old, solid_pot],
        name="flux",
    )
    f_a, f_b = swap(pay_a, pay_b, "dev")
    flux_own, halo_mask = call(
        mask_kernel,
        [shaped(nx, nx, 256), shaped(nx, 8, 256)],
        [flux_all, lists, yy_b],
        [vmem(3, nx, 8, LANES)],
        name="mask",
    )
    weight, scale, field, made = call(
        ready_kernel,
        [shaped(*ext)] * 3 + [token_shape],
        [conc_old, phase_label, phi_old, y_a, y_b, x_a, x_b, yy_a, yy_b, xx_a, xx_b],
        name="ready",
    )
    pay_a, pay_b = call(
        flux_pack_x_kernel, [shaped(15, 8, 256)] * 2, [flux_own, f_a, f_b, halo_mask, made], name="flux_pack_x"
    )
    fx_a, fx_b = swap(pay_a, pay_b, "grp")
    fine_two, fine_source, fine_first, inner_mid = call(
        potential_inner_kernel,
        [shaped(*ext)] * 3 + [shaped(half, half, 256)],
        [flux_own, halo_mask, f_a, f_b, weight, scale, field],
        [vmem(nx, 8, 256), vmem(half, 2, nx, LANES)],
        name="potential_inner",
    )
    edge = (16, nx + 2 * HALO, 256)
    edge_two, edge_source, source_mid, pay_a, pay_b = call(
        potential_edge_kernel,
        [shaped(*edge), shaped(*edge), shaped(half, half, 256), shaped(4 * half, 256), shaped(4 * half, 256)],
        [fx_a, fx_b, weight, scale, field, fine_two, fine_source, fine_first, inner_mid],
        [vmem(*edge), vmem(2, 2, nx, LANES)],
        name="potential_edge",
    )
    m_a, m_b = swap(pay_a, pay_b, "dev")
    concentration, flux, stored = call(
        store_kernel,
        [shaped(nx, nx, 256), shaped(nx, nx, 256), token_shape],
        [conc_new, flux_own],
        [pltpu.SemaphoreType.DMA((8,))],
        out_specs=[FAR, FAR, WHOLE],
        name="store",
    )
    wide = (quarter, 32, 256)
    rho, load, made = call(
        coarse_ready_kernel,
        [shaped(quarter, quarter, 256), shaped(8, LANES), token_shape],
        [conduct_coarse, yy_a, yy_b],
        [vmem(*wide)] * 4,
        name="coarse_ready",
    )
    pay_a, pay_b = call(
        mid_pack_x_kernel, [shaped(3 * HALO, 8, 256)] * 2, [source_mid, m_a, m_b, made, stored], name="mid_pack_x"
    )
    mx_a, mx_b = swap(pay_a, pay_b, "grp")
    mid_two, mid_source, mid_weight, source_coarse, wide_coarse, pay_a, pay_b, sums = call(
        mid_kernel,
        [shaped(*ext_mid)] * 3
        + [shaped(quarter, 12, 256), shaped(quarter, 12, 256), shaped(72, 256), shaped(80, 256), shaped(8, 256)],
        [source_mid, conduct_mid, yy_a, yy_b, xx_a, xx_b, m_a, m_b, mx_a, mx_b, rho, load],
        [vmem(*ext_mid)] * 2 + [vmem(8, 2, half + 2 * HALO, LANES)] * 2,
        name="middle",
    )
    c_a, c_b = swap(pay_a, pay_b, "dev")
    sums = sums + c_b[72:80]
    distance = 2
    while distance < peers:
        sums = sums + exchange(sums, distance)
        distance *= 2
    (error,) = call(
        coarse_kernel,
        [shaped(8, 16, 256)],
        [source_coarse, wide_coarse, yy_a, yy_b, c_a, c_b],
        [vmem(*wide)] * 4,
        name="coarse",
    )
    error, pay_a, pay_b = call(
        shift_kernel, [shaped(8, 16, 256), shaped(2, 16, 256), shaped(2, 16, 256)], [error, sums], name="shift"
    )
    e_a, e_b = swap(pay_a, pay_b, "grp")
    begun, zero, one, fine_one, fine_last = call(
        finish_inner_kernel,
        [shaped(nx, nx, 256), shaped(*ext_mid), shaped(*ext_mid), shaped(*ext), shaped(*ext)],
        [error, mid_two, mid_source, mid_weight, fine_two, fine_source, weight],
        [vmem(*ext_mid), vmem(8, 2, 2, 16, LANES), vmem(half + 2 * HALO, 3, 2, 16, LANES), vmem(nx, nx, 256)]
        + [pltpu.SemaphoreType.DMA((2,))],
        out_specs=[FAR] + [WHOLE] * 4,
        name="finish_inner",
    )
    finish_args = [e_a, e_b, mid_two, mid_source, mid_weight, fine_two, edge_two, fine_source, edge_source, weight]
    finish_args += [zero, one, fine_one, fine_last, begun]
    (potential,) = call(
        finish_edge_kernel,
        [shaped(nx, nx, 256)],
        finish_args,
        [vmem(*ext_mid), vmem(*ext_mid), vmem(*ext), vmem(*ext)]
        + [vmem(4, 2, 2, 16, LANES), vmem(6, 3, 2, 16, LANES), vmem(nx, nx, 256)]
        + [pltpu.SemaphoreType.DMA((2,))],
        in_specs=[WHOLE] * (len(finish_args) - 1) + [FAR],
        out_specs=[FAR],
        aliases={len(finish_args) - 1: 0},
        name="finish_edge",
    )
    return (concentration, flux, potential)


def solution(mesh):
    brick = P("grp", "dev", None)
    return jax.shard_map(
        body,
        mesh=mesh,
        in_specs=(brick, brick, brick, brick, P("grp", "dev"), brick),
        out_specs=(brick, brick, brick),
        check_vma=False,
    )
```

```python
import jax
import jax.numpy as jnp
from jax import lax
from jax.experimental import pallas as pl
from jax.experimental.pallas import tpu as pltpu
from jax.sharding import PartitionSpec as P


F32 = jnp.float32
MASS = 0.05
OMEGA = 0.8
DIFFUSION_TABLE = (1.5, 0.1, 0.4)
RATIO_TABLE = tuple(d / (1.0 + 6.0 * d) for d in DIFFUSION_TABLE)
INVERSE_TABLE = tuple(1.0 / (1.0 + 6.0 * d) for d in DIFFUSION_TABLE)
CONDUCT_TABLE = (1.0, 0.3, 0.6)
KINETIC_TABLE = (0.2, 1.0, 0.5)
SWEEPS = 4
COARSE_SWEEPS = 8
COARSE_NEAR = 8
HALO = 4
LANES = 128
VMEM_LIMIT = 28 * 1024 * 1024
VMEM_MOST = 58 * 1024 * 1024


def shaped(*shape):
    return jax.ShapeDtypeStruct(shape, F32)


WHOLE = pl.BlockSpec(memory_space=pltpu.VMEM)
FAR = pl.BlockSpec(memory_space=pltpu.HBM)


def call(kernel, outs, args, scratch=(), in_specs=None, out_specs=None, limit=VMEM_LIMIT, aliases=None, flops=10**6, name=None):
    size = sum(4 * a.size for a in args) + sum(4 * o.size for o in outs)
    return pl.pallas_call(
        kernel,
        out_shape=tuple(outs),
        in_specs=in_specs or [WHOLE] * len(args),
        out_specs=tuple(out_specs or [WHOLE] * len(outs)),
        scratch_shapes=list(scratch),
        input_output_aliases=aliases or {},
        compiler_params=pltpu.CompilerParams(vmem_limit_bytes=limit),
        cost_estimate=pl.CostEstimate(flops=flops, bytes_accessed=size, transcendentals=0),
        name=name,
    )(*args)


def vmem(*shape):
    return pltpu.VMEM(shape, F32)


def iota(shape, dim):
    return lax.broadcasted_iota(jnp.int32, shape, dim)


def pick(label, table):
    return jnp.where(label == 0, table[0], jnp.where(label == 1, table[1], table[2])).astype(F32)


def loop(low, high, body, unroll=8):
    steps = (high - low) // unroll

    def step(i, carry):
        for u in range(unroll):
            body(low + i * unroll + u)
        return carry

    if steps > 1:
        lax.fori_loop(0, steps, step, 0)
    else:
        steps = 0
    for x in range(low + steps * unroll, high):
        body(x)


def odd(axis):
    return lax.rem(lax.axis_index(axis), 2) == 1


def along_y(v):
    return pltpu.roll(v, 1, 0) + pltpu.roll(v, v.shape[0] - 1, 0)


def along_z(v):
    low, high = v[:, :LANES], v[:, LANES:]
    lane = iota(low.shape, 1)
    first, last = lane == 0, lane == LANES - 1
    low_up, high_up = pltpu.roll(low, 1, 1), pltpu.roll(high, 1, 1)
    low_down, high_down = pltpu.roll(low, LANES - 1, 1), pltpu.roll(high, LANES - 1, 1)
    low_sum = jnp.where(first, 0.0, low_up) + jnp.where(last, high_down, low_down)
    high_sum = jnp.where(first, low_up, high_up) + jnp.where(last, 0.0, high_down)
    return jnp.concatenate([low_sum, high_sum], axis=1)


def upper(shape=(8, 256)):
    return iota(shape, 0) < HALO


def twice(tile, scratch):
    for h in range(2):
        part = tile[:, h * LANES : (h + 1) * LANES]
        scratch[h, pl.ds(0, 8, stride=2), :] = part
        scratch[h, pl.ds(1, 8, stride=2), :] = part
    return jnp.concatenate([scratch[0], scratch[1]], axis=1)


def pair_rows(v, scratch):
    half = v.shape[0] // 2
    parts = []
    for h in range(2):
        scratch[h] = v[:, h * LANES : (h + 1) * LANES]
        parts.append(scratch[h, pl.ds(0, half, stride=2), :] + scratch[h, pl.ds(1, half, stride=2), :])
    return jnp.concatenate(parts, axis=1)


def either(flag, if_true, if_false):
    return jnp.where(flag, if_true, if_false)


def y_sides(r_a, r_b, at, count):
    flag = odd("dev")
    a, b = r_a[at : at + count, :], r_b[at : at + count, :]
    return either(flag, a, b), either(flag, b, a)


def x_sides(r_a, r_b, index):
    flag = odd("grp")
    a, b = r_a[index], r_b[index]
    return either(flag, a, b), either(flag, b, a)


def send_y(pay_a, pay_b, at, first, last):
    flag = odd("dev")
    n = first.shape[0]
    pay_a[at : at + n, :] = either(flag, last, first)
    pay_b[at : at + n, :] = either(flag, first, last)


def send_x(pay_a, pay_b, index, first, last):
    flag = odd("grp")
    pay_a[index] = either(flag, last, first)
    pay_b[index] = either(flag, first, last)


def halo_tile(after, before):
    parts = [after]
    if after.shape[0] < HALO:
        parts.append(jnp.zeros((2 * HALO - 2 * after.shape[0], after.shape[1]), F32))
    return jnp.concatenate(parts + [before], axis=0)


def first_pack_kernel(
    conc, label, owner, block, pay_a, pay_b, own_lists, c_first, c_last, l_first, l_last, own_owner, own_block, sems
):
    nx = conc.shape[0]
    copies = [pltpu.make_async_copy(owner, own_owner, sems.at[4]), pltpu.make_async_copy(block, own_block, sems.at[5])]
    for i, (ref, at, to) in enumerate(((conc, 0, c_first), (conc, 28, c_last), (label, 0, l_first), (label, 28, l_last))):
        copies.append(pltpu.make_async_copy(ref.at[:, pl.ds(at, 4), :], to, sems.at[i]))
    for c in copies:
        c.start()
    for c in copies:
        c.wait()
    named = jnp.concatenate([own_owner[...], own_block[...], jnp.zeros((6, 256), jnp.int32)], axis=0).astype(F32)
    own_lists[...] = named
    for x in range(nx):
        send_y(pay_a, pay_b, 7 * x, c_first[x], c_last[x])
        send_y(pay_a, pay_b, 7 * x + 4, l_first[x, 0:3, :].astype(F32), l_last[x, 1:4, :].astype(F32))


def own_kernel(conc, label, phi, named, mid, coarse, pay_a, pay_b, lists, gain, base, pairs, pairs_2):
    nx = conc.shape[0]
    half = nx // 2
    lists[...] = named[0:2, :]

    def coefficients(i):
        gain[i] = pick(label[i], RATIO_TABLE)
        base[i] = conc[i] * pick(label[i], INVERSE_TABLE)

    loop(0, nx, coefficients, 4)

    def coarsen(i):
        total = conc[2 * i] * pick(label[2 * i], CONDUCT_TABLE) + conc[2 * i + 1] * pick(label[2 * i + 1], CONDUCT_TABLE)
        mid[i] = 0.25 * pair_rows(total, pairs.at[i])

    loop(0, half, coarsen, 4)
    for i in range(half // 2):
        coarse[i] = 0.25 * pair_rows(mid[2 * i] + mid[2 * i + 1], pairs_2.at[i])
    for k in range(HALO):
        for t in range(4):
            rows = slice(8 * t, 8 * t + 8)
            send_x(pay_a, pay_b, 4 * k + t, phi[k, rows, :], phi[nx - HALO + k, rows, :])
        for t in range(2):
            rows = slice(8 * t, 8 * t + 8)
            send_x(pay_a, pay_b, 16 + 2 * k + t, mid[k, rows, :], mid[half - HALO + k, rows, :])


def first_pack_x_kernel(conc, label, r_a, r_b, token, pay_a, pay_b):
    nx = conc.shape[0]

    def plane(ref, k, t, offset, count):
        if t < 4:
            return ref[k, 8 * t : 8 * t + 8, :].astype(F32)
        return halo_tile(*y_sides(r_a, r_b, 7 * k + offset, count))

    for t in range(5):
        for k in range(HALO):
            send_x(pay_a, pay_b, 5 * k + t, plane(conc, k, t, 0, 4), plane(conc, nx - HALO + k, t, 0, 4))
        for k in range(3):
            send_x(pay_a, pay_b, 20 + 5 * k + t, plane(label, k, t, 4, 3), plane(label, nx - 3 + k, t, 4, 3))


def corner_rows(n, reach):
    counts = [min(HALO, k + reach) for k in range(HALO)]
    counts = counts + [HALO] * n + counts[::-1]
    return counts, [sum(counts[:i]) for i in range(len(counts))]


def second_rows(nx):
    phi, mid = (sum(corner_rows(n, reach)[0]) for n, reach in ((nx, 0), (nx // 2, 1)))
    return phi, phi + mid, phi + mid + 64


def second_pack_kernel(phi, mid, coarse, lists, x_a, x_b, pay_a, pay_b):
    nx = phi.shape[0]
    starts = second_rows(nx)

    def put(own, n, reach, index, base):
        counts, at = corner_rows(n, reach)
        tiles = own.shape[1] // 8
        for x in range(n):
            send_y(pay_a, pay_b, base + at[HALO + x], own[x, 0:4, :], own[x, 8 * tiles - 4 : 8 * tiles, :])
        for k in range(HALO):
            first_after, first_before = x_sides(x_a, x_b, index + tiles * k)
            last_after, last_before = x_sides(x_a, x_b, index + tiles * k + tiles - 1)
            for x, first, last in ((k, first_before, last_before), (HALO + n + k, first_after, last_after)):
                if counts[x]:
                    send_y(pay_a, pay_b, base + at[x], first[0 : counts[x]], last[8 - counts[x] : 8])

    put(phi, nx, 0, 0, 0)
    put(mid, nx // 2, 1, 16, starts[0])
    base = starts[1]
    for x in range(8):
        pay_a[base + 8 * x : base + 8 * x + 8, :] = coarse[x]
        pay_b[base + 8 * x : base + 8 * x + 8, :] = coarse[x]
    base = starts[2]
    pay_b[base : base + lists.shape[0], :] = lists[...]


def second_halo(r_a, r_b, n, reach, x, base):
    counts, at = corner_rows(n, reach)
    if not counts[x]:
        return jnp.zeros((8, 256), F32)
    return halo_tile(*y_sides(r_a, r_b, base + at[x], counts[x]))


def wide_rows(own, after_own, before_own, after, before):
    gap = jnp.zeros((6, 256), F32)
    return jnp.concatenate([own, after_own, after, gap, before, before_own], axis=0)


def flux_plane(c, solid, phi, label):
    drive = 0.5 * (solid - phi)
    logc = jnp.log(c)
    return pick(label, KINETIC_TABLE) * (jnp.exp(drive + 0.4 * logc) - jnp.exp(0.6 * logc - drive))


def around_plane(before, v, after):
    return (before + after) + (along_y(v) + along_z(v))


def sweeps_inner_kernel(
    conc, label, phi, solid, gain, base, y_a, y_b, zero, first, second, third, gain_far, base_far, out, flux
):
    nx = conc.shape[0]

    def own(i):
        zero[i, 0:32, :] = conc[i]

    loop(0, nx, own)
    for i in range(nx):
        c = halo_tile(*y_sides(y_a, y_b, 7 * i, 4))
        lab = halo_tile(*y_sides(y_a, y_b, 7 * i + 4, 3))
        zero[i, 32:40, :] = c
        gain_far[i] = jnp.where(c > 0.0, pick(lab, RATIO_TABLE), 0.0)
        base_far[i] = c * pick(lab, INVERSE_TABLE)
    fields = (zero, first, second, third)
    for s in range(1, SWEEPS):
        old, new = fields[s - 1], fields[s]

        def sweep(i, old=old, new=new):
            g = jnp.concatenate([gain[i], gain_far[i]], axis=0)
            b = jnp.concatenate([base[i], base_far[i]], axis=0)
            new[i] = b + g * around_plane(old[i - 1], old[i], old[i + 1])

        loop(s, nx - s, sweep)

    def last(i):
        c = base[i] + gain[i] * around_plane(third[i - 1], third[i], third[i + 1])[0:32, :]
        out[i] = c
        flux[i] = flux_plane(c, solid[i], phi[i], label[i])

    loop(SWEEPS, nx - SWEEPS, last, 4)


def sweeps_edge_kernel(
    x_a, x_b, label, phi, solid, gain, base, zero, first, second, third, gain_far, base_far, out_inner, flux_inner,
    out, flux, pay_a, pay_b, zero_x, first_x, second_x, third_x,
):
    nx = out.shape[0]
    inner = (zero, first, second, third)
    edge = (zero_x, first_x, second_x, third_x)

    def copy(i):
        out[i] = out_inner[i]
        flux[i] = flux_inner[i]

    loop(SWEEPS, nx - SWEEPS, copy)
    for side in range(2):
        plane = lambda k, side=side: k if side == 0 else nx - 1 - k
        row = lambda k, side=side: 8 * side + HALO + k
        far = lambda k, index, side=side: x_sides(x_a, x_b, index)[1 - side]
        gains, bases = {}, {}
        for j in range(1, HALO + 1):
            k = HALO - j if side == 0 else j - 1
            zero_x[row(-j)] = jnp.concatenate([far(k, 5 * k + t) for t in range(5)], axis=0)
            if j < HALO:
                k = HALO - 1 - j if side == 0 else j - 1
                lab = jnp.concatenate([far(k, 20 + 5 * k + t) for t in range(5)], axis=0)
                c = zero_x[row(-j)]
                gains[-j] = jnp.where(c > 0.0, pick(lab, RATIO_TABLE), 0.0)
                bases[-j] = c * pick(lab, INVERSE_TABLE)
        for k in range(SWEEPS):
            gains[k] = jnp.concatenate([gain[plane(k)], gain_far[plane(k)]], axis=0)
            bases[k] = jnp.concatenate([base[plane(k)], base_far[plane(k)]], axis=0)
        for s in range(1, SWEEPS + 1):

            def old(k, s=s):
                return inner[s - 1][plane(k)] if k >= s - 1 else edge[s - 1][row(k)]

            for k in range(s - SWEEPS, s):
                c = bases[k] + gains[k] * around_plane(old(k - 1), old(k), old(k + 1))
                if s < SWEEPS:
                    edge[s][row(k)] = c
                else:
                    c = c[0:32, :]
                    out[plane(k)] = c
                    flux[plane(k)] = flux_plane(c, solid[plane(k)], phi[plane(k)], label[plane(k)])
    for x in range(nx):
        send_y(pay_a, pay_b, 3 * x, flux[x, 0:3, :], flux[x, 29:32, :])


def mask_kernel(flux_all, lists, far, flux, halo_mask, marked):
    nx = flux_all.shape[0]
    rows = lists.shape[0]
    pieces = [lists[i : i + 1, :] for i in range(rows)] + [far[i : i + 1, :] for i in range(far.shape[0] - rows, far.shape[0])]
    owner = jnp.concatenate(pieces[0::2], axis=1).astype(jnp.int32)
    block = jnp.concatenate(pieces[1::2], axis=1).astype(jnp.int32)
    entries = owner.shape[1]
    hit_column = (iota((LANES, entries), 0) == lax.rem(block, 64)).astype(jnp.bfloat16)
    at_row = lax.shift_right_arithmetic(block, 6)
    here = lax.axis_index("dev")
    for j in range(3):
        mine = jnp.where(owner == here + j - 1, at_row, -1)
        hit_row = (iota((nx, entries), 0) == mine).astype(jnp.bfloat16)
        named = lax.dot_general(hit_row, hit_column, (((1,), (1,)), ((), ())), preferred_element_type=F32)
        for i in range(nx):
            marked[j, i] = jnp.broadcast_to(named[i : i + 1, :], (8, LANES))
    is_row = lax.div(iota((32, LANES), 1), 2) == iota((32, LANES), 0)
    row, pair = iota((8, LANES), 0), lax.div(iota((8, LANES), 1), 2)
    is_after = (row < 3) & (pair == row)
    is_before = (row >= 5) & (pair == row + 24)
    spread = (lax.rem(iota((LANES, 256), 0), 2) == lax.div(iota((LANES, 256), 1), LANES)).astype(jnp.bfloat16)

    def plane(i):
        marks = jnp.where(is_row, jnp.concatenate([marked[1, i]] * 4, axis=0), 0.0)
        beyond = jnp.where(is_after, marked[2, i], jnp.where(is_before, marked[0, i], 0.0))
        marks = jnp.concatenate([marks, beyond], axis=0).astype(jnp.bfloat16)
        listed = jnp.dot(marks, spread, preferred_element_type=F32) > 0.5
        flux[i] = jnp.where(listed[0:32], flux_all[i], 0.0)
        halo_mask[i] = jnp.where(listed[32:40], 1.0, 0.0)

    loop(0, nx, plane, 4)


def store_kernel(conc, flux, conc_out, flux_out, token, sems):
    copies = []
    for i, (ref, to) in enumerate(((conc, conc_out), (flux, flux_out))):
        for j in range(4):
            rows = pl.ds(8 * j, 8)
            copies.append(pltpu.make_async_copy(ref.at[rows], to.at[rows], sems.at[4 * i + j]))
            copies[-1].start()
    token[...] = jnp.zeros(token.shape, F32)
    for c in copies:
        c.wait()


def ready_kernel(conc, label, phi, y_a, y_b, x_a, x_b, yy_a, yy_b, xx_a, xx_b, weight, scale, field, token):
    nx = conc.shape[0]
    token[...] = jnp.zeros(token.shape, F32)

    def put(x, rows, c, lab, p):
        conduct = c * pick(lab, CONDUCT_TABLE)
        factor = OMEGA / (MASS + 6.0 * conduct)
        weight[x, rows, :] = conduct * factor
        scale[x, rows, :] = factor
        field[x, rows, :] = p

    def own(i):
        put(HALO + i, slice(0, 32), conc[i], label[i], phi[i])

    loop(0, nx, own, 4)
    low = slice(32, 40)
    for i in range(nx):
        c = halo_tile(*y_sides(y_a, y_b, 7 * i, 4))
        lab = halo_tile(*y_sides(y_a, y_b, 7 * i + 4, 3))
        put(HALO + i, low, c, lab, second_halo(yy_a, yy_b, nx, 0, HALO + i, 0))
    for t in range(5):
        rows = slice(8 * t, 8 * t + 8)
        for k in range(HALO):
            c_after, c_before = x_sides(x_a, x_b, 5 * k + t)
            l_after = x_sides(x_a, x_b, 20 + 5 * min(k, 2) + t)[0]
            l_before = x_sides(x_a, x_b, 20 + 5 * max(k - 1, 0) + t)[1]
            if t < 4:
                p_after, p_before = x_sides(xx_a, xx_b, 4 * k + t)
            else:
                p_after = second_halo(yy_a, yy_b, nx, 0, HALO + nx + k, 0)
                p_before = second_halo(yy_a, yy_b, nx, 0, k, 0)
            put(k, rows, c_before, l_before, p_before)
            put(HALO + nx + k, rows, c_after, l_after, p_after)


def flux_pack_x_kernel(flux, r_a, r_b, mask, token, pay_a, pay_b):
    nx = flux.shape[0]

    def tile(x, t):
        if t < 4:
            return flux[x, 8 * t : 8 * t + 8, :]
        return mask[x] * halo_tile(*y_sides(r_a, r_b, 3 * x, 3))

    for k in range(3):
        for t in range(5):
            send_x(pay_a, pay_b, 5 * k + t, tile(k, t), tile(nx - 3 + k, t))


def first_sweep(field, weight, scale, x, rows, flux):
    p = field[x]
    near = (field[x - 1] + field[x + 1]) + (along_y(p) + along_z(p))
    b = scale[x, rows, :] * (MASS * p[rows, :] + flux)
    return b, 0.2 * p[rows, :] + weight[x, rows, :] * near[rows, :] + b


def potential_inner_kernel(flux, mask, y_a, y_b, weight, scale, field, after_two, source, first, source_mid, far, pairs):
    nx = flux.shape[0]
    for i in range(nx):
        far[i] = mask[i] * halo_tile(*y_sides(y_a, y_b, 3 * i, 3))

    def own(i):
        x = HALO + i
        f = jnp.concatenate([flux[i], far[i]], axis=0)
        source[x], first[x] = first_sweep(field, weight, scale, x, slice(0, 40), f)

    loop(0, nx, own)

    def around(values, x):
        v = values[x]
        return v, weight[x] * ((values[x - 1] + values[x + 1]) + (along_y(v) + along_z(v)))

    def sweep(x):
        v, near = around(first, x)
        after_two[x] = 0.2 * v + (source[x] + near)

    loop(HALO + 1, HALO + nx - 1, sweep)

    def remainder(x):
        v, near = around(after_two, x)
        return ((source[x] - OMEGA * v) + near)[0:32, :] / scale[x, 0:32, :]

    def coarsen(i):
        x = HALO + 2 * i
        source_mid[i] = 0.25 * pair_rows(remainder(x) + remainder(x + 1), pairs.at[i])

    loop(1, nx // 2 - 1, coarsen, 4)


def potential_edge_kernel(
    x_a, x_b, weight, scale, field, inner_two, inner_source, inner_first, inner_mid,
    edge_two, edge_source, source_mid, pay_a, pay_b, first, pairs,
):
    half = source_mid.shape[0]
    nx = 2 * half
    for side, face in ((0, HALO), (1, HALO + nx)):
        base = 8 * side + HALO - face
        for k in range(3):
            x = face - 3 + k if side == 0 else face + k
            f = jnp.concatenate([x_sides(x_a, x_b, 5 * k + t)[1 - side] for t in range(5)], axis=0)
            edge_source[base + x], first[base + x] = first_sweep(field, weight, scale, x, slice(0, 40), f)

        def first_of(x, base=base):
            return inner_first[x] if HALO <= x < HALO + nx else first[base + x]

        def source_of(x, base=base):
            return inner_source[x] if HALO <= x < HALO + nx else edge_source[base + x]

        def two_of(x, base=base):
            return inner_two[x] if HALO < x < HALO + nx - 1 else edge_two[base + x]

        for x in range(face - 2, face + 1) if side == 0 else range(face - 1, face + 2):
            v = first_of(x)
            near = weight[x] * ((first_of(x - 1) + first_of(x + 1)) + (along_y(v) + along_z(v)))
            edge_two[base + x] = 0.2 * v + (source_of(x) + near)
        total = 0.0
        at = face if side == 0 else face - 2
        for x in (at, at + 1):
            v = two_of(x)
            near = weight[x] * ((two_of(x - 1) + two_of(x + 1)) + (along_y(v) + along_z(v)))
            total = total + ((source_of(x) - OMEGA * v) + near)[0:32, :] / scale[x, 0:32, :]
        source_mid[0 if side == 0 else half - 1] = 0.25 * pair_rows(total, pairs.at[side])
    for x in range(1, half - 1):
        source_mid[x] = inner_mid[x]
    for x in range(half):
        send_y(pay_a, pay_b, 4 * x, source_mid[x, 0:4, :], source_mid[x, 12:16, :])


def mid_pack_x_kernel(field, r_a, r_b, token, token_2, pay_a, pay_b):
    n = field.shape[0]

    def tile(x, t):
        if t < 2:
            return field[x, 8 * t : 8 * t + 8, :]
        return halo_tile(*y_sides(r_a, r_b, 4 * x, 4))

    for k in range(HALO):
        for t in range(3):
            send_x(pay_a, pay_b, 3 * k + t, tile(k, t), tile(n - HALO + k, t))


def mid_kernel(
    source_own, conduct_own, yy_a, yy_b, xx_a, xx_b, y_a, y_b, x_a, x_b, rho, load,
    after_two, source, weight, coarse, conduct, pay_a, pay_b, part, scale, mid_conduct, pairs, pairs_2,
):
    n = source_own.shape[0]
    base = second_rows(2 * n)[0]

    def put(x, rows, b, k):
        factor = OMEGA / (MASS + 3.0 * k)
        weight[x, rows, :] = k * factor
        scale[x, rows, :] = factor
        source[x, rows, :] = factor * b
        mid_conduct[x, rows, :] = k

    def far(x):
        return second_halo(yy_a, yy_b, n, 1, x, base)

    for i in range(n):
        put(HALO + i, slice(0, 16), source_own[i], conduct_own[i])
        put(HALO + i, slice(16, 24), halo_tile(*y_sides(y_a, y_b, 4 * i, 4)), far(HALO + i))
    for k in range(HALO):
        for t in range(3):
            rows = slice(8 * t, 8 * t + 8)
            b_after, b_before = x_sides(x_a, x_b, 3 * k + t)
            if t < 2:
                c_after, c_before = x_sides(xx_a, xx_b, 16 + 2 * k + t)
            else:
                c_after, c_before = far(HALO + n + k), far(k)
            put(k, rows, b_before, c_before)
            put(HALO + n + k, rows, b_after, c_after)

    def around(values, x):
        v = values[x]
        return v, weight[x] * (0.25 * ((values[x - 1] + values[x + 1]) + along_y(v)) + along_z(v))

    def sweep(x):
        v, near = around(source, x)
        after_two[x] = 0.2 * v + (source[x] + near)

    loop(1, n + 2 * HALO - 1, sweep, 11)

    def remainder(x):
        v, near = around(after_two, x)
        return ((source[x] - OMEGA * v) + near) / scale[x]

    total = jnp.zeros((8, 256), F32)
    for i in range(n // 2):
        x = HALO + 2 * i
        value = 0.25 * pair_rows(remainder(x) + remainder(x + 1), pairs.at[i])
        k = 0.25 * pair_rows(mid_conduct[x] + mid_conduct[x + 1], pairs_2.at[i])
        coarse[i] = value
        conduct[i] = k
        send_y(pay_a, pay_b, 9 * i, value[1:9], jnp.concatenate([value[11:12], value[0:7]], axis=0))
        send_y(pay_a, pay_b, 9 * i + 8, k[8:9], k[11:12])
        total += rho[i] * value[0:8]
    sums = jnp.concatenate([total[:, :LANES] + total[:, LANES:], load[...]], axis=1)
    pay_b[72:80, :] = sums
    part[...] = sums


COARSE_W = 0.0625


def coarse_ready_kernel(own, r_a, r_b, rho, load, token, one, two, conduct, scale):
    token[...] = jnp.zeros(token.shape, F32)
    base = r_a.shape[0] - 64
    for x in range(8):
        after, before = y_sides(r_a, r_b, base + 8 * x, 8)
        k = jnp.concatenate([own[x], after, jnp.zeros((8, 256), F32), before], axis=0)
        conduct[x] = k
        scale[x] = OMEGA / (MASS + 2.25 * k)
        one[x] = jnp.ones(k.shape, F32)
    fields = (one, two)
    for s in range(COARSE_SWEEPS):
        old, new = fields[s % 2], fields[(s + 1) % 2]
        for x in range(8):
            near = [conduct[i] * old[i] if 0 <= i < 8 else None for i in (x - 1, x, x + 1)]
            inner = along_y(near[1])
            for other in (near[0], near[2]):
                if other is not None:
                    inner = inner + other
            new[x] = 0.2 * old[x] + scale[x] * (COARSE_W * inner + along_z(near[1]))
    last = fields[COARSE_SWEEPS % 2]
    peer, peers = lax.axis_index("dev"), lax.axis_size("dev")
    row, z = iota((8, 256), 0), iota((8, 256), 1)
    edge_y = ((row == 0) & (peer == 0)) | ((row == 7) & (peer == peers - 1))
    edge = edge_y.astype(F32) * COARSE_W + ((z == 0) | (z == 255)).astype(F32)
    total = jnp.zeros((8, 256), F32)
    for x in range(8):
        rho[x] = last[x, 0:8, :]
        total += MASS + own[x] * (edge + (COARSE_W if x in (0, 7) else 0.0))
    load[...] = total[:, :LANES] + total[:, LANES:]


def coarse_kernel(own, conduct, far_a, far_b, r_a, r_b, error, source, weight, one, two):
    base = far_a.shape[0] - 64
    for x in range(8):
        after, before = y_sides(r_a, r_b, 9 * x, 8)
        b = wide_rows(own[x, 0:8, :], own[x, 8:9, :], own[x, 11:12, :], after, before)
        last_after, last_before = y_sides(r_a, r_b, 9 * x + 8, 1)
        after, before = y_sides(far_a, far_b, base + 8 * x, 8)
        after = jnp.concatenate([after[1:8], last_after], axis=0)
        before = jnp.concatenate([last_before, before[0:7]], axis=0)
        k = wide_rows(conduct[x, 0:8, :], conduct[x, 8:9, :], conduct[x, 11:12, :], after, before)
        factor = OMEGA / (MASS + 2.25 * k)
        weight[x] = k * factor
        source[x] = factor * b
    old = source
    for s in range(1, COARSE_SWEEPS):
        new = one if s % 2 else two
        for x in range(8):
            v = old[x]
            inner = along_y(v)
            if x > 0:
                inner = inner + old[x - 1]
            if x < 7:
                inner = inner + old[x + 1]
            new[x] = 0.2 * v + (source[x] + weight[x] * (COARSE_W * inner + along_z(v)))
        old = new
    for x in range(8):
        error[x, 0:8, :] = old[x, 0:8, :]
        error[x, 8:16, :] = jnp.where(upper(), old[x, 8:16, :], old[x, 24:32, :])


def shift_kernel(error, *rest):
    terms, (out, pay_a, pay_b) = rest[:-3], rest[-3:]
    sums = sum(t[...] for t in terms)
    resid = jnp.sum(sums[:, :LANES])
    load = jnp.sum(sums[:, LANES:])
    shift_c = jnp.full((16, 256), resid, F32) / jnp.full((16, 256), load, F32)
    for x in range(8):
        out[x] = error[x] + shift_c
    for k in range(2):
        send_x(pay_a, pay_b, k, out[k], out[6 + k])


def squeeze(tile):
    return jnp.where(iota((8, 256), 0) < 2, tile, pltpu.roll(tile, 4, 0))


def spread_coarse(plane, room):
    return jnp.concatenate([twice(plane[0:8], room.at[0]), twice(squeeze(plane[8:16]), room.at[1])[0:8]], axis=0)


def spread_mid(plane, room):
    parts = [twice(plane[0:8], room.at[0]), twice(plane[8:16], room.at[1]), twice(squeeze(plane[16:24]), room.at[2])[0:8]]
    return jnp.concatenate(parts, axis=0)


def smoothed(before, v, after, weight, source, w):
    inner = (before + after) + along_y(v)
    return source + (0.2 * v + weight * (w * inner + along_z(v)))


def finish_inner_kernel(
    error, mid_two, mid_source, mid_weight, fine_two, fine_source, fine_weight,
    out, zero, one, fine_one, fine_last, two, dup, dup_2, result, sems,
):
    n = mid_two.shape[0]
    nf = fine_two.shape[0]
    for c in range(8):
        spread = spread_coarse(error[c], dup.at[c])
        for x in (2 * c + HALO, 2 * c + 1 + HALO):
            zero[x] = jnp.where(mid_weight[x] > 0.0, mid_two[x] + spread, 0.0)

    def sweep_mid(x, old, new):
        new[x] = smoothed(old[x - 1], old[x], old[x + 1], mid_weight[x], mid_source[x], 0.25)

    for x in range(HALO + 1, n - HALO - 1):
        sweep_mid(x, zero, one)
    for x in range(HALO + 2, n - HALO - 2):
        sweep_mid(x, one, two)

    def lift(m):
        spread = spread_mid(two[m], dup_2.at[m])
        x = 2 * m - HALO
        fine_one[x] = fine_two[x] + spread
        fine_one[x + 1] = fine_two[x + 1] + spread

    loop(HALO + 2, n - HALO - 2, lift, 6)

    def sweep_one(x):
        fine_last[x] = smoothed(fine_one[x - 1], fine_one[x], fine_one[x + 1], fine_weight[x], fine_source[x], 1.0)

    low, high = 2 * HALO + 1, nf - 2 * HALO - 1
    loop(low, high, sweep_one, 11)
    copies = []
    low, high = low + 1, high - 1
    for j in range(2):
        mid = low + (high - low) // 2
        for x in range(low, mid) if j == 0 else range(mid, high):
            v = smoothed(fine_last[x - 1], fine_last[x], fine_last[x + 1], fine_weight[x], fine_source[x], 1.0)
            result[x - HALO] = v[0:32, :]
        rows = pl.ds(low - HALO, mid - low) if j == 0 else pl.ds(mid - HALO, high - mid)
        copies.append(pltpu.make_async_copy(result.at[rows], out.at[rows], sems.at[j]))
        copies[-1].start()
    for c in copies:
        c.wait()


def finish_edge_kernel(
    x_a, x_b, mid_two, mid_source, mid_weight, fine_two, edge_two, fine_source, edge_source, fine_weight,
    zero, one, fine_one, fine_last, begun, out, zero_edge, one_edge, fine_edge, last_edge, dup, dup_2, result, sems,
):
    n = mid_two.shape[0]
    nf = fine_two.shape[0]
    nx = nf - 2 * HALO
    copies = []
    planes = x_sides(x_a, x_b, slice(0, 2))
    for side in (0, 1):
        sign = 1 if side == 0 else -1
        at = lambda k, side=side: HALO + k if side == 0 else n - HALO - 1 - k
        fine = lambda k, side=side: HALO + k if side == 0 else nf - HALO - 1 - k
        base = 8 * side + (0 if side == 0 else HALO - HALO - nx)
        for c in range(2):
            plane = planes[1 - side][c]
            spread = spread_coarse(plane, dup.at[2 * side + c])
            first = 2 * c if side == 0 else n - HALO + 2 * c
            for x in (first, first + 1):
                zero_edge[x] = jnp.where(mid_weight[x] > 0.0, mid_two[x] + spread, 0.0)

        def zero_of(k):
            return zero[at(k)] if k >= 0 else zero_edge[at(k)]

        def one_of(k):
            return one[at(k)] if k >= 1 else one_edge[at(k)]

        for k in range(-2, 1):
            x = at(k)
            one_edge[x] = smoothed(zero_of(k - 1), zero_of(k), zero_of(k + 1), mid_weight[x], mid_source[x], 0.25)
        for k in range(-1, 2):
            x = at(k)
            value = smoothed(one_of(k - 1), one_of(k), one_of(k + 1), mid_weight[x], mid_source[x], 0.25)
            spread = spread_mid(value, dup_2.at[3 * side + k + 1])
            for f in (fine(2 * k), fine(2 * k + 1)):
                inside = HALO < f < nf - HALO - 1
                before = fine_two[f] if inside else edge_two[base + f]
                fine_edge[f] = before + spread

        def fine_of(k):
            return fine_one[fine(k)] if k >= 4 else fine_edge[fine(k)]

        def last_of(k):
            return fine_last[fine(k)] if k >= 5 else last_edge[fine(k)]

        for k in range(-1, 5):
            f = fine(k)
            source = fine_source[f] if HALO <= f < nf - HALO else edge_source[base + f]
            last_edge[f] = smoothed(fine_of(k - 1), fine_of(k), fine_of(k + 1), fine_weight[f], source, 1.0)
        for k in range(6):
            f = fine(k)
            v = smoothed(last_of(k - 1), last_of(k), last_of(k + 1), fine_weight[f], fine_source[f], 1.0)
            result[f - HALO] = v[0:32, :]
        rows = pl.ds(0, 6) if side == 0 else pl.ds(nx - 6, 6)
        copies.append(pltpu.make_async_copy(result.at[rows], out.at[rows], sems.at[side]))
        copies[-1].start()
    for c in copies:
        c.wait()


def both_ways(pairs):
    return pairs + [(j, i) for i, j in pairs]


def swap(pay_a, pay_b, axis):
    size = lax.axis_size(axis)
    pairs_a = [(i, i + 1) for i in range(1, size - 1, 2)]
    pairs_b = [(i, i + 1) for i in range(0, size - 1, 2)]
    return lax.ppermute(pay_a, axis, both_ways(pairs_a)), lax.ppermute(pay_b, axis, both_ways(pairs_b))


def exchange(value, distance):
    return lax.ppermute(value, "dev", [(i, i ^ distance) for i in range(lax.axis_size("dev"))])


def body(conc_old, phi_old, solid_pot, phase_label, iface_block, iface_owner):
    peers = lax.axis_size("dev")
    nx = conc_old.shape[0]
    half = nx // 2
    quarter = nx // 4
    ext = (nx + 2 * HALO, nx + 2 * HALO, 256)
    ext_mid = (half + 2 * HALO, half + 2 * HALO, 256)
    token_shape = shaped(8, LANES)

    pay_a, pay_b, own_lists = call(
        first_pack_kernel,
        [shaped(7 * nx, 256)] * 2 + [shaped(8, 256)],
        [conc_old, phase_label, iface_owner.reshape(1, -1), iface_block],
        [vmem(nx, HALO, 256)] * 2
        + [pltpu.VMEM((nx, HALO, 256), jnp.int32)] * 2
        + [pltpu.VMEM((1, 256), jnp.int32)] * 2
        + [pltpu.SemaphoreType.DMA((6,))],
        in_specs=[FAR] * 4,
        limit=VMEM_MOST,
        name="first_pack",
    )
    y_a, y_b = swap(pay_a, pay_b, "dev")
    conduct_mid, conduct_coarse, pay_a, pay_b, lists, gain, base = call(
        own_kernel,
        [shaped(half, half, 256), shaped(quarter, quarter, 256), shaped(24, 8, 256), shaped(24, 8, 256)]
        + [shaped(2, 256), shaped(nx, nx, 256), shaped(nx, nx, 256)],
        [conc_old, phase_label, phi_old, own_lists],
        [vmem(half, 2, nx, LANES), vmem(quarter, 2, half, LANES)],
        name="own",
    )
    xx_a, xx_b = swap(pay_a, pay_b, "grp")
    distance = peers // 2
    while distance > 1:
        lists = jnp.concatenate([lists, exchange(lists, distance)], axis=0)
        distance //= 2
    far_rows = second_rows(nx)[2]
    far_pay = call(
        second_pack_kernel,
        [shaped(far_rows, 256), shaped(far_rows + peers, 256)],
        [phi_old, conduct_mid, conduct_coarse, lists, xx_a, xx_b],
        name="second_pack",
    )
    yy_a, yy_b = swap(*far_pay, "dev")
    pay_a, pay_b = call(
        first_pack_x_kernel,
        [shaped(35, 8, 256)] * 2,
        [conc_old, phase_label, y_a, y_b, conduct_coarse],
        name="first_pack_x",
    )
    x_a, x_b = swap(pay_a, pay_b, "grp")

    ext_y = (nx, nx + 2 * HALO, 256)
    zero, first, second, third, gain_far, base_far, conc_inner, flux_inner = call(
        sweeps_inner_kernel,
        [shaped(*ext_y)] * 4 + [shaped(nx, 8, 256)] * 2 + [shaped(nx, nx, 256)] * 2,
        [conc_old, phase_label, phi_old, solid_pot, gain, base, y_a, y_b],
        name="sweeps_inner",
    )
    edge_args = [x_a, x_b, phase_label, phi_old, solid_pot, gain, base, zero, first, second, third]
    conc_new, flux_all, pay_a, pay_b = call(
        sweeps_edge_kernel,
        [shaped(nx, nx, 256), shaped(nx, nx, 256), shaped(3 * nx, 256), shaped(3 * nx, 256)],
        edge_args + [gain_far, base_far, conc_inner, flux_inner],
        [vmem(16, nx + 2 * HALO, 256)] * 4,
        name="sweeps_edge",
    )
    f_a, f_b = swap(pay_a, pay_b, "dev")
    flux_own, halo_mask = call(
        mask_kernel,
        [shaped(nx, nx, 256), shaped(nx, 8, 256)],
        [flux_all, lists, yy_b],
        [vmem(3, nx, 8, LANES)],
        name="mask",
    )
    weight, scale, field, made = call(
        ready_kernel,
        [shaped(*ext)] * 3 + [token_shape],
        [conc_old, phase_label, phi_old, y_a, y_b, x_a, x_b, yy_a, yy_b, xx_a, xx_b],
        name="ready",
    )
    pay_a, pay_b = call(
        flux_pack_x_kernel, [shaped(15, 8, 256)] * 2, [flux_own, f_a, f_b, halo_mask, made], name="flux_pack_x"
    )
    fx_a, fx_b = swap(pay_a, pay_b, "grp")
    fine_two, fine_source, fine_first, inner_mid = call(
        potential_inner_kernel,
        [shaped(*ext)] * 3 + [shaped(half, half, 256)],
        [flux_own, halo_mask, f_a, f_b, weight, scale, field],
        [vmem(nx, 8, 256), vmem(half, 2, nx, LANES)],
        name="potential_inner",
    )
    edge = (16, nx + 2 * HALO, 256)
    edge_two, edge_source, source_mid, pay_a, pay_b = call(
        potential_edge_kernel,
        [shaped(*edge), shaped(*edge), shaped(half, half, 256), shaped(4 * half, 256), shaped(4 * half, 256)],
        [fx_a, fx_b, weight, scale, field, fine_two, fine_source, fine_first, inner_mid],
        [vmem(*edge), vmem(2, 2, nx, LANES)],
        name="potential_edge",
    )
    m_a, m_b = swap(pay_a, pay_b, "dev")
    concentration, flux, stored = call(
        store_kernel,
        [shaped(nx, nx, 256), shaped(nx, nx, 256), token_shape],
        [conc_new, flux_own],
        [pltpu.SemaphoreType.DMA((8,))],
        out_specs=[FAR, FAR, WHOLE],
        name="store",
    )
    wide = (quarter, 32, 256)
    rho, load, made = call(
        coarse_ready_kernel,
        [shaped(quarter, quarter, 256), shaped(8, LANES), token_shape],
        [conduct_coarse, yy_a, yy_b],
        [vmem(*wide)] * 4,
        name="coarse_ready",
    )
    pay_a, pay_b = call(
        mid_pack_x_kernel, [shaped(3 * HALO, 8, 256)] * 2, [source_mid, m_a, m_b, made, stored], name="mid_pack_x"
    )
    mx_a, mx_b = swap(pay_a, pay_b, "grp")
    mid_two, mid_source, mid_weight, source_coarse, wide_coarse, pay_a, pay_b, sums = call(
        mid_kernel,
        [shaped(*ext_mid)] * 3
        + [shaped(quarter, 12, 256), shaped(quarter, 12, 256), shaped(72, 256), shaped(80, 256), shaped(8, 256)],
        [source_mid, conduct_mid, yy_a, yy_b, xx_a, xx_b, m_a, m_b, mx_a, mx_b, rho, load],
        [vmem(*ext_mid)] * 2 + [vmem(8, 2, half + 2 * HALO, LANES)] * 2,
        name="middle",
    )
    c_a, c_b = swap(pay_a, pay_b, "dev")
    sums = sums + c_b[72:80]
    others = [exchange(sums, distance) for distance in range(2, peers, 2)]
    (error,) = call(
        coarse_kernel,
        [shaped(8, 16, 256)],
        [source_coarse, wide_coarse, yy_a, yy_b, c_a, c_b],
        [vmem(*wide)] * 4,
        name="coarse",
    )
    error, pay_a, pay_b = call(
        shift_kernel, [shaped(8, 16, 256), shaped(2, 16, 256), shaped(2, 16, 256)], [error, sums] + others, name="shift"
    )
    e_a, e_b = swap(pay_a, pay_b, "grp")
    begun, zero, one, fine_one, fine_last = call(
        finish_inner_kernel,
        [shaped(nx, nx, 256), shaped(*ext_mid), shaped(*ext_mid), shaped(*ext), shaped(*ext)],
        [error, mid_two, mid_source, mid_weight, fine_two, fine_source, weight],
        [vmem(*ext_mid), vmem(8, 2, 2, 16, LANES), vmem(half + 2 * HALO, 3, 2, 16, LANES), vmem(nx, nx, 256)]
        + [pltpu.SemaphoreType.DMA((2,))],
        out_specs=[FAR] + [WHOLE] * 4,
        name="finish_inner",
    )
    finish_args = [e_a, e_b, mid_two, mid_source, mid_weight, fine_two, edge_two, fine_source, edge_source, weight]
    finish_args += [zero, one, fine_one, fine_last, begun]
    (potential,) = call(
        finish_edge_kernel,
        [shaped(nx, nx, 256)],
        finish_args,
        [vmem(*ext_mid), vmem(*ext_mid), vmem(*ext), vmem(*ext)]
        + [vmem(4, 2, 2, 16, LANES), vmem(6, 3, 2, 16, LANES), vmem(nx, nx, 256)]
        + [pltpu.SemaphoreType.DMA((2,))],
        in_specs=[WHOLE] * (len(finish_args) - 1) + [FAR],
        out_specs=[FAR],
        aliases={len(finish_args) - 1: 0},
        name="finish_edge",
    )
    return (concentration, flux, potential)


def solution(mesh):
    brick = P("grp", "dev", None)
    return jax.shard_map(
        body,
        mesh=mesh,
        in_specs=(brick, brick, brick, brick, P("grp", "dev"), brick),
        out_specs=(brick, brick, brick),
        check_vma=False,
    )
```

```python
import jax
import jax.numpy as jnp
from jax import lax
from jax.experimental import pallas as pl
from jax.experimental.pallas import tpu as pltpu
from jax.sharding import PartitionSpec as P


F32 = jnp.float32
MASS = 0.05
OMEGA = 0.8
DIFFUSION_TABLE = (1.5, 0.1, 0.4)
RATIO_TABLE = tuple(d / (1.0 + 6.0 * d) for d in DIFFUSION_TABLE)
INVERSE_TABLE = tuple(1.0 / (1.0 + 6.0 * d) for d in DIFFUSION_TABLE)
CONDUCT_TABLE = (1.0, 0.3, 0.6)
KINETIC_TABLE = (0.2, 1.0, 0.5)
SWEEPS = 4
COARSE_SWEEPS = 8
COARSE_NEAR = 8
HALO = 4
LANES = 128
VMEM_LIMIT = 28 * 1024 * 1024
VMEM_MOST = 58 * 1024 * 1024


def shaped(*shape):
    return jax.ShapeDtypeStruct(shape, F32)


WHOLE = pl.BlockSpec(memory_space=pltpu.VMEM)
FAR = pl.BlockSpec(memory_space=pltpu.HBM)


def call(kernel, outs, args, scratch=(), in_specs=None, out_specs=None, limit=VMEM_LIMIT, aliases=None, flops=10**6, name=None):
    size = sum(4 * a.size for a in args) + sum(4 * o.size for o in outs)
    return pl.pallas_call(
        kernel,
        out_shape=tuple(outs),
        in_specs=in_specs or [WHOLE] * len(args),
        out_specs=tuple(out_specs or [WHOLE] * len(outs)),
        scratch_shapes=list(scratch),
        input_output_aliases=aliases or {},
        compiler_params=pltpu.CompilerParams(vmem_limit_bytes=limit),
        cost_estimate=pl.CostEstimate(flops=flops, bytes_accessed=size, transcendentals=0),
        name=name,
    )(*args)


def vmem(*shape):
    return pltpu.VMEM(shape, F32)


def iota(shape, dim):
    return lax.broadcasted_iota(jnp.int32, shape, dim)


def pick(label, table):
    return jnp.where(label == 0, table[0], jnp.where(label == 1, table[1], table[2])).astype(F32)


def loop(low, high, body, unroll=8):
    steps = (high - low) // unroll

    def step(i, carry):
        for u in range(unroll):
            body(low + i * unroll + u)
        return carry

    if steps > 1:
        lax.fori_loop(0, steps, step, 0)
    else:
        steps = 0
    for x in range(low + steps * unroll, high):
        body(x)


def odd(axis):
    return lax.rem(lax.axis_index(axis), 2) == 1


def along_y(v):
    return pltpu.roll(v, 1, 0) + pltpu.roll(v, v.shape[0] - 1, 0)


def along_z(v):
    low, high = v[:, :LANES], v[:, LANES:]
    lane = iota(low.shape, 1)
    first, last = lane == 0, lane == LANES - 1
    low_up, high_up = pltpu.roll(low, 1, 1), pltpu.roll(high, 1, 1)
    low_down, high_down = pltpu.roll(low, LANES - 1, 1), pltpu.roll(high, LANES - 1, 1)
    low_sum = jnp.where(first, 0.0, low_up) + jnp.where(last, high_down, low_down)
    high_sum = jnp.where(first, low_up, high_up) + jnp.where(last, 0.0, high_down)
    return jnp.concatenate([low_sum, high_sum], axis=1)


def upper(shape=(8, 256)):
    return iota(shape, 0) < HALO


def twice(tile, scratch):
    for h in range(2):
        part = tile[:, h * LANES : (h + 1) * LANES]
        scratch[h, pl.ds(0, 8, stride=2), :] = part
        scratch[h, pl.ds(1, 8, stride=2), :] = part
    return jnp.concatenate([scratch[0], scratch[1]], axis=1)


def pair_rows(v, scratch):
    half = v.shape[0] // 2
    parts = []
    for h in range(2):
        scratch[h] = v[:, h * LANES : (h + 1) * LANES]
        parts.append(scratch[h, pl.ds(0, half, stride=2), :] + scratch[h, pl.ds(1, half, stride=2), :])
    return jnp.concatenate(parts, axis=1)


def either(flag, if_true, if_false):
    return jnp.where(flag, if_true, if_false)


def y_sides(r_a, r_b, at, count):
    flag = odd("dev")
    a, b = r_a[at : at + count, :], r_b[at : at + count, :]
    return either(flag, a, b), either(flag, b, a)


def x_sides(r_a, r_b, index):
    flag = odd("grp")
    a, b = r_a[index], r_b[index]
    return either(flag, a, b), either(flag, b, a)


def send_y(pay_a, pay_b, at, first, last):
    flag = odd("dev")
    n = first.shape[0]
    pay_a[at : at + n, :] = either(flag, last, first)
    pay_b[at : at + n, :] = either(flag, first, last)


def send_x(pay_a, pay_b, index, first, last):
    flag = odd("grp")
    pay_a[index] = either(flag, last, first)
    pay_b[index] = either(flag, first, last)


def halo_tile(after, before):
    parts = [after]
    if after.shape[0] < HALO:
        parts.append(jnp.zeros((2 * HALO - 2 * after.shape[0], after.shape[1]), F32))
    return jnp.concatenate(parts + [before], axis=0)


def first_pack_kernel(
    conc, label, owner, block, pay_a, pay_b, own_lists, c_first, c_last, l_first, l_last, own_owner, own_block, sems
):
    nx = conc.shape[0]
    copies = [pltpu.make_async_copy(owner, own_owner, sems.at[4]), pltpu.make_async_copy(block, own_block, sems.at[5])]
    for i, (ref, at, to) in enumerate(((conc, 0, c_first), (conc, 28, c_last), (label, 0, l_first), (label, 28, l_last))):
        copies.append(pltpu.make_async_copy(ref.at[:, pl.ds(at, 4), :], to, sems.at[i]))
    for c in copies:
        c.start()
    for c in copies:
        c.wait()
    named = jnp.concatenate([own_owner[...], own_block[...], jnp.zeros((6, 256), jnp.int32)], axis=0).astype(F32)
    own_lists[...] = named
    for x in range(nx):
        send_y(pay_a, pay_b, 7 * x, c_first[x], c_last[x])
        send_y(pay_a, pay_b, 7 * x + 4, l_first[x, 0:3, :].astype(F32), l_last[x, 1:4, :].astype(F32))


def own_kernel(conc, label, phi, named, mid, coarse, pay_a, pay_b, lists, gain, base, pairs, pairs_2):
    nx = conc.shape[0]
    half = nx // 2
    lists[...] = named[0:2, :]

    def coefficients(i):
        gain[i] = pick(label[i], RATIO_TABLE)
        base[i] = conc[i] * pick(label[i], INVERSE_TABLE)

    loop(0, nx, coefficients, 4)

    def coarsen(i):
        total = conc[2 * i] * pick(label[2 * i], CONDUCT_TABLE) + conc[2 * i + 1] * pick(label[2 * i + 1], CONDUCT_TABLE)
        mid[i] = 0.25 * pair_rows(total, pairs.at[i])

    loop(0, half, coarsen, 4)
    for i in range(half // 2):
        coarse[i] = 0.25 * pair_rows(mid[2 * i] + mid[2 * i + 1], pairs_2.at[i])
    for k in range(HALO):
        for t in range(4):
            rows = slice(8 * t, 8 * t + 8)
            send_x(pay_a, pay_b, 4 * k + t, phi[k, rows, :], phi[nx - HALO + k, rows, :])
        for t in range(2):
            rows = slice(8 * t, 8 * t + 8)
            send_x(pay_a, pay_b, 16 + 2 * k + t, mid[k, rows, :], mid[half - HALO + k, rows, :])


def first_pack_x_kernel(conc, label, r_a, r_b, token, pay_a, pay_b):
    nx = conc.shape[0]

    def plane(ref, k, t, offset, count):
        if t < 4:
            return ref[k, 8 * t : 8 * t + 8, :].astype(F32)
        return halo_tile(*y_sides(r_a, r_b, 7 * k + offset, count))

    for t in range(5):
        for k in range(HALO):
            send_x(pay_a, pay_b, 5 * k + t, plane(conc, k, t, 0, 4), plane(conc, nx - HALO + k, t, 0, 4))
        for k in range(3):
            send_x(pay_a, pay_b, 20 + 5 * k + t, plane(label, k, t, 4, 3), plane(label, nx - 3 + k, t, 4, 3))


def corner_rows(n, reach):
    counts = [min(HALO, k + reach) for k in range(HALO)]
    counts = counts + [HALO] * n + counts[::-1]
    return counts, [sum(counts[:i]) for i in range(len(counts))]


def extended_rows(n, reach):
    return sum(corner_rows(n, reach)[0])


def send_extended(pay_a, pay_b, own, x_a, x_b, index, reach):
    n = own.shape[0]
    counts, at = corner_rows(n, reach)
    tiles = own.shape[1] // 8
    for x in range(n):
        send_y(pay_a, pay_b, at[HALO + x], own[x, 0:4, :], own[x, 8 * tiles - 4 : 8 * tiles, :])
    for k in range(HALO):
        first_after, first_before = x_sides(x_a, x_b, index + tiles * k)
        last_after, last_before = x_sides(x_a, x_b, index + tiles * k + tiles - 1)
        for x, first, last in ((k, first_before, last_before), (HALO + n + k, first_after, last_after)):
            if counts[x]:
                send_y(pay_a, pay_b, at[x], first[0 : counts[x]], last[8 - counts[x] : 8])


def second_pack_kernel(phi, lists, x_a, x_b, pay_a, pay_b):
    send_extended(pay_a, pay_b, phi, x_a, x_b, 0, 0)
    base = pay_a.shape[0]
    pay_b[base : base + lists.shape[0], :] = lists[...]


def third_pack_kernel(mid, coarse, x_a, x_b, pay_a, pay_b):
    send_extended(pay_a, pay_b, mid, x_a, x_b, 16, 1)
    base = pay_a.shape[0] - 64
    for x in range(8):
        pay_a[base + 8 * x : base + 8 * x + 8, :] = coarse[x]
        pay_b[base + 8 * x : base + 8 * x + 8, :] = coarse[x]


def second_halo(r_a, r_b, n, reach, x):
    counts, at = corner_rows(n, reach)
    if not counts[x]:
        return jnp.zeros((8, 256), F32)
    return halo_tile(*y_sides(r_a, r_b, at[x], counts[x]))


def wide_rows(own, after_own, before_own, after, before):
    gap = jnp.zeros((6, 256), F32)
    return jnp.concatenate([own, after_own, after, gap, before, before_own], axis=0)


def flux_plane(c, solid, phi, label):
    drive = 0.5 * (solid - phi)
    logc = jnp.log(c)
    return pick(label, KINETIC_TABLE) * (jnp.exp(drive + 0.4 * logc) - jnp.exp(0.6 * logc - drive))


def around_plane(before, v, after):
    return (before + after) + (along_y(v) + along_z(v))


def sweeps_inner_kernel(
    conc, label, phi, solid, gain, base, y_a, y_b, zero, first, second, third, gain_far, base_far, out, flux
):
    nx = conc.shape[0]

    def own(i):
        zero[i, 0:32, :] = conc[i]

    loop(0, nx, own)
    for i in range(nx):
        c = halo_tile(*y_sides(y_a, y_b, 7 * i, 4))
        lab = halo_tile(*y_sides(y_a, y_b, 7 * i + 4, 3))
        zero[i, 32:40, :] = c
        gain_far[i] = jnp.where(c > 0.0, pick(lab, RATIO_TABLE), 0.0)
        base_far[i] = c * pick(lab, INVERSE_TABLE)
    fields = (zero, first, second, third)
    for s in range(1, SWEEPS):
        old, new = fields[s - 1], fields[s]

        def sweep(i, old=old, new=new):
            g = jnp.concatenate([gain[i], gain_far[i]], axis=0)
            b = jnp.concatenate([base[i], base_far[i]], axis=0)
            new[i] = b + g * around_plane(old[i - 1], old[i], old[i + 1])

        loop(s, nx - s, sweep)

    def last(i):
        c = base[i] + gain[i] * around_plane(third[i - 1], third[i], third[i + 1])[0:32, :]
        out[i] = c
        flux[i] = flux_plane(c, solid[i], phi[i], label[i])

    loop(SWEEPS, nx - SWEEPS, last, 4)


def sweeps_edge_kernel(
    x_a, x_b, label, phi, solid, gain, base, zero, first, second, third, gain_far, base_far, out_inner, flux_inner,
    out, flux, pay_a, pay_b, zero_x, first_x, second_x, third_x,
):
    nx = out.shape[0]
    inner = (zero, first, second, third)
    edge = (zero_x, first_x, second_x, third_x)

    def copy(i):
        out[i] = out_inner[i]
        flux[i] = flux_inner[i]

    loop(SWEEPS, nx - SWEEPS, copy)
    for side in range(2):
        plane = lambda k, side=side: k if side == 0 else nx - 1 - k
        row = lambda k, side=side: 8 * side + HALO + k
        far = lambda k, index, side=side: x_sides(x_a, x_b, index)[1 - side]
        gains, bases = {}, {}
        for j in range(1, HALO + 1):
            k = HALO - j if side == 0 else j - 1
            zero_x[row(-j)] = jnp.concatenate([far(k, 5 * k + t) for t in range(5)], axis=0)
            if j < HALO:
                k = HALO - 1 - j if side == 0 else j - 1
                lab = jnp.concatenate([far(k, 20 + 5 * k + t) for t in range(5)], axis=0)
                c = zero_x[row(-j)]
                gains[-j] = jnp.where(c > 0.0, pick(lab, RATIO_TABLE), 0.0)
                bases[-j] = c * pick(lab, INVERSE_TABLE)
        for k in range(SWEEPS):
            gains[k] = jnp.concatenate([gain[plane(k)], gain_far[plane(k)]], axis=0)
            bases[k] = jnp.concatenate([base[plane(k)], base_far[plane(k)]], axis=0)
        for s in range(1, SWEEPS + 1):

            def old(k, s=s):
                return inner[s - 1][plane(k)] if k >= s - 1 else edge[s - 1][row(k)]

            for k in range(s - SWEEPS, s):
                c = bases[k] + gains[k] * around_plane(old(k - 1), old(k), old(k + 1))
                if s < SWEEPS:
                    edge[s][row(k)] = c
                else:
                    c = c[0:32, :]
                    out[plane(k)] = c
                    flux[plane(k)] = flux_plane(c, solid[plane(k)], phi[plane(k)], label[plane(k)])
    for x in range(nx):
        send_y(pay_a, pay_b, 3 * x, flux[x, 0:3, :], flux[x, 29:32, :])


def mask_kernel(flux_all, lists, far, flux, halo_mask, marked):
    nx = flux_all.shape[0]
    rows = lists.shape[0]
    pieces = [lists[i : i + 1, :] for i in range(rows)] + [far[i : i + 1, :] for i in range(far.shape[0] - rows, far.shape[0])]
    owner = jnp.concatenate(pieces[0::2], axis=1).astype(jnp.int32)
    block = jnp.concatenate(pieces[1::2], axis=1).astype(jnp.int32)
    entries = owner.shape[1]
    hit_column = (iota((64, entries), 0) == lax.rem(block, 64)).astype(jnp.bfloat16)
    reach = owner - lax.axis_index("dev") + 1
    at_row = jnp.where((reach >= 0) & (reach < 3), reach * nx + lax.shift_right_arithmetic(block, 6), -1)
    hit_row = (iota((3 * nx, entries), 0) == at_row).astype(jnp.bfloat16)
    named = lax.dot_general(hit_row, hit_column, (((1,), (1,)), ((), ())), preferred_element_type=F32)
    named = jnp.concatenate([named, jnp.zeros((3 * nx, LANES - 64), F32)], axis=1)
    for j in range(3):
        for i in range(nx):
            marked[j, i] = jnp.broadcast_to(named[j * nx + i : j * nx + i + 1, :], (8, LANES))
    is_row = lax.div(iota((32, LANES), 1), 2) == iota((32, LANES), 0)
    row, pair = iota((8, LANES), 0), lax.div(iota((8, LANES), 1), 2)
    is_after = (row < 3) & (pair == row)
    is_before = (row >= 5) & (pair == row + 24)
    spread = (lax.rem(iota((LANES, 256), 0), 2) == lax.div(iota((LANES, 256), 1), LANES)).astype(jnp.bfloat16)

    def plane(i):
        marks = jnp.where(is_row, jnp.concatenate([marked[1, i]] * 4, axis=0), 0.0)
        beyond = jnp.where(is_after, marked[2, i], jnp.where(is_before, marked[0, i], 0.0))
        marks = jnp.concatenate([marks, beyond], axis=0).astype(jnp.bfloat16)
        listed = jnp.dot(marks, spread, preferred_element_type=F32) > 0.5
        flux[i] = jnp.where(listed[0:32], flux_all[i], 0.0)
        halo_mask[i] = jnp.where(listed[32:40], 1.0, 0.0)

    loop(0, nx, plane, 16)


def store_kernel(conc, flux, conc_out, flux_out, token, sems):
    copies = []
    for i, (ref, to) in enumerate(((conc, conc_out), (flux, flux_out))):
        for j in range(4):
            rows = pl.ds(8 * j, 8)
            copies.append(pltpu.make_async_copy(ref.at[rows], to.at[rows], sems.at[4 * i + j]))
            copies[-1].start()
    token[...] = jnp.zeros(token.shape, F32)
    for c in copies:
        c.wait()


def ready_kernel(conc, label, phi, y_a, y_b, x_a, x_b, yy_a, yy_b, xx_a, xx_b, weight, scale, field, token):
    nx = conc.shape[0]
    token[...] = jnp.zeros(token.shape, F32)

    def put(x, rows, c, lab, p):
        conduct = c * pick(lab, CONDUCT_TABLE)
        factor = OMEGA / (MASS + 6.0 * conduct)
        weight[x, rows, :] = conduct * factor
        scale[x, rows, :] = factor
        field[x, rows, :] = p

    def own(i):
        put(HALO + i, slice(0, 32), conc[i], label[i], phi[i])

    loop(0, nx, own, 4)
    low = slice(32, 40)
    for i in range(nx):
        c = halo_tile(*y_sides(y_a, y_b, 7 * i, 4))
        lab = halo_tile(*y_sides(y_a, y_b, 7 * i + 4, 3))
        put(HALO + i, low, c, lab, second_halo(yy_a, yy_b, nx, 0, HALO + i))
    for t in range(5):
        rows = slice(8 * t, 8 * t + 8)
        for k in range(HALO):
            c_after, c_before = x_sides(x_a, x_b, 5 * k + t)
            l_after = x_sides(x_a, x_b, 20 + 5 * min(k, 2) + t)[0]
            l_before = x_sides(x_a, x_b, 20 + 5 * max(k - 1, 0) + t)[1]
            if t < 4:
                p_after, p_before = x_sides(xx_a, xx_b, 4 * k + t)
            else:
                p_after = second_halo(yy_a, yy_b, nx, 0, HALO + nx + k)
                p_before = second_halo(yy_a, yy_b, nx, 0, k)
            put(k, rows, c_before, l_before, p_before)
            put(HALO + nx + k, rows, c_after, l_after, p_after)


def flux_pack_x_kernel(flux, r_a, r_b, mask, token, pay_a, pay_b):
    nx = flux.shape[0]

    def tile(x, t):
        if t < 4:
            return flux[x, 8 * t : 8 * t + 8, :]
        return mask[x] * halo_tile(*y_sides(r_a, r_b, 3 * x, 3))

    for k in range(3):
        for t in range(5):
            send_x(pay_a, pay_b, 5 * k + t, tile(k, t), tile(nx - 3 + k, t))


def first_sweep(field, weight, scale, x, rows, flux):
    p = field[x]
    near = (field[x - 1] + field[x + 1]) + (along_y(p) + along_z(p))
    b = scale[x, rows, :] * (MASS * p[rows, :] + flux)
    return b, 0.2 * p[rows, :] + weight[x, rows, :] * near[rows, :] + b


def potential_inner_kernel(flux, mask, y_a, y_b, weight, scale, field, after_two, source, first, source_mid, far, pairs):
    nx = flux.shape[0]
    for i in range(nx):
        far[i] = mask[i] * halo_tile(*y_sides(y_a, y_b, 3 * i, 3))

    def own(i):
        x = HALO + i
        f = jnp.concatenate([flux[i], far[i]], axis=0)
        source[x], first[x] = first_sweep(field, weight, scale, x, slice(0, 40), f)

    loop(0, nx, own)

    def around(values, x):
        v = values[x]
        return v, weight[x] * ((values[x - 1] + values[x + 1]) + (along_y(v) + along_z(v)))

    def sweep(x):
        v, near = around(first, x)
        after_two[x] = 0.2 * v + (source[x] + near)

    loop(HALO + 1, HALO + nx - 1, sweep)

    def remainder(x):
        v, near = around(after_two, x)
        return ((source[x] - OMEGA * v) + near)[0:32, :] / scale[x, 0:32, :]

    def coarsen(i):
        x = HALO + 2 * i
        source_mid[i] = 0.25 * pair_rows(remainder(x) + remainder(x + 1), pairs.at[i])

    loop(1, nx // 2 - 1, coarsen, 4)


def potential_edge_kernel(
    x_a, x_b, weight, scale, field, inner_two, inner_source, inner_first, inner_mid,
    edge_two, edge_source, source_mid, pay_a, pay_b, first, pairs,
):
    half = source_mid.shape[0]
    nx = 2 * half
    for side, face in ((0, HALO), (1, HALO + nx)):
        base = 8 * side + HALO - face
        for k in range(3):
            x = face - 3 + k if side == 0 else face + k
            f = jnp.concatenate([x_sides(x_a, x_b, 5 * k + t)[1 - side] for t in range(5)], axis=0)
            edge_source[base + x], first[base + x] = first_sweep(field, weight, scale, x, slice(0, 40), f)

        def first_of(x, base=base):
            return inner_first[x] if HALO <= x < HALO + nx else first[base + x]

        def source_of(x, base=base):
            return inner_source[x] if HALO <= x < HALO + nx else edge_source[base + x]

        def two_of(x, base=base):
            return inner_two[x] if HALO < x < HALO + nx - 1 else edge_two[base + x]

        for x in range(face - 2, face + 1) if side == 0 else range(face - 1, face + 2):
            v = first_of(x)
            near = weight[x] * ((first_of(x - 1) + first_of(x + 1)) + (along_y(v) + along_z(v)))
            edge_two[base + x] = 0.2 * v + (source_of(x) + near)
        total = 0.0
        at = face if side == 0 else face - 2
        for x in (at, at + 1):
            v = two_of(x)
            near = weight[x] * ((two_of(x - 1) + two_of(x + 1)) + (along_y(v) + along_z(v)))
            total = total + ((source_of(x) - OMEGA * v) + near)[0:32, :] / scale[x, 0:32, :]
        source_mid[0 if side == 0 else half - 1] = 0.25 * pair_rows(total, pairs.at[side])
    for x in range(1, half - 1):
        source_mid[x] = inner_mid[x]
    for x in range(half):
        send_y(pay_a, pay_b, 4 * x, source_mid[x, 0:4, :], source_mid[x, 12:16, :])


def mid_pack_x_kernel(field, r_a, r_b, token, pay_a, pay_b):
    n = field.shape[0]

    def tile(x, t):
        if t < 2:
            return field[x, 8 * t : 8 * t + 8, :]
        return halo_tile(*y_sides(r_a, r_b, 4 * x, 4))

    for k in range(HALO):
        for t in range(3):
            send_x(pay_a, pay_b, 3 * k + t, tile(k, t), tile(n - HALO + k, t))


def mid_kernel(
    source_own, conduct_own, yy_a, yy_b, xx_a, xx_b, y_a, y_b, x_a, x_b, rho, load,
    after_two, source, weight, coarse, conduct, pay_a, pay_b, part, scale, mid_conduct, pairs, pairs_2,
):
    n = source_own.shape[0]

    def put(x, rows, b, k):
        factor = OMEGA / (MASS + 3.0 * k)
        weight[x, rows, :] = k * factor
        scale[x, rows, :] = factor
        source[x, rows, :] = factor * b
        mid_conduct[x, rows, :] = k

    def far(x):
        return second_halo(yy_a, yy_b, n, 1, x)

    for i in range(n):
        put(HALO + i, slice(0, 16), source_own[i], conduct_own[i])
        put(HALO + i, slice(16, 24), halo_tile(*y_sides(y_a, y_b, 4 * i, 4)), far(HALO + i))
    for k in range(HALO):
        for t in range(3):
            rows = slice(8 * t, 8 * t + 8)
            b_after, b_before = x_sides(x_a, x_b, 3 * k + t)
            if t < 2:
                c_after, c_before = x_sides(xx_a, xx_b, 16 + 2 * k + t)
            else:
                c_after, c_before = far(HALO + n + k), far(k)
            put(k, rows, b_before, c_before)
            put(HALO + n + k, rows, b_after, c_after)

    def around(values, x):
        v = values[x]
        return v, weight[x] * (0.25 * ((values[x - 1] + values[x + 1]) + along_y(v)) + along_z(v))

    def sweep(x):
        v, near = around(source, x)
        after_two[x] = 0.2 * v + (source[x] + near)

    loop(1, n + 2 * HALO - 1, sweep, 11)

    def remainder(x):
        v, near = around(after_two, x)
        return ((source[x] - OMEGA * v) + near) / scale[x]

    total = jnp.zeros((8, 256), F32)
    for i in range(n // 2):
        x = HALO + 2 * i
        value = 0.25 * pair_rows(remainder(x) + remainder(x + 1), pairs.at[i])
        k = 0.25 * pair_rows(mid_conduct[x] + mid_conduct[x + 1], pairs_2.at[i])
        coarse[i] = value
        conduct[i] = k
        send_y(pay_a, pay_b, 9 * i, value[1:9], jnp.concatenate([value[11:12], value[0:7]], axis=0))
        send_y(pay_a, pay_b, 9 * i + 8, k[8:9], k[11:12])
        total += rho[i] * value[0:8]
    sums = jnp.concatenate([total[:, :LANES] + total[:, LANES:], load[...]], axis=1)
    pay_b[72:80, :] = sums
    part[...] = sums


COARSE_W = 0.0625


def coarse_ready_kernel(own, r_a, r_b, rho, load, one, two, conduct, scale):
    base = r_a.shape[0] - 64
    for x in range(8):
        after, before = y_sides(r_a, r_b, base + 8 * x, 8)
        k = jnp.concatenate([own[x], after, jnp.zeros((8, 256), F32), before], axis=0)
        conduct[x] = k
        scale[x] = OMEGA / (MASS + 2.25 * k)
        one[x] = jnp.ones(k.shape, F32)
    fields = (one, two)
    for s in range(COARSE_SWEEPS):
        old, new = fields[s % 2], fields[(s + 1) % 2]
        for x in range(8):
            near = [conduct[i] * old[i] if 0 <= i < 8 else None for i in (x - 1, x, x + 1)]
            inner = along_y(near[1])
            for other in (near[0], near[2]):
                if other is not None:
                    inner = inner + other
            new[x] = 0.2 * old[x] + scale[x] * (COARSE_W * inner + along_z(near[1]))
    last = fields[COARSE_SWEEPS % 2]
    peer, peers = lax.axis_index("dev"), lax.axis_size("dev")
    row, z = iota((8, 256), 0), iota((8, 256), 1)
    edge_y = ((row == 0) & (peer == 0)) | ((row == 7) & (peer == peers - 1))
    edge = edge_y.astype(F32) * COARSE_W + ((z == 0) | (z == 255)).astype(F32)
    total = jnp.zeros((8, 256), F32)
    for x in range(8):
        rho[x] = last[x, 0:8, :]
        total += MASS + own[x] * (edge + (COARSE_W if x in (0, 7) else 0.0))
    load[...] = total[:, :LANES] + total[:, LANES:]


def coarse_kernel(own, conduct, far_a, far_b, r_a, r_b, error, source, weight, one, two):
    base = far_a.shape[0] - 64
    for x in range(8):
        after, before = y_sides(r_a, r_b, 9 * x, 8)
        b = wide_rows(own[x, 0:8, :], own[x, 8:9, :], own[x, 11:12, :], after, before)
        last_after, last_before = y_sides(r_a, r_b, 9 * x + 8, 1)
        after, before = y_sides(far_a, far_b, base + 8 * x, 8)
        after = jnp.concatenate([after[1:8], last_after], axis=0)
        before = jnp.concatenate([last_before, before[0:7]], axis=0)
        k = wide_rows(conduct[x, 0:8, :], conduct[x, 8:9, :], conduct[x, 11:12, :], after, before)
        factor = OMEGA / (MASS + 2.25 * k)
        weight[x] = k * factor
        source[x] = factor * b
    old = source
    for s in range(1, COARSE_SWEEPS):
        new = one if s % 2 else two
        for x in range(8):
            v = old[x]
            inner = along_y(v)
            if x > 0:
                inner = inner + old[x - 1]
            if x < 7:
                inner = inner + old[x + 1]
            new[x] = 0.2 * v + (source[x] + weight[x] * (COARSE_W * inner + along_z(v)))
        old = new
    for x in range(8):
        error[x, 0:8, :] = old[x, 0:8, :]
        error[x, 8:16, :] = jnp.where(upper(), old[x, 8:16, :], old[x, 24:32, :])


def shift_kernel(error, *rest):
    terms, (out, pay_a, pay_b) = rest[:-3], rest[-3:]
    sums = sum(t[...] for t in terms)
    resid = jnp.sum(sums[:, :LANES])
    load = jnp.sum(sums[:, LANES:])
    shift_c = jnp.full((16, 256), resid, F32) / jnp.full((16, 256), load, F32)
    for x in range(8):
        out[x] = error[x] + shift_c
    for k in range(2):
        send_x(pay_a, pay_b, k, out[k], out[6 + k])


def squeeze(tile):
    return jnp.where(iota((8, 256), 0) < 2, tile, pltpu.roll(tile, 4, 0))


def spread_coarse(plane, room):
    return jnp.concatenate([twice(plane[0:8], room.at[0]), twice(squeeze(plane[8:16]), room.at[1])[0:8]], axis=0)


def spread_mid(plane, room):
    parts = [twice(plane[0:8], room.at[0]), twice(plane[8:16], room.at[1]), twice(squeeze(plane[16:24]), room.at[2])[0:8]]
    return jnp.concatenate(parts, axis=0)


def smoothed(before, v, after, weight, source, w):
    inner = (before + after) + along_y(v)
    return source + (0.2 * v + weight * (w * inner + along_z(v)))


def finish_inner_kernel(
    error, mid_two, mid_source, mid_weight, fine_two, fine_source, fine_weight,
    out, zero, one, fine_one, fine_last, two, dup, dup_2, result, sems,
):
    n = mid_two.shape[0]
    nf = fine_two.shape[0]
    for c in range(8):
        spread = spread_coarse(error[c], dup.at[c])
        for x in (2 * c + HALO, 2 * c + 1 + HALO):
            zero[x] = jnp.where(mid_weight[x] > 0.0, mid_two[x] + spread, 0.0)

    def sweep_mid(x, old, new):
        new[x] = smoothed(old[x - 1], old[x], old[x + 1], mid_weight[x], mid_source[x], 0.25)

    for x in range(HALO + 1, n - HALO - 1):
        sweep_mid(x, zero, one)
    for x in range(HALO + 2, n - HALO - 2):
        sweep_mid(x, one, two)

    def lift(m):
        spread = spread_mid(two[m], dup_2.at[m])
        x = 2 * m - HALO
        fine_one[x] = fine_two[x] + spread
        fine_one[x + 1] = fine_two[x + 1] + spread

    loop(HALO + 2, n - HALO - 2, lift, 6)

    def sweep_one(x):
        fine_last[x] = smoothed(fine_one[x - 1], fine_one[x], fine_one[x + 1], fine_weight[x], fine_source[x], 1.0)

    low, high = 2 * HALO + 1, nf - 2 * HALO - 1
    loop(low, high, sweep_one, 11)
    copies = []
    low, high = low + 1, high - 1
    for j in range(2):
        mid = low + (high - low) // 2
        for x in range(low, mid) if j == 0 else range(mid, high):
            v = smoothed(fine_last[x - 1], fine_last[x], fine_last[x + 1], fine_weight[x], fine_source[x], 1.0)
            result[x - HALO] = v[0:32, :]
        rows = pl.ds(low - HALO, mid - low) if j == 0 else pl.ds(mid - HALO, high - mid)
        copies.append(pltpu.make_async_copy(result.at[rows], out.at[rows], sems.at[j]))
        copies[-1].start()
    for c in copies:
        c.wait()


def finish_edge_kernel(
    x_a, x_b, mid_two, mid_source, mid_weight, fine_two, edge_two, fine_source, edge_source, fine_weight,
    zero, one, fine_one, fine_last, begun, out, zero_edge, one_edge, fine_edge, last_edge, dup, dup_2, result, sems,
):
    n = mid_two.shape[0]
    nf = fine_two.shape[0]
    nx = nf - 2 * HALO
    copies = []
    planes = x_sides(x_a, x_b, slice(0, 2))
    for side in (0, 1):
        sign = 1 if side == 0 else -1
        at = lambda k, side=side: HALO + k if side == 0 else n - HALO - 1 - k
        fine = lambda k, side=side: HALO + k if side == 0 else nf - HALO - 1 - k
        base = 8 * side + (0 if side == 0 else HALO - HALO - nx)
        for c in range(2):
            plane = planes[1 - side][c]
            spread = spread_coarse(plane, dup.at[2 * side + c])
            first = 2 * c if side == 0 else n - HALO + 2 * c
            for x in (first, first + 1):
                zero_edge[x] = jnp.where(mid_weight[x] > 0.0, mid_two[x] + spread, 0.0)

        def zero_of(k):
            return zero[at(k)] if k >= 0 else zero_edge[at(k)]

        def one_of(k):
            return one[at(k)] if k >= 1 else one_edge[at(k)]

        for k in range(-2, 1):
            x = at(k)
            one_edge[x] = smoothed(zero_of(k - 1), zero_of(k), zero_of(k + 1), mid_weight[x], mid_source[x], 0.25)
        for k in range(-1, 2):
            x = at(k)
            value = smoothed(one_of(k - 1), one_of(k), one_of(k + 1), mid_weight[x], mid_source[x], 0.25)
            spread = spread_mid(value, dup_2.at[3 * side + k + 1])
            for f in (fine(2 * k), fine(2 * k + 1)):
                inside = HALO < f < nf - HALO - 1
                before = fine_two[f] if inside else edge_two[base + f]
                fine_edge[f] = before + spread

        def fine_of(k):
            return fine_one[fine(k)] if k >= 4 else fine_edge[fine(k)]

        def last_of(k):
            return fine_last[fine(k)] if k >= 5 else last_edge[fine(k)]

        for k in range(-1, 5):
            f = fine(k)
            source = fine_source[f] if HALO <= f < nf - HALO else edge_source[base + f]
            last_edge[f] = smoothed(fine_of(k - 1), fine_of(k), fine_of(k + 1), fine_weight[f], source, 1.0)
        for k in range(6):
            f = fine(k)
            v = smoothed(last_of(k - 1), last_of(k), last_of(k + 1), fine_weight[f], fine_source[f], 1.0)
            result[f - HALO] = v[0:32, :]
        rows = pl.ds(0, 6) if side == 0 else pl.ds(nx - 6, 6)
        copies.append(pltpu.make_async_copy(result.at[rows], out.at[rows], sems.at[side]))
        copies[-1].start()
    for c in copies:
        c.wait()


def both_ways(pairs):
    return pairs + [(j, i) for i, j in pairs]


def swap(pay_a, pay_b, axis):
    size = lax.axis_size(axis)
    pairs_a = [(i, i + 1) for i in range(1, size - 1, 2)]
    pairs_b = [(i, i + 1) for i in range(0, size - 1, 2)]
    return lax.ppermute(pay_a, axis, both_ways(pairs_a)), lax.ppermute(pay_b, axis, both_ways(pairs_b))


def exchange(value, distance):
    return lax.ppermute(value, "dev", [(i, i ^ distance) for i in range(lax.axis_size("dev"))])


def body(conc_old, phi_old, solid_pot, phase_label, iface_block, iface_owner):
    peers = lax.axis_size("dev")
    nx = conc_old.shape[0]
    half = nx // 2
    quarter = nx // 4
    ext = (nx + 2 * HALO, nx + 2 * HALO, 256)
    ext_mid = (half + 2 * HALO, half + 2 * HALO, 256)
    token_shape = shaped(8, LANES)

    pay_a, pay_b, own_lists = call(
        first_pack_kernel,
        [shaped(7 * nx, 256)] * 2 + [shaped(8, 256)],
        [conc_old, phase_label, iface_owner.reshape(1, -1), iface_block],
        [vmem(nx, HALO, 256)] * 2
        + [pltpu.VMEM((nx, HALO, 256), jnp.int32)] * 2
        + [pltpu.VMEM((1, 256), jnp.int32)] * 2
        + [pltpu.SemaphoreType.DMA((6,))],
        in_specs=[FAR] * 4,
        limit=VMEM_MOST,
        name="first_pack",
    )
    y_a, y_b = swap(pay_a, pay_b, "dev")
    conduct_mid, conduct_coarse, pay_a, pay_b, lists, gain, base = call(
        own_kernel,
        [shaped(half, half, 256), shaped(quarter, quarter, 256), shaped(24, 8, 256), shaped(24, 8, 256)]
        + [shaped(2, 256), shaped(nx, nx, 256), shaped(nx, nx, 256)],
        [conc_old, phase_label, phi_old, own_lists],
        [vmem(half, 2, nx, LANES), vmem(quarter, 2, half, LANES)],
        name="own",
    )
    xx_a, xx_b = swap(pay_a, pay_b, "grp")
    distance = peers // 2
    while distance > 1:
        lists = jnp.concatenate([lists, exchange(lists, distance)], axis=0)
        distance //= 2
    rows = extended_rows(nx, 0)
    far_pay = call(
        second_pack_kernel,
        [shaped(rows, 256), shaped(rows + peers, 256)],
        [phi_old, lists, xx_a, xx_b],
        name="second_pack",
    )
    yy_a, yy_b = swap(*far_pay, "dev")
    pay_a, pay_b = call(
        first_pack_x_kernel,
        [shaped(35, 8, 256)] * 2,
        [conc_old, phase_label, y_a, y_b, conduct_coarse],
        name="first_pack_x",
    )
    x_a, x_b = swap(pay_a, pay_b, "grp")

    ext_y = (nx, nx + 2 * HALO, 256)
    zero, first, second, third, gain_far, base_far, conc_inner, flux_inner = call(
        sweeps_inner_kernel,
        [shaped(*ext_y)] * 4 + [shaped(nx, 8, 256)] * 2 + [shaped(nx, nx, 256)] * 2,
        [conc_old, phase_label, phi_old, solid_pot, gain, base, y_a, y_b],
        name="sweeps_inner",
    )
    edge_args = [x_a, x_b, phase_label, phi_old, solid_pot, gain, base, zero, first, second, third]
    conc_new, flux_all, pay_a, pay_b = call(
        sweeps_edge_kernel,
        [shaped(nx, nx, 256), shaped(nx, nx, 256), shaped(3 * nx, 256), shaped(3 * nx, 256)],
        edge_args + [gain_far, base_far, conc_inner, flux_inner],
        [vmem(16, nx + 2 * HALO, 256)] * 4,
        name="sweeps_edge",
    )
    f_a, f_b = swap(pay_a, pay_b, "dev")
    flux_own, halo_mask = call(
        mask_kernel,
        [shaped(nx, nx, 256), shaped(nx, 8, 256)],
        [flux_all, lists, yy_b],
        [vmem(3, nx, 8, LANES)],
        name="mask",
    )
    weight, scale, field, made = call(
        ready_kernel,
        [shaped(*ext)] * 3 + [token_shape],
        [conc_old, phase_label, phi_old, y_a, y_b, x_a, x_b, yy_a, yy_b, xx_a, xx_b],
        name="ready",
    )
    pay_a, pay_b = call(
        flux_pack_x_kernel, [shaped(15, 8, 256)] * 2, [flux_own, f_a, f_b, halo_mask, made], name="flux_pack_x"
    )
    fx_a, fx_b = swap(pay_a, pay_b, "grp")
    fine_two, fine_source, fine_first, inner_mid = call(
        potential_inner_kernel,
        [shaped(*ext)] * 3 + [shaped(half, half, 256)],
        [flux_own, halo_mask, f_a, f_b, weight, scale, field],
        [vmem(nx, 8, 256), vmem(half, 2, nx, LANES)],
        name="potential_inner",
    )
    edge = (16, nx + 2 * HALO, 256)
    edge_two, edge_source, source_mid, pay_a, pay_b = call(
        potential_edge_kernel,
        [shaped(*edge), shaped(*edge), shaped(half, half, 256), shaped(4 * half, 256), shaped(4 * half, 256)],
        [fx_a, fx_b, weight, scale, field, fine_two, fine_source, fine_first, inner_mid],
        [vmem(*edge), vmem(2, 2, nx, LANES)],
        name="potential_edge",
    )
    m_a, m_b = swap(pay_a, pay_b, "dev")
    rows = extended_rows(half, 1) + 64
    far_pay = call(
        third_pack_kernel, [shaped(rows, 256)] * 2, [conduct_mid, conduct_coarse, xx_a, xx_b], name="third_pack"
    )
    k_a, k_b = swap(*far_pay, "dev")
    concentration, flux, stored = call(
        store_kernel,
        [shaped(nx, nx, 256), shaped(nx, nx, 256), token_shape],
        [conc_new, flux_own],
        [pltpu.SemaphoreType.DMA((8,))],
        out_specs=[FAR, FAR, WHOLE],
        name="store",
    )
    wide = (quarter, 32, 256)
    rho, load = call(
        coarse_ready_kernel,
        [shaped(quarter, quarter, 256), shaped(8, LANES)],
        [conduct_coarse, k_a, k_b],
        [vmem(*wide)] * 4,
        name="coarse_ready",
    )
    pay_a, pay_b = call(
        mid_pack_x_kernel, [shaped(3 * HALO, 8, 256)] * 2, [source_mid, m_a, m_b, stored], name="mid_pack_x"
    )
    mx_a, mx_b = swap(pay_a, pay_b, "grp")
    mid_two, mid_source, mid_weight, source_coarse, wide_coarse, pay_a, pay_b, sums = call(
        mid_kernel,
        [shaped(*ext_mid)] * 3
        + [shaped(quarter, 12, 256), shaped(quarter, 12, 256), shaped(72, 256), shaped(80, 256), shaped(8, 256)],
        [source_mid, conduct_mid, k_a, k_b, xx_a, xx_b, m_a, m_b, mx_a, mx_b, rho, load],
        [vmem(*ext_mid)] * 2 + [vmem(8, 2, half + 2 * HALO, LANES)] * 2,
        name="middle",
    )
    c_a, c_b = swap(pay_a, pay_b, "dev")
    sums = sums + c_b[72:80]
    others = [exchange(sums, distance) for distance in range(peers - 2, 0, -2)]
    (error,) = call(
        coarse_kernel,
        [shaped(8, 16, 256)],
        [source_coarse, wide_coarse, k_a, k_b, c_a, c_b],
        [vmem(*wide)] * 4,
        name="coarse",
    )
    error, pay_a, pay_b = call(
        shift_kernel, [shaped(8, 16, 256), shaped(2, 16, 256), shaped(2, 16, 256)], [error, sums] + others, name="shift"
    )
    e_a, e_b = swap(pay_a, pay_b, "grp")
    begun, zero, one, fine_one, fine_last = call(
        finish_inner_kernel,
        [shaped(nx, nx, 256), shaped(*ext_mid), shaped(*ext_mid), shaped(*ext), shaped(*ext)],
        [error, mid_two, mid_source, mid_weight, fine_two, fine_source, weight],
        [vmem(*ext_mid), vmem(8, 2, 2, 16, LANES), vmem(half + 2 * HALO, 3, 2, 16, LANES), vmem(nx, nx, 256)]
        + [pltpu.SemaphoreType.DMA((2,))],
        out_specs=[FAR] + [WHOLE] * 4,
        name="finish_inner",
    )
    finish_args = [e_a, e_b, mid_two, mid_source, mid_weight, fine_two, edge_two, fine_source, edge_source, weight]
    finish_args += [zero, one, fine_one, fine_last, begun]
    (potential,) = call(
        finish_edge_kernel,
        [shaped(nx, nx, 256)],
        finish_args,
        [vmem(*ext_mid), vmem(*ext_mid), vmem(*ext), vmem(*ext)]
        + [vmem(4, 2, 2, 16, LANES), vmem(6, 3, 2, 16, LANES), vmem(nx, nx, 256)]
        + [pltpu.SemaphoreType.DMA((2,))],
        in_specs=[WHOLE] * (len(finish_args) - 1) + [FAR],
        out_specs=[FAR],
        aliases={len(finish_args) - 1: 0},
        name="finish_edge",
    )
    return (concentration, flux, potential)


def solution(mesh):
    brick = P("grp", "dev", None)
    return jax.shard_map(
        body,
        mesh=mesh,
        in_specs=(brick, brick, brick, brick, P("grp", "dev"), brick),
        out_specs=(brick, brick, brick),
        check_vma=False,
    )
```

```python
import jax
import jax.numpy as jnp
from jax import lax
from jax.experimental import pallas as pl
from jax.experimental.pallas import tpu as pltpu
from jax.sharding import PartitionSpec as P


F32 = jnp.float32
MASS = 0.05
OMEGA = 0.8
DIFFUSION_TABLE = (1.5, 0.1, 0.4)
RATIO_TABLE = tuple(d / (1.0 + 6.0 * d) for d in DIFFUSION_TABLE)
INVERSE_TABLE = tuple(1.0 / (1.0 + 6.0 * d) for d in DIFFUSION_TABLE)
CONDUCT_TABLE = (1.0, 0.3, 0.6)
KINETIC_TABLE = (0.2, 1.0, 0.5)
SWEEPS = 4
COARSE_SWEEPS = 8
COARSE_NEAR = 8
HALO = 4
LANES = 128
VMEM_LIMIT = 28 * 1024 * 1024
VMEM_MOST = 58 * 1024 * 1024


def shaped(*shape):
    return jax.ShapeDtypeStruct(shape, F32)


WHOLE = pl.BlockSpec(memory_space=pltpu.VMEM)
FAR = pl.BlockSpec(memory_space=pltpu.HBM)


def call(kernel, outs, args, scratch=(), in_specs=None, out_specs=None, limit=VMEM_LIMIT, aliases=None, name=None):
    size = sum(4 * a.size for a in args) + sum(4 * o.size for o in outs)
    return pl.pallas_call(
        kernel,
        out_shape=tuple(outs),
        in_specs=in_specs or [WHOLE] * len(args),
        out_specs=tuple(out_specs or [WHOLE] * len(outs)),
        scratch_shapes=list(scratch),
        input_output_aliases=aliases or {},
        compiler_params=pltpu.CompilerParams(vmem_limit_bytes=limit),
        cost_estimate=pl.CostEstimate(flops=10**6, bytes_accessed=size, transcendentals=0),
        name=name,
    )(*args)


def vmem(*shape):
    return pltpu.VMEM(shape, F32)


def iota(shape, dim):
    return lax.broadcasted_iota(jnp.int32, shape, dim)


def pick(label, table):
    return jnp.where(label == 0, table[0], jnp.where(label == 1, table[1], table[2])).astype(F32)


def loop(low, high, body, unroll=8):
    steps = (high - low) // unroll

    def step(i, carry):
        for u in range(unroll):
            body(low + i * unroll + u)
        return carry

    if steps > 1:
        lax.fori_loop(0, steps, step, 0)
    else:
        steps = 0
    for x in range(low + steps * unroll, high):
        body(x)


def odd(axis):
    return lax.rem(lax.axis_index(axis), 2) == 1


def along_y(v):
    return pltpu.roll(v, 1, 0) + pltpu.roll(v, v.shape[0] - 1, 0)


def along_z(v):
    low, high = v[:, :LANES], v[:, LANES:]
    lane = iota(low.shape, 1)
    first, last = lane == 0, lane == LANES - 1
    low_up, high_up = pltpu.roll(low, 1, 1), pltpu.roll(high, 1, 1)
    low_down, high_down = pltpu.roll(low, LANES - 1, 1), pltpu.roll(high, LANES - 1, 1)
    low_sum = jnp.where(first, 0.0, low_up) + jnp.where(last, high_down, low_down)
    high_sum = jnp.where(first, low_up, high_up) + jnp.where(last, 0.0, high_down)
    return jnp.concatenate([low_sum, high_sum], axis=1)


def upper(shape=(8, 256)):
    return iota(shape, 0) < HALO


def twice(tile, scratch):
    for h in range(2):
        part = tile[:, h * LANES : (h + 1) * LANES]
        scratch[h, pl.ds(0, 8, stride=2), :] = part
        scratch[h, pl.ds(1, 8, stride=2), :] = part
    return jnp.concatenate([scratch[0], scratch[1]], axis=1)


def pair_rows(v, scratch):
    half = v.shape[0] // 2
    parts = []
    for h in range(2):
        scratch[h] = v[:, h * LANES : (h + 1) * LANES]
        parts.append(scratch[h, pl.ds(0, half, stride=2), :] + scratch[h, pl.ds(1, half, stride=2), :])
    return jnp.concatenate(parts, axis=1)


def either(flag, if_true, if_false):
    return jnp.where(flag, if_true, if_false)


def y_sides(r_a, r_b, at, count):
    flag = odd("dev")
    a, b = r_a[at : at + count, :], r_b[at : at + count, :]
    return either(flag, a, b), either(flag, b, a)


def x_sides(r_a, r_b, index):
    flag = odd("grp")
    a, b = r_a[index], r_b[index]
    return either(flag, a, b), either(flag, b, a)


def send_y(pay_a, pay_b, at, first, last):
    flag = odd("dev")
    n = first.shape[0]
    pay_a[at : at + n, :] = either(flag, last, first)
    pay_b[at : at + n, :] = either(flag, first, last)


def send_x(pay_a, pay_b, index, first, last):
    flag = odd("grp")
    pay_a[index] = either(flag, last, first)
    pay_b[index] = either(flag, first, last)


def halo_tile(after, before):
    parts = [after]
    if after.shape[0] < HALO:
        parts.append(jnp.zeros((2 * HALO - 2 * after.shape[0], after.shape[1]), F32))
    return jnp.concatenate(parts + [before], axis=0)


def first_pack_kernel(
    conc, label, owner, block, pay_a, pay_b, own_lists, c_first, c_last, l_first, l_last, own_owner, own_block, sems
):
    nx = conc.shape[0]
    copies = [pltpu.make_async_copy(owner, own_owner, sems.at[4]), pltpu.make_async_copy(block, own_block, sems.at[5])]
    for i, (ref, at, to) in enumerate(((conc, 0, c_first), (conc, 28, c_last), (label, 0, l_first), (label, 28, l_last))):
        copies.append(pltpu.make_async_copy(ref.at[:, pl.ds(at, 4), :], to, sems.at[i]))
    for c in copies:
        c.start()
    for c in copies:
        c.wait()
    named = jnp.concatenate([own_owner[...], own_block[...], jnp.zeros((6, 256), jnp.int32)], axis=0).astype(F32)
    own_lists[...] = named
    for x in range(nx):
        send_y(pay_a, pay_b, 7 * x, c_first[x], c_last[x])
        send_y(pay_a, pay_b, 7 * x + 4, l_first[x, 0:3, :].astype(F32), l_last[x, 1:4, :].astype(F32))


def own_kernel(conc, label, phi, named, mid, coarse, pay_a, pay_b, lists, gain, base, pairs, pairs_2):
    nx = conc.shape[0]
    half = nx // 2
    lists[...] = named[0:2, :]

    def coefficients(i):
        gain[i] = pick(label[i], RATIO_TABLE)
        base[i] = conc[i] * pick(label[i], INVERSE_TABLE)

    loop(0, nx, coefficients, 4)

    def coarsen(i):
        total = conc[2 * i] * pick(label[2 * i], CONDUCT_TABLE) + conc[2 * i + 1] * pick(label[2 * i + 1], CONDUCT_TABLE)
        mid[i] = 0.25 * pair_rows(total, pairs.at[i])

    loop(0, half, coarsen, 4)
    for i in range(half // 2):
        coarse[i] = 0.25 * pair_rows(mid[2 * i] + mid[2 * i + 1], pairs_2.at[i])
    for k in range(HALO):
        for t in range(4):
            rows = slice(8 * t, 8 * t + 8)
            send_x(pay_a, pay_b, 4 * k + t, phi[k, rows, :], phi[nx - HALO + k, rows, :])
        for t in range(2):
            rows = slice(8 * t, 8 * t + 8)
            send_x(pay_a, pay_b, 16 + 2 * k + t, mid[k, rows, :], mid[half - HALO + k, rows, :])


def first_pack_x_kernel(conc, label, r_a, r_b, token, pay_a, pay_b):
    nx = conc.shape[0]

    def plane(ref, k, t, offset, count):
        if t < 4:
            return ref[k, 8 * t : 8 * t + 8, :].astype(F32)
        return halo_tile(*y_sides(r_a, r_b, 7 * k + offset, count))

    for t in range(5):
        for k in range(HALO):
            send_x(pay_a, pay_b, 5 * k + t, plane(conc, k, t, 0, 4), plane(conc, nx - HALO + k, t, 0, 4))
        for k in range(3):
            send_x(pay_a, pay_b, 20 + 5 * k + t, plane(label, k, t, 4, 3), plane(label, nx - 3 + k, t, 4, 3))


def corner_rows(n, reach):
    counts = [min(HALO, k + reach) for k in range(HALO)]
    counts = counts + [HALO] * n + counts[::-1]
    return counts, [sum(counts[:i]) for i in range(len(counts))]


def second_rows(nx):
    phi, mid = (sum(corner_rows(n, reach)[0]) for n, reach in ((nx, 0), (nx // 2, 1)))
    return phi, phi + mid


def second_pack_kernel(phi, mid, x_a, x_b, pay_a, pay_b):
    nx = phi.shape[0]
    starts = second_rows(nx)

    def put(own, n, reach, index, base):
        counts, at = corner_rows(n, reach)
        tiles = own.shape[1] // 8
        for x in range(n):
            send_y(pay_a, pay_b, base + at[HALO + x], own[x, 0:4, :], own[x, 8 * tiles - 4 : 8 * tiles, :])
        for k in range(HALO):
            first_after, first_before = x_sides(x_a, x_b, index + tiles * k)
            last_after, last_before = x_sides(x_a, x_b, index + tiles * k + tiles - 1)
            for x, first, last in ((k, first_before, last_before), (HALO + n + k, first_after, last_after)):
                if counts[x]:
                    send_y(pay_a, pay_b, base + at[x], first[0 : counts[x]], last[8 - counts[x] : 8])

    put(phi, nx, 0, 0, 0)
    put(mid, nx // 2, 1, 16, starts[0])


def second_halo(r_a, r_b, n, reach, x, base):
    counts, at = corner_rows(n, reach)
    if not counts[x]:
        return jnp.zeros((8, 256), F32)
    return halo_tile(*y_sides(r_a, r_b, base + at[x], counts[x]))


def wide_rows(own, after_own, before_own, after, before):
    gap = jnp.zeros((6, 256), F32)
    return jnp.concatenate([own, after_own, after, gap, before, before_own], axis=0)


def flux_plane(c, solid, phi, label):
    drive = 0.5 * (solid - phi)
    logc = jnp.log(c)
    return pick(label, KINETIC_TABLE) * (jnp.exp(drive + 0.4 * logc) - jnp.exp(0.6 * logc - drive))


def around_plane(before, v, after):
    return (before + after) + (along_y(v) + along_z(v))


def sweeps_inner_kernel(
    conc, label, phi, solid, gain, base, y_a, y_b, zero, first, second, third, gain_far, base_far, out, flux
):
    nx = conc.shape[0]

    def own(i):
        zero[i, 0:32, :] = conc[i]

    loop(0, nx, own)
    for i in range(nx):
        c = halo_tile(*y_sides(y_a, y_b, 7 * i, 4))
        lab = halo_tile(*y_sides(y_a, y_b, 7 * i + 4, 3))
        zero[i, 32:40, :] = c
        gain_far[i] = jnp.where(c > 0.0, pick(lab, RATIO_TABLE), 0.0)
        base_far[i] = c * pick(lab, INVERSE_TABLE)
    fields = (zero, first, second, third)
    for s in range(1, SWEEPS):
        old, new = fields[s - 1], fields[s]

        def sweep(i, old=old, new=new):
            g = jnp.concatenate([gain[i], gain_far[i]], axis=0)
            b = jnp.concatenate([base[i], base_far[i]], axis=0)
            new[i] = b + g * around_plane(old[i - 1], old[i], old[i + 1])

        loop(s, nx - s, sweep)

    def last(i):
        c = base[i] + gain[i] * around_plane(third[i - 1], third[i], third[i + 1])[0:32, :]
        out[i] = c
        flux[i] = flux_plane(c, solid[i], phi[i], label[i])

    loop(SWEEPS, nx - SWEEPS, last, 4)


def sweeps_edge_kernel(
    x_a, x_b, label, phi, solid, gain, base, zero, first, second, third, gain_far, base_far, out_inner, flux_inner, lists,
    out, flux, pay_a, pay_b, zero_x, first_x, second_x, third_x,
):
    nx = out.shape[0]
    inner = (zero, first, second, third)
    edge = (zero_x, first_x, second_x, third_x)

    def copy(i):
        out[i] = out_inner[i]
        flux[i] = flux_inner[i]

    loop(SWEEPS, nx - SWEEPS, copy)
    for side in range(2):
        plane = lambda k, side=side: k if side == 0 else nx - 1 - k
        row = lambda k, side=side: 8 * side + HALO + k
        far = lambda k, index, side=side: x_sides(x_a, x_b, index)[1 - side]
        gains, bases = {}, {}
        for j in range(1, HALO + 1):
            k = HALO - j if side == 0 else j - 1
            zero_x[row(-j)] = jnp.concatenate([far(k, 5 * k + t) for t in range(5)], axis=0)
            if j < HALO:
                k = HALO - 1 - j if side == 0 else j - 1
                lab = jnp.concatenate([far(k, 20 + 5 * k + t) for t in range(5)], axis=0)
                c = zero_x[row(-j)]
                gains[-j] = jnp.where(c > 0.0, pick(lab, RATIO_TABLE), 0.0)
                bases[-j] = c * pick(lab, INVERSE_TABLE)
        for k in range(SWEEPS):
            gains[k] = jnp.concatenate([gain[plane(k)], gain_far[plane(k)]], axis=0)
            bases[k] = jnp.concatenate([base[plane(k)], base_far[plane(k)]], axis=0)
        for s in range(1, SWEEPS + 1):

            def old(k, s=s):
                return inner[s - 1][plane(k)] if k >= s - 1 else edge[s - 1][row(k)]

            for k in range(s - SWEEPS, s):
                c = bases[k] + gains[k] * around_plane(old(k - 1), old(k), old(k + 1))
                if s < SWEEPS:
                    edge[s][row(k)] = c
                else:
                    c = c[0:32, :]
                    out[plane(k)] = c
                    flux[plane(k)] = flux_plane(c, solid[plane(k)], phi[plane(k)], label[plane(k)])
    for x in range(nx):
        send_y(pay_a, pay_b, 3 * x, flux[x, 0:3, :], flux[x, 29:32, :])
    pay_b[3 * nx : 3 * nx + lists.shape[0], :] = lists[...]


def mask_kernel(flux_all, lists, far, token, token_2, flux, halo_mask, marked):
    nx = flux_all.shape[0]
    rows = lists.shape[0]
    pieces = [lists[i : i + 1, :] for i in range(rows)] + [far[i : i + 1, :] for i in range(far.shape[0] - rows, far.shape[0])]
    owner = jnp.concatenate(pieces[0::2], axis=1).astype(jnp.int32)
    block = jnp.concatenate(pieces[1::2], axis=1).astype(jnp.int32)
    entries = owner.shape[1]
    hit_column = (iota((64, entries), 0) == lax.rem(block, 64)).astype(jnp.bfloat16)
    reach = owner - lax.axis_index("dev") + 1
    at_row = jnp.where((reach >= 0) & (reach < 3), reach * nx + lax.shift_right_arithmetic(block, 6), -1)
    hit_row = (iota((3 * nx, entries), 0) == at_row).astype(jnp.bfloat16)
    named = lax.dot_general(hit_row, hit_column, (((1,), (1,)), ((), ())), preferred_element_type=F32)
    named = jnp.concatenate([named, jnp.zeros((3 * nx, LANES - 64), F32)], axis=1)
    for j in range(3):
        for i in range(nx):
            marked[j, i] = jnp.broadcast_to(named[j * nx + i : j * nx + i + 1, :], (8, LANES))
    is_row = lax.div(iota((32, LANES), 1), 2) == iota((32, LANES), 0)
    row, pair = iota((8, LANES), 0), lax.div(iota((8, LANES), 1), 2)
    is_after = (row < 3) & (pair == row)
    is_before = (row >= 5) & (pair == row + 24)
    spread = (lax.rem(iota((LANES, 256), 0), 2) == lax.div(iota((LANES, 256), 1), LANES)).astype(jnp.bfloat16)

    def plane(i):
        marks = jnp.where(is_row, jnp.concatenate([marked[1, i]] * 4, axis=0), 0.0)
        beyond = jnp.where(is_after, marked[2, i], jnp.where(is_before, marked[0, i], 0.0))
        marks = jnp.concatenate([marks, beyond], axis=0).astype(jnp.bfloat16)
        listed = jnp.dot(marks, spread, preferred_element_type=F32) > 0.5
        flux[i] = jnp.where(listed[0:32], flux_all[i], 0.0)
        halo_mask[i] = jnp.where(listed[32:40], 1.0, 0.0)

    loop(0, nx, plane, 16)


def store_kernel(conc, flux, conc_out, flux_out, token, sems):
    copies = []
    for i, (ref, to) in enumerate(((conc, conc_out), (flux, flux_out))):
        for j in range(4):
            rows = pl.ds(8 * j, 8)
            copies.append(pltpu.make_async_copy(ref.at[rows], to.at[rows], sems.at[4 * i + j]))
            copies[-1].start()
    token[...] = jnp.zeros(token.shape, F32)
    for c in copies:
        c.wait()


def ready_kernel(conc, label, y_a, y_b, x_a, x_b, weight, scale, token):
    nx = conc.shape[0]
    token[...] = jnp.zeros(token.shape, F32)

    def put(x, rows, c, lab):
        conduct = c * pick(lab, CONDUCT_TABLE)
        factor = OMEGA / (MASS + 6.0 * conduct)
        weight[x, rows, :] = conduct * factor
        scale[x, rows, :] = factor

    def own(i):
        put(HALO + i, slice(0, 32), conc[i], label[i])

    loop(0, nx, own, 4)
    for i in range(nx):
        c = halo_tile(*y_sides(y_a, y_b, 7 * i, 4))
        lab = halo_tile(*y_sides(y_a, y_b, 7 * i + 4, 3))
        put(HALO + i, slice(32, 40), c, lab)
    for t in range(5):
        rows = slice(8 * t, 8 * t + 8)
        for k in range(HALO):
            c_after, c_before = x_sides(x_a, x_b, 5 * k + t)
            l_after = x_sides(x_a, x_b, 20 + 5 * min(k, 2) + t)[0]
            l_before = x_sides(x_a, x_b, 20 + 5 * max(k - 1, 0) + t)[1]
            put(k, rows, c_before, l_before)
            put(HALO + nx + k, rows, c_after, l_after)


def place_phi(phi, yy_a, yy_b, xx_a, xx_b, field):
    nx = phi.shape[0]

    def own(i):
        field[HALO + i, 0:32, :] = phi[i]

    loop(0, nx, own)
    for x in range(nx + 2 * HALO):
        field[x, 32:40, :] = second_halo(yy_a, yy_b, nx, 0, x, 0)
    for t in range(4):
        for k in range(HALO):
            after, before = x_sides(xx_a, xx_b, 4 * k + t)
            field[k, 8 * t : 8 * t + 8, :] = before
            field[HALO + nx + k, 8 * t : 8 * t + 8, :] = after


def flux_pack_x_kernel(flux, r_a, r_b, mask, token, pay_a, pay_b):
    nx = flux.shape[0]

    def tile(x, t):
        if t < 4:
            return flux[x, 8 * t : 8 * t + 8, :]
        return mask[x] * halo_tile(*y_sides(r_a, r_b, 3 * x, 3))

    for k in range(3):
        for t in range(5):
            send_x(pay_a, pay_b, 5 * k + t, tile(k, t), tile(nx - 3 + k, t))


def first_sweep(field, weight, scale, x, rows, flux):
    p = field[x]
    near = (field[x - 1] + field[x + 1]) + (along_y(p) + along_z(p))
    b = scale[x, rows, :] * (MASS * p[rows, :] + flux)
    return b, 0.2 * p[rows, :] + weight[x, rows, :] * near[rows, :] + b


def potential_inner_kernel(
    flux, mask, y_a, y_b, phi, yy_a, yy_b, xx_a, xx_b, weight, scale, after_two, source, first, source_mid, field, far, pairs
):
    nx = flux.shape[0]
    place_phi(phi, yy_a, yy_b, xx_a, xx_b, field)
    for i in range(nx):
        far[i] = mask[i] * halo_tile(*y_sides(y_a, y_b, 3 * i, 3))

    def own(i):
        x = HALO + i
        f = jnp.concatenate([flux[i], far[i]], axis=0)
        source[x], first[x] = first_sweep(field, weight, scale, x, slice(0, 40), f)

    loop(0, nx, own)

    def around(values, x):
        v = values[x]
        return v, weight[x] * ((values[x - 1] + values[x + 1]) + (along_y(v) + along_z(v)))

    def sweep(x):
        v, near = around(first, x)
        after_two[x] = 0.2 * v + (source[x] + near)

    loop(HALO + 1, HALO + nx - 1, sweep)

    def remainder(x):
        v, near = around(after_two, x)
        return ((source[x] - OMEGA * v) + near)[0:32, :] / scale[x, 0:32, :]

    def coarsen(i):
        x = HALO + 2 * i
        source_mid[i] = 0.25 * pair_rows(remainder(x) + remainder(x + 1), pairs.at[i])

    loop(1, nx // 2 - 1, coarsen, 4)


def potential_edge_kernel(
    x_a, x_b, weight, scale, field, inner_two, inner_source, inner_first, inner_mid,
    coarse, edge_two, edge_source, source_mid, pay_a, pay_b, first, pairs,
):
    half = source_mid.shape[0]
    nx = 2 * half
    for side, face in ((0, HALO), (1, HALO + nx)):
        base = 8 * side + HALO - face
        for k in range(3):
            x = face - 3 + k if side == 0 else face + k
            f = jnp.concatenate([x_sides(x_a, x_b, 5 * k + t)[1 - side] for t in range(5)], axis=0)
            edge_source[base + x], first[base + x] = first_sweep(field, weight, scale, x, slice(0, 40), f)

        def first_of(x, base=base):
            return inner_first[x] if HALO <= x < HALO + nx else first[base + x]

        def source_of(x, base=base):
            return inner_source[x] if HALO <= x < HALO + nx else edge_source[base + x]

        def two_of(x, base=base):
            return inner_two[x] if HALO < x < HALO + nx - 1 else edge_two[base + x]

        for x in range(face - 2, face + 1) if side == 0 else range(face - 1, face + 2):
            v = first_of(x)
            near = weight[x] * ((first_of(x - 1) + first_of(x + 1)) + (along_y(v) + along_z(v)))
            edge_two[base + x] = 0.2 * v + (source_of(x) + near)
        total = 0.0
        at = face if side == 0 else face - 2
        for x in (at, at + 1):
            v = two_of(x)
            near = weight[x] * ((two_of(x - 1) + two_of(x + 1)) + (along_y(v) + along_z(v)))
            total = total + ((source_of(x) - OMEGA * v) + near)[0:32, :] / scale[x, 0:32, :]
        source_mid[0 if side == 0 else half - 1] = 0.25 * pair_rows(total, pairs.at[side])
    for x in range(1, half - 1):
        source_mid[x] = inner_mid[x]
    for x in range(half):
        send_y(pay_a, pay_b, 4 * x, source_mid[x, 0:4, :], source_mid[x, 12:16, :])
    base = 4 * half
    for x in range(8):
        pay_a[base + 8 * x : base + 8 * x + 8, :] = coarse[x]
        pay_b[base + 8 * x : base + 8 * x + 8, :] = coarse[x]


def mid_pack_x_kernel(field, r_a, r_b, token, pay_a, pay_b):
    n = field.shape[0]

    def tile(x, t):
        if t < 2:
            return field[x, 8 * t : 8 * t + 8, :]
        return halo_tile(*y_sides(r_a, r_b, 4 * x, 4))

    for k in range(HALO):
        for t in range(3):
            send_x(pay_a, pay_b, 3 * k + t, tile(k, t), tile(n - HALO + k, t))


def mid_kernel(
    source_own, conduct_own, yy_a, yy_b, xx_a, xx_b, y_a, y_b, x_a, x_b, rho, load,
    after_two, source, weight, coarse, conduct, pay_a, pay_b, part, scale, mid_conduct, pairs, pairs_2,
):
    n = source_own.shape[0]
    base = second_rows(2 * n)[0]

    def put(x, rows, b, k):
        factor = OMEGA / (MASS + 3.0 * k)
        weight[x, rows, :] = k * factor
        scale[x, rows, :] = factor
        source[x, rows, :] = factor * b
        mid_conduct[x, rows, :] = k

    def far(x):
        return second_halo(yy_a, yy_b, n, 1, x, base)

    for i in range(n):
        put(HALO + i, slice(0, 16), source_own[i], conduct_own[i])
        put(HALO + i, slice(16, 24), halo_tile(*y_sides(y_a, y_b, 4 * i, 4)), far(HALO + i))
    for k in range(HALO):
        for t in range(3):
            rows = slice(8 * t, 8 * t + 8)
            b_after, b_before = x_sides(x_a, x_b, 3 * k + t)
            if t < 2:
                c_after, c_before = x_sides(xx_a, xx_b, 16 + 2 * k + t)
            else:
                c_after, c_before = far(HALO + n + k), far(k)
            put(k, rows, b_before, c_before)
            put(HALO + n + k, rows, b_after, c_after)

    def around(values, x):
        v = values[x]
        return v, weight[x] * (0.25 * ((values[x - 1] + values[x + 1]) + along_y(v)) + along_z(v))

    def sweep(x):
        v, near = around(source, x)
        after_two[x] = 0.2 * v + (source[x] + near)

    loop(1, n + 2 * HALO - 1, sweep, 11)

    def remainder(x):
        v, near = around(after_two, x)
        return ((source[x] - OMEGA * v) + near) / scale[x]

    total = jnp.zeros((8, 256), F32)
    for i in range(n // 2):
        x = HALO + 2 * i
        value = 0.25 * pair_rows(remainder(x) + remainder(x + 1), pairs.at[i])
        k = 0.25 * pair_rows(mid_conduct[x] + mid_conduct[x + 1], pairs_2.at[i])
        coarse[i] = value
        conduct[i] = k
        send_y(pay_a, pay_b, 9 * i, value[1:9], jnp.concatenate([value[11:12], value[0:7]], axis=0))
        send_y(pay_a, pay_b, 9 * i + 8, k[8:9], k[11:12])
        total += rho[i] * value[0:8]
    sums = jnp.concatenate([total[:, :LANES] + total[:, LANES:], load[...]], axis=1)
    pay_b[72:80, :] = sums
    part[...] = sums


COARSE_W = 0.0625


def coarse_ready_kernel(own, r_a, r_b, rho, load, one, two, conduct, scale):
    base = r_a.shape[0] - 64
    for x in range(8):
        after, before = y_sides(r_a, r_b, base + 8 * x, 8)
        k = jnp.concatenate([own[x], after, jnp.zeros((8, 256), F32), before], axis=0)
        conduct[x] = k
        scale[x] = OMEGA / (MASS + 2.25 * k)
        one[x] = jnp.ones(k.shape, F32)
    fields = (one, two)
    for s in range(COARSE_SWEEPS):
        old, new = fields[s % 2], fields[(s + 1) % 2]
        for x in range(8):
            near = [conduct[i] * old[i] if 0 <= i < 8 else None for i in (x - 1, x, x + 1)]
            inner = along_y(near[1])
            for other in (near[0], near[2]):
                if other is not None:
                    inner = inner + other
            new[x] = 0.2 * old[x] + scale[x] * (COARSE_W * inner + along_z(near[1]))
    last = fields[COARSE_SWEEPS % 2]
    peer, peers = lax.axis_index("dev"), lax.axis_size("dev")
    row, z = iota((8, 256), 0), iota((8, 256), 1)
    edge_y = ((row == 0) & (peer == 0)) | ((row == 7) & (peer == peers - 1))
    edge = edge_y.astype(F32) * COARSE_W + ((z == 0) | (z == 255)).astype(F32)
    total = jnp.zeros((8, 256), F32)
    for x in range(8):
        rho[x] = last[x, 0:8, :]
        total += MASS + own[x] * (edge + (COARSE_W if x in (0, 7) else 0.0))
    load[...] = total[:, :LANES] + total[:, LANES:]


def coarse_kernel(own, conduct, far_a, far_b, r_a, r_b, error, source, weight, one, two):
    base = far_a.shape[0] - 64
    for x in range(8):
        after, before = y_sides(r_a, r_b, 9 * x, 8)
        b = wide_rows(own[x, 0:8, :], own[x, 8:9, :], own[x, 11:12, :], after, before)
        last_after, last_before = y_sides(r_a, r_b, 9 * x + 8, 1)
        after, before = y_sides(far_a, far_b, base + 8 * x, 8)
        after = jnp.concatenate([after[1:8], last_after], axis=0)
        before = jnp.concatenate([last_before, before[0:7]], axis=0)
        k = wide_rows(conduct[x, 0:8, :], conduct[x, 8:9, :], conduct[x, 11:12, :], after, before)
        factor = OMEGA / (MASS + 2.25 * k)
        weight[x] = k * factor
        source[x] = factor * b
    old = source
    for s in range(1, COARSE_SWEEPS):
        new = one if s % 2 else two
        for x in range(8):
            v = old[x]
            inner = along_y(v)
            if x > 0:
                inner = inner + old[x - 1]
            if x < 7:
                inner = inner + old[x + 1]
            new[x] = 0.2 * v + (source[x] + weight[x] * (COARSE_W * inner + along_z(v)))
        old = new
    for x in range(8):
        error[x, 0:8, :] = old[x, 0:8, :]
        error[x, 8:16, :] = jnp.where(upper(), old[x, 8:16, :], old[x, 24:32, :])


def shift_kernel(error, *rest):
    terms, (out, pay_a, pay_b) = rest[:-3], rest[-3:]
    sums = sum(t[...] for t in terms)
    resid = jnp.sum(sums[:, :LANES])
    load = jnp.sum(sums[:, LANES:])
    shift_c = jnp.full((16, 256), resid, F32) / jnp.full((16, 256), load, F32)
    for x in range(8):
        out[x] = error[x] + shift_c
    for k in range(2):
        send_x(pay_a, pay_b, k, out[k], out[6 + k])


def squeeze(tile):
    return jnp.where(iota((8, 256), 0) < 2, tile, pltpu.roll(tile, 4, 0))


def spread_coarse(plane, room):
    return jnp.concatenate([twice(plane[0:8], room.at[0]), twice(squeeze(plane[8:16]), room.at[1])[0:8]], axis=0)


def spread_mid(plane, room):
    parts = [twice(plane[0:8], room.at[0]), twice(plane[8:16], room.at[1]), twice(squeeze(plane[16:24]), room.at[2])[0:8]]
    return jnp.concatenate(parts, axis=0)


def smoothed(before, v, after, weight, source, w):
    inner = (before + after) + along_y(v)
    return source + (0.2 * v + weight * (w * inner + along_z(v)))


def finish_inner_kernel(
    error, mid_two, mid_source, mid_weight, fine_two, fine_source, fine_weight,
    out, zero, one, fine_one, fine_last, two, dup, dup_2, result, sems,
):
    n = mid_two.shape[0]
    nf = fine_two.shape[0]
    for c in range(8):
        spread = spread_coarse(error[c], dup.at[c])
        for x in (2 * c + HALO, 2 * c + 1 + HALO):
            zero[x] = jnp.where(mid_weight[x] > 0.0, mid_two[x] + spread, 0.0)

    def sweep_mid(x, old, new):
        new[x] = smoothed(old[x - 1], old[x], old[x + 1], mid_weight[x], mid_source[x], 0.25)

    for x in range(HALO + 1, n - HALO - 1):
        sweep_mid(x, zero, one)
    for x in range(HALO + 2, n - HALO - 2):
        sweep_mid(x, one, two)

    def lift(m):
        spread = spread_mid(two[m], dup_2.at[m])
        x = 2 * m - HALO
        fine_one[x] = fine_two[x] + spread
        fine_one[x + 1] = fine_two[x + 1] + spread

    loop(HALO + 2, n - HALO - 2, lift, 6)

    def sweep_one(x):
        fine_last[x] = smoothed(fine_one[x - 1], fine_one[x], fine_one[x + 1], fine_weight[x], fine_source[x], 1.0)

    low, high = 2 * HALO + 1, nf - 2 * HALO - 1
    loop(low, high, sweep_one, 11)
    copies = []
    low, high = low + 1, high - 1
    for j in range(2):
        mid = low + (high - low) // 2
        for x in range(low, mid) if j == 0 else range(mid, high):
            v = smoothed(fine_last[x - 1], fine_last[x], fine_last[x + 1], fine_weight[x], fine_source[x], 1.0)
            result[x - HALO] = v[0:32, :]
        rows = pl.ds(low - HALO, mid - low) if j == 0 else pl.ds(mid - HALO, high - mid)
        copies.append(pltpu.make_async_copy(result.at[rows], out.at[rows], sems.at[j]))
        copies[-1].start()
    for c in copies:
        c.wait()


def finish_edge_kernel(
    x_a, x_b, mid_two, mid_source, mid_weight, fine_two, edge_two, fine_source, edge_source, fine_weight,
    zero, one, fine_one, fine_last, begun, out, zero_edge, one_edge, fine_edge, last_edge, dup, dup_2, result, sems,
):
    n = mid_two.shape[0]
    nf = fine_two.shape[0]
    nx = nf - 2 * HALO
    copies = []
    planes = x_sides(x_a, x_b, slice(0, 2))
    for side in (0, 1):
        sign = 1 if side == 0 else -1
        at = lambda k, side=side: HALO + k if side == 0 else n - HALO - 1 - k
        fine = lambda k, side=side: HALO + k if side == 0 else nf - HALO - 1 - k
        base = 8 * side + (0 if side == 0 else HALO - HALO - nx)
        for c in range(2):
            plane = planes[1 - side][c]
            spread = spread_coarse(plane, dup.at[2 * side + c])
            first = 2 * c if side == 0 else n - HALO + 2 * c
            for x in (first, first + 1):
                zero_edge[x] = jnp.where(mid_weight[x] > 0.0, mid_two[x] + spread, 0.0)

        def zero_of(k):
            return zero[at(k)] if k >= 0 else zero_edge[at(k)]

        def one_of(k):
            return one[at(k)] if k >= 1 else one_edge[at(k)]

        for k in range(-2, 1):
            x = at(k)
            one_edge[x] = smoothed(zero_of(k - 1), zero_of(k), zero_of(k + 1), mid_weight[x], mid_source[x], 0.25)
        for k in range(-1, 2):
            x = at(k)
            value = smoothed(one_of(k - 1), one_of(k), one_of(k + 1), mid_weight[x], mid_source[x], 0.25)
            spread = spread_mid(value, dup_2.at[3 * side + k + 1])
            for f in (fine(2 * k), fine(2 * k + 1)):
                inside = HALO < f < nf - HALO - 1
                before = fine_two[f] if inside else edge_two[base + f]
                fine_edge[f] = before + spread

        def fine_of(k):
            return fine_one[fine(k)] if k >= 4 else fine_edge[fine(k)]

        def last_of(k):
            return fine_last[fine(k)] if k >= 5 else last_edge[fine(k)]

        for k in range(-1, 5):
            f = fine(k)
            source = fine_source[f] if HALO <= f < nf - HALO else edge_source[base + f]
            last_edge[f] = smoothed(fine_of(k - 1), fine_of(k), fine_of(k + 1), fine_weight[f], source, 1.0)
        for k in range(6):
            f = fine(k)
            v = smoothed(last_of(k - 1), last_of(k), last_of(k + 1), fine_weight[f], fine_source[f], 1.0)
            result[f - HALO] = v[0:32, :]
        rows = pl.ds(0, 6) if side == 0 else pl.ds(nx - 6, 6)
        copies.append(pltpu.make_async_copy(result.at[rows], out.at[rows], sems.at[side]))
        copies[-1].start()
    for c in copies:
        c.wait()


def both_ways(pairs):
    return pairs + [(j, i) for i, j in pairs]


def swap(pay_a, pay_b, axis):
    size = lax.axis_size(axis)
    pairs_a = [(i, i + 1) for i in range(1, size - 1, 2)]
    pairs_b = [(i, i + 1) for i in range(0, size - 1, 2)]
    return lax.ppermute(pay_a, axis, both_ways(pairs_a)), lax.ppermute(pay_b, axis, both_ways(pairs_b))


def exchange(value, distance):
    return lax.ppermute(value, "dev", [(i, i ^ distance) for i in range(lax.axis_size("dev"))])


def body(conc_old, phi_old, solid_pot, phase_label, iface_block, iface_owner):
    peers = lax.axis_size("dev")
    nx = conc_old.shape[0]
    half = nx // 2
    quarter = nx // 4
    ext = (nx + 2 * HALO, nx + 2 * HALO, 256)
    ext_mid = (half + 2 * HALO, half + 2 * HALO, 256)
    token_shape = shaped(8, LANES)

    pay_a, pay_b, own_lists = call(
        first_pack_kernel,
        [shaped(7 * nx, 256)] * 2 + [shaped(8, 256)],
        [conc_old, phase_label, iface_owner.reshape(1, -1), iface_block],
        [vmem(nx, HALO, 256)] * 2
        + [pltpu.VMEM((nx, HALO, 256), jnp.int32)] * 2
        + [pltpu.VMEM((1, 256), jnp.int32)] * 2
        + [pltpu.SemaphoreType.DMA((6,))],
        in_specs=[FAR] * 4,
        limit=VMEM_MOST,
        name="first_pack",
    )
    y_a, y_b = swap(pay_a, pay_b, "dev")
    conduct_mid, conduct_coarse, pay_a, pay_b, lists, gain, base = call(
        own_kernel,
        [shaped(half, half, 256), shaped(quarter, quarter, 256), shaped(24, 8, 256), shaped(24, 8, 256)]
        + [shaped(2, 256), shaped(nx, nx, 256), shaped(nx, nx, 256)],
        [conc_old, phase_label, phi_old, own_lists],
        [vmem(half, 2, nx, LANES), vmem(quarter, 2, half, LANES)],
        name="own",
    )
    xx_a, xx_b = swap(pay_a, pay_b, "grp")
    lists = jnp.concatenate([lists] + [exchange(lists, distance) for distance in range(peers - 2, 0, -2)], axis=0)
    far_rows = second_rows(nx)[1]
    far_pay = call(
        second_pack_kernel,
        [shaped(far_rows, 256)] * 2,
        [phi_old, conduct_mid, xx_a, xx_b],
        name="second_pack",
    )
    yy_a, yy_b = swap(*far_pay, "dev")
    pay_a, pay_b = call(
        first_pack_x_kernel,
        [shaped(35, 8, 256)] * 2,
        [conc_old, phase_label, y_a, y_b, lists],
        name="first_pack_x",
    )
    x_a, x_b = swap(pay_a, pay_b, "grp")

    ext_y = (nx, nx + 2 * HALO, 256)
    zero, first, second, third, gain_far, base_far, conc_inner, flux_inner = call(
        sweeps_inner_kernel,
        [shaped(*ext_y)] * 4 + [shaped(nx, 8, 256)] * 2 + [shaped(nx, nx, 256)] * 2,
        [conc_old, phase_label, phi_old, solid_pot, gain, base, y_a, y_b],
        name="sweeps_inner",
    )
    edge_args = [x_a, x_b, phase_label, phi_old, solid_pot, gain, base, zero, first, second, third]
    conc_new, flux_all, pay_a, pay_b = call(
        sweeps_edge_kernel,
        [shaped(nx, nx, 256), shaped(nx, nx, 256), shaped(3 * nx, 256), shaped(3 * nx + peers, 256)],
        edge_args + [gain_far, base_far, conc_inner, flux_inner, lists],
        [vmem(16, nx + 2 * HALO, 256)] * 4,
        name="sweeps_edge",
    )
    f_a, f_b = swap(pay_a, pay_b, "dev")
    flux_own, halo_mask = call(
        mask_kernel,
        [shaped(nx, nx, 256), shaped(nx, 8, 256)],
        [flux_all, lists, f_b, yy_a, yy_b],
        [vmem(3, nx, 8, LANES)],
        name="mask",
    )
    weight, scale, made = call(
        ready_kernel,
        [shaped(*ext)] * 2 + [token_shape],
        [conc_old, phase_label, y_a, y_b, x_a, x_b],
        name="ready",
    )
    pay_a, pay_b = call(
        flux_pack_x_kernel, [shaped(15, 8, 256)] * 2, [flux_own, f_a, f_b, halo_mask, made], name="flux_pack_x"
    )
    fx_a, fx_b = swap(pay_a, pay_b, "grp")
    fine_two, fine_source, fine_first, inner_mid, field = call(
        potential_inner_kernel,
        [shaped(*ext)] * 3 + [shaped(half, half, 256), shaped(*ext)],
        [flux_own, halo_mask, f_a, f_b, phi_old, yy_a, yy_b, xx_a, xx_b, weight, scale],
        [vmem(nx, 8, 256), vmem(half, 2, nx, LANES)],
        name="potential_inner",
    )
    edge = (16, nx + 2 * HALO, 256)
    edge_two, edge_source, source_mid, pay_a, pay_b = call(
        potential_edge_kernel,
        [shaped(*edge), shaped(*edge), shaped(half, half, 256)] + [shaped(4 * half + 64, 256)] * 2,
        [fx_a, fx_b, weight, scale, field, fine_two, fine_source, fine_first, inner_mid, conduct_coarse],
        [vmem(*edge), vmem(2, 2, nx, LANES)],
        name="potential_edge",
    )
    m_a, m_b = swap(pay_a, pay_b, "dev")
    concentration, flux, stored = call(
        store_kernel,
        [shaped(nx, nx, 256), shaped(nx, nx, 256), token_shape],
        [conc_new, flux_own],
        [pltpu.SemaphoreType.DMA((8,))],
        out_specs=[FAR, FAR, WHOLE],
        name="store",
    )
    wide = (quarter, 32, 256)
    rho, load = call(
        coarse_ready_kernel,
        [shaped(quarter, quarter, 256), shaped(8, LANES)],
        [conduct_coarse, m_a, m_b],
        [vmem(*wide)] * 4,
        name="coarse_ready",
    )
    pay_a, pay_b = call(
        mid_pack_x_kernel, [shaped(3 * HALO, 8, 256)] * 2, [source_mid, m_a, m_b, stored], name="mid_pack_x"
    )
    mx_a, mx_b = swap(pay_a, pay_b, "grp")
    mid_two, mid_source, mid_weight, source_coarse, wide_coarse, pay_a, pay_b, sums = call(
        mid_kernel,
        [shaped(*ext_mid)] * 3
        + [shaped(quarter, 12, 256), shaped(quarter, 12, 256), shaped(72, 256), shaped(80, 256), shaped(8, 256)],
        [source_mid, conduct_mid, yy_a, yy_b, xx_a, xx_b, m_a, m_b, mx_a, mx_b, rho, load],
        [vmem(*ext_mid)] * 2 + [vmem(8, 2, half + 2 * HALO, LANES)] * 2,
        name="middle",
    )
    c_a, c_b = swap(pay_a, pay_b, "dev")
    sums = sums + c_b[72:80]
    others = [exchange(sums, distance) for distance in range(peers - 2, 0, -2)]
    (error,) = call(
        coarse_kernel,
        [shaped(8, 16, 256)],
        [source_coarse, wide_coarse, m_a, m_b, c_a, c_b],
        [vmem(*wide)] * 4,
        name="coarse",
    )
    error, pay_a, pay_b = call(
        shift_kernel, [shaped(8, 16, 256), shaped(2, 16, 256), shaped(2, 16, 256)], [error, sums] + others, name="shift"
    )
    e_a, e_b = swap(pay_a, pay_b, "grp")
    begun, zero, one, fine_one, fine_last = call(
        finish_inner_kernel,
        [shaped(nx, nx, 256), shaped(*ext_mid), shaped(*ext_mid), shaped(*ext), shaped(*ext)],
        [error, mid_two, mid_source, mid_weight, fine_two, fine_source, weight],
        [vmem(*ext_mid), vmem(8, 2, 2, 16, LANES), vmem(half + 2 * HALO, 3, 2, 16, LANES), vmem(nx, nx, 256)]
        + [pltpu.SemaphoreType.DMA((2,))],
        out_specs=[FAR] + [WHOLE] * 4,
        name="finish_inner",
    )
    finish_args = [e_a, e_b, mid_two, mid_source, mid_weight, fine_two, edge_two, fine_source, edge_source, weight]
    finish_args += [zero, one, fine_one, fine_last, begun]
    (potential,) = call(
        finish_edge_kernel,
        [shaped(nx, nx, 256)],
        finish_args,
        [vmem(*ext_mid), vmem(*ext_mid), vmem(*ext), vmem(*ext)]
        + [vmem(4, 2, 2, 16, LANES), vmem(6, 3, 2, 16, LANES), vmem(nx, nx, 256)]
        + [pltpu.SemaphoreType.DMA((2,))],
        in_specs=[WHOLE] * (len(finish_args) - 1) + [FAR],
        out_specs=[FAR],
        aliases={len(finish_args) - 1: 0},
        name="finish_edge",
    )
    return (concentration, flux, potential)


def solution(mesh):
    brick = P("grp", "dev", None)
    return jax.shard_map(
        body,
        mesh=mesh,
        in_specs=(brick, brick, brick, brick, P("grp", "dev"), brick),
        out_specs=(brick, brick, brick),
        check_vma=False,
    )
```

```python
import jax
import jax.numpy as jnp
from jax import lax
from jax.experimental import pallas as pl
from jax.experimental.pallas import tpu as pltpu
from jax.sharding import PartitionSpec as P


F32 = jnp.float32
MASS = 0.05
OMEGA = 0.8
DIFFUSION_TABLE = (1.5, 0.1, 0.4)
RATIO_TABLE = tuple(d / (1.0 + 6.0 * d) for d in DIFFUSION_TABLE)
INVERSE_TABLE = tuple(1.0 / (1.0 + 6.0 * d) for d in DIFFUSION_TABLE)
CONDUCT_TABLE = (1.0, 0.3, 0.6)
KINETIC_TABLE = (0.2, 1.0, 0.5)
SWEEPS = 4
COARSE_SWEEPS = 8
COARSE_NEAR = 8
HALO = 4
LANES = 128
VMEM_LIMIT = 28 * 1024 * 1024
VMEM_MOST = 58 * 1024 * 1024


def shaped(*shape):
    return jax.ShapeDtypeStruct(shape, F32)


WHOLE = pl.BlockSpec(memory_space=pltpu.VMEM)
FAR = pl.BlockSpec(memory_space=pltpu.HBM)


def call(kernel, outs, args, scratch=(), in_specs=None, out_specs=None, limit=VMEM_LIMIT, aliases=None, flops=10**6, name=None):
    size = sum(4 * a.size for a in args) + sum(4 * o.size for o in outs)
    return pl.pallas_call(
        kernel,
        out_shape=tuple(outs),
        in_specs=in_specs or [WHOLE] * len(args),
        out_specs=tuple(out_specs or [WHOLE] * len(outs)),
        scratch_shapes=list(scratch),
        input_output_aliases=aliases or {},
        compiler_params=pltpu.CompilerParams(vmem_limit_bytes=limit),
        cost_estimate=pl.CostEstimate(flops=flops, bytes_accessed=size, transcendentals=0),
        name=name,
    )(*args)


def vmem(*shape):
    return pltpu.VMEM(shape, F32)


def iota(shape, dim):
    return lax.broadcasted_iota(jnp.int32, shape, dim)


def pick(label, table):
    return jnp.where(label == 0, table[0], jnp.where(label == 1, table[1], table[2])).astype(F32)


def loop(low, high, body, unroll=8):
    steps = (high - low) // unroll

    def step(i, carry):
        for u in range(unroll):
            body(low + i * unroll + u)
        return carry

    if steps > 1:
        lax.fori_loop(0, steps, step, 0)
    else:
        steps = 0
    for x in range(low + steps * unroll, high):
        body(x)


def odd(axis):
    return lax.rem(lax.axis_index(axis), 2) == 1


def along_y(v):
    return pltpu.roll(v, 1, 0) + pltpu.roll(v, v.shape[0] - 1, 0)


def along_z(v):
    low, high = v[:, :LANES], v[:, LANES:]
    lane = iota(low.shape, 1)
    first, last = lane == 0, lane == LANES - 1
    low_up, high_up = pltpu.roll(low, 1, 1), pltpu.roll(high, 1, 1)
    low_down, high_down = pltpu.roll(low, LANES - 1, 1), pltpu.roll(high, LANES - 1, 1)
    low_sum = jnp.where(first, 0.0, low_up) + jnp.where(last, high_down, low_down)
    high_sum = jnp.where(first, low_up, high_up) + jnp.where(last, 0.0, high_down)
    return jnp.concatenate([low_sum, high_sum], axis=1)


def upper(shape=(8, 256)):
    return iota(shape, 0) < HALO


def twice(tile, scratch):
    for h in range(2):
        part = tile[:, h * LANES : (h + 1) * LANES]
        scratch[h, pl.ds(0, 8, stride=2), :] = part
        scratch[h, pl.ds(1, 8, stride=2), :] = part
    return jnp.concatenate([scratch[0], scratch[1]], axis=1)


def pair_rows(v, scratch):
    half = v.shape[0] // 2
    parts = []
    for h in range(2):
        scratch[h] = v[:, h * LANES : (h + 1) * LANES]
        parts.append(scratch[h, pl.ds(0, half, stride=2), :] + scratch[h, pl.ds(1, half, stride=2), :])
    return jnp.concatenate(parts, axis=1)


def either(flag, if_true, if_false):
    return jnp.where(flag, if_true, if_false)


def y_sides(r_a, r_b, at, count):
    flag = odd("dev")
    a, b = r_a[at : at + count, :], r_b[at : at + count, :]
    return either(flag, a, b), either(flag, b, a)


def x_sides(r_a, r_b, index):
    flag = odd("grp")
    a, b = r_a[index], r_b[index]
    return either(flag, a, b), either(flag, b, a)


def send_y(pay_a, pay_b, at, first, last):
    flag = odd("dev")
    n = first.shape[0]
    pay_a[at : at + n, :] = either(flag, last, first)
    pay_b[at : at + n, :] = either(flag, first, last)


def send_x(pay_a, pay_b, index, first, last):
    flag = odd("grp")
    pay_a[index] = either(flag, last, first)
    pay_b[index] = either(flag, first, last)


def halo_tile(after, before):
    parts = [after]
    if after.shape[0] < HALO:
        parts.append(jnp.zeros((2 * HALO - 2 * after.shape[0], after.shape[1]), F32))
    return jnp.concatenate(parts + [before], axis=0)


def first_pack_kernel(
    conc, label, owner, block, pay_a, pay_b, own_lists, c_first, c_last, l_first, l_last, own_owner, own_block, sems
):
    nx = conc.shape[0]
    copies = [pltpu.make_async_copy(owner, own_owner, sems.at[4]), pltpu.make_async_copy(block, own_block, sems.at[5])]
    for i, (ref, at, to) in enumerate(((conc, 0, c_first), (conc, 28, c_last), (label, 0, l_first), (label, 28, l_last))):
        copies.append(pltpu.make_async_copy(ref.at[:, pl.ds(at, 4), :], to, sems.at[i]))
    for c in copies:
        c.start()
    for c in copies:
        c.wait()
    named = jnp.concatenate([own_owner[...], own_block[...], jnp.zeros((6, 256), jnp.int32)], axis=0).astype(F32)
    own_lists[...] = named
    for x in range(nx):
        send_y(pay_a, pay_b, 7 * x, c_first[x], c_last[x])
        send_y(pay_a, pay_b, 7 * x + 4, l_first[x, 0:3, :].astype(F32), l_last[x, 1:4, :].astype(F32))


def own_kernel(conc, label, phi, named, mid, coarse, pay_a, pay_b, lists, gain, base, pairs, pairs_2):
    nx = conc.shape[0]
    half = nx // 2
    lists[...] = named[0:2, :]

    def coefficients(i):
        gain[i] = pick(label[i], RATIO_TABLE)
        base[i] = conc[i] * pick(label[i], INVERSE_TABLE)

    loop(0, nx, coefficients, 4)

    def coarsen(i):
        total = conc[2 * i] * pick(label[2 * i], CONDUCT_TABLE) + conc[2 * i + 1] * pick(label[2 * i + 1], CONDUCT_TABLE)
        mid[i] = 0.25 * pair_rows(total, pairs.at[i])

    loop(0, half, coarsen, 4)
    for i in range(half // 2):
        coarse[i] = 0.25 * pair_rows(mid[2 * i] + mid[2 * i + 1], pairs_2.at[i])
    for k in range(HALO):
        for t in range(4):
            rows = slice(8 * t, 8 * t + 8)
            send_x(pay_a, pay_b, 4 * k + t, phi[k, rows, :], phi[nx - HALO + k, rows, :])
        for t in range(2):
            rows = slice(8 * t, 8 * t + 8)
            send_x(pay_a, pay_b, 16 + 2 * k + t, mid[k, rows, :], mid[half - HALO + k, rows, :])


def first_pack_x_kernel(conc, label, r_a, r_b, token, pay_a, pay_b):
    nx = conc.shape[0]

    def plane(ref, k, t, offset, count):
        if t < 4:
            return ref[k, 8 * t : 8 * t + 8, :].astype(F32)
        return halo_tile(*y_sides(r_a, r_b, 7 * k + offset, count))

    for t in range(5):
        for k in range(HALO):
            send_x(pay_a, pay_b, 5 * k + t, plane(conc, k, t, 0, 4), plane(conc, nx - HALO + k, t, 0, 4))
        for k in range(3):
            send_x(pay_a, pay_b, 20 + 5 * k + t, plane(label, k, t, 4, 3), plane(label, nx - 3 + k, t, 4, 3))


def corner_rows(n, reach):
    counts = [min(HALO, k + reach) for k in range(HALO)]
    counts = counts + [HALO] * n + counts[::-1]
    return counts, [sum(counts[:i]) for i in range(len(counts))]


def second_rows(nx):
    phi, mid = (sum(corner_rows(n, reach)[0]) for n, reach in ((nx, 0), (nx // 2, 1)))
    return phi, phi + mid, phi + mid + 64


def second_pack_kernel(phi, mid, coarse, lists, x_a, x_b, pay_a, pay_b):
    nx = phi.shape[0]
    starts = second_rows(nx)

    def put(own, n, reach, index, base):
        counts, at = corner_rows(n, reach)
        tiles = own.shape[1] // 8
        for x in range(n):
            send_y(pay_a, pay_b, base + at[HALO + x], own[x, 0:4, :], own[x, 8 * tiles - 4 : 8 * tiles, :])
        for k in range(HALO):
            first_after, first_before = x_sides(x_a, x_b, index + tiles * k)
            last_after, last_before = x_sides(x_a, x_b, index + tiles * k + tiles - 1)
            for x, first, last in ((k, first_before, last_before), (HALO + n + k, first_after, last_after)):
                if counts[x]:
                    send_y(pay_a, pay_b, base + at[x], first[0 : counts[x]], last[8 - counts[x] : 8])

    put(phi, nx, 0, 0, 0)
    put(mid, nx // 2, 1, 16, starts[0])
    base = starts[1]
    for x in range(8):
        pay_a[base + 8 * x : base + 8 * x + 8, :] = coarse[x]
        pay_b[base + 8 * x : base + 8 * x + 8, :] = coarse[x]
    base = starts[2]
    pay_b[base : base + lists.shape[0], :] = lists[...]


def second_halo(r_a, r_b, n, reach, x, base):
    counts, at = corner_rows(n, reach)
    if not counts[x]:
        return jnp.zeros((8, 256), F32)
    return halo_tile(*y_sides(r_a, r_b, base + at[x], counts[x]))


def wide_rows(own, after_own, before_own, after, before):
    gap = jnp.zeros((6, 256), F32)
    return jnp.concatenate([own, after_own, after, gap, before, before_own], axis=0)


def sweeps_kernel(conc, label, gain_own, base_own, y_a, y_b, x_a, x_b, out, one, two, gain_far, base_far, gain_x, base_x):
    nx = conc.shape[0]

    def own(i):
        one[HALO + i, 0:32, :] = conc[i]

    loop(0, nx, own)
    for i in range(nx):
        c = halo_tile(*y_sides(y_a, y_b, 7 * i, 4))
        lab = halo_tile(*y_sides(y_a, y_b, 7 * i + 4, 3))
        one[HALO + i, 32:40, :] = c
        gain_far[i] = jnp.where(c > 0.0, pick(lab, RATIO_TABLE), 0.0)
        base_far[i] = c * pick(lab, INVERSE_TABLE)

    def put(x, rows, c, lab):
        one[x, rows, :] = c
        at = x if x < HALO else x - nx
        gain_x[at, rows, :] = jnp.where(c > 0.0, pick(lab, RATIO_TABLE), 0.0)
        base_x[at, rows, :] = c * pick(lab, INVERSE_TABLE)

    for t in range(5):
        rows = slice(8 * t, 8 * t + 8)
        for k in range(HALO):
            c_after, c_before = x_sides(x_a, x_b, 5 * k + t)
            l_after = x_sides(x_a, x_b, 20 + 5 * min(k, 2) + t)[0]
            l_before = x_sides(x_a, x_b, 20 + 5 * max(k - 1, 0) + t)[1]
            put(k, rows, c_before, l_before)
            put(HALO + nx + k, rows, c_after, l_after)

    def neighbours(old, x):
        mid = old[x]
        return (old[x - 1] + old[x + 1]) + (along_y(mid) + along_z(mid))

    fields = (one, two)
    for s in range(1, SWEEPS):
        old, new = fields[(s - 1) % 2], fields[s % 2]

        def sweep(i, old=old, new=new):
            gain = jnp.concatenate([gain_own[i], gain_far[i]], axis=0)
            base = jnp.concatenate([base_own[i], base_far[i]], axis=0)
            new[HALO + i] = base + gain * neighbours(old, HALO + i)

        loop(0, nx, sweep)
        for k in range(s, HALO):
            for x, at in ((k, k), (2 * HALO + nx - 1 - k, 2 * HALO - 1 - k)):
                new[x] = base_x[at] + gain_x[at] * neighbours(old, x)

    old = fields[(SWEEPS - 1) % 2]

    def last(i):
        out[i] = base_own[i] + gain_own[i] * neighbours(old, HALO + i)[0:32, :]

    loop(0, nx, last)


def flux_kernel(conc, label, phi, solid, flux, pay_a, pay_b):
    nx = conc.shape[0]

    def plane(i):
        drive = 0.5 * (solid[i] - phi[i])
        logc = jnp.log(conc[i])
        value = jnp.exp(drive + 0.4 * logc) - jnp.exp(0.6 * logc - drive)
        flux[i] = pick(label[i], KINETIC_TABLE) * value

    loop(0, nx, plane, 4)
    for x in range(nx):
        send_y(pay_a, pay_b, 3 * x, flux[x, 0:3, :], flux[x, 29:32, :])


def mask_kernel(flux_all, lists, far, flux, halo_mask, marked):
    nx = flux_all.shape[0]
    rows = lists.shape[0]
    pieces = [lists[i : i + 1, :] for i in range(rows)] + [far[i : i + 1, :] for i in range(far.shape[0] - rows, far.shape[0])]
    owner = jnp.concatenate(pieces[0::2], axis=1).astype(jnp.int32)
    block = jnp.concatenate(pieces[1::2], axis=1).astype(jnp.int32)
    entries = owner.shape[1]
    hit_column = (iota((64, entries), 0) == lax.rem(block, 64)).astype(jnp.bfloat16)
    reach = owner - lax.axis_index("dev") + 1
    at_row = jnp.where((reach >= 0) & (reach < 3), reach * nx + lax.shift_right_arithmetic(block, 6), -1)
    hit_row = (iota((3 * nx, entries), 0) == at_row).astype(jnp.bfloat16)
    named = lax.dot_general(hit_row, hit_column, (((1,), (1,)), ((), ())), preferred_element_type=F32)
    named = jnp.concatenate([named, jnp.zeros((3 * nx, LANES - 64), F32)], axis=1)
    for j in range(3):
        for i in range(nx):
            marked[j, i] = jnp.broadcast_to(named[j * nx + i : j * nx + i + 1, :], (8, LANES))
    is_row = lax.div(iota((32, LANES), 1), 2) == iota((32, LANES), 0)
    row, pair = iota((8, LANES), 0), lax.div(iota((8, LANES), 1), 2)
    is_after = (row < 3) & (pair == row)
    is_before = (row >= 5) & (pair == row + 24)
    spread = (lax.rem(iota((LANES, 256), 0), 2) == lax.div(iota((LANES, 256), 1), LANES)).astype(jnp.bfloat16)

    def plane(i):
        marks = jnp.where(is_row, jnp.concatenate([marked[1, i]] * 4, axis=0), 0.0)
        beyond = jnp.where(is_after, marked[2, i], jnp.where(is_before, marked[0, i], 0.0))
        marks = jnp.concatenate([marks, beyond], axis=0).astype(jnp.bfloat16)
        listed = jnp.dot(marks, spread, preferred_element_type=F32) > 0.5
        flux[i] = jnp.where(listed[0:32], flux_all[i], 0.0)
        halo_mask[i] = jnp.where(listed[32:40], 1.0, 0.0)

    loop(0, nx, plane, 16)


def store_kernel(conc, flux, conc_out, flux_out, token, sems):
    copies = []
    for i, (ref, to) in enumerate(((conc, conc_out), (flux, flux_out))):
        for j in range(4):
            rows = pl.ds(8 * j, 8)
            copies.append(pltpu.make_async_copy(ref.at[rows], to.at[rows], sems.at[4 * i + j]))
            copies[-1].start()
    token[...] = jnp.zeros(token.shape, F32)
    for c in copies:
        c.wait()


def ready_kernel(conc, label, y_a, y_b, x_a, x_b, weight, scale, token):
    nx = conc.shape[0]
    token[...] = jnp.zeros(token.shape, F32)

    def put(x, rows, c, lab):
        conduct = c * pick(lab, CONDUCT_TABLE)
        factor = OMEGA / (MASS + 6.0 * conduct)
        weight[x, rows, :] = conduct * factor
        scale[x, rows, :] = factor

    def own(i):
        put(HALO + i, slice(0, 32), conc[i], label[i])

    loop(0, nx, own, 4)
    for i in range(nx):
        c = halo_tile(*y_sides(y_a, y_b, 7 * i, 4))
        lab = halo_tile(*y_sides(y_a, y_b, 7 * i + 4, 3))
        put(HALO + i, slice(32, 40), c, lab)
    for t in range(5):
        rows = slice(8 * t, 8 * t + 8)
        for k in range(HALO):
            c_after, c_before = x_sides(x_a, x_b, 5 * k + t)
            l_after = x_sides(x_a, x_b, 20 + 5 * min(k, 2) + t)[0]
            l_before = x_sides(x_a, x_b, 20 + 5 * max(k - 1, 0) + t)[1]
            put(k, rows, c_before, l_before)
            put(HALO + nx + k, rows, c_after, l_after)


def place_phi(phi, yy_a, yy_b, xx_a, xx_b, field):
    nx = phi.shape[0]

    def own(i):
        field[HALO + i, 0:32, :] = phi[i]

    loop(0, nx, own)
    for x in range(nx + 2 * HALO):
        field[x, 32:40, :] = second_halo(yy_a, yy_b, nx, 0, x, 0)
    for t in range(4):
        for k in range(HALO):
            after, before = x_sides(xx_a, xx_b, 4 * k + t)
            field[k, 8 * t : 8 * t + 8, :] = before
            field[HALO + nx + k, 8 * t : 8 * t + 8, :] = after


def flux_pack_x_kernel(flux, r_a, r_b, mask, token, pay_a, pay_b):
    nx = flux.shape[0]

    def tile(x, t):
        if t < 4:
            return flux[x, 8 * t : 8 * t + 8, :]
        return mask[x] * halo_tile(*y_sides(r_a, r_b, 3 * x, 3))

    for k in range(3):
        for t in range(5):
            send_x(pay_a, pay_b, 5 * k + t, tile(k, t), tile(nx - 3 + k, t))


def first_sweep(field, weight, scale, x, rows, flux):
    p = field[x]
    near = (field[x - 1] + field[x + 1]) + (along_y(p) + along_z(p))
    b = scale[x, rows, :] * (MASS * p[rows, :] + flux)
    return b, 0.2 * p[rows, :] + weight[x, rows, :] * near[rows, :] + b


def potential_inner_kernel(
    flux, mask, y_a, y_b, phi, yy_a, yy_b, xx_a, xx_b, weight, scale, after_two, source, first, source_mid, field, far, pairs
):
    nx = flux.shape[0]
    place_phi(phi, yy_a, yy_b, xx_a, xx_b, field)
    for i in range(nx):
        far[i] = mask[i] * halo_tile(*y_sides(y_a, y_b, 3 * i, 3))

    def own(i):
        x = HALO + i
        f = jnp.concatenate([flux[i], far[i]], axis=0)
        source[x], first[x] = first_sweep(field, weight, scale, x, slice(0, 40), f)

    loop(0, nx, own)

    def around(values, x):
        v = values[x]
        return v, weight[x] * ((values[x - 1] + values[x + 1]) + (along_y(v) + along_z(v)))

    def sweep(x):
        v, near = around(first, x)
        after_two[x] = 0.2 * v + (source[x] + near)

    loop(HALO + 1, HALO + nx - 1, sweep)

    def remainder(x):
        v, near = around(after_two, x)
        return ((source[x] - OMEGA * v) + near)[0:32, :] / scale[x, 0:32, :]

    def coarsen(i):
        x = HALO + 2 * i
        source_mid[i] = 0.25 * pair_rows(remainder(x) + remainder(x + 1), pairs.at[i])

    loop(1, nx // 2 - 1, coarsen, 4)


def potential_edge_kernel(
    x_a, x_b, weight, scale, field, inner_two, inner_source, inner_first, inner_mid,
    edge_two, edge_source, source_mid, pay_a, pay_b, first, pairs,
):
    half = source_mid.shape[0]
    nx = 2 * half
    for side, face in ((0, HALO), (1, HALO + nx)):
        base = 8 * side + HALO - face
        for k in range(3):
            x = face - 3 + k if side == 0 else face + k
            f = jnp.concatenate([x_sides(x_a, x_b, 5 * k + t)[1 - side] for t in range(5)], axis=0)
            edge_source[base + x], first[base + x] = first_sweep(field, weight, scale, x, slice(0, 40), f)

        def first_of(x, base=base):
            return inner_first[x] if HALO <= x < HALO + nx else first[base + x]

        def source_of(x, base=base):
            return inner_source[x] if HALO <= x < HALO + nx else edge_source[base + x]

        def two_of(x, base=base):
            return inner_two[x] if HALO < x < HALO + nx - 1 else edge_two[base + x]

        for x in range(face - 2, face + 1) if side == 0 else range(face - 1, face + 2):
            v = first_of(x)
            near = weight[x] * ((first_of(x - 1) + first_of(x + 1)) + (along_y(v) + along_z(v)))
            edge_two[base + x] = 0.2 * v + (source_of(x) + near)
        total = 0.0
        at = face if side == 0 else face - 2
        for x in (at, at + 1):
            v = two_of(x)
            near = weight[x] * ((two_of(x - 1) + two_of(x + 1)) + (along_y(v) + along_z(v)))
            total = total + ((source_of(x) - OMEGA * v) + near)[0:32, :] / scale[x, 0:32, :]
        source_mid[0 if side == 0 else half - 1] = 0.25 * pair_rows(total, pairs.at[side])
    for x in range(1, half - 1):
        source_mid[x] = inner_mid[x]
    for x in range(half):
        send_y(pay_a, pay_b, 4 * x, source_mid[x, 0:4, :], source_mid[x, 12:16, :])


def mid_pack_x_kernel(field, r_a, r_b, token, token_2, pay_a, pay_b):
    n = field.shape[0]

    def tile(x, t):
        if t < 2:
            return field[x, 8 * t : 8 * t + 8, :]
        return halo_tile(*y_sides(r_a, r_b, 4 * x, 4))

    for k in range(HALO):
        for t in range(3):
            send_x(pay_a, pay_b, 3 * k + t, tile(k, t), tile(n - HALO + k, t))


def mid_kernel(
    source_own, conduct_own, yy_a, yy_b, xx_a, xx_b, y_a, y_b, x_a, x_b, rho, load,
    after_two, source, weight, coarse, conduct, pay_a, pay_b, part, scale, mid_conduct, pairs, pairs_2,
):
    n = source_own.shape[0]
    base = second_rows(2 * n)[0]

    def put(x, rows, b, k):
        factor = OMEGA / (MASS + 3.0 * k)
        weight[x, rows, :] = k * factor
        scale[x, rows, :] = factor
        source[x, rows, :] = factor * b
        mid_conduct[x, rows, :] = k

    def far(x):
        return second_halo(yy_a, yy_b, n, 1, x, base)

    for i in range(n):
        put(HALO + i, slice(0, 16), source_own[i], conduct_own[i])
        put(HALO + i, slice(16, 24), halo_tile(*y_sides(y_a, y_b, 4 * i, 4)), far(HALO + i))
    for k in range(HALO):
        for t in range(3):
            rows = slice(8 * t, 8 * t + 8)
            b_after, b_before = x_sides(x_a, x_b, 3 * k + t)
            if t < 2:
                c_after, c_before = x_sides(xx_a, xx_b, 16 + 2 * k + t)
            else:
                c_after, c_before = far(HALO + n + k), far(k)
            put(k, rows, b_before, c_before)
            put(HALO + n + k, rows, b_after, c_after)

    def around(values, x):
        v = values[x]
        return v, weight[x] * (0.25 * ((values[x - 1] + values[x + 1]) + along_y(v)) + along_z(v))

    def sweep(x):
        v, near = around(source, x)
        after_two[x] = 0.2 * v + (source[x] + near)

    loop(1, n + 2 * HALO - 1, sweep, 11)

    def remainder(x):
        v, near = around(after_two, x)
        return ((source[x] - OMEGA * v) + near) / scale[x]

    total = jnp.zeros((8, 256), F32)
    for i in range(n // 2):
        x = HALO + 2 * i
        value = 0.25 * pair_rows(remainder(x) + remainder(x + 1), pairs.at[i])
        k = 0.25 * pair_rows(mid_conduct[x] + mid_conduct[x + 1], pairs_2.at[i])
        coarse[i] = value
        conduct[i] = k
        send_y(pay_a, pay_b, 9 * i, value[1:9], jnp.concatenate([value[11:12], value[0:7]], axis=0))
        send_y(pay_a, pay_b, 9 * i + 8, k[8:9], k[11:12])
        total += rho[i] * value[0:8]
    sums = jnp.concatenate([total[:, :LANES] + total[:, LANES:], load[...]], axis=1)
    part[...] = sums


COARSE_W = 0.0625


def coarse_ready_kernel(own, r_a, r_b, rho, load, token, one, two, conduct, scale):
    token[...] = jnp.zeros(token.shape, F32)
    base = r_a.shape[0] - 64
    for x in range(8):
        after, before = y_sides(r_a, r_b, base + 8 * x, 8)
        k = jnp.concatenate([own[x], after, jnp.zeros((8, 256), F32), before], axis=0)
        conduct[x] = k
        scale[x] = OMEGA / (MASS + 2.25 * k)
        one[x] = jnp.ones(k.shape, F32)
    fields = (one, two)
    for s in range(COARSE_SWEEPS):
        old, new = fields[s % 2], fields[(s + 1) % 2]
        for x in range(8):
            near = [conduct[i] * old[i] if 0 <= i < 8 else None for i in (x - 1, x, x + 1)]
            inner = along_y(near[1])
            for other in (near[0], near[2]):
                if other is not None:
                    inner = inner + other
            new[x] = 0.2 * old[x] + scale[x] * (COARSE_W * inner + along_z(near[1]))
    last = fields[COARSE_SWEEPS % 2]
    peer, peers = lax.axis_index("dev"), lax.axis_size("dev")
    row, z = iota((8, 256), 0), iota((8, 256), 1)
    edge_y = ((row == 0) & (peer == 0)) | ((row == 7) & (peer == peers - 1))
    edge = edge_y.astype(F32) * COARSE_W + ((z == 0) | (z == 255)).astype(F32)
    total = jnp.zeros((8, 256), F32)
    for x in range(8):
        rho[x] = last[x, 0:8, :]
        total += MASS + own[x] * (edge + (COARSE_W if x in (0, 7) else 0.0))
    load[...] = total[:, :LANES] + total[:, LANES:]


def late_kernel(pay, token, out):
    out[...] = pay[...]


def coarse_kernel(own, conduct, far_a, far_b, r_a, r_b, error, source, weight, one, two):
    base = far_a.shape[0] - 64
    for x in range(8):
        after, before = y_sides(r_a, r_b, 9 * x, 8)
        b = wide_rows(own[x, 0:8, :], own[x, 8:9, :], own[x, 11:12, :], after, before)
        last_after, last_before = y_sides(r_a, r_b, 9 * x + 8, 1)
        after, before = y_sides(far_a, far_b, base + 8 * x, 8)
        after = jnp.concatenate([after[1:8], last_after], axis=0)
        before = jnp.concatenate([last_before, before[0:7]], axis=0)
        k = wide_rows(conduct[x, 0:8, :], conduct[x, 8:9, :], conduct[x, 11:12, :], after, before)
        factor = OMEGA / (MASS + 2.25 * k)
        weight[x] = k * factor
        source[x] = factor * b
    old = source
    for s in range(1, COARSE_SWEEPS):
        new = one if s % 2 else two
        for x in range(8):
            v = old[x]
            inner = along_y(v)
            if x > 0:
                inner = inner + old[x - 1]
            if x < 7:
                inner = inner + old[x + 1]
            new[x] = 0.2 * v + (source[x] + weight[x] * (COARSE_W * inner + along_z(v)))
        old = new
    for x in range(8):
        error[x, 0:8, :] = old[x, 0:8, :]
        error[x, 8:16, :] = jnp.where(upper(), old[x, 8:16, :], old[x, 24:32, :])


def shift_kernel(error, sums_own, sums_other, out, pay_a, pay_b):
    sums = sums_own[...] + sums_other[...]
    resid = jnp.sum(sums[:, :LANES])
    load = jnp.sum(sums[:, LANES:])
    shift_c = jnp.full((16, 256), resid, F32) / jnp.full((16, 256), load, F32)
    for x in range(8):
        out[x] = error[x] + shift_c
    for k in range(2):
        send_x(pay_a, pay_b, k, out[k], out[6 + k])


def squeeze(tile):
    return jnp.where(iota((8, 256), 0) < 2, tile, pltpu.roll(tile, 4, 0))


def spread_coarse(plane, room):
    return jnp.concatenate([twice(plane[0:8], room.at[0]), twice(squeeze(plane[8:16]), room.at[1])[0:8]], axis=0)


def spread_mid(plane, room):
    parts = [twice(plane[0:8], room.at[0]), twice(plane[8:16], room.at[1]), twice(squeeze(plane[16:24]), room.at[2])[0:8]]
    return jnp.concatenate(parts, axis=0)


def smoothed(before, v, after, weight, source, w):
    inner = (before + after) + along_y(v)
    return source + (0.2 * v + weight * (w * inner + along_z(v)))


def finish_inner_kernel(
    error, mid_two, mid_source, mid_weight, fine_two, fine_source, fine_weight,
    out, zero, one, fine_one, fine_last, two, dup, dup_2, result, sems,
):
    n = mid_two.shape[0]
    nf = fine_two.shape[0]
    for c in range(8):
        spread = spread_coarse(error[c], dup.at[c])
        for x in (2 * c + HALO, 2 * c + 1 + HALO):
            zero[x] = jnp.where(mid_weight[x] > 0.0, mid_two[x] + spread, 0.0)

    def sweep_mid(x, old, new):
        new[x] = smoothed(old[x - 1], old[x], old[x + 1], mid_weight[x], mid_source[x], 0.25)

    for x in range(HALO + 1, n - HALO - 1):
        sweep_mid(x, zero, one)
    for x in range(HALO + 2, n - HALO - 2):
        sweep_mid(x, one, two)

    def lift(m):
        spread = spread_mid(two[m], dup_2.at[m])
        x = 2 * m - HALO
        fine_one[x] = fine_two[x] + spread
        fine_one[x + 1] = fine_two[x + 1] + spread

    loop(HALO + 2, n - HALO - 2, lift, 6)

    def sweep_one(x):
        fine_last[x] = smoothed(fine_one[x - 1], fine_one[x], fine_one[x + 1], fine_weight[x], fine_source[x], 1.0)

    low, high = 2 * HALO + 1, nf - 2 * HALO - 1
    loop(low, high, sweep_one, 11)
    copies = []
    low, high = low + 1, high - 1
    for j in range(2):
        mid = low + (high - low) // 2
        for x in range(low, mid) if j == 0 else range(mid, high):
            v = smoothed(fine_last[x - 1], fine_last[x], fine_last[x + 1], fine_weight[x], fine_source[x], 1.0)
            result[x - HALO] = v[0:32, :]
        rows = pl.ds(low - HALO, mid - low) if j == 0 else pl.ds(mid - HALO, high - mid)
        copies.append(pltpu.make_async_copy(result.at[rows], out.at[rows], sems.at[j]))
        copies[-1].start()
    for c in copies:
        c.wait()


def finish_edge_kernel(
    x_a, x_b, mid_two, mid_source, mid_weight, fine_two, edge_two, fine_source, edge_source, fine_weight,
    zero, one, fine_one, fine_last, begun, out, zero_edge, one_edge, fine_edge, last_edge, dup, dup_2, result, sems,
):
    n = mid_two.shape[0]
    nf = fine_two.shape[0]
    nx = nf - 2 * HALO
    copies = []
    planes = x_sides(x_a, x_b, slice(0, 2))
    for side in (0, 1):
        sign = 1 if side == 0 else -1
        at = lambda k, side=side: HALO + k if side == 0 else n - HALO - 1 - k
        fine = lambda k, side=side: HALO + k if side == 0 else nf - HALO - 1 - k
        base = 8 * side + (0 if side == 0 else HALO - HALO - nx)
        for c in range(2):
            plane = planes[1 - side][c]
            spread = spread_coarse(plane, dup.at[2 * side + c])
            first = 2 * c if side == 0 else n - HALO + 2 * c
            for x in (first, first + 1):
                zero_edge[x] = jnp.where(mid_weight[x] > 0.0, mid_two[x] + spread, 0.0)

        def zero_of(k):
            return zero[at(k)] if k >= 0 else zero_edge[at(k)]

        def one_of(k):
            return one[at(k)] if k >= 1 else one_edge[at(k)]

        for k in range(-2, 1):
            x = at(k)
            one_edge[x] = smoothed(zero_of(k - 1), zero_of(k), zero_of(k + 1), mid_weight[x], mid_source[x], 0.25)
        for k in range(-1, 2):
            x = at(k)
            value = smoothed(one_of(k - 1), one_of(k), one_of(k + 1), mid_weight[x], mid_source[x], 0.25)
            spread = spread_mid(value, dup_2.at[3 * side + k + 1])
            for f in (fine(2 * k), fine(2 * k + 1)):
                inside = HALO < f < nf - HALO - 1
                before = fine_two[f] if inside else edge_two[base + f]
                fine_edge[f] = before + spread

        def fine_of(k):
            return fine_one[fine(k)] if k >= 4 else fine_edge[fine(k)]

        def last_of(k):
            return fine_last[fine(k)] if k >= 5 else last_edge[fine(k)]

        for k in range(-1, 5):
            f = fine(k)
            source = fine_source[f] if HALO <= f < nf - HALO else edge_source[base + f]
            last_edge[f] = smoothed(fine_of(k - 1), fine_of(k), fine_of(k + 1), fine_weight[f], source, 1.0)
        for k in range(6):
            f = fine(k)
            v = smoothed(last_of(k - 1), last_of(k), last_of(k + 1), fine_weight[f], fine_source[f], 1.0)
            result[f - HALO] = v[0:32, :]
        rows = pl.ds(0, 6) if side == 0 else pl.ds(nx - 6, 6)
        copies.append(pltpu.make_async_copy(result.at[rows], out.at[rows], sems.at[side]))
        copies[-1].start()
    for c in copies:
        c.wait()


def both_ways(pairs):
    return pairs + [(j, i) for i, j in pairs]


def swap(pay_a, pay_b, axis):
    size = lax.axis_size(axis)
    pairs_a = [(i, i + 1) for i in range(1, size - 1, 2)]
    pairs_b = [(i, i + 1) for i in range(0, size - 1, 2)]
    return lax.ppermute(pay_a, axis, both_ways(pairs_a)), lax.ppermute(pay_b, axis, both_ways(pairs_b))


def exchange(value, distance):
    return lax.ppermute(value, "dev", [(i, i ^ distance) for i in range(lax.axis_size("dev"))])


def body(conc_old, phi_old, solid_pot, phase_label, iface_block, iface_owner):
    peers = lax.axis_size("dev")
    nx = conc_old.shape[0]
    half = nx // 2
    quarter = nx // 4
    ext = (nx + 2 * HALO, nx + 2 * HALO, 256)
    ext_mid = (half + 2 * HALO, half + 2 * HALO, 256)
    token_shape = shaped(8, LANES)

    pay_a, pay_b, own_lists = call(
        first_pack_kernel,
        [shaped(7 * nx, 256)] * 2 + [shaped(8, 256)],
        [conc_old, phase_label, iface_owner.reshape(1, -1), iface_block],
        [vmem(nx, HALO, 256)] * 2
        + [pltpu.VMEM((nx, HALO, 256), jnp.int32)] * 2
        + [pltpu.VMEM((1, 256), jnp.int32)] * 2
        + [pltpu.SemaphoreType.DMA((6,))],
        in_specs=[FAR] * 4,
        limit=VMEM_MOST,
        name="first_pack",
    )
    y_a, y_b = swap(pay_a, pay_b, "dev")
    conduct_mid, conduct_coarse, pay_a, pay_b, lists, gain, base = call(
        own_kernel,
        [shaped(half, half, 256), shaped(quarter, quarter, 256), shaped(24, 8, 256), shaped(24, 8, 256)]
        + [shaped(2, 256), shaped(nx, nx, 256), shaped(nx, nx, 256)],
        [conc_old, phase_label, phi_old, own_lists],
        [vmem(half, 2, nx, LANES), vmem(quarter, 2, half, LANES)],
        name="own",
    )
    xx_a, xx_b = swap(pay_a, pay_b, "grp")
    distance = peers // 2
    while distance > 1:
        lists = jnp.concatenate([lists, exchange(lists, distance)], axis=0)
        distance //= 2
    far_rows = second_rows(nx)[2]
    far_pay = call(
        second_pack_kernel,
        [shaped(far_rows, 256), shaped(far_rows + peers, 256)],
        [phi_old, conduct_mid, conduct_coarse, lists, xx_a, xx_b],
        name="second_pack",
    )
    yy_a, yy_b = swap(*far_pay, "dev")
    pay_a, pay_b = call(
        first_pack_x_kernel,
        [shaped(35, 8, 256)] * 2,
        [conc_old, phase_label, y_a, y_b, conduct_coarse],
        name="first_pack_x",
    )
    x_a, x_b = swap(pay_a, pay_b, "grp")

    (conc_new,) = call(
        sweeps_kernel,
        [shaped(nx, nx, 256)],
        [conc_old, phase_label, gain, base, y_a, y_b, x_a, x_b],
        [vmem(*ext)] * 2 + [vmem(nx, 8, 256)] * 2 + [vmem(2 * HALO, nx + 2 * HALO, 256)] * 2,
        name="sweeps",
    )
    flux_all, pay_a, pay_b = call(
        flux_kernel,
        [shaped(nx, nx, 256), shaped(3 * nx, 256), shaped(3 * nx, 256)],
        [conc_new, phase_label, phi_old, solid_pot],
        name="flux",
    )
    f_a, f_b = swap(pay_a, pay_b, "dev")
    flux_own, halo_mask = call(
        mask_kernel,
        [shaped(nx, nx, 256), shaped(nx, 8, 256)],
        [flux_all, lists, yy_b],
        [vmem(3, nx, 8, LANES)],
        name="mask",
    )
    weight, scale, made = call(
        ready_kernel,
        [shaped(*ext)] * 2 + [token_shape],
        [conc_old, phase_label, y_a, y_b, x_a, x_b],
        name="ready",
    )
    pay_a, pay_b = call(
        flux_pack_x_kernel, [shaped(15, 8, 256)] * 2, [flux_own, f_a, f_b, halo_mask, made], name="flux_pack_x"
    )
    fx_a, fx_b = swap(pay_a, pay_b, "grp")
    fine_two, fine_source, fine_first, inner_mid, field = call(
        potential_inner_kernel,
        [shaped(*ext)] * 3 + [shaped(half, half, 256), shaped(*ext)],
        [flux_own, halo_mask, f_a, f_b, phi_old, yy_a, yy_b, xx_a, xx_b, weight, scale],
        [vmem(nx, 8, 256), vmem(half, 2, nx, LANES)],
        name="potential_inner",
    )
    edge = (16, nx + 2 * HALO, 256)
    edge_two, edge_source, source_mid, pay_a, pay_b = call(
        potential_edge_kernel,
        [shaped(*edge), shaped(*edge), shaped(half, half, 256), shaped(4 * half, 256), shaped(4 * half, 256)],
        [fx_a, fx_b, weight, scale, field, fine_two, fine_source, fine_first, inner_mid],
        [vmem(*edge), vmem(2, 2, nx, LANES)],
        name="potential_edge",
    )
    m_a, m_b = swap(pay_a, pay_b, "dev")
    concentration, flux, stored = call(
        store_kernel,
        [shaped(nx, nx, 256), shaped(nx, nx, 256), token_shape],
        [conc_new, flux_own],
        [pltpu.SemaphoreType.DMA((8,))],
        out_specs=[FAR, FAR, WHOLE],
        name="store",
    )
    wide = (quarter, 32, 256)
    rho, load, made = call(
        coarse_ready_kernel,
        [shaped(quarter, quarter, 256), shaped(8, LANES), token_shape],
        [conduct_coarse, yy_a, yy_b],
        [vmem(*wide)] * 4,
        name="coarse_ready",
    )
    pay_a, pay_b = call(
        mid_pack_x_kernel, [shaped(3 * HALO, 8, 256)] * 2, [source_mid, m_a, m_b, made, stored], name="mid_pack_x"
    )
    mx_a, mx_b = swap(pay_a, pay_b, "grp")
    mid_two, mid_source, mid_weight, source_coarse, wide_coarse, pay_a, pay_b, sums = call(
        mid_kernel,
        [shaped(*ext_mid)] * 3
        + [shaped(quarter, 12, 256), shaped(quarter, 12, 256), shaped(72, 256), shaped(72, 256), shaped(8, 256)],
        [source_mid, conduct_mid, yy_a, yy_b, xx_a, xx_b, m_a, m_b, mx_a, mx_b, rho, load],
        [vmem(*ext_mid)] * 2 + [vmem(8, 2, half + 2 * HALO, LANES)] * 2,
        name="middle",
    )
    distance = peers // 2
    early = sums = sums + exchange(sums, distance)
    while distance > 2:
        distance //= 2
        sums = sums + exchange(sums, distance)
    (pay_b,) = call(late_kernel, [shaped(72, 256)], [pay_b, early], name="late")
    c_a, c_b = swap(pay_a, pay_b, "dev")
    other_sums = exchange(sums, 1)
    (error,) = call(
        coarse_kernel,
        [shaped(8, 16, 256)],
        [source_coarse, wide_coarse, yy_a, yy_b, c_a, c_b],
        [vmem(*wide)] * 4,
        name="coarse",
    )
    error, pay_a, pay_b = call(
        shift_kernel, [shaped(8, 16, 256), shaped(2, 16, 256), shaped(2, 16, 256)], [error, sums, other_sums], name="shift"
    )
    e_a, e_b = swap(pay_a, pay_b, "grp")
    begun, zero, one, fine_one, fine_last = call(
        finish_inner_kernel,
        [shaped(nx, nx, 256), shaped(*ext_mid), shaped(*ext_mid), shaped(*ext), shaped(*ext)],
        [error, mid_two, mid_source, mid_weight, fine_two, fine_source, weight],
        [vmem(*ext_mid), vmem(8, 2, 2, 16, LANES), vmem(half + 2 * HALO, 3, 2, 16, LANES), vmem(nx, nx, 256)]
        + [pltpu.SemaphoreType.DMA((2,))],
        out_specs=[FAR] + [WHOLE] * 4,
        name="finish_inner",
    )
    finish_args = [e_a, e_b, mid_two, mid_source, mid_weight, fine_two, edge_two, fine_source, edge_source, weight]
    finish_args += [zero, one, fine_one, fine_last, begun]
    (potential,) = call(
        finish_edge_kernel,
        [shaped(nx, nx, 256)],
        finish_args,
        [vmem(*ext_mid), vmem(*ext_mid), vmem(*ext), vmem(*ext)]
        + [vmem(4, 2, 2, 16, LANES), vmem(6, 3, 2, 16, LANES), vmem(nx, nx, 256)]
        + [pltpu.SemaphoreType.DMA((2,))],
        in_specs=[WHOLE] * (len(finish_args) - 1) + [FAR],
        out_specs=[FAR],
        aliases={len(finish_args) - 1: 0},
        name="finish_edge",
    )
    return (concentration, flux, potential)


def solution(mesh):
    brick = P("grp", "dev", None)
    return jax.shard_map(
        body,
        mesh=mesh,
        in_specs=(brick, brick, brick, brick, P("grp", "dev"), brick),
        out_specs=(brick, brick, brick),
        check_vma=False,
    )
```

```python
import jax
import jax.numpy as jnp
from jax import lax
from jax.experimental import pallas as pl
from jax.experimental.pallas import tpu as pltpu
from jax.sharding import PartitionSpec as P


F32 = jnp.float32
MASS = 0.05
OMEGA = 0.8
DIFFUSION_TABLE = (1.5, 0.1, 0.4)
RATIO_TABLE = tuple(d / (1.0 + 6.0 * d) for d in DIFFUSION_TABLE)
INVERSE_TABLE = tuple(1.0 / (1.0 + 6.0 * d) for d in DIFFUSION_TABLE)
CONDUCT_TABLE = (1.0, 0.3, 0.6)
KINETIC_TABLE = (0.2, 1.0, 0.5)
SWEEPS = 4
COARSE_SWEEPS = 8
COARSE_NEAR = 8
HALO = 4
LANES = 128
VMEM_LIMIT = 28 * 1024 * 1024
VMEM_MOST = 58 * 1024 * 1024


def shaped(*shape):
    return jax.ShapeDtypeStruct(shape, F32)


WHOLE = pl.BlockSpec(memory_space=pltpu.VMEM)
FAR = pl.BlockSpec(memory_space=pltpu.HBM)


def call(kernel, outs, args, scratch=(), in_specs=None, out_specs=None, limit=VMEM_LIMIT, aliases=None, flops=10**6, name=None):
    size = sum(4 * a.size for a in args) + sum(4 * o.size for o in outs)
    return pl.pallas_call(
        kernel,
        out_shape=tuple(outs),
        in_specs=in_specs or [WHOLE] * len(args),
        out_specs=tuple(out_specs or [WHOLE] * len(outs)),
        scratch_shapes=list(scratch),
        input_output_aliases=aliases or {},
        compiler_params=pltpu.CompilerParams(vmem_limit_bytes=limit),
        cost_estimate=pl.CostEstimate(flops=flops, bytes_accessed=size, transcendentals=0),
        name=name,
    )(*args)


def vmem(*shape):
    return pltpu.VMEM(shape, F32)


def iota(shape, dim):
    return lax.broadcasted_iota(jnp.int32, shape, dim)


def pick(label, table):
    return jnp.where(label == 0, table[0], jnp.where(label == 1, table[1], table[2])).astype(F32)


def loop(low, high, body, unroll=8):
    steps = (high - low) // unroll

    def step(i, carry):
        for u in range(unroll):
            body(low + i * unroll + u)
        return carry

    if steps > 1:
        lax.fori_loop(0, steps, step, 0)
    else:
        steps = 0
    for x in range(low + steps * unroll, high):
        body(x)


def odd(axis):
    return lax.rem(lax.axis_index(axis), 2) == 1


def along_y(v):
    return pltpu.roll(v, 1, 0) + pltpu.roll(v, v.shape[0] - 1, 0)


def along_z(v):
    low, high = v[:, :LANES], v[:, LANES:]
    lane = iota(low.shape, 1)
    first, last = lane == 0, lane == LANES - 1
    low_up, high_up = pltpu.roll(low, 1, 1), pltpu.roll(high, 1, 1)
    low_down, high_down = pltpu.roll(low, LANES - 1, 1), pltpu.roll(high, LANES - 1, 1)
    low_sum = jnp.where(first, 0.0, low_up) + jnp.where(last, high_down, low_down)
    high_sum = jnp.where(first, low_up, high_up) + jnp.where(last, 0.0, high_down)
    return jnp.concatenate([low_sum, high_sum], axis=1)


def upper(shape=(8, 256)):
    return iota(shape, 0) < HALO


def twice(tile, scratch):
    for h in range(2):
        part = tile[:, h * LANES : (h + 1) * LANES]
        scratch[h, pl.ds(0, 8, stride=2), :] = part
        scratch[h, pl.ds(1, 8, stride=2), :] = part
    return jnp.concatenate([scratch[0], scratch[1]], axis=1)


def pair_rows(v, scratch):
    half = v.shape[0] // 2
    parts = []
    for h in range(2):
        scratch[h] = v[:, h * LANES : (h + 1) * LANES]
        parts.append(scratch[h, pl.ds(0, half, stride=2), :] + scratch[h, pl.ds(1, half, stride=2), :])
    return jnp.concatenate(parts, axis=1)


def either(flag, if_true, if_false):
    return jnp.where(flag, if_true, if_false)


def y_sides(r_a, r_b, at, count):
    flag = odd("dev")
    a, b = r_a[at : at + count, :], r_b[at : at + count, :]
    return either(flag, a, b), either(flag, b, a)


def x_sides(r_a, r_b, index):
    flag = odd("grp")
    a, b = r_a[index], r_b[index]
    return either(flag, a, b), either(flag, b, a)


def send_y(pay_a, pay_b, at, first, last):
    flag = odd("dev")
    n = first.shape[0]
    pay_a[at : at + n, :] = either(flag, last, first)
    pay_b[at : at + n, :] = either(flag, first, last)


def send_x(pay_a, pay_b, index, first, last):
    flag = odd("grp")
    pay_a[index] = either(flag, last, first)
    pay_b[index] = either(flag, first, last)


def halo_tile(after, before):
    parts = [after]
    if after.shape[0] < HALO:
        parts.append(jnp.zeros((2 * HALO - 2 * after.shape[0], after.shape[1]), F32))
    return jnp.concatenate(parts + [before], axis=0)


def first_pack_kernel(
    conc, label, owner, block, pay_a, pay_b, own_lists, c_first, c_last, l_first, l_last, own_owner, own_block, sems
):
    nx = conc.shape[0]
    copies = [pltpu.make_async_copy(owner, own_owner, sems.at[4]), pltpu.make_async_copy(block, own_block, sems.at[5])]
    for i, (ref, at, to) in enumerate(((conc, 0, c_first), (conc, 28, c_last), (label, 0, l_first), (label, 28, l_last))):
        copies.append(pltpu.make_async_copy(ref.at[:, pl.ds(at, 4), :], to, sems.at[i]))
    for c in copies:
        c.start()
    for c in copies:
        c.wait()
    named = jnp.concatenate([own_owner[...], own_block[...], jnp.zeros((6, 256), jnp.int32)], axis=0).astype(F32)
    own_lists[...] = named
    for x in range(nx):
        send_y(pay_a, pay_b, 7 * x, c_first[x], c_last[x])
        send_y(pay_a, pay_b, 7 * x + 4, l_first[x, 0:3, :].astype(F32), l_last[x, 1:4, :].astype(F32))


def own_kernel(conc, label, phi, named, mid, coarse, pay_a, pay_b, lists, gain, base, pairs, pairs_2):
    nx = conc.shape[0]
    half = nx // 2
    lists[...] = named[0:2, :]

    def coefficients(i):
        gain[i] = pick(label[i], RATIO_TABLE)
        base[i] = conc[i] * pick(label[i], INVERSE_TABLE)

    loop(0, nx, coefficients, 4)

    def coarsen(i):
        total = conc[2 * i] * pick(label[2 * i], CONDUCT_TABLE) + conc[2 * i + 1] * pick(label[2 * i + 1], CONDUCT_TABLE)
        mid[i] = 0.25 * pair_rows(total, pairs.at[i])

    loop(0, half, coarsen, 4)
    for i in range(half // 2):
        coarse[i] = 0.25 * pair_rows(mid[2 * i] + mid[2 * i + 1], pairs_2.at[i])
    for k in range(HALO):
        for t in range(4):
            rows = slice(8 * t, 8 * t + 8)
            send_x(pay_a, pay_b, 4 * k + t, phi[k, rows, :], phi[nx - HALO + k, rows, :])
        for t in range(2):
            rows = slice(8 * t, 8 * t + 8)
            send_x(pay_a, pay_b, 16 + 2 * k + t, mid[k, rows, :], mid[half - HALO + k, rows, :])


def first_pack_x_kernel(conc, label, r_a, r_b, token, pay_a, pay_b):
    nx = conc.shape[0]

    def plane(ref, k, t, offset, count):
        if t < 4:
            return ref[k, 8 * t : 8 * t + 8, :].astype(F32)
        return halo_tile(*y_sides(r_a, r_b, 7 * k + offset, count))

    for t in range(5):
        for k in range(HALO):
            send_x(pay_a, pay_b, 5 * k + t, plane(conc, k, t, 0, 4), plane(conc, nx - HALO + k, t, 0, 4))
        for k in range(3):
            send_x(pay_a, pay_b, 20 + 5 * k + t, plane(label, k, t, 4, 3), plane(label, nx - 3 + k, t, 4, 3))


def corner_rows(n, reach):
    counts = [min(HALO, k + reach) for k in range(HALO)]
    counts = counts + [HALO] * n + counts[::-1]
    return counts, [sum(counts[:i]) for i in range(len(counts))]


def second_rows(nx):
    phi, mid = (sum(corner_rows(n, reach)[0]) for n, reach in ((nx, 0), (nx // 2, 1)))
    return phi, phi + mid, phi + mid + 64


def second_pack_kernel(phi, mid, coarse, lists, x_a, x_b, pay_a, pay_b):
    nx = phi.shape[0]
    starts = second_rows(nx)

    def put(own, n, reach, index, base):
        counts, at = corner_rows(n, reach)
        tiles = own.shape[1] // 8
        for x in range(n):
            send_y(pay_a, pay_b, base + at[HALO + x], own[x, 0:4, :], own[x, 8 * tiles - 4 : 8 * tiles, :])
        for k in range(HALO):
            first_after, first_before = x_sides(x_a, x_b, index + tiles * k)
            last_after, last_before = x_sides(x_a, x_b, index + tiles * k + tiles - 1)
            for x, first, last in ((k, first_before, last_before), (HALO + n + k, first_after, last_after)):
                if counts[x]:
                    send_y(pay_a, pay_b, base + at[x], first[0 : counts[x]], last[8 - counts[x] : 8])

    put(phi, nx, 0, 0, 0)
    put(mid, nx // 2, 1, 16, starts[0])
    base = starts[1]
    for x in range(8):
        pay_a[base + 8 * x : base + 8 * x + 8, :] = coarse[x]
        pay_b[base + 8 * x : base + 8 * x + 8, :] = coarse[x]
    base = starts[2]
    pay_b[base : base + lists.shape[0], :] = lists[...]


def second_halo(r_a, r_b, n, reach, x, base):
    counts, at = corner_rows(n, reach)
    if not counts[x]:
        return jnp.zeros((8, 256), F32)
    return halo_tile(*y_sides(r_a, r_b, base + at[x], counts[x]))


def wide_rows(own, after_own, before_own, after, before):
    gap = jnp.zeros((6, 256), F32)
    return jnp.concatenate([own, after_own, after, gap, before, before_own], axis=0)


def sweeps_kernel(conc, label, gain_own, base_own, y_a, y_b, x_a, x_b, out, one, two, gain_far, base_far, gain_x, base_x):
    nx = conc.shape[0]

    def own(i):
        one[HALO + i, 0:32, :] = conc[i]

    loop(0, nx, own)
    for i in range(nx):
        c = halo_tile(*y_sides(y_a, y_b, 7 * i, 4))
        lab = halo_tile(*y_sides(y_a, y_b, 7 * i + 4, 3))
        one[HALO + i, 32:40, :] = c
        gain_far[i] = jnp.where(c > 0.0, pick(lab, RATIO_TABLE), 0.0)
        base_far[i] = c * pick(lab, INVERSE_TABLE)

    def put(x, rows, c, lab):
        one[x, rows, :] = c
        at = x if x < HALO else x - nx
        gain_x[at, rows, :] = jnp.where(c > 0.0, pick(lab, RATIO_TABLE), 0.0)
        base_x[at, rows, :] = c * pick(lab, INVERSE_TABLE)

    for t in range(5):
        rows = slice(8 * t, 8 * t + 8)
        for k in range(HALO):
            c_after, c_before = x_sides(x_a, x_b, 5 * k + t)
            l_after = x_sides(x_a, x_b, 20 + 5 * min(k, 2) + t)[0]
            l_before = x_sides(x_a, x_b, 20 + 5 * max(k - 1, 0) + t)[1]
            put(k, rows, c_before, l_before)
            put(HALO + nx + k, rows, c_after, l_after)

    def neighbours(old, x):
        mid = old[x]
        return (old[x - 1] + old[x + 1]) + (along_y(mid) + along_z(mid))

    fields = (one, two)
    for s in range(1, SWEEPS):
        old, new = fields[(s - 1) % 2], fields[s % 2]

        def sweep(i, old=old, new=new):
            gain = jnp.concatenate([gain_own[i], gain_far[i]], axis=0)
            base = jnp.concatenate([base_own[i], base_far[i]], axis=0)
            new[HALO + i] = base + gain * neighbours(old, HALO + i)

        loop(0, nx, sweep)
        for k in range(s, HALO):
            for x, at in ((k, k), (2 * HALO + nx - 1 - k, 2 * HALO - 1 - k)):
                new[x] = base_x[at] + gain_x[at] * neighbours(old, x)

    old = fields[(SWEEPS - 1) % 2]

    def last(i):
        out[i] = base_own[i] + gain_own[i] * neighbours(old, HALO + i)[0:32, :]

    loop(0, nx, last)


def flux_kernel(conc, label, phi, solid, flux, pay_a, pay_b):
    nx = conc.shape[0]

    def plane(i):
        drive = 0.5 * (solid[i] - phi[i])
        logc = jnp.log(conc[i])
        value = jnp.exp(drive + 0.4 * logc) - jnp.exp(0.6 * logc - drive)
        flux[i] = pick(label[i], KINETIC_TABLE) * value

    loop(0, nx, plane, 4)
    for x in range(nx):
        send_y(pay_a, pay_b, 3 * x, flux[x, 0:3, :], flux[x, 29:32, :])


def mask_kernel(flux_all, lists, far, flux, halo_mask, marked):
    nx = flux_all.shape[0]
    rows = lists.shape[0]
    pieces = [lists[i : i + 1, :] for i in range(rows)] + [far[i : i + 1, :] for i in range(far.shape[0] - rows, far.shape[0])]
    owner = jnp.concatenate(pieces[0::2], axis=1).astype(jnp.int32)
    block = jnp.concatenate(pieces[1::2], axis=1).astype(jnp.int32)
    entries = owner.shape[1]
    hit_column = (iota((64, entries), 0) == lax.rem(block, 64)).astype(jnp.bfloat16)
    reach = owner - lax.axis_index("dev") + 1
    at_row = jnp.where((reach >= 0) & (reach < 3), reach * nx + lax.shift_right_arithmetic(block, 6), -1)
    hit_row = (iota((3 * nx, entries), 0) == at_row).astype(jnp.bfloat16)
    named = lax.dot_general(hit_row, hit_column, (((1,), (1,)), ((), ())), preferred_element_type=F32)
    named = jnp.concatenate([named, jnp.zeros((3 * nx, LANES - 64), F32)], axis=1)
    for j in range(3):
        for i in range(nx):
            marked[j, i] = jnp.broadcast_to(named[j * nx + i : j * nx + i + 1, :], (8, LANES))
    is_row = lax.div(iota((32, LANES), 1), 2) == iota((32, LANES), 0)
    row, pair = iota((8, LANES), 0), lax.div(iota((8, LANES), 1), 2)
    is_after = (row < 3) & (pair == row)
    is_before = (row >= 5) & (pair == row + 24)
    spread = (lax.rem(iota((LANES, 256), 0), 2) == lax.div(iota((LANES, 256), 1), LANES)).astype(jnp.bfloat16)

    def plane(i):
        marks = jnp.where(is_row, jnp.concatenate([marked[1, i]] * 4, axis=0), 0.0)
        beyond = jnp.where(is_after, marked[2, i], jnp.where(is_before, marked[0, i], 0.0))
        marks = jnp.concatenate([marks, beyond], axis=0).astype(jnp.bfloat16)
        listed = jnp.dot(marks, spread, preferred_element_type=F32) > 0.5
        flux[i] = jnp.where(listed[0:32], flux_all[i], 0.0)
        halo_mask[i] = jnp.where(listed[32:40], 1.0, 0.0)

    loop(0, nx, plane, 16)


def store_kernel(conc, flux, conc_out, flux_out, token, sems):
    copies = []
    for i, (ref, to) in enumerate(((conc, conc_out), (flux, flux_out))):
        for j in range(4):
            rows = pl.ds(8 * j, 8)
            copies.append(pltpu.make_async_copy(ref.at[rows], to.at[rows], sems.at[4 * i + j]))
            copies[-1].start()
    token[...] = jnp.zeros(token.shape, F32)
    for c in copies:
        c.wait()


def ready_kernel(conc, label, y_a, y_b, x_a, x_b, weight, scale, token):
    nx = conc.shape[0]
    token[...] = jnp.zeros(token.shape, F32)

    def put(x, rows, c, lab):
        conduct = c * pick(lab, CONDUCT_TABLE)
        factor = OMEGA / (MASS + 6.0 * conduct)
        weight[x, rows, :] = conduct * factor
        scale[x, rows, :] = factor

    def own(i):
        put(HALO + i, slice(0, 32), conc[i], label[i])

    loop(0, nx, own, 4)
    for i in range(nx):
        c = halo_tile(*y_sides(y_a, y_b, 7 * i, 4))
        lab = halo_tile(*y_sides(y_a, y_b, 7 * i + 4, 3))
        put(HALO + i, slice(32, 40), c, lab)
    for t in range(5):
        rows = slice(8 * t, 8 * t + 8)
        for k in range(HALO):
            c_after, c_before = x_sides(x_a, x_b, 5 * k + t)
            l_after = x_sides(x_a, x_b, 20 + 5 * min(k, 2) + t)[0]
            l_before = x_sides(x_a, x_b, 20 + 5 * max(k - 1, 0) + t)[1]
            put(k, rows, c_before, l_before)
            put(HALO + nx + k, rows, c_after, l_after)


def place_phi(phi, yy_a, yy_b, xx_a, xx_b, field):
    nx = phi.shape[0]

    def own(i):
        field[HALO + i, 0:32, :] = phi[i]

    loop(0, nx, own)
    for x in range(nx + 2 * HALO):
        field[x, 32:40, :] = second_halo(yy_a, yy_b, nx, 0, x, 0)
    for t in range(4):
        for k in range(HALO):
            after, before = x_sides(xx_a, xx_b, 4 * k + t)
            field[k, 8 * t : 8 * t + 8, :] = before
            field[HALO + nx + k, 8 * t : 8 * t + 8, :] = after


def flux_pack_x_kernel(flux, r_a, r_b, mask, token, pay_a, pay_b):
    nx = flux.shape[0]

    def tile(x, t):
        if t < 4:
            return flux[x, 8 * t : 8 * t + 8, :]
        return mask[x] * halo_tile(*y_sides(r_a, r_b, 3 * x, 3))

    for k in range(3):
        for t in range(5):
            send_x(pay_a, pay_b, 5 * k + t, tile(k, t), tile(nx - 3 + k, t))


def first_sweep(field, weight, scale, x, rows, flux):
    p = field[x]
    near = (field[x - 1] + field[x + 1]) + (along_y(p) + along_z(p))
    b = scale[x, rows, :] * (MASS * p[rows, :] + flux)
    return b, 0.2 * p[rows, :] + weight[x, rows, :] * near[rows, :] + b


def potential_inner_kernel(
    flux, mask, y_a, y_b, phi, yy_a, yy_b, xx_a, xx_b, weight, scale, after_two, source, first, source_mid, field, far, pairs
):
    nx = flux.shape[0]
    place_phi(phi, yy_a, yy_b, xx_a, xx_b, field)
    for i in range(nx):
        far[i] = mask[i] * halo_tile(*y_sides(y_a, y_b, 3 * i, 3))

    def own(i):
        x = HALO + i
        f = jnp.concatenate([flux[i], far[i]], axis=0)
        source[x], first[x] = first_sweep(field, weight, scale, x, slice(0, 40), f)

    loop(0, nx, own)

    def around(values, x):
        v = values[x]
        return v, weight[x] * ((values[x - 1] + values[x + 1]) + (along_y(v) + along_z(v)))

    def sweep(x):
        v, near = around(first, x)
        after_two[x] = 0.2 * v + (source[x] + near)

    loop(HALO + 1, HALO + nx - 1, sweep)

    def remainder(x):
        v, near = around(after_two, x)
        return ((source[x] - OMEGA * v) + near)[0:32, :] / scale[x, 0:32, :]

    def coarsen(i):
        x = HALO + 2 * i
        source_mid[i] = 0.25 * pair_rows(remainder(x) + remainder(x + 1), pairs.at[i])

    loop(1, nx // 2 - 1, coarsen, 4)


def potential_edge_kernel(
    x_a, x_b, weight, scale, field, inner_two, inner_source, inner_first, inner_mid,
    edge_two, edge_source, source_mid, pay_a, pay_b, first, pairs,
):
    half = source_mid.shape[0]
    nx = 2 * half
    for side, face in ((0, HALO), (1, HALO + nx)):
        base = 8 * side + HALO - face
        for k in range(3):
            x = face - 3 + k if side == 0 else face + k
            f = jnp.concatenate([x_sides(x_a, x_b, 5 * k + t)[1 - side] for t in range(5)], axis=0)
            edge_source[base + x], first[base + x] = first_sweep(field, weight, scale, x, slice(0, 40), f)

        def first_of(x, base=base):
            return inner_first[x] if HALO <= x < HALO + nx else first[base + x]

        def source_of(x, base=base):
            return inner_source[x] if HALO <= x < HALO + nx else edge_source[base + x]

        def two_of(x, base=base):
            return inner_two[x] if HALO < x < HALO + nx - 1 else edge_two[base + x]

        for x in range(face - 2, face + 1) if side == 0 else range(face - 1, face + 2):
            v = first_of(x)
            near = weight[x] * ((first_of(x - 1) + first_of(x + 1)) + (along_y(v) + along_z(v)))
            edge_two[base + x] = 0.2 * v + (source_of(x) + near)
        total = 0.0
        at = face if side == 0 else face - 2
        for x in (at, at + 1):
            v = two_of(x)
            near = weight[x] * ((two_of(x - 1) + two_of(x + 1)) + (along_y(v) + along_z(v)))
            total = total + ((source_of(x) - OMEGA * v) + near)[0:32, :] / scale[x, 0:32, :]
        source_mid[0 if side == 0 else half - 1] = 0.25 * pair_rows(total, pairs.at[side])
    for x in range(1, half - 1):
        source_mid[x] = inner_mid[x]
    for x in range(half):
        send_y(pay_a, pay_b, 4 * x, source_mid[x, 0:4, :], source_mid[x, 12:16, :])


def mid_pack_x_kernel(field, r_a, r_b, token, token_2, pay_a, pay_b):
    n = field.shape[0]

    def tile(x, t):
        if t < 2:
            return field[x, 8 * t : 8 * t + 8, :]
        return halo_tile(*y_sides(r_a, r_b, 4 * x, 4))

    for k in range(HALO):
        for t in range(3):
            send_x(pay_a, pay_b, 3 * k + t, tile(k, t), tile(n - HALO + k, t))


def mid_kernel(
    source_own, conduct_own, yy_a, yy_b, xx_a, xx_b, y_a, y_b, x_a, x_b, rho, load,
    after_two, source, weight, coarse, conduct, pay_a, pay_b, part, scale, mid_conduct, pairs, pairs_2,
):
    n = source_own.shape[0]
    base = second_rows(2 * n)[0]

    def put(x, rows, b, k):
        factor = OMEGA / (MASS + 3.0 * k)
        weight[x, rows, :] = k * factor
        scale[x, rows, :] = factor
        source[x, rows, :] = factor * b
        mid_conduct[x, rows, :] = k

    def far(x):
        return second_halo(yy_a, yy_b, n, 1, x, base)

    for i in range(n):
        put(HALO + i, slice(0, 16), source_own[i], conduct_own[i])
        put(HALO + i, slice(16, 24), halo_tile(*y_sides(y_a, y_b, 4 * i, 4)), far(HALO + i))
    for k in range(HALO):
        for t in range(3):
            rows = slice(8 * t, 8 * t + 8)
            b_after, b_before = x_sides(x_a, x_b, 3 * k + t)
            if t < 2:
                c_after, c_before = x_sides(xx_a, xx_b, 16 + 2 * k + t)
            else:
                c_after, c_before = far(HALO + n + k), far(k)
            put(k, rows, b_before, c_before)
            put(HALO + n + k, rows, b_after, c_after)

    def around(values, x):
        v = values[x]
        return v, weight[x] * (0.25 * ((values[x - 1] + values[x + 1]) + along_y(v)) + along_z(v))

    def sweep(x):
        v, near = around(source, x)
        after_two[x] = 0.2 * v + (source[x] + near)

    loop(1, n + 2 * HALO - 1, sweep, 11)

    def remainder(x):
        v, near = around(after_two, x)
        return ((source[x] - OMEGA * v) + near) / scale[x]

    total = jnp.zeros((8, 256), F32)
    for i in range(n // 2):
        x = HALO + 2 * i
        value = 0.25 * pair_rows(remainder(x) + remainder(x + 1), pairs.at[i])
        k = 0.25 * pair_rows(mid_conduct[x] + mid_conduct[x + 1], pairs_2.at[i])
        coarse[i] = value
        conduct[i] = k
        send_y(pay_a, pay_b, 9 * i, value[1:9], jnp.concatenate([value[11:12], value[0:7]], axis=0))
        send_y(pay_a, pay_b, 9 * i + 8, k[8:9], k[11:12])
        total += rho[i] * value[0:8]
    sums = jnp.concatenate([total[:, :LANES] + total[:, LANES:], load[...]], axis=1)
    pay_b[72:80, :] = sums
    part[...] = sums


COARSE_W = 0.0625


def coarse_ready_kernel(own, r_a, r_b, rho, load, token, one, two, conduct, scale):
    token[...] = jnp.zeros(token.shape, F32)
    base = r_a.shape[0] - 64
    for x in range(8):
        after, before = y_sides(r_a, r_b, base + 8 * x, 8)
        k = jnp.concatenate([own[x], after, jnp.zeros((8, 256), F32), before], axis=0)
        conduct[x] = k
        scale[x] = OMEGA / (MASS + 2.25 * k)
        one[x] = jnp.ones(k.shape, F32)
    fields = (one, two)
    for s in range(COARSE_SWEEPS):
        old, new = fields[s % 2], fields[(s + 1) % 2]
        for x in range(8):
            near = [conduct[i] * old[i] if 0 <= i < 8 else None for i in (x - 1, x, x + 1)]
            inner = along_y(near[1])
            for other in (near[0], near[2]):
                if other is not None:
                    inner = inner + other
            new[x] = 0.2 * old[x] + scale[x] * (COARSE_W * inner + along_z(near[1]))
    last = fields[COARSE_SWEEPS % 2]
    peer, peers = lax.axis_index("dev"), lax.axis_size("dev")
    row, z = iota((8, 256), 0), iota((8, 256), 1)
    edge_y = ((row == 0) & (peer == 0)) | ((row == 7) & (peer == peers - 1))
    edge = edge_y.astype(F32) * COARSE_W + ((z == 0) | (z == 255)).astype(F32)
    total = jnp.zeros((8, 256), F32)
    for x in range(8):
        rho[x] = last[x, 0:8, :]
        total += MASS + own[x] * (edge + (COARSE_W if x in (0, 7) else 0.0))
    load[...] = total[:, :LANES] + total[:, LANES:]


def pair_kernel(sums, other, out):
    total = sums[...] + other[72:80, :]
    resid, load = total[:, :LANES], total[:, LANES:]
    tile = jnp.concatenate([resid[0:4] + resid[4:8], load[0:4] + load[4:8]], axis=0)
    for i in range(out.shape[0]):
        out[i] = tile


def coarse_kernel(own, conduct, far_a, far_b, r_a, r_b, error, source, weight, one, two):
    base = far_a.shape[0] - 64
    for x in range(8):
        after, before = y_sides(r_a, r_b, 9 * x, 8)
        b = wide_rows(own[x, 0:8, :], own[x, 8:9, :], own[x, 11:12, :], after, before)
        last_after, last_before = y_sides(r_a, r_b, 9 * x + 8, 1)
        after, before = y_sides(far_a, far_b, base + 8 * x, 8)
        after = jnp.concatenate([after[1:8], last_after], axis=0)
        before = jnp.concatenate([last_before, before[0:7]], axis=0)
        k = wide_rows(conduct[x, 0:8, :], conduct[x, 8:9, :], conduct[x, 11:12, :], after, before)
        factor = OMEGA / (MASS + 2.25 * k)
        weight[x] = k * factor
        source[x] = factor * b
    old = source
    for s in range(1, COARSE_SWEEPS):
        new = one if s % 2 else two
        for x in range(8):
            v = old[x]
            inner = along_y(v)
            if x > 0:
                inner = inner + old[x - 1]
            if x < 7:
                inner = inner + old[x + 1]
            new[x] = 0.2 * v + (source[x] + weight[x] * (COARSE_W * inner + along_z(v)))
        old = new
    for x in range(8):
        error[x, 0:8, :] = old[x, 0:8, :]
        error[x, 8:16, :] = jnp.where(upper(), old[x, 8:16, :], old[x, 24:32, :])


def shift_kernel(error, sums, out, pay_a, pay_b):
    total = jnp.sum(sums[...], axis=0)
    resid = jnp.sum(total[0:4])
    load = jnp.sum(total[4:8])
    shift_c = jnp.full((16, 256), resid, F32) / jnp.full((16, 256), load, F32)
    for x in range(8):
        out[x] = error[x] + shift_c
    for k in range(2):
        send_x(pay_a, pay_b, k, out[k], out[6 + k])


def squeeze(tile):
    return jnp.where(iota((8, 256), 0) < 2, tile, pltpu.roll(tile, 4, 0))


def spread_coarse(plane, room):
    return jnp.concatenate([twice(plane[0:8], room.at[0]), twice(squeeze(plane[8:16]), room.at[1])[0:8]], axis=0)


def spread_mid(plane, room):
    parts = [twice(plane[0:8], room.at[0]), twice(plane[8:16], room.at[1]), twice(squeeze(plane[16:24]), room.at[2])[0:8]]
    return jnp.concatenate(parts, axis=0)


def smoothed(before, v, after, weight, source, w):
    inner = (before + after) + along_y(v)
    return source + (0.2 * v + weight * (w * inner + along_z(v)))


def finish_inner_kernel(
    error, mid_two, mid_source, mid_weight, fine_two, fine_source, fine_weight,
    out, zero, one, fine_one, fine_last, two, dup, dup_2, result, sems,
):
    n = mid_two.shape[0]
    nf = fine_two.shape[0]
    for c in range(8):
        spread = spread_coarse(error[c], dup.at[c])
        for x in (2 * c + HALO, 2 * c + 1 + HALO):
            zero[x] = jnp.where(mid_weight[x] > 0.0, mid_two[x] + spread, 0.0)

    def sweep_mid(x, old, new):
        new[x] = smoothed(old[x - 1], old[x], old[x + 1], mid_weight[x], mid_source[x], 0.25)

    for x in range(HALO + 1, n - HALO - 1):
        sweep_mid(x, zero, one)
    for x in range(HALO + 2, n - HALO - 2):
        sweep_mid(x, one, two)

    def lift(m):
        spread = spread_mid(two[m], dup_2.at[m])
        x = 2 * m - HALO
        fine_one[x] = fine_two[x] + spread
        fine_one[x + 1] = fine_two[x + 1] + spread

    loop(HALO + 2, n - HALO - 2, lift, 6)

    def sweep_one(x):
        fine_last[x] = smoothed(fine_one[x - 1], fine_one[x], fine_one[x + 1], fine_weight[x], fine_source[x], 1.0)

    low, high = 2 * HALO + 1, nf - 2 * HALO - 1
    loop(low, high, sweep_one, 11)
    copies = []
    low, high = low + 1, high - 1
    for j in range(2):
        mid = low + (high - low) // 2
        for x in range(low, mid) if j == 0 else range(mid, high):
            v = smoothed(fine_last[x - 1], fine_last[x], fine_last[x + 1], fine_weight[x], fine_source[x], 1.0)
            result[x - HALO] = v[0:32, :]
        rows = pl.ds(low - HALO, mid - low) if j == 0 else pl.ds(mid - HALO, high - mid)
        copies.append(pltpu.make_async_copy(result.at[rows], out.at[rows], sems.at[j]))
        copies[-1].start()
    for c in copies:
        c.wait()


def finish_edge_kernel(
    x_a, x_b, mid_two, mid_source, mid_weight, fine_two, edge_two, fine_source, edge_source, fine_weight,
    zero, one, fine_one, fine_last, begun, out, zero_edge, one_edge, fine_edge, last_edge, dup, dup_2, result, sems,
):
    n = mid_two.shape[0]
    nf = fine_two.shape[0]
    nx = nf - 2 * HALO
    copies = []
    planes = x_sides(x_a, x_b, slice(0, 2))
    for side in (0, 1):
        sign = 1 if side == 0 else -1
        at = lambda k, side=side: HALO + k if side == 0 else n - HALO - 1 - k
        fine = lambda k, side=side: HALO + k if side == 0 else nf - HALO - 1 - k
        base = 8 * side + (0 if side == 0 else HALO - HALO - nx)
        for c in range(2):
            plane = planes[1 - side][c]
            spread = spread_coarse(plane, dup.at[2 * side + c])
            first = 2 * c if side == 0 else n - HALO + 2 * c
            for x in (first, first + 1):
                zero_edge[x] = jnp.where(mid_weight[x] > 0.0, mid_two[x] + spread, 0.0)

        def zero_of(k):
            return zero[at(k)] if k >= 0 else zero_edge[at(k)]

        def one_of(k):
            return one[at(k)] if k >= 1 else one_edge[at(k)]

        for k in range(-2, 1):
            x = at(k)
            one_edge[x] = smoothed(zero_of(k - 1), zero_of(k), zero_of(k + 1), mid_weight[x], mid_source[x], 0.25)
        for k in range(-1, 2):
            x = at(k)
            value = smoothed(one_of(k - 1), one_of(k), one_of(k + 1), mid_weight[x], mid_source[x], 0.25)
            spread = spread_mid(value, dup_2.at[3 * side + k + 1])
            for f in (fine(2 * k), fine(2 * k + 1)):
                inside = HALO < f < nf - HALO - 1
                before = fine_two[f] if inside else edge_two[base + f]
                fine_edge[f] = before + spread

        def fine_of(k):
            return fine_one[fine(k)] if k >= 4 else fine_edge[fine(k)]

        def last_of(k):
            return fine_last[fine(k)] if k >= 5 else last_edge[fine(k)]

        for k in range(-1, 5):
            f = fine(k)
            source = fine_source[f] if HALO <= f < nf - HALO else edge_source[base + f]
            last_edge[f] = smoothed(fine_of(k - 1), fine_of(k), fine_of(k + 1), fine_weight[f], source, 1.0)
        for k in range(6):
            f = fine(k)
            v = smoothed(last_of(k - 1), last_of(k), last_of(k + 1), fine_weight[f], fine_source[f], 1.0)
            result[f - HALO] = v[0:32, :]
        rows = pl.ds(0, 6) if side == 0 else pl.ds(nx - 6, 6)
        copies.append(pltpu.make_async_copy(result.at[rows], out.at[rows], sems.at[side]))
        copies[-1].start()
    for c in copies:
        c.wait()


def both_ways(pairs):
    return pairs + [(j, i) for i, j in pairs]


def swap(pay_a, pay_b, axis):
    size = lax.axis_size(axis)
    pairs_a = [(i, i + 1) for i in range(1, size - 1, 2)]
    pairs_b = [(i, i + 1) for i in range(0, size - 1, 2)]
    return lax.ppermute(pay_a, axis, both_ways(pairs_a)), lax.ppermute(pay_b, axis, both_ways(pairs_b))


def exchange(value, distance):
    return lax.ppermute(value, "dev", [(i, i ^ distance) for i in range(lax.axis_size("dev"))])


def body(conc_old, phi_old, solid_pot, phase_label, iface_block, iface_owner):
    peers = lax.axis_size("dev")
    nx = conc_old.shape[0]
    half = nx // 2
    quarter = nx // 4
    ext = (nx + 2 * HALO, nx + 2 * HALO, 256)
    ext_mid = (half + 2 * HALO, half + 2 * HALO, 256)
    token_shape = shaped(8, LANES)

    pay_a, pay_b, own_lists = call(
        first_pack_kernel,
        [shaped(7 * nx, 256)] * 2 + [shaped(8, 256)],
        [conc_old, phase_label, iface_owner.reshape(1, -1), iface_block],
        [vmem(nx, HALO, 256)] * 2
        + [pltpu.VMEM((nx, HALO, 256), jnp.int32)] * 2
        + [pltpu.VMEM((1, 256), jnp.int32)] * 2
        + [pltpu.SemaphoreType.DMA((6,))],
        in_specs=[FAR] * 4,
        limit=VMEM_MOST,
        name="first_pack",
    )
    y_a, y_b = swap(pay_a, pay_b, "dev")
    conduct_mid, conduct_coarse, pay_a, pay_b, lists, gain, base = call(
        own_kernel,
        [shaped(half, half, 256), shaped(quarter, quarter, 256), shaped(24, 8, 256), shaped(24, 8, 256)]
        + [shaped(2, 256), shaped(nx, nx, 256), shaped(nx, nx, 256)],
        [conc_old, phase_label, phi_old, own_lists],
        [vmem(half, 2, nx, LANES), vmem(quarter, 2, half, LANES)],
        name="own",
    )
    xx_a, xx_b = swap(pay_a, pay_b, "grp")
    distance = peers // 2
    while distance > 1:
        lists = jnp.concatenate([lists, exchange(lists, distance)], axis=0)
        distance //= 2
    far_rows = second_rows(nx)[2]
    far_pay = call(
        second_pack_kernel,
        [shaped(far_rows, 256), shaped(far_rows + peers, 256)],
        [phi_old, conduct_mid, conduct_coarse, lists, xx_a, xx_b],
        name="second_pack",
    )
    yy_a, yy_b = swap(*far_pay, "dev")
    pay_a, pay_b = call(
        first_pack_x_kernel,
        [shaped(35, 8, 256)] * 2,
        [conc_old, phase_label, y_a, y_b, conduct_coarse],
        name="first_pack_x",
    )
    x_a, x_b = swap(pay_a, pay_b, "grp")

    (conc_new,) = call(
        sweeps_kernel,
        [shaped(nx, nx, 256)],
        [conc_old, phase_label, gain, base, y_a, y_b, x_a, x_b],
        [vmem(*ext)] * 2 + [vmem(nx, 8, 256)] * 2 + [vmem(2 * HALO, nx + 2 * HALO, 256)] * 2,
        name="sweeps",
    )
    flux_all, pay_a, pay_b = call(
        flux_kernel,
        [shaped(nx, nx, 256), shaped(3 * nx, 256), shaped(3 * nx, 256)],
        [conc_new, phase_label, phi_old, solid_pot],
        name="flux",
    )
    f_a, f_b = swap(pay_a, pay_b, "dev")
    flux_own, halo_mask = call(
        mask_kernel,
        [shaped(nx, nx, 256), shaped(nx, 8, 256)],
        [flux_all, lists, yy_b],
        [vmem(3, nx, 8, LANES)],
        name="mask",
    )
    weight, scale, made = call(
        ready_kernel,
        [shaped(*ext)] * 2 + [token_shape],
        [conc_old, phase_label, y_a, y_b, x_a, x_b],
        name="ready",
    )
    pay_a, pay_b = call(
        flux_pack_x_kernel, [shaped(15, 8, 256)] * 2, [flux_own, f_a, f_b, halo_mask, made], name="flux_pack_x"
    )
    fx_a, fx_b = swap(pay_a, pay_b, "grp")
    fine_two, fine_source, fine_first, inner_mid, field = call(
        potential_inner_kernel,
        [shaped(*ext)] * 3 + [shaped(half, half, 256), shaped(*ext)],
        [flux_own, halo_mask, f_a, f_b, phi_old, yy_a, yy_b, xx_a, xx_b, weight, scale],
        [vmem(nx, 8, 256), vmem(half, 2, nx, LANES)],
        name="potential_inner",
    )
    edge = (16, nx + 2 * HALO, 256)
    edge_two, edge_source, source_mid, pay_a, pay_b = call(
        potential_edge_kernel,
        [shaped(*edge), shaped(*edge), shaped(half, half, 256), shaped(4 * half, 256), shaped(4 * half, 256)],
        [fx_a, fx_b, weight, scale, field, fine_two, fine_source, fine_first, inner_mid],
        [vmem(*edge), vmem(2, 2, nx, LANES)],
        name="potential_edge",
    )
    m_a, m_b = swap(pay_a, pay_b, "dev")
    concentration, flux, stored = call(
        store_kernel,
        [shaped(nx, nx, 256), shaped(nx, nx, 256), token_shape],
        [conc_new, flux_own],
        [pltpu.SemaphoreType.DMA((8,))],
        out_specs=[FAR, FAR, WHOLE],
        name="store",
    )
    wide = (quarter, 32, 256)
    rho, load, made = call(
        coarse_ready_kernel,
        [shaped(quarter, quarter, 256), shaped(8, LANES), token_shape],
        [conduct_coarse, yy_a, yy_b],
        [vmem(*wide)] * 4,
        name="coarse_ready",
    )
    pay_a, pay_b = call(
        mid_pack_x_kernel, [shaped(3 * HALO, 8, 256)] * 2, [source_mid, m_a, m_b, made, stored], name="mid_pack_x"
    )
    mx_a, mx_b = swap(pay_a, pay_b, "grp")
    mid_two, mid_source, mid_weight, source_coarse, wide_coarse, pay_a, pay_b, sums = call(
        mid_kernel,
        [shaped(*ext_mid)] * 3
        + [shaped(quarter, 12, 256), shaped(quarter, 12, 256), shaped(72, 256), shaped(80, 256), shaped(8, 256)],
        [source_mid, conduct_mid, yy_a, yy_b, xx_a, xx_b, m_a, m_b, mx_a, mx_b, rho, load],
        [vmem(*ext_mid)] * 2 + [vmem(8, 2, half + 2 * HALO, LANES)] * 2,
        name="middle",
    )
    c_a, c_b = swap(pay_a, pay_b, "dev")
    groups = [list(range(0, peers, 2)), list(range(1, peers, 2))]
    (sums,) = call(pair_kernel, [shaped(peers // 2, 8, LANES)], [sums, c_b], name="pair")
    sums = lax.all_to_all(sums, "dev", 0, 0, axis_index_groups=groups, tiled=True)
    (error,) = call(
        coarse_kernel,
        [shaped(8, 16, 256)],
        [source_coarse, wide_coarse, yy_a, yy_b, c_a, c_b],
        [vmem(*wide)] * 4,
        name="coarse",
    )
    error, pay_a, pay_b = call(
        shift_kernel, [shaped(8, 16, 256), shaped(2, 16, 256), shaped(2, 16, 256)], [error, sums], name="shift"
    )
    e_a, e_b = swap(pay_a, pay_b, "grp")
    begun, zero, one, fine_one, fine_last = call(
        finish_inner_kernel,
        [shaped(nx, nx, 256), shaped(*ext_mid), shaped(*ext_mid), shaped(*ext), shaped(*ext)],
        [error, mid_two, mid_source, mid_weight, fine_two, fine_source, weight],
        [vmem(*ext_mid), vmem(8, 2, 2, 16, LANES), vmem(half + 2 * HALO, 3, 2, 16, LANES), vmem(nx, nx, 256)]
        + [pltpu.SemaphoreType.DMA((2,))],
        out_specs=[FAR] + [WHOLE] * 4,
        name="finish_inner",
    )
    finish_args = [e_a, e_b, mid_two, mid_source, mid_weight, fine_two, edge_two, fine_source, edge_source, weight]
    finish_args += [zero, one, fine_one, fine_last, begun]
    (potential,) = call(
        finish_edge_kernel,
        [shaped(nx, nx, 256)],
        finish_args,
        [vmem(*ext_mid), vmem(*ext_mid), vmem(*ext), vmem(*ext)]
        + [vmem(4, 2, 2, 16, LANES), vmem(6, 3, 2, 16, LANES), vmem(nx, nx, 256)]
        + [pltpu.SemaphoreType.DMA((2,))],
        in_specs=[WHOLE] * (len(finish_args) - 1) + [FAR],
        out_specs=[FAR],
        aliases={len(finish_args) - 1: 0},
        name="finish_edge",
    )
    return (concentration, flux, potential)


def solution(mesh):
    brick = P("grp", "dev", None)
    return jax.shard_map(
        body,
        mesh=mesh,
        in_specs=(brick, brick, brick, brick, P("grp", "dev"), brick),
        out_specs=(brick, brick, brick),
        check_vma=False,
    )
```

```python
import jax
import jax.numpy as jnp
from jax import lax
from jax.experimental import pallas as pl
from jax.experimental.pallas import tpu as pltpu
from jax.sharding import PartitionSpec as P


F32 = jnp.float32
MASS = 0.05
OMEGA = 0.8
DIFFUSION_TABLE = (1.5, 0.1, 0.4)
RATIO_TABLE = tuple(d / (1.0 + 6.0 * d) for d in DIFFUSION_TABLE)
INVERSE_TABLE = tuple(1.0 / (1.0 + 6.0 * d) for d in DIFFUSION_TABLE)
CONDUCT_TABLE = (1.0, 0.3, 0.6)
KINETIC_TABLE = (0.2, 1.0, 0.5)
SWEEPS = 4
COARSE_SWEEPS = 8
COARSE_NEAR = 8
HALO = 4
LANES = 128
VMEM_LIMIT = 28 * 1024 * 1024
VMEM_MOST = 58 * 1024 * 1024


def shaped(*shape):
    return jax.ShapeDtypeStruct(shape, F32)


WHOLE = pl.BlockSpec(memory_space=pltpu.VMEM)
FAR = pl.BlockSpec(memory_space=pltpu.HBM)


def call(kernel, outs, args, scratch=(), in_specs=None, out_specs=None, limit=VMEM_LIMIT, aliases=None, flops=10**6, name=None):
    size = sum(4 * a.size for a in args) + sum(4 * o.size for o in outs)
    return pl.pallas_call(
        kernel,
        out_shape=tuple(outs),
        in_specs=in_specs or [WHOLE] * len(args),
        out_specs=tuple(out_specs or [WHOLE] * len(outs)),
        scratch_shapes=list(scratch),
        input_output_aliases=aliases or {},
        compiler_params=pltpu.CompilerParams(vmem_limit_bytes=limit),
        cost_estimate=pl.CostEstimate(flops=flops, bytes_accessed=size, transcendentals=0),
        name=name,
    )(*args)


def vmem(*shape):
    return pltpu.VMEM(shape, F32)


def iota(shape, dim):
    return lax.broadcasted_iota(jnp.int32, shape, dim)


def pick(label, table):
    return jnp.where(label == 0, table[0], jnp.where(label == 1, table[1], table[2])).astype(F32)


def loop(low, high, body, unroll=8):
    steps = (high - low) // unroll

    def step(i, carry):
        for u in range(unroll):
            body(low + i * unroll + u)
        return carry

    if steps > 1:
        lax.fori_loop(0, steps, step, 0)
    else:
        steps = 0
    for x in range(low + steps * unroll, high):
        body(x)


def odd(axis):
    return lax.rem(lax.axis_index(axis), 2) == 1


def along_y(v):
    return pltpu.roll(v, 1, 0) + pltpu.roll(v, v.shape[0] - 1, 0)


def along_z(v):
    low, high = v[:, :LANES], v[:, LANES:]
    lane = iota(low.shape, 1)
    first, last = lane == 0, lane == LANES - 1
    low_up, high_up = pltpu.roll(low, 1, 1), pltpu.roll(high, 1, 1)
    low_down, high_down = pltpu.roll(low, LANES - 1, 1), pltpu.roll(high, LANES - 1, 1)
    low_sum = jnp.where(first, 0.0, low_up) + jnp.where(last, high_down, low_down)
    high_sum = jnp.where(first, low_up, high_up) + jnp.where(last, 0.0, high_down)
    return jnp.concatenate([low_sum, high_sum], axis=1)


def upper(shape=(8, 256)):
    return iota(shape, 0) < HALO


def twice(tile, scratch):
    for h in range(2):
        part = tile[:, h * LANES : (h + 1) * LANES]
        scratch[h, pl.ds(0, 8, stride=2), :] = part
        scratch[h, pl.ds(1, 8, stride=2), :] = part
    return jnp.concatenate([scratch[0], scratch[1]], axis=1)


def pair_rows(v, scratch):
    half = v.shape[0] // 2
    parts = []
    for h in range(2):
        scratch[h] = v[:, h * LANES : (h + 1) * LANES]
        parts.append(scratch[h, pl.ds(0, half, stride=2), :] + scratch[h, pl.ds(1, half, stride=2), :])
    return jnp.concatenate(parts, axis=1)


def either(flag, if_true, if_false):
    return jnp.where(flag, if_true, if_false)


def y_sides(r_a, r_b, at, count):
    flag = odd("dev")
    a, b = r_a[at : at + count, :], r_b[at : at + count, :]
    return either(flag, a, b), either(flag, b, a)


def x_sides(r_a, r_b, index):
    flag = odd("grp")
    a, b = r_a[index], r_b[index]
    return either(flag, a, b), either(flag, b, a)


def send_y(pay_a, pay_b, at, first, last):
    flag = odd("dev")
    n = first.shape[0]
    pay_a[at : at + n, :] = either(flag, last, first)
    pay_b[at : at + n, :] = either(flag, first, last)


def send_x(pay_a, pay_b, index, first, last):
    flag = odd("grp")
    pay_a[index] = either(flag, last, first)
    pay_b[index] = either(flag, first, last)


def halo_tile(after, before):
    parts = [after]
    if after.shape[0] < HALO:
        parts.append(jnp.zeros((2 * HALO - 2 * after.shape[0], after.shape[1]), F32))
    return jnp.concatenate(parts + [before], axis=0)


def first_pack_kernel(
    conc, label, owner, block, pay_a, pay_b, own_lists, c_first, c_last, l_first, l_last, own_owner, own_block, sems
):
    nx = conc.shape[0]
    copies = [pltpu.make_async_copy(owner, own_owner, sems.at[4]), pltpu.make_async_copy(block, own_block, sems.at[5])]
    for i, (ref, at, to) in enumerate(((conc, 0, c_first), (conc, 28, c_last), (label, 0, l_first), (label, 28, l_last))):
        copies.append(pltpu.make_async_copy(ref.at[:, pl.ds(at, 4), :], to, sems.at[i]))
    for c in copies:
        c.start()
    for c in copies:
        c.wait()
    named = jnp.concatenate([own_owner[...], own_block[...], jnp.zeros((6, 256), jnp.int32)], axis=0).astype(F32)
    own_lists[...] = named
    for x in range(nx):
        send_y(pay_a, pay_b, 7 * x, c_first[x], c_last[x])
        send_y(pay_a, pay_b, 7 * x + 4, l_first[x, 0:3, :].astype(F32), l_last[x, 1:4, :].astype(F32))


def own_kernel(conc, label, phi, named, mid, coarse, pay_a, pay_b, lists, gain, base, pairs, pairs_2):
    nx = conc.shape[0]
    half = nx // 2
    lists[...] = named[0:2, :]

    def coefficients(i):
        gain[i] = pick(label[i], RATIO_TABLE)
        base[i] = conc[i] * pick(label[i], INVERSE_TABLE)

    loop(0, nx, coefficients, 4)

    def coarsen(i):
        total = conc[2 * i] * pick(label[2 * i], CONDUCT_TABLE) + conc[2 * i + 1] * pick(label[2 * i + 1], CONDUCT_TABLE)
        mid[i] = 0.25 * pair_rows(total, pairs.at[i])

    loop(0, half, coarsen, 4)
    for i in range(half // 2):
        coarse[i] = 0.25 * pair_rows(mid[2 * i] + mid[2 * i + 1], pairs_2.at[i])
    for k in range(HALO):
        for t in range(4):
            rows = slice(8 * t, 8 * t + 8)
            send_x(pay_a, pay_b, 4 * k + t, phi[k, rows, :], phi[nx - HALO + k, rows, :])
        for t in range(2):
            rows = slice(8 * t, 8 * t + 8)
            send_x(pay_a, pay_b, 16 + 2 * k + t, mid[k, rows, :], mid[half - HALO + k, rows, :])


def first_pack_x_kernel(conc, label, r_a, r_b, token, pay_a, pay_b):
    nx = conc.shape[0]

    def plane(ref, k, t, offset, count):
        if t < 4:
            return ref[k, 8 * t : 8 * t + 8, :].astype(F32)
        return halo_tile(*y_sides(r_a, r_b, 7 * k + offset, count))

    for t in range(5):
        for k in range(HALO):
            send_x(pay_a, pay_b, 5 * k + t, plane(conc, k, t, 0, 4), plane(conc, nx - HALO + k, t, 0, 4))
        for k in range(3):
            send_x(pay_a, pay_b, 20 + 5 * k + t, plane(label, k, t, 4, 3), plane(label, nx - 3 + k, t, 4, 3))


def corner_rows(n, reach):
    counts = [min(HALO, k + reach) for k in range(HALO)]
    counts = counts + [HALO] * n + counts[::-1]
    return counts, [sum(counts[:i]) for i in range(len(counts))]


def second_rows(nx):
    phi, mid = (sum(corner_rows(n, reach)[0]) for n, reach in ((nx, 0), (nx // 2, 1)))
    return phi, phi + mid, phi + mid + 64


def second_pack_kernel(phi, mid, coarse, lists, x_a, x_b, pay_a, pay_b):
    nx = phi.shape[0]
    starts = second_rows(nx)

    def put(own, n, reach, index, base):
        counts, at = corner_rows(n, reach)
        tiles = own.shape[1] // 8
        for x in range(n):
            send_y(pay_a, pay_b, base + at[HALO + x], own[x, 0:4, :], own[x, 8 * tiles - 4 : 8 * tiles, :])
        for k in range(HALO):
            first_after, first_before = x_sides(x_a, x_b, index + tiles * k)
            last_after, last_before = x_sides(x_a, x_b, index + tiles * k + tiles - 1)
            for x, first, last in ((k, first_before, last_before), (HALO + n + k, first_after, last_after)):
                if counts[x]:
                    send_y(pay_a, pay_b, base + at[x], first[0 : counts[x]], last[8 - counts[x] : 8])

    put(phi, nx, 0, 0, 0)
    put(mid, nx // 2, 1, 16, starts[0])
    base = starts[1]
    for x in range(8):
        pay_a[base + 8 * x : base + 8 * x + 8, :] = coarse[x]
        pay_b[base + 8 * x : base + 8 * x + 8, :] = coarse[x]
    base = starts[2]
    pay_b[base : base + lists.shape[0], :] = lists[...]


def second_halo(r_a, r_b, n, reach, x, base):
    counts, at = corner_rows(n, reach)
    if not counts[x]:
        return jnp.zeros((8, 256), F32)
    return halo_tile(*y_sides(r_a, r_b, base + at[x], counts[x]))


def wide_rows(own, after_own, before_own, after, before):
    gap = jnp.zeros((6, 256), F32)
    return jnp.concatenate([own, after_own, after, gap, before, before_own], axis=0)


def sweeps_kernel(conc, label, gain_own, base_own, y_a, y_b, x_a, x_b, out, one, two, gain_far, base_far, gain_x, base_x):
    nx = conc.shape[0]

    def own(i):
        one[HALO + i, 0:32, :] = conc[i]

    loop(0, nx, own)
    for i in range(nx):
        c = halo_tile(*y_sides(y_a, y_b, 7 * i, 4))
        lab = halo_tile(*y_sides(y_a, y_b, 7 * i + 4, 3))
        one[HALO + i, 32:40, :] = c
        gain_far[i] = jnp.where(c > 0.0, pick(lab, RATIO_TABLE), 0.0)
        base_far[i] = c * pick(lab, INVERSE_TABLE)

    def put(x, rows, c, lab):
        one[x, rows, :] = c
        at = x if x < HALO else x - nx
        gain_x[at, rows, :] = jnp.where(c > 0.0, pick(lab, RATIO_TABLE), 0.0)
        base_x[at, rows, :] = c * pick(lab, INVERSE_TABLE)

    for t in range(5):
        rows = slice(8 * t, 8 * t + 8)
        for k in range(HALO):
            c_after, c_before = x_sides(x_a, x_b, 5 * k + t)
            l_after = x_sides(x_a, x_b, 20 + 5 * min(k, 2) + t)[0]
            l_before = x_sides(x_a, x_b, 20 + 5 * max(k - 1, 0) + t)[1]
            put(k, rows, c_before, l_before)
            put(HALO + nx + k, rows, c_after, l_after)

    def neighbours(old, x):
        mid = old[x]
        return (old[x - 1] + old[x + 1]) + (along_y(mid) + along_z(mid))

    fields = (one, two)
    for s in range(1, SWEEPS):
        old, new = fields[(s - 1) % 2], fields[s % 2]

        def sweep(i, old=old, new=new):
            gain = jnp.concatenate([gain_own[i], gain_far[i]], axis=0)
            base = jnp.concatenate([base_own[i], base_far[i]], axis=0)
            new[HALO + i] = base + gain * neighbours(old, HALO + i)

        loop(0, nx, sweep)
        for k in range(s, HALO):
            for x, at in ((k, k), (2 * HALO + nx - 1 - k, 2 * HALO - 1 - k)):
                new[x] = base_x[at] + gain_x[at] * neighbours(old, x)

    old = fields[(SWEEPS - 1) % 2]

    def last(i):
        out[i] = base_own[i] + gain_own[i] * neighbours(old, HALO + i)[0:32, :]

    loop(0, nx, last)


def flux_kernel(conc, label, phi, solid, flux, pay_a, pay_b):
    nx = conc.shape[0]

    def plane(i):
        drive = 0.5 * (solid[i] - phi[i])
        logc = jnp.log(conc[i])
        value = jnp.exp(drive + 0.4 * logc) - jnp.exp(0.6 * logc - drive)
        flux[i] = pick(label[i], KINETIC_TABLE) * value

    loop(0, nx, plane, 4)
    for x in range(nx):
        send_y(pay_a, pay_b, 3 * x, flux[x, 0:3, :], flux[x, 29:32, :])


def mask_kernel(flux_all, lists, far, flux, halo_mask, marked):
    nx = flux_all.shape[0]
    rows = lists.shape[0]
    pieces = [lists[i : i + 1, :] for i in range(rows)] + [far[i : i + 1, :] for i in range(far.shape[0] - rows, far.shape[0])]
    owner = jnp.concatenate(pieces[0::2], axis=1).astype(jnp.int32)
    block = jnp.concatenate(pieces[1::2], axis=1).astype(jnp.int32)
    entries = owner.shape[1]
    hit_column = (iota((64, entries), 0) == lax.rem(block, 64)).astype(jnp.bfloat16)
    reach = owner - lax.axis_index("dev") + 1
    at_row = jnp.where((reach >= 0) & (reach < 3), reach * nx + lax.shift_right_arithmetic(block, 6), -1)
    hit_row = (iota((3 * nx, entries), 0) == at_row).astype(jnp.bfloat16)
    named = lax.dot_general(hit_row, hit_column, (((1,), (1,)), ((), ())), preferred_element_type=F32)
    named = jnp.concatenate([named, jnp.zeros((3 * nx, LANES - 64), F32)], axis=1)
    for j in range(3):
        for i in range(nx):
            marked[j, i] = jnp.broadcast_to(named[j * nx + i : j * nx + i + 1, :], (8, LANES))
    is_row = lax.div(iota((32, LANES), 1), 2) == iota((32, LANES), 0)
    row, pair = iota((8, LANES), 0), lax.div(iota((8, LANES), 1), 2)
    is_after = (row < 3) & (pair == row)
    is_before = (row >= 5) & (pair == row + 24)
    spread = (lax.rem(iota((LANES, 256), 0), 2) == lax.div(iota((LANES, 256), 1), LANES)).astype(jnp.bfloat16)

    def plane(i):
        marks = jnp.where(is_row, jnp.concatenate([marked[1, i]] * 4, axis=0), 0.0)
        beyond = jnp.where(is_after, marked[2, i], jnp.where(is_before, marked[0, i], 0.0))
        marks = jnp.concatenate([marks, beyond], axis=0).astype(jnp.bfloat16)
        listed = jnp.dot(marks, spread, preferred_element_type=F32) > 0.5
        flux[i] = jnp.where(listed[0:32], flux_all[i], 0.0)
        halo_mask[i] = jnp.where(listed[32:40], 1.0, 0.0)

    loop(0, nx, plane, 16)


def store_kernel(conc, flux, conc_out, flux_out, token, sems):
    copies = []
    for i, (ref, to) in enumerate(((conc, conc_out), (flux, flux_out))):
        for j in range(4):
            rows = pl.ds(8 * j, 8)
            copies.append(pltpu.make_async_copy(ref.at[rows], to.at[rows], sems.at[4 * i + j]))
            copies[-1].start()
    token[...] = jnp.zeros(token.shape, F32)
    for c in copies:
        c.wait()


def ready_kernel(conc, label, y_a, y_b, x_a, x_b, weight, scale, token):
    nx = conc.shape[0]
    token[...] = jnp.zeros(token.shape, F32)

    def put(x, rows, c, lab):
        conduct = c * pick(lab, CONDUCT_TABLE)
        factor = OMEGA / (MASS + 6.0 * conduct)
        weight[x, rows, :] = conduct * factor
        scale[x, rows, :] = factor

    def own(i):
        put(HALO + i, slice(0, 32), conc[i], label[i])

    loop(0, nx, own, 4)
    for i in range(nx):
        c = halo_tile(*y_sides(y_a, y_b, 7 * i, 4))
        lab = halo_tile(*y_sides(y_a, y_b, 7 * i + 4, 3))
        put(HALO + i, slice(32, 40), c, lab)
    for t in range(5):
        rows = slice(8 * t, 8 * t + 8)
        for k in range(HALO):
            c_after, c_before = x_sides(x_a, x_b, 5 * k + t)
            l_after = x_sides(x_a, x_b, 20 + 5 * min(k, 2) + t)[0]
            l_before = x_sides(x_a, x_b, 20 + 5 * max(k - 1, 0) + t)[1]
            put(k, rows, c_before, l_before)
            put(HALO + nx + k, rows, c_after, l_after)


def place_phi(phi, yy_a, yy_b, xx_a, xx_b, field):
    nx = phi.shape[0]

    def own(i):
        field[HALO + i, 0:32, :] = phi[i]

    loop(0, nx, own)
    for x in range(nx + 2 * HALO):
        field[x, 32:40, :] = second_halo(yy_a, yy_b, nx, 0, x, 0)
    for t in range(4):
        for k in range(HALO):
            after, before = x_sides(xx_a, xx_b, 4 * k + t)
            field[k, 8 * t : 8 * t + 8, :] = before
            field[HALO + nx + k, 8 * t : 8 * t + 8, :] = after


def flux_pack_x_kernel(flux, r_a, r_b, mask, token, pay_a, pay_b):
    nx = flux.shape[0]

    def tile(x, t):
        if t < 4:
            return flux[x, 8 * t : 8 * t + 8, :]
        return mask[x] * halo_tile(*y_sides(r_a, r_b, 3 * x, 3))

    for k in range(3):
        for t in range(5):
            send_x(pay_a, pay_b, 5 * k + t, tile(k, t), tile(nx - 3 + k, t))


def first_sweep(field, weight, scale, x, rows, flux):
    p = field[x]
    near = (field[x - 1] + field[x + 1]) + (along_y(p) + along_z(p))
    b = scale[x, rows, :] * (MASS * p[rows, :] + flux)
    return b, 0.2 * p[rows, :] + weight[x, rows, :] * near[rows, :] + b


def potential_inner_kernel(
    flux, mask, y_a, y_b, phi, yy_a, yy_b, xx_a, xx_b, weight, scale, after_two, source, first, source_mid, field, far, pairs
):
    nx = flux.shape[0]
    place_phi(phi, yy_a, yy_b, xx_a, xx_b, field)
    for i in range(nx):
        far[i] = mask[i] * halo_tile(*y_sides(y_a, y_b, 3 * i, 3))

    def own(i):
        x = HALO + i
        f = jnp.concatenate([flux[i], far[i]], axis=0)
        source[x], first[x] = first_sweep(field, weight, scale, x, slice(0, 40), f)

    loop(0, nx, own)

    def around(values, x):
        v = values[x]
        return v, weight[x] * ((values[x - 1] + values[x + 1]) + (along_y(v) + along_z(v)))

    def sweep(x):
        v, near = around(first, x)
        after_two[x] = 0.2 * v + (source[x] + near)

    loop(HALO + 1, HALO + nx - 1, sweep)

    def remainder(x):
        v, near = around(after_two, x)
        return ((source[x] - OMEGA * v) + near)[0:32, :] / scale[x, 0:32, :]

    def coarsen(i):
        x = HALO + 2 * i
        source_mid[i] = 0.25 * pair_rows(remainder(x) + remainder(x + 1), pairs.at[i])

    loop(1, nx // 2 - 1, coarsen, 4)


def potential_edge_kernel(
    x_a, x_b, weight, scale, field, inner_two, inner_source, inner_first, inner_mid,
    edge_two, edge_source, source_mid, pay_a, pay_b, first, pairs,
):
    half = source_mid.shape[0]
    nx = 2 * half
    for side, face in ((0, HALO), (1, HALO + nx)):
        base = 8 * side + HALO - face
        for k in range(3):
            x = face - 3 + k if side == 0 else face + k
            f = jnp.concatenate([x_sides(x_a, x_b, 5 * k + t)[1 - side] for t in range(5)], axis=0)
            edge_source[base + x], first[base + x] = first_sweep(field, weight, scale, x, slice(0, 40), f)

        def first_of(x, base=base):
            return inner_first[x] if HALO <= x < HALO + nx else first[base + x]

        def source_of(x, base=base):
            return inner_source[x] if HALO <= x < HALO + nx else edge_source[base + x]

        def two_of(x, base=base):
            return inner_two[x] if HALO < x < HALO + nx - 1 else edge_two[base + x]

        for x in range(face - 2, face + 1) if side == 0 else range(face - 1, face + 2):
            v = first_of(x)
            near = weight[x] * ((first_of(x - 1) + first_of(x + 1)) + (along_y(v) + along_z(v)))
            edge_two[base + x] = 0.2 * v + (source_of(x) + near)
        total = 0.0
        at = face if side == 0 else face - 2
        for x in (at, at + 1):
            v = two_of(x)
            near = weight[x] * ((two_of(x - 1) + two_of(x + 1)) + (along_y(v) + along_z(v)))
            total = total + ((source_of(x) - OMEGA * v) + near)[0:32, :] / scale[x, 0:32, :]
        source_mid[0 if side == 0 else half - 1] = 0.25 * pair_rows(total, pairs.at[side])
    for x in range(1, half - 1):
        source_mid[x] = inner_mid[x]
    for x in range(half):
        send_y(pay_a, pay_b, 4 * x, source_mid[x, 0:4, :], source_mid[x, 12:16, :])


def mid_pack_x_kernel(field, r_a, r_b, token, token_2, pay_a, pay_b):
    n = field.shape[0]

    def tile(x, t):
        if t < 2:
            return field[x, 8 * t : 8 * t + 8, :]
        return halo_tile(*y_sides(r_a, r_b, 4 * x, 4))

    for k in range(HALO):
        for t in range(3):
            send_x(pay_a, pay_b, 3 * k + t, tile(k, t), tile(n - HALO + k, t))


def mid_kernel(
    source_own, conduct_own, yy_a, yy_b, xx_a, xx_b, y_a, y_b, x_a, x_b, rho, load,
    after_two, source, weight, coarse, conduct, pay_a, pay_b, part, scale, mid_conduct, pairs, pairs_2,
):
    n = source_own.shape[0]
    base = second_rows(2 * n)[0]

    def put(x, rows, b, k):
        factor = OMEGA / (MASS + 3.0 * k)
        weight[x, rows, :] = k * factor
        scale[x, rows, :] = factor
        source[x, rows, :] = factor * b
        mid_conduct[x, rows, :] = k

    def far(x):
        return second_halo(yy_a, yy_b, n, 1, x, base)

    for i in range(n):
        put(HALO + i, slice(0, 16), source_own[i], conduct_own[i])
        put(HALO + i, slice(16, 24), halo_tile(*y_sides(y_a, y_b, 4 * i, 4)), far(HALO + i))
    for k in range(HALO):
        for t in range(3):
            rows = slice(8 * t, 8 * t + 8)
            b_after, b_before = x_sides(x_a, x_b, 3 * k + t)
            if t < 2:
                c_after, c_before = x_sides(xx_a, xx_b, 16 + 2 * k + t)
            else:
                c_after, c_before = far(HALO + n + k), far(k)
            put(k, rows, b_before, c_before)
            put(HALO + n + k, rows, b_after, c_after)

    def around(values, x):
        v = values[x]
        return v, weight[x] * (0.25 * ((values[x - 1] + values[x + 1]) + along_y(v)) + along_z(v))

    def sweep(x):
        v, near = around(source, x)
        after_two[x] = 0.2 * v + (source[x] + near)

    loop(1, n + 2 * HALO - 1, sweep, 11)

    def remainder(x):
        v, near = around(after_two, x)
        return ((source[x] - OMEGA * v) + near) / scale[x]

    total = jnp.zeros((8, 256), F32)
    for i in range(n // 2):
        x = HALO + 2 * i
        value = 0.25 * pair_rows(remainder(x) + remainder(x + 1), pairs.at[i])
        k = 0.25 * pair_rows(mid_conduct[x] + mid_conduct[x + 1], pairs_2.at[i])
        coarse[i] = value
        conduct[i] = k
        send_y(pay_a, pay_b, 9 * i, value[1:9], jnp.concatenate([value[11:12], value[0:7]], axis=0))
        send_y(pay_a, pay_b, 9 * i + 8, k[8:9], k[11:12])
        total += rho[i] * value[0:8]
    sums = jnp.concatenate([total[:, :LANES] + total[:, LANES:], load[...]], axis=1)
    pay_b[72:80, :] = sums
    part[...] = sums


COARSE_W = 0.0625


def coarse_ready_kernel(own, r_a, r_b, rho, load, token, one, two, conduct, scale):
    token[...] = jnp.zeros(token.shape, F32)
    base = r_a.shape[0] - 64
    for x in range(8):
        after, before = y_sides(r_a, r_b, base + 8 * x, 8)
        k = jnp.concatenate([own[x], after, jnp.zeros((8, 256), F32), before], axis=0)
        conduct[x] = k
        scale[x] = OMEGA / (MASS + 2.25 * k)
        one[x] = jnp.ones(k.shape, F32)
    fields = (one, two)
    for s in range(COARSE_SWEEPS):
        old, new = fields[s % 2], fields[(s + 1) % 2]
        for x in range(8):
            near = [conduct[i] * old[i] if 0 <= i < 8 else None for i in (x - 1, x, x + 1)]
            inner = along_y(near[1])
            for other in (near[0], near[2]):
                if other is not None:
                    inner = inner + other
            new[x] = 0.2 * old[x] + scale[x] * (COARSE_W * inner + along_z(near[1]))
    last = fields[COARSE_SWEEPS % 2]
    peer, peers = lax.axis_index("dev"), lax.axis_size("dev")
    row, z = iota((8, 256), 0), iota((8, 256), 1)
    edge_y = ((row == 0) & (peer == 0)) | ((row == 7) & (peer == peers - 1))
    edge = edge_y.astype(F32) * COARSE_W + ((z == 0) | (z == 255)).astype(F32)
    total = jnp.zeros((8, 256), F32)
    for x in range(8):
        rho[x] = last[x, 0:8, :]
        total += MASS + own[x] * (edge + (COARSE_W if x in (0, 7) else 0.0))
    load[...] = total[:, :LANES] + total[:, LANES:]


def coarse_kernel(own, conduct, far_a, far_b, r_a, r_b, error, source, weight, one, two):
    base = far_a.shape[0] - 64
    for x in range(8):
        after, before = y_sides(r_a, r_b, 9 * x, 8)
        b = wide_rows(own[x, 0:8, :], own[x, 8:9, :], own[x, 11:12, :], after, before)
        last_after, last_before = y_sides(r_a, r_b, 9 * x + 8, 1)
        after, before = y_sides(far_a, far_b, base + 8 * x, 8)
        after = jnp.concatenate([after[1:8], last_after], axis=0)
        before = jnp.concatenate([last_before, before[0:7]], axis=0)
        k = wide_rows(conduct[x, 0:8, :], conduct[x, 8:9, :], conduct[x, 11:12, :], after, before)
        factor = OMEGA / (MASS + 2.25 * k)
        weight[x] = k * factor
        source[x] = factor * b
    old = source
    for s in range(1, COARSE_SWEEPS):
        new = one if s % 2 else two
        for x in range(8):
            v = old[x]
            inner = along_y(v)
            if x > 0:
                inner = inner + old[x - 1]
            if x < 7:
                inner = inner + old[x + 1]
            new[x] = 0.2 * v + (source[x] + weight[x] * (COARSE_W * inner + along_z(v)))
        old = new
    for x in range(8):
        error[x, 0:8, :] = old[x, 0:8, :]
        error[x, 8:16, :] = jnp.where(upper(), old[x, 8:16, :], old[x, 24:32, :])


def squeeze(tile):
    return jnp.where(iota((8, 256), 0) < 2, tile, pltpu.roll(tile, 4, 0))


def spread_coarse(plane, room):
    return jnp.concatenate([twice(plane[0:8], room.at[0]), twice(squeeze(plane[8:16]), room.at[1])[0:8]], axis=0)


def spread_mid(plane, room):
    parts = [twice(plane[0:8], room.at[0]), twice(plane[8:16], room.at[1]), twice(squeeze(plane[16:24]), room.at[2])[0:8]]
    return jnp.concatenate(parts, axis=0)


def smoothed(before, v, after, weight, source, w):
    inner = (before + after) + along_y(v)
    return source + (0.2 * v + weight * (w * inner + along_z(v)))


def is_early():
    return lax.axis_index("grp") < lax.axis_size("grp") // 2


def finish_inner(error, fields, kept, out, scratch):
    mid_two, mid_source, mid_weight, fine_two, fine_source, fine_weight = fields
    zero, one, two, fine_one, fine_last, dup, dup_2, result, sems = scratch
    n = mid_two.shape[0]
    nf = fine_two.shape[0]
    for c in range(8):
        spread = spread_coarse(error[c], dup.at[c])
        for x in (2 * c + HALO, 2 * c + 1 + HALO):
            zero[x] = jnp.where(mid_weight[x] > 0.0, mid_two[x] + spread, 0.0)

    def sweep_mid(x, old, new):
        new[x] = smoothed(old[x - 1], old[x], old[x + 1], mid_weight[x], mid_source[x], 0.25)

    for x in range(HALO + 1, n - HALO - 1):
        sweep_mid(x, zero, one)
    for x in range(HALO + 2, n - HALO - 2):
        sweep_mid(x, one, two)

    def lift(m):
        spread = spread_mid(two[m], dup_2.at[m])
        x = 2 * m - HALO
        fine_one[x] = fine_two[x] + spread
        fine_one[x + 1] = fine_two[x + 1] + spread

    loop(HALO + 2, n - HALO - 2, lift, 6)

    def sweep_one(x):
        fine_last[x] = smoothed(fine_one[x - 1], fine_one[x], fine_one[x + 1], fine_weight[x], fine_source[x], 1.0)

    low, high = 2 * HALO + 1, nf - 2 * HALO - 1
    loop(low, high, sweep_one, 11)
    for field, first, to in ((zero, 0, kept[0]), (one, 1, kept[1]), (fine_one, 4, kept[2]), (fine_last, 5, kept[3])):
        for j in range(2):
            to[j] = field[HALO + first + j]
            to[2 + j] = field[field.shape[0] - HALO - 1 - first - j]
    copies = []
    low, high = low + 1, high - 1
    for j in range(2):
        mid = low + (high - low) // 2
        for x in range(low, mid) if j == 0 else range(mid, high):
            v = smoothed(fine_last[x - 1], fine_last[x], fine_last[x + 1], fine_weight[x], fine_source[x], 1.0)
            result[x - HALO] = v[0:32, :]
        rows = pl.ds(low - HALO, mid - low) if j == 0 else pl.ds(mid - HALO, high - mid)
        copies.append(pltpu.make_async_copy(result.at[rows], out.at[rows], sems.at[j]))
        copies[-1].start()
    for c in copies:
        c.wait()


def finish_early_kernel(error, sums, *rest):
    fields, (shifted, pay_a, pay_b, out), kept, scratch = rest[:6], rest[6:10], rest[10:14], rest[14:]
    resid = jnp.sum(sums[:, :LANES])
    load = jnp.sum(sums[:, LANES:])
    shift_c = jnp.full((16, 256), resid, F32) / jnp.full((16, 256), load, F32)
    for x in range(8):
        shifted[x] = error[x] + shift_c
    for k in range(2):
        send_x(pay_a, pay_b, k, shifted[k], shifted[6 + k])

    @pl.when(is_early())
    def _():
        finish_inner(shifted, fields, kept, out, scratch)


def finish_late_kernel(error, *rest):
    fields, kept_early, out, kept, scratch = rest[:6], rest[6:10], rest[11], rest[12:16], rest[16:]

    @pl.when(is_early())
    def _():
        for a, b in zip(kept_early, kept):
            b[...] = a[...]

    @pl.when(jnp.logical_not(is_early()))
    def _():
        finish_inner(error, fields, kept, out, scratch)


def finish_edge_kernel(
    x_a, x_b, mid_two, mid_source, mid_weight, fine_two, edge_two, fine_source, edge_source, fine_weight,
    zero, one, fine_one, fine_last, begun, out, zero_edge, one_edge, fine_edge, last_edge, dup, dup_2, result, sems,
):
    n = mid_two.shape[0]
    nf = fine_two.shape[0]
    nx = nf - 2 * HALO
    copies = []
    planes = x_sides(x_a, x_b, slice(0, 2))
    for side in (0, 1):
        sign = 1 if side == 0 else -1
        at = lambda k, side=side: HALO + k if side == 0 else n - HALO - 1 - k
        fine = lambda k, side=side: HALO + k if side == 0 else nf - HALO - 1 - k
        base = 8 * side + (0 if side == 0 else HALO - HALO - nx)
        for c in range(2):
            plane = planes[1 - side][c]
            spread = spread_coarse(plane, dup.at[2 * side + c])
            first = 2 * c if side == 0 else n - HALO + 2 * c
            for x in (first, first + 1):
                zero_edge[x] = jnp.where(mid_weight[x] > 0.0, mid_two[x] + spread, 0.0)

        def zero_of(k, side=side):
            return zero[2 * side + k] if k >= 0 else zero_edge[at(k)]

        def one_of(k, side=side):
            return one[2 * side + k - 1] if k >= 1 else one_edge[at(k)]

        for k in range(-2, 1):
            x = at(k)
            one_edge[x] = smoothed(zero_of(k - 1), zero_of(k), zero_of(k + 1), mid_weight[x], mid_source[x], 0.25)
        for k in range(-1, 2):
            x = at(k)
            value = smoothed(one_of(k - 1), one_of(k), one_of(k + 1), mid_weight[x], mid_source[x], 0.25)
            spread = spread_mid(value, dup_2.at[3 * side + k + 1])
            for f in (fine(2 * k), fine(2 * k + 1)):
                inside = HALO < f < nf - HALO - 1
                before = fine_two[f] if inside else edge_two[base + f]
                fine_edge[f] = before + spread

        def fine_of(k, side=side):
            return fine_one[2 * side + k - 4] if k >= 4 else fine_edge[fine(k)]

        def last_of(k, side=side):
            return fine_last[2 * side + k - 5] if k >= 5 else last_edge[fine(k)]

        for k in range(-1, 5):
            f = fine(k)
            source = fine_source[f] if HALO <= f < nf - HALO else edge_source[base + f]
            last_edge[f] = smoothed(fine_of(k - 1), fine_of(k), fine_of(k + 1), fine_weight[f], source, 1.0)
        for k in range(6):
            f = fine(k)
            v = smoothed(last_of(k - 1), last_of(k), last_of(k + 1), fine_weight[f], fine_source[f], 1.0)
            result[f - HALO] = v[0:32, :]
        rows = pl.ds(0, 6) if side == 0 else pl.ds(nx - 6, 6)
        copies.append(pltpu.make_async_copy(result.at[rows], out.at[rows], sems.at[side]))
        copies[-1].start()
    for c in copies:
        c.wait()


def both_ways(pairs):
    return pairs + [(j, i) for i, j in pairs]


def swap(pay_a, pay_b, axis):
    size = lax.axis_size(axis)
    pairs_a = [(i, i + 1) for i in range(1, size - 1, 2)]
    pairs_b = [(i, i + 1) for i in range(0, size - 1, 2)]
    return lax.ppermute(pay_a, axis, both_ways(pairs_a)), lax.ppermute(pay_b, axis, both_ways(pairs_b))


def exchange(value, distance):
    return lax.ppermute(value, "dev", [(i, i ^ distance) for i in range(lax.axis_size("dev"))])


def body(conc_old, phi_old, solid_pot, phase_label, iface_block, iface_owner):
    peers = lax.axis_size("dev")
    nx = conc_old.shape[0]
    half = nx // 2
    quarter = nx // 4
    ext = (nx + 2 * HALO, nx + 2 * HALO, 256)
    ext_mid = (half + 2 * HALO, half + 2 * HALO, 256)
    token_shape = shaped(8, LANES)

    pay_a, pay_b, own_lists = call(
        first_pack_kernel,
        [shaped(7 * nx, 256)] * 2 + [shaped(8, 256)],
        [conc_old, phase_label, iface_owner.reshape(1, -1), iface_block],
        [vmem(nx, HALO, 256)] * 2
        + [pltpu.VMEM((nx, HALO, 256), jnp.int32)] * 2
        + [pltpu.VMEM((1, 256), jnp.int32)] * 2
        + [pltpu.SemaphoreType.DMA((6,))],
        in_specs=[FAR] * 4,
        limit=VMEM_MOST,
        name="first_pack",
    )
    y_a, y_b = swap(pay_a, pay_b, "dev")
    conduct_mid, conduct_coarse, pay_a, pay_b, lists, gain, base = call(
        own_kernel,
        [shaped(half, half, 256), shaped(quarter, quarter, 256), shaped(24, 8, 256), shaped(24, 8, 256)]
        + [shaped(2, 256), shaped(nx, nx, 256), shaped(nx, nx, 256)],
        [conc_old, phase_label, phi_old, own_lists],
        [vmem(half, 2, nx, LANES), vmem(quarter, 2, half, LANES)],
        name="own",
    )
    xx_a, xx_b = swap(pay_a, pay_b, "grp")
    distance = peers // 2
    while distance > 1:
        lists = jnp.concatenate([lists, exchange(lists, distance)], axis=0)
        distance //= 2
    far_rows = second_rows(nx)[2]
    far_pay = call(
        second_pack_kernel,
        [shaped(far_rows, 256), shaped(far_rows + peers, 256)],
        [phi_old, conduct_mid, conduct_coarse, lists, xx_a, xx_b],
        name="second_pack",
    )
    yy_a, yy_b = swap(*far_pay, "dev")
    pay_a, pay_b = call(
        first_pack_x_kernel,
        [shaped(35, 8, 256)] * 2,
        [conc_old, phase_label, y_a, y_b, conduct_coarse],
        name="first_pack_x",
    )
    x_a, x_b = swap(pay_a, pay_b, "grp")

    (conc_new,) = call(
        sweeps_kernel,
        [shaped(nx, nx, 256)],
        [conc_old, phase_label, gain, base, y_a, y_b, x_a, x_b],
        [vmem(*ext)] * 2 + [vmem(nx, 8, 256)] * 2 + [vmem(2 * HALO, nx + 2 * HALO, 256)] * 2,
        name="sweeps",
    )
    flux_all, pay_a, pay_b = call(
        flux_kernel,
        [shaped(nx, nx, 256), shaped(3 * nx, 256), shaped(3 * nx, 256)],
        [conc_new, phase_label, phi_old, solid_pot],
        name="flux",
    )
    f_a, f_b = swap(pay_a, pay_b, "dev")
    flux_own, halo_mask = call(
        mask_kernel,
        [shaped(nx, nx, 256), shaped(nx, 8, 256)],
        [flux_all, lists, yy_b],
        [vmem(3, nx, 8, LANES)],
        name="mask",
    )
    weight, scale, made = call(
        ready_kernel,
        [shaped(*ext)] * 2 + [token_shape],
        [conc_old, phase_label, y_a, y_b, x_a, x_b],
        name="ready",
    )
    pay_a, pay_b = call(
        flux_pack_x_kernel, [shaped(15, 8, 256)] * 2, [flux_own, f_a, f_b, halo_mask, made], name="flux_pack_x"
    )
    fx_a, fx_b = swap(pay_a, pay_b, "grp")
    fine_two, fine_source, fine_first, inner_mid, field = call(
        potential_inner_kernel,
        [shaped(*ext)] * 3 + [shaped(half, half, 256), shaped(*ext)],
        [flux_own, halo_mask, f_a, f_b, phi_old, yy_a, yy_b, xx_a, xx_b, weight, scale],
        [vmem(nx, 8, 256), vmem(half, 2, nx, LANES)],
        name="potential_inner",
    )
    edge = (16, nx + 2 * HALO, 256)
    edge_two, edge_source, source_mid, pay_a, pay_b = call(
        potential_edge_kernel,
        [shaped(*edge), shaped(*edge), shaped(half, half, 256), shaped(4 * half, 256), shaped(4 * half, 256)],
        [fx_a, fx_b, weight, scale, field, fine_two, fine_source, fine_first, inner_mid],
        [vmem(*edge), vmem(2, 2, nx, LANES)],
        name="potential_edge",
    )
    m_a, m_b = swap(pay_a, pay_b, "dev")
    concentration, flux, stored = call(
        store_kernel,
        [shaped(nx, nx, 256), shaped(nx, nx, 256), token_shape],
        [conc_new, flux_own],
        [pltpu.SemaphoreType.DMA((8,))],
        out_specs=[FAR, FAR, WHOLE],
        name="store",
    )
    wide = (quarter, 32, 256)
    rho, load, made = call(
        coarse_ready_kernel,
        [shaped(quarter, quarter, 256), shaped(8, LANES), token_shape],
        [conduct_coarse, yy_a, yy_b],
        [vmem(*wide)] * 4,
        name="coarse_ready",
    )
    pay_a, pay_b = call(
        mid_pack_x_kernel, [shaped(3 * HALO, 8, 256)] * 2, [source_mid, m_a, m_b, made, stored], name="mid_pack_x"
    )
    mx_a, mx_b = swap(pay_a, pay_b, "grp")
    mid_two, mid_source, mid_weight, source_coarse, wide_coarse, pay_a, pay_b, sums = call(
        mid_kernel,
        [shaped(*ext_mid)] * 3
        + [shaped(quarter, 12, 256), shaped(quarter, 12, 256), shaped(72, 256), shaped(80, 256), shaped(8, 256)],
        [source_mid, conduct_mid, yy_a, yy_b, xx_a, xx_b, m_a, m_b, mx_a, mx_b, rho, load],
        [vmem(*ext_mid)] * 2 + [vmem(8, 2, half + 2 * HALO, LANES)] * 2,
        name="middle",
    )
    c_a, c_b = swap(pay_a, pay_b, "dev")
    sums = sums + c_b[72:80]
    distance = 2
    while distance < peers:
        sums = sums + exchange(sums, distance)
        distance *= 2
    (error,) = call(
        coarse_kernel,
        [shaped(8, 16, 256)],
        [source_coarse, wide_coarse, yy_a, yy_b, c_a, c_b],
        [vmem(*wide)] * 4,
        name="coarse",
    )
    fields = [mid_two, mid_source, mid_weight, fine_two, fine_source, weight]
    kept = [shaped(4, half + 2 * HALO, 256)] * 2 + [shaped(4, nx + 2 * HALO, 256)] * 2
    scratch = [vmem(*ext_mid)] * 3 + [vmem(*ext)] * 2
    scratch += [vmem(8, 2, 2, 16, LANES), vmem(half + 2 * HALO, 3, 2, 16, LANES), vmem(nx, nx, 256)]
    scratch += [pltpu.SemaphoreType.DMA((2,))]
    error, pay_a, pay_b, begun, *kept_early = call(
        finish_early_kernel,
        [shaped(8, 16, 256), shaped(2, 16, 256), shaped(2, 16, 256), shaped(nx, nx, 256)] + kept,
        [error, sums] + fields,
        scratch,
        out_specs=[WHOLE] * 3 + [FAR] + [WHOLE] * 4,
        name="finish_early",
    )
    e_a, e_b = swap(pay_a, pay_b, "grp")
    begun, zero, one, fine_one, fine_last = call(
        finish_late_kernel,
        [shaped(nx, nx, 256)] + kept,
        [error] + fields + kept_early + [begun],
        scratch,
        in_specs=[WHOLE] * 11 + [FAR],
        out_specs=[FAR] + [WHOLE] * 4,
        aliases={11: 0},
        name="finish_late",
    )
    finish_args = [e_a, e_b, mid_two, mid_source, mid_weight, fine_two, edge_two, fine_source, edge_source, weight]
    finish_args += [zero, one, fine_one, fine_last, begun]
    (potential,) = call(
        finish_edge_kernel,
        [shaped(nx, nx, 256)],
        finish_args,
        [vmem(*ext_mid), vmem(*ext_mid), vmem(*ext), vmem(*ext)]
        + [vmem(4, 2, 2, 16, LANES), vmem(6, 3, 2, 16, LANES), vmem(nx, nx, 256)]
        + [pltpu.SemaphoreType.DMA((2,))],
        in_specs=[WHOLE] * (len(finish_args) - 1) + [FAR],
        out_specs=[FAR],
        aliases={len(finish_args) - 1: 0},
        name="finish_edge",
    )
    return (concentration, flux, potential)


def solution(mesh):
    brick = P("grp", "dev", None)
    return jax.shard_map(
        body,
        mesh=mesh,
        in_specs=(brick, brick, brick, brick, P("grp", "dev"), brick),
        out_specs=(brick, brick, brick),
        check_vma=False,
    )
```

```python
import jax
import jax.numpy as jnp
from jax import lax
from jax.experimental import pallas as pl
from jax.experimental.pallas import tpu as pltpu
from jax.sharding import PartitionSpec as P


F32 = jnp.float32
MASS = 0.05
OMEGA = 0.8
DIFFUSION_TABLE = (1.5, 0.1, 0.4)
RATIO_TABLE = tuple(d / (1.0 + 6.0 * d) for d in DIFFUSION_TABLE)
INVERSE_TABLE = tuple(1.0 / (1.0 + 6.0 * d) for d in DIFFUSION_TABLE)
CONDUCT_TABLE = (1.0, 0.3, 0.6)
KINETIC_TABLE = (0.2, 1.0, 0.5)
SWEEPS = 4
COARSE_SWEEPS = 8
COARSE_NEAR = 8
HALO = 4
LANES = 128
VMEM_LIMIT = 28 * 1024 * 1024
VMEM_MOST = 58 * 1024 * 1024


def shaped(*shape):
    return jax.ShapeDtypeStruct(shape, F32)


WHOLE = pl.BlockSpec(memory_space=pltpu.VMEM)
FAR = pl.BlockSpec(memory_space=pltpu.HBM)


def call(kernel, outs, args, scratch=(), in_specs=None, out_specs=None, limit=VMEM_LIMIT, aliases=None, flops=10**6, name=None):
    size = sum(4 * a.size for a in args) + sum(4 * o.size for o in outs)
    return pl.pallas_call(
        kernel,
        out_shape=tuple(outs),
        in_specs=in_specs or [WHOLE] * len(args),
        out_specs=tuple(out_specs or [WHOLE] * len(outs)),
        scratch_shapes=list(scratch),
        input_output_aliases=aliases or {},
        compiler_params=pltpu.CompilerParams(vmem_limit_bytes=limit),
        cost_estimate=pl.CostEstimate(flops=flops, bytes_accessed=size, transcendentals=0),
        name=name,
    )(*args)


def vmem(*shape):
    return pltpu.VMEM(shape, F32)


def iota(shape, dim):
    return lax.broadcasted_iota(jnp.int32, shape, dim)


def pick(label, table):
    return jnp.where(label == 0, table[0], jnp.where(label == 1, table[1], table[2])).astype(F32)


def loop(low, high, body, unroll=8):
    steps = (high - low) // unroll

    def step(i, carry):
        for u in range(unroll):
            body(low + i * unroll + u)
        return carry

    if steps > 1:
        lax.fori_loop(0, steps, step, 0)
    else:
        steps = 0
    for x in range(low + steps * unroll, high):
        body(x)


def odd(axis):
    return lax.rem(lax.axis_index(axis), 2) == 1


def along_y(v):
    return pltpu.roll(v, 1, 0) + pltpu.roll(v, v.shape[0] - 1, 0)


def along_z(v):
    low, high = v[:, :LANES], v[:, LANES:]
    lane = iota(low.shape, 1)
    first, last = lane == 0, lane == LANES - 1
    low_up, high_up = pltpu.roll(low, 1, 1), pltpu.roll(high, 1, 1)
    low_down, high_down = pltpu.roll(low, LANES - 1, 1), pltpu.roll(high, LANES - 1, 1)
    low_sum = jnp.where(first, 0.0, low_up) + jnp.where(last, high_down, low_down)
    high_sum = jnp.where(first, low_up, high_up) + jnp.where(last, 0.0, high_down)
    return jnp.concatenate([low_sum, high_sum], axis=1)


def upper(shape=(8, 256)):
    return iota(shape, 0) < HALO


def twice(tile, scratch):
    for h in range(2):
        part = tile[:, h * LANES : (h + 1) * LANES]
        scratch[h, pl.ds(0, 8, stride=2), :] = part
        scratch[h, pl.ds(1, 8, stride=2), :] = part
    return jnp.concatenate([scratch[0], scratch[1]], axis=1)


def pair_rows(v, scratch):
    half = v.shape[0] // 2
    parts = []
    for h in range(2):
        scratch[h] = v[:, h * LANES : (h + 1) * LANES]
        parts.append(scratch[h, pl.ds(0, half, stride=2), :] + scratch[h, pl.ds(1, half, stride=2), :])
    return jnp.concatenate(parts, axis=1)


def either(flag, if_true, if_false):
    return jnp.where(flag, if_true, if_false)


def y_sides(r_a, r_b, at, count):
    flag = odd("dev")
    a, b = r_a[at : at + count, :], r_b[at : at + count, :]
    return either(flag, a, b), either(flag, b, a)


def x_sides(r_a, r_b, index):
    flag = odd("grp")
    a, b = r_a[index], r_b[index]
    return either(flag, a, b), either(flag, b, a)


def send_y(pay_a, pay_b, at, first, last):
    flag = odd("dev")
    n = first.shape[0]
    pay_a[at : at + n, :] = either(flag, last, first)
    pay_b[at : at + n, :] = either(flag, first, last)


def send_x(pay_a, pay_b, index, first, last):
    flag = odd("grp")
    pay_a[index] = either(flag, last, first)
    pay_b[index] = either(flag, first, last)


def halo_tile(after, before):
    parts = [after]
    if after.shape[0] < HALO:
        parts.append(jnp.zeros((2 * HALO - 2 * after.shape[0], after.shape[1]), F32))
    return jnp.concatenate(parts + [before], axis=0)


def first_pack_kernel(
    conc, label, owner, block, pay_a, pay_b, own_lists, c_first, c_last, l_first, l_last, own_owner, own_block, sems
):
    nx = conc.shape[0]
    copies = [pltpu.make_async_copy(owner, own_owner, sems.at[4]), pltpu.make_async_copy(block, own_block, sems.at[5])]
    for i, (ref, at, to) in enumerate(((conc, 0, c_first), (conc, 28, c_last), (label, 0, l_first), (label, 28, l_last))):
        copies.append(pltpu.make_async_copy(ref.at[:, pl.ds(at, 4), :], to, sems.at[i]))
    for c in copies:
        c.start()
    for c in copies:
        c.wait()
    named = jnp.concatenate([own_owner[...], own_block[...], jnp.zeros((6, 256), jnp.int32)], axis=0).astype(F32)
    own_lists[...] = named
    for x in range(nx):
        send_y(pay_a, pay_b, 7 * x, c_first[x], c_last[x])
        send_y(pay_a, pay_b, 7 * x + 4, l_first[x, 0:3, :].astype(F32), l_last[x, 1:4, :].astype(F32))


def own_kernel(conc, label, phi, named, mid, coarse, pay_a, pay_b, lists, gain, base, pairs, pairs_2):
    nx = conc.shape[0]
    half = nx // 2
    lists[...] = named[0:2, :]

    def coefficients(i):
        gain[i] = pick(label[i], RATIO_TABLE)
        base[i] = conc[i] * pick(label[i], INVERSE_TABLE)

    loop(0, nx, coefficients, 4)

    def coarsen(i):
        total = conc[2 * i] * pick(label[2 * i], CONDUCT_TABLE) + conc[2 * i + 1] * pick(label[2 * i + 1], CONDUCT_TABLE)
        mid[i] = 0.25 * pair_rows(total, pairs.at[i])

    loop(0, half, coarsen, 4)
    for i in range(half // 2):
        coarse[i] = 0.25 * pair_rows(mid[2 * i] + mid[2 * i + 1], pairs_2.at[i])
    for k in range(HALO):
        for t in range(4):
            rows = slice(8 * t, 8 * t + 8)
            send_x(pay_a, pay_b, 4 * k + t, phi[k, rows, :], phi[nx - HALO + k, rows, :])
    for k in range(MID_HALO):
        for t in range(2):
            rows = slice(8 * t, 8 * t + 8)
            send_x(pay_a, pay_b, 16 + 2 * k + t, mid[k, rows, :], mid[half - MID_HALO + k, rows, :])


def first_pack_x_kernel(conc, label, r_a, r_b, token, pay_a, pay_b):
    nx = conc.shape[0]

    def plane(ref, k, t, offset, count):
        if t < 4:
            return ref[k, 8 * t : 8 * t + 8, :].astype(F32)
        return halo_tile(*y_sides(r_a, r_b, 7 * k + offset, count))

    for t in range(5):
        for k in range(HALO):
            send_x(pay_a, pay_b, 5 * k + t, plane(conc, k, t, 0, 4), plane(conc, nx - HALO + k, t, 0, 4))
        for k in range(3):
            send_x(pay_a, pay_b, 20 + 5 * k + t, plane(label, k, t, 4, 3), plane(label, nx - 3 + k, t, 4, 3))


MID_HALO = 3


def corner_rows(n, width, reach):
    counts = [min(width, k + reach) for k in range(width)]
    counts = counts + [width] * n + counts[::-1]
    return counts, [sum(counts[:i]) for i in range(len(counts))]


def second_rows(nx):
    phi = sum(corner_rows(nx, HALO, 0)[0])
    mid = sum(corner_rows(nx // 2, MID_HALO, 1)[0])
    return phi, phi + mid, phi + mid + 64


def second_pack_kernel(phi, mid, coarse, lists, x_a, x_b, pay_a, pay_b):
    nx = phi.shape[0]
    starts = second_rows(nx)

    def put(own, width, reach, index, base):
        n = own.shape[0]
        counts, at = corner_rows(n, width, reach)
        tiles = own.shape[1] // 8
        for x in range(n):
            send_y(pay_a, pay_b, base + at[width + x], own[x, 0:width, :], own[x, 8 * tiles - width : 8 * tiles, :])
        for k in range(width):
            first_after, first_before = x_sides(x_a, x_b, index + tiles * k)
            last_after, last_before = x_sides(x_a, x_b, index + tiles * k + tiles - 1)
            for x, first, last in ((k, first_before, last_before), (width + n + k, first_after, last_after)):
                if counts[x]:
                    send_y(pay_a, pay_b, base + at[x], first[0 : counts[x]], last[8 - counts[x] : 8])

    put(phi, HALO, 0, 0, 0)
    put(mid, MID_HALO, 1, 16, starts[0])
    base = starts[1]
    for x in range(8):
        pay_a[base + 8 * x : base + 8 * x + 8, :] = coarse[x]
        pay_b[base + 8 * x : base + 8 * x + 8, :] = coarse[x]
    base = starts[2]
    pay_b[base : base + lists.shape[0], :] = lists[...]


def second_halo(r_a, r_b, n, width, reach, x, base):
    counts, at = corner_rows(n, width, reach)
    x = x - HALO + width
    if x < 0 or x >= len(counts) or not counts[x]:
        return jnp.zeros((8, 256), F32)
    return halo_tile(*y_sides(r_a, r_b, base + at[x], counts[x]))


def wide_rows(own, after_own, before_own, after, before):
    gap = jnp.zeros((6, 256), F32)
    return jnp.concatenate([own, after_own, after, gap, before, before_own], axis=0)


def sweeps_kernel(conc, label, gain_own, base_own, y_a, y_b, x_a, x_b, out, one, two, gain_far, base_far, gain_x, base_x):
    nx = conc.shape[0]

    def own(i):
        one[HALO + i, 0:32, :] = conc[i]

    loop(0, nx, own)
    for i in range(nx):
        c = halo_tile(*y_sides(y_a, y_b, 7 * i, 4))
        lab = halo_tile(*y_sides(y_a, y_b, 7 * i + 4, 3))
        one[HALO + i, 32:40, :] = c
        gain_far[i] = jnp.where(c > 0.0, pick(lab, RATIO_TABLE), 0.0)
        base_far[i] = c * pick(lab, INVERSE_TABLE)

    def put(x, rows, c, lab):
        one[x, rows, :] = c
        at = x if x < HALO else x - nx
        gain_x[at, rows, :] = jnp.where(c > 0.0, pick(lab, RATIO_TABLE), 0.0)
        base_x[at, rows, :] = c * pick(lab, INVERSE_TABLE)

    for t in range(5):
        rows = slice(8 * t, 8 * t + 8)
        for k in range(HALO):
            c_after, c_before = x_sides(x_a, x_b, 5 * k + t)
            l_after = x_sides(x_a, x_b, 20 + 5 * min(k, 2) + t)[0]
            l_before = x_sides(x_a, x_b, 20 + 5 * max(k - 1, 0) + t)[1]
            put(k, rows, c_before, l_before)
            put(HALO + nx + k, rows, c_after, l_after)

    def neighbours(old, x):
        mid = old[x]
        return (old[x - 1] + old[x + 1]) + (along_y(mid) + along_z(mid))

    fields = (one, two)
    for s in range(1, SWEEPS):
        old, new = fields[(s - 1) % 2], fields[s % 2]

        def sweep(i, old=old, new=new):
            gain = jnp.concatenate([gain_own[i], gain_far[i]], axis=0)
            base = jnp.concatenate([base_own[i], base_far[i]], axis=0)
            new[HALO + i] = base + gain * neighbours(old, HALO + i)

        loop(0, nx, sweep)
        for k in range(s, HALO):
            for x, at in ((k, k), (2 * HALO + nx - 1 - k, 2 * HALO - 1 - k)):
                new[x] = base_x[at] + gain_x[at] * neighbours(old, x)

    old = fields[(SWEEPS - 1) % 2]

    def last(i):
        out[i] = base_own[i] + gain_own[i] * neighbours(old, HALO + i)[0:32, :]

    loop(0, nx, last)


def flux_kernel(conc, label, phi, solid, flux, pay_a, pay_b):
    nx = conc.shape[0]

    def plane(i):
        drive = 0.5 * (solid[i] - phi[i])
        logc = jnp.log(conc[i])
        value = jnp.exp(drive + 0.4 * logc) - jnp.exp(0.6 * logc - drive)
        flux[i] = pick(label[i], KINETIC_TABLE) * value

    loop(0, nx, plane, 4)
    for x in range(nx):
        send_y(pay_a, pay_b, 3 * x, flux[x, 0:3, :], flux[x, 29:32, :])


def mask_kernel(flux_all, lists, far, flux, halo_mask, marked):
    nx = flux_all.shape[0]
    rows = lists.shape[0]
    pieces = [lists[i : i + 1, :] for i in range(rows)] + [far[i : i + 1, :] for i in range(far.shape[0] - rows, far.shape[0])]
    owner = jnp.concatenate(pieces[0::2], axis=1).astype(jnp.int32)
    block = jnp.concatenate(pieces[1::2], axis=1).astype(jnp.int32)
    entries = owner.shape[1]
    hit_column = (iota((64, entries), 0) == lax.rem(block, 64)).astype(jnp.bfloat16)
    reach = owner - lax.axis_index("dev") + 1
    at_row = jnp.where((reach >= 0) & (reach < 3), reach * nx + lax.shift_right_arithmetic(block, 6), -1)
    hit_row = (iota((3 * nx, entries), 0) == at_row).astype(jnp.bfloat16)
    named = lax.dot_general(hit_row, hit_column, (((1,), (1,)), ((), ())), preferred_element_type=F32)
    named = jnp.concatenate([named, jnp.zeros((3 * nx, LANES - 64), F32)], axis=1)
    for j in range(3):
        for i in range(nx):
            marked[j, i] = jnp.broadcast_to(named[j * nx + i : j * nx + i + 1, :], (8, LANES))
    is_row = lax.div(iota((32, LANES), 1), 2) == iota((32, LANES), 0)
    row, pair = iota((8, LANES), 0), lax.div(iota((8, LANES), 1), 2)
    is_after = (row < 3) & (pair == row)
    is_before = (row >= 5) & (pair == row + 24)
    spread = (lax.rem(iota((LANES, 256), 0), 2) == lax.div(iota((LANES, 256), 1), LANES)).astype(jnp.bfloat16)

    def plane(i):
        marks = jnp.where(is_row, jnp.concatenate([marked[1, i]] * 4, axis=0), 0.0)
        beyond = jnp.where(is_after, marked[2, i], jnp.where(is_before, marked[0, i], 0.0))
        marks = jnp.concatenate([marks, beyond], axis=0).astype(jnp.bfloat16)
        listed = jnp.dot(marks, spread, preferred_element_type=F32) > 0.5
        flux[i] = jnp.where(listed[0:32], flux_all[i], 0.0)
        halo_mask[i] = jnp.where(listed[32:40], 1.0, 0.0)

    loop(0, nx, plane, 16)


def store_kernel(conc, flux, conc_out, flux_out, token, sems):
    copies = []
    for i, (ref, to) in enumerate(((conc, conc_out), (flux, flux_out))):
        for j in range(4):
            rows = pl.ds(8 * j, 8)
            copies.append(pltpu.make_async_copy(ref.at[rows], to.at[rows], sems.at[4 * i + j]))
            copies[-1].start()
    token[...] = jnp.zeros(token.shape, F32)
    for c in copies:
        c.wait()


def ready_kernel(conc, label, y_a, y_b, x_a, x_b, weight, scale, token):
    nx = conc.shape[0]
    token[...] = jnp.zeros(token.shape, F32)

    def put(x, rows, c, lab):
        conduct = c * pick(lab, CONDUCT_TABLE)
        factor = OMEGA / (MASS + 6.0 * conduct)
        weight[x, rows, :] = conduct * factor
        scale[x, rows, :] = factor

    def own(i):
        put(HALO + i, slice(0, 32), conc[i], label[i])

    loop(0, nx, own, 4)
    for i in range(nx):
        c = halo_tile(*y_sides(y_a, y_b, 7 * i, 4))
        lab = halo_tile(*y_sides(y_a, y_b, 7 * i + 4, 3))
        put(HALO + i, slice(32, 40), c, lab)
    for t in range(5):
        rows = slice(8 * t, 8 * t + 8)
        for k in range(HALO):
            c_after, c_before = x_sides(x_a, x_b, 5 * k + t)
            l_after = x_sides(x_a, x_b, 20 + 5 * min(k, 2) + t)[0]
            l_before = x_sides(x_a, x_b, 20 + 5 * max(k - 1, 0) + t)[1]
            put(k, rows, c_before, l_before)
            put(HALO + nx + k, rows, c_after, l_after)


def place_phi(phi, yy_a, yy_b, xx_a, xx_b, field):
    nx = phi.shape[0]

    def own(i):
        field[HALO + i, 0:32, :] = phi[i]

    loop(0, nx, own)
    for x in range(nx + 2 * HALO):
        field[x, 32:40, :] = second_halo(yy_a, yy_b, nx, HALO, 0, x, 0)
    for t in range(4):
        for k in range(HALO):
            after, before = x_sides(xx_a, xx_b, 4 * k + t)
            field[k, 8 * t : 8 * t + 8, :] = before
            field[HALO + nx + k, 8 * t : 8 * t + 8, :] = after


def flux_pack_x_kernel(flux, r_a, r_b, mask, token, pay_a, pay_b):
    nx = flux.shape[0]

    def tile(x, t):
        if t < 4:
            return flux[x, 8 * t : 8 * t + 8, :]
        return mask[x] * halo_tile(*y_sides(r_a, r_b, 3 * x, 3))

    for k in range(3):
        for t in range(5):
            send_x(pay_a, pay_b, 5 * k + t, tile(k, t), tile(nx - 3 + k, t))


def first_sweep(field, weight, scale, x, rows, flux):
    p = field[x]
    near = (field[x - 1] + field[x + 1]) + (along_y(p) + along_z(p))
    b = scale[x, rows, :] * (MASS * p[rows, :] + flux)
    return b, 0.2 * p[rows, :] + weight[x, rows, :] * near[rows, :] + b


def potential_inner_kernel(
    flux, mask, y_a, y_b, phi, yy_a, yy_b, xx_a, xx_b, weight, scale, after_two, source, first, source_mid, field, far, pairs
):
    nx = flux.shape[0]
    place_phi(phi, yy_a, yy_b, xx_a, xx_b, field)
    for i in range(nx):
        far[i] = mask[i] * halo_tile(*y_sides(y_a, y_b, 3 * i, 3))

    def own(i):
        x = HALO + i
        f = jnp.concatenate([flux[i], far[i]], axis=0)
        source[x], first[x] = first_sweep(field, weight, scale, x, slice(0, 40), f)

    loop(0, nx, own)

    def around(values, x):
        v = values[x]
        return v, weight[x] * ((values[x - 1] + values[x + 1]) + (along_y(v) + along_z(v)))

    def sweep(x):
        v, near = around(first, x)
        after_two[x] = 0.2 * v + (source[x] + near)

    loop(HALO + 1, HALO + nx - 1, sweep)

    def remainder(x):
        v, near = around(after_two, x)
        return ((source[x] - OMEGA * v) + near)[0:32, :] / scale[x, 0:32, :]

    def coarsen(i):
        x = HALO + 2 * i
        source_mid[i] = 0.25 * pair_rows(remainder(x) + remainder(x + 1), pairs.at[i])

    loop(1, nx // 2 - 1, coarsen, 4)


def mid_factor(conduct):
    return OMEGA / (MASS + 3.0 * conduct)


def potential_edge_kernel(
    x_a, x_b, weight, scale, field, inner_two, inner_source, inner_first, inner_mid, conduct_mid,
    edge_two, edge_source, source_mid, pay_a, pay_b, first, pairs,
):
    half = source_mid.shape[0]
    nx = 2 * half
    for side, face in ((0, HALO), (1, HALO + nx)):
        base = 8 * side + HALO - face
        for k in range(3):
            x = face - 3 + k if side == 0 else face + k
            f = jnp.concatenate([x_sides(x_a, x_b, 5 * k + t)[1 - side] for t in range(5)], axis=0)
            edge_source[base + x], first[base + x] = first_sweep(field, weight, scale, x, slice(0, 40), f)

        def first_of(x, base=base):
            return inner_first[x] if HALO <= x < HALO + nx else first[base + x]

        def source_of(x, base=base):
            return inner_source[x] if HALO <= x < HALO + nx else edge_source[base + x]

        def two_of(x, base=base):
            return inner_two[x] if HALO < x < HALO + nx - 1 else edge_two[base + x]

        for x in range(face - 2, face + 1) if side == 0 else range(face - 1, face + 2):
            v = first_of(x)
            near = weight[x] * ((first_of(x - 1) + first_of(x + 1)) + (along_y(v) + along_z(v)))
            edge_two[base + x] = 0.2 * v + (source_of(x) + near)
        total = 0.0
        at = face if side == 0 else face - 2
        for x in (at, at + 1):
            v = two_of(x)
            near = weight[x] * ((two_of(x - 1) + two_of(x + 1)) + (along_y(v) + along_z(v)))
            total = total + ((source_of(x) - OMEGA * v) + near)[0:32, :] / scale[x, 0:32, :]
        at = 0 if side == 0 else half - 1
        source_mid[at] = mid_factor(conduct_mid[at]) * (0.25 * pair_rows(total, pairs.at[side]))
    for x in range(1, half - 1):
        source_mid[x] = mid_factor(conduct_mid[x]) * inner_mid[x]
    for x in range(half):
        send_y(pay_a, pay_b, 4 * x, source_mid[x, 0:4, :], source_mid[x, 12:16, :])


def mid_pack_x_kernel(field, r_a, r_b, token, token_2, pay_a, pay_b):
    n = field.shape[0]

    def tile(x, t):
        if t < 2:
            return field[x, 8 * t : 8 * t + 8, :]
        return halo_tile(*y_sides(r_a, r_b, 4 * x, 4))

    for k in range(HALO):
        for t in range(3):
            send_x(pay_a, pay_b, 3 * k + t, tile(k, t), tile(n - HALO + k, t))


def mid_kernel(
    source_own, conduct_own, yy_a, yy_b, xx_a, xx_b, y_a, y_b, x_a, x_b, rho, load,
    after_two, source, weight, coarse, conduct, pay_a, pay_b, part, scale, mid_conduct, pairs, pairs_2,
):
    n = source_own.shape[0]
    base = second_rows(2 * n)[0]

    def put(x, rows, b, k):
        factor = mid_factor(k)
        weight[x, rows, :] = k * factor
        scale[x, rows, :] = factor
        source[x, rows, :] = b
        mid_conduct[x, rows, :] = k

    def far(x):
        return second_halo(yy_a, yy_b, n, MID_HALO, 1, x, base)

    for i in range(n):
        put(HALO + i, slice(0, 16), source_own[i], conduct_own[i])
        put(HALO + i, slice(16, 24), halo_tile(*y_sides(y_a, y_b, 4 * i, 4)), far(HALO + i))
    for k in range(HALO):
        for t in range(3):
            rows = slice(8 * t, 8 * t + 8)
            b_after, b_before = x_sides(x_a, x_b, 3 * k + t)
            if t < 2:
                none = jnp.zeros((8, 256), F32)
                c_before = x_sides(xx_a, xx_b, 16 + 2 * (k - 1) + t)[1] if k > 0 else none
                c_after = x_sides(xx_a, xx_b, 16 + 2 * k + t)[0] if k < MID_HALO else none
            else:
                c_after, c_before = far(HALO + n + k), far(k)
            put(k, rows, b_before, c_before)
            put(HALO + n + k, rows, b_after, c_after)

    def around(values, x):
        v = values[x]
        return v, weight[x] * (0.25 * ((values[x - 1] + values[x + 1]) + along_y(v)) + along_z(v))

    def sweep(x):
        v, near = around(source, x)
        after_two[x] = 0.2 * v + (source[x] + near)

    loop(1, n + 2 * HALO - 1, sweep, 11)

    def remainder(x):
        v, near = around(after_two, x)
        return ((source[x] - OMEGA * v) + near) / scale[x]

    total = jnp.zeros((8, 256), F32)
    for i in range(n // 2):
        x = HALO + 2 * i
        value = 0.25 * pair_rows(remainder(x) + remainder(x + 1), pairs.at[i])
        k = 0.25 * pair_rows(mid_conduct[x] + mid_conduct[x + 1], pairs_2.at[i])
        coarse[i] = value
        conduct[i] = k
        send_y(pay_a, pay_b, 9 * i, value[1:9], jnp.concatenate([value[11:12], value[0:7]], axis=0))
        send_y(pay_a, pay_b, 9 * i + 8, k[8:9], k[11:12])
        total += rho[i] * value[0:8]
    sums = jnp.concatenate([total[:, :LANES] + total[:, LANES:], load[...]], axis=1)
    pay_b[72:80, :] = sums
    part[...] = sums


COARSE_W = 0.0625


def coarse_ready_kernel(own, r_a, r_b, rho, load, token, one, two, conduct, scale):
    token[...] = jnp.zeros(token.shape, F32)
    base = r_a.shape[0] - 64
    for x in range(8):
        after, before = y_sides(r_a, r_b, base + 8 * x, 8)
        k = jnp.concatenate([own[x], after, jnp.zeros((8, 256), F32), before], axis=0)
        conduct[x] = k
        scale[x] = OMEGA / (MASS + 2.25 * k)
        one[x] = jnp.ones(k.shape, F32)
    fields = (one, two)
    for s in range(COARSE_SWEEPS):
        old, new = fields[s % 2], fields[(s + 1) % 2]
        for x in range(8):
            near = [conduct[i] * old[i] if 0 <= i < 8 else None for i in (x - 1, x, x + 1)]
            inner = along_y(near[1])
            for other in (near[0], near[2]):
                if other is not None:
                    inner = inner + other
            new[x] = 0.2 * old[x] + scale[x] * (COARSE_W * inner + along_z(near[1]))
    last = fields[COARSE_SWEEPS % 2]
    peer, peers = lax.axis_index("dev"), lax.axis_size("dev")
    row, z = iota((8, 256), 0), iota((8, 256), 1)
    edge_y = ((row == 0) & (peer == 0)) | ((row == 7) & (peer == peers - 1))
    edge = edge_y.astype(F32) * COARSE_W + ((z == 0) | (z == 255)).astype(F32)
    total = jnp.zeros((8, 256), F32)
    for x in range(8):
        rho[x] = last[x, 0:8, :]
        total += MASS + own[x] * (edge + (COARSE_W if x in (0, 7) else 0.0))
    load[...] = total[:, :LANES] + total[:, LANES:]


def coarse_kernel(own, conduct, far_a, far_b, r_a, r_b, error, source, weight, one, two):
    base = far_a.shape[0] - 64
    for x in range(8):
        after, before = y_sides(r_a, r_b, 9 * x, 8)
        b = wide_rows(own[x, 0:8, :], own[x, 8:9, :], own[x, 11:12, :], after, before)
        last_after, last_before = y_sides(r_a, r_b, 9 * x + 8, 1)
        after, before = y_sides(far_a, far_b, base + 8 * x, 8)
        after = jnp.concatenate([after[1:8], last_after], axis=0)
        before = jnp.concatenate([last_before, before[0:7]], axis=0)
        k = wide_rows(conduct[x, 0:8, :], conduct[x, 8:9, :], conduct[x, 11:12, :], after, before)
        factor = OMEGA / (MASS + 2.25 * k)
        weight[x] = k * factor
        source[x] = factor * b
    old = source
    for s in range(1, COARSE_SWEEPS):
        new = one if s % 2 else two
        for x in range(8):
            v = old[x]
            inner = along_y(v)
            if x > 0:
                inner = inner + old[x - 1]
            if x < 7:
                inner = inner + old[x + 1]
            new[x] = 0.2 * v + (source[x] + weight[x] * (COARSE_W * inner + along_z(v)))
        old = new
    for x in range(8):
        error[x, 0:8, :] = old[x, 0:8, :]
        error[x, 8:16, :] = jnp.where(upper(), old[x, 8:16, :], old[x, 24:32, :])


def squeeze(tile):
    return jnp.where(iota((8, 256), 0) < 2, tile, pltpu.roll(tile, 4, 0))


def spread_coarse(plane, room):
    return jnp.concatenate([twice(plane[0:8], room.at[0]), twice(squeeze(plane[8:16]), room.at[1])[0:8]], axis=0)


def spread_mid(plane, room):
    parts = [twice(plane[0:8], room.at[0]), twice(plane[8:16], room.at[1]), twice(squeeze(plane[16:24]), room.at[2])[0:8]]
    return jnp.concatenate(parts, axis=0)


def smoothed(before, v, after, weight, source, w):
    inner = (before + after) + along_y(v)
    return source + (0.2 * v + weight * (w * inner + along_z(v)))


def is_early():
    return (lax.axis_index("grp") < lax.axis_size("grp") // 2) | odd("grp")


def finish_inner(error, fields, kept, out, scratch):
    mid_two, mid_source, mid_weight, fine_two, fine_source, fine_weight = fields
    zero, one, two, fine_one, fine_last, dup, dup_2, result, sems = scratch
    n = mid_two.shape[0]
    nf = fine_two.shape[0]
    for c in range(8):
        spread = spread_coarse(error[c], dup.at[c])
        for x in (2 * c + HALO, 2 * c + 1 + HALO):
            zero[x] = jnp.where(mid_weight[x] > 0.0, mid_two[x] + spread, 0.0)

    def sweep_mid(x, old, new):
        new[x] = smoothed(old[x - 1], old[x], old[x + 1], mid_weight[x], mid_source[x], 0.25)

    for x in range(HALO + 1, n - HALO - 1):
        sweep_mid(x, zero, one)
    for x in range(HALO + 2, n - HALO - 2):
        sweep_mid(x, one, two)

    def lift(m):
        spread = spread_mid(two[m], dup_2.at[m])
        x = 2 * m - HALO
        fine_one[x] = fine_two[x] + spread
        fine_one[x + 1] = fine_two[x + 1] + spread

    loop(HALO + 2, n - HALO - 2, lift, 6)

    def sweep_one(x):
        fine_last[x] = smoothed(fine_one[x - 1], fine_one[x], fine_one[x + 1], fine_weight[x], fine_source[x], 1.0)

    low, high = 2 * HALO + 1, nf - 2 * HALO - 1
    loop(low, high, sweep_one, 11)
    for field, first, to in ((zero, 0, kept[0]), (one, 1, kept[1]), (fine_one, 4, kept[2]), (fine_last, 5, kept[3])):
        for j in range(2):
            to[j] = field[HALO + first + j]
            to[2 + j] = field[field.shape[0] - HALO - 1 - first - j]
    copies = []
    low, high = low + 1, high - 1
    for j in range(2):
        mid = low + (high - low) // 2
        for x in range(low, mid) if j == 0 else range(mid, high):
            v = smoothed(fine_last[x - 1], fine_last[x], fine_last[x + 1], fine_weight[x], fine_source[x], 1.0)
            result[x - HALO] = v[0:32, :]
        rows = pl.ds(low - HALO, mid - low) if j == 0 else pl.ds(mid - HALO, high - mid)
        copies.append(pltpu.make_async_copy(result.at[rows], out.at[rows], sems.at[j]))
        copies[-1].start()
    for c in copies:
        c.wait()


def finish_early_kernel(error, sums, *rest):
    fields, (shifted, pay_a, pay_b, out), kept, scratch = rest[:6], rest[6:10], rest[10:14], rest[14:]
    resid = jnp.sum(sums[:, :LANES])
    load = jnp.sum(sums[:, LANES:])
    shift_c = jnp.full((16, 256), resid, F32) / jnp.full((16, 256), load, F32)
    for x in range(8):
        shifted[x] = error[x] + shift_c
    for k in range(2):
        send_x(pay_a, pay_b, k, shifted[k], shifted[6 + k])

    @pl.when(is_early())
    def _():
        finish_inner(shifted, fields, kept, out, scratch)


def finish_late_kernel(error, *rest):
    fields, kept_early, out, kept, scratch = rest[:6], rest[6:10], rest[11], rest[12:16], rest[16:]

    @pl.when(is_early())
    def _():
        for a, b in zip(kept_early, kept):
            b[...] = a[...]

    @pl.when(jnp.logical_not(is_early()))
    def _():
        finish_inner(error, fields, kept, out, scratch)


def finish_edge(
    side, planes, mid_two, mid_source, mid_weight, fine_two, edge_two, fine_source, edge_source, fine_weight,
    zero, one, fine_one, fine_last, out, zero_edge, one_edge, fine_edge, last_edge, dup, dup_2, result, sem,
):
    n = mid_two.shape[0]
    nf = fine_two.shape[0]
    nx = nf - 2 * HALO
    at = lambda k: HALO + k if side == 0 else n - HALO - 1 - k
    fine = lambda k: HALO + k if side == 0 else nf - HALO - 1 - k
    base = 0 if side == 0 else 8 - nx
    for c in range(2):
        spread = spread_coarse(planes[c], dup.at[c])
        first = 2 * c if side == 0 else n - HALO + 2 * c
        for x in (first, first + 1):
            zero_edge[x] = jnp.where(mid_weight[x] > 0.0, mid_two[x] + spread, 0.0)

    def zero_of(k):
        return zero[2 * side + k] if k >= 0 else zero_edge[at(k)]

    def one_of(k):
        return one[2 * side + k - 1] if k >= 1 else one_edge[at(k)]

    for k in range(-2, 1):
        x = at(k)
        one_edge[x] = smoothed(zero_of(k - 1), zero_of(k), zero_of(k + 1), mid_weight[x], mid_source[x], 0.25)
    for k in range(-1, 2):
        x = at(k)
        value = smoothed(one_of(k - 1), one_of(k), one_of(k + 1), mid_weight[x], mid_source[x], 0.25)
        spread = spread_mid(value, dup_2.at[k + 1])
        for f in (fine(2 * k), fine(2 * k + 1)):
            inside = HALO < f < nf - HALO - 1
            before = fine_two[f] if inside else edge_two[base + f]
            fine_edge[f] = before + spread

    def fine_of(k):
        return fine_one[2 * side + k - 4] if k >= 4 else fine_edge[fine(k)]

    def last_of(k):
        return fine_last[2 * side + k - 5] if k >= 5 else last_edge[fine(k)]

    for k in range(-1, 5):
        f = fine(k)
        source = fine_source[f] if HALO <= f < nf - HALO else edge_source[base + f]
        last_edge[f] = smoothed(fine_of(k - 1), fine_of(k), fine_of(k + 1), fine_weight[f], source, 1.0)
    for k in range(6):
        f = fine(k)
        v = smoothed(last_of(k - 1), last_of(k), last_of(k + 1), fine_weight[f], fine_source[f], 1.0)
        result[f - HALO] = v[0:32, :]
    rows = pl.ds(0, 6) if side == 0 else pl.ds(nx - 6, 6)
    copy = pltpu.make_async_copy(result.at[rows], out.at[rows], sem)
    copy.start()
    copy.wait()


def finish_edge_kernel(second):
    def kernel(planes, *rest):
        fields, out, scratch = rest[:12], rest[13], rest[14:]
        after = odd("grp") if second else jnp.logical_not(odd("grp"))

        @pl.when(after)
        def _():
            finish_edge(1, planes, *fields, out, *scratch)

        @pl.when(jnp.logical_not(after))
        def _():
            finish_edge(0, planes, *fields, out, *scratch)

    return kernel


def both_ways(pairs):
    return pairs + [(j, i) for i, j in pairs]


def swap(pay_a, pay_b, axis):
    size = lax.axis_size(axis)
    pairs_a = [(i, i + 1) for i in range(1, size - 1, 2)]
    pairs_b = [(i, i + 1) for i in range(0, size - 1, 2)]
    return lax.ppermute(pay_a, axis, both_ways(pairs_a)), lax.ppermute(pay_b, axis, both_ways(pairs_b))


def exchange(value, distance):
    return lax.ppermute(value, "dev", [(i, i ^ distance) for i in range(lax.axis_size("dev"))])


def body(conc_old, phi_old, solid_pot, phase_label, iface_block, iface_owner):
    peers = lax.axis_size("dev")
    nx = conc_old.shape[0]
    half = nx // 2
    quarter = nx // 4
    ext = (nx + 2 * HALO, nx + 2 * HALO, 256)
    ext_mid = (half + 2 * HALO, half + 2 * HALO, 256)
    token_shape = shaped(8, LANES)

    pay_a, pay_b, own_lists = call(
        first_pack_kernel,
        [shaped(7 * nx, 256)] * 2 + [shaped(8, 256)],
        [conc_old, phase_label, iface_owner.reshape(1, -1), iface_block],
        [vmem(nx, HALO, 256)] * 2
        + [pltpu.VMEM((nx, HALO, 256), jnp.int32)] * 2
        + [pltpu.VMEM((1, 256), jnp.int32)] * 2
        + [pltpu.SemaphoreType.DMA((6,))],
        in_specs=[FAR] * 4,
        limit=VMEM_MOST,
        name="first_pack",
    )
    y_a, y_b = swap(pay_a, pay_b, "dev")
    conduct_mid, conduct_coarse, pay_a, pay_b, lists, gain, base = call(
        own_kernel,
        [shaped(half, half, 256), shaped(quarter, quarter, 256), shaped(22, 8, 256), shaped(22, 8, 256)]
        + [shaped(2, 256), shaped(nx, nx, 256), shaped(nx, nx, 256)],
        [conc_old, phase_label, phi_old, own_lists],
        [vmem(half, 2, nx, LANES), vmem(quarter, 2, half, LANES)],
        name="own",
    )
    xx_a, xx_b = swap(pay_a, pay_b, "grp")
    distance = peers // 2
    while distance > 1:
        lists = jnp.concatenate([lists, exchange(lists, distance)], axis=0)
        distance //= 2
    far_rows = second_rows(nx)[2]
    far_pay = call(
        second_pack_kernel,
        [shaped(far_rows, 256), shaped(far_rows + peers, 256)],
        [phi_old, conduct_mid, conduct_coarse, lists, xx_a, xx_b],
        name="second_pack",
    )
    yy_a, yy_b = swap(*far_pay, "dev")
    pay_a, pay_b = call(
        first_pack_x_kernel,
        [shaped(35, 8, 256)] * 2,
        [conc_old, phase_label, y_a, y_b, conduct_coarse],
        name="first_pack_x",
    )
    x_a, x_b = swap(pay_a, pay_b, "grp")

    (conc_new,) = call(
        sweeps_kernel,
        [shaped(nx, nx, 256)],
        [conc_old, phase_label, gain, base, y_a, y_b, x_a, x_b],
        [vmem(*ext)] * 2 + [vmem(nx, 8, 256)] * 2 + [vmem(2 * HALO, nx + 2 * HALO, 256)] * 2,
        name="sweeps",
    )
    flux_all, pay_a, pay_b = call(
        flux_kernel,
        [shaped(nx, nx, 256), shaped(3 * nx, 256), shaped(3 * nx, 256)],
        [conc_new, phase_label, phi_old, solid_pot],
        name="flux",
    )
    f_a, f_b = swap(pay_a, pay_b, "dev")
    flux_own, halo_mask = call(
        mask_kernel,
        [shaped(nx, nx, 256), shaped(nx, 8, 256)],
        [flux_all, lists, yy_b],
        [vmem(3, nx, 8, LANES)],
        name="mask",
    )
    weight, scale, made = call(
        ready_kernel,
        [shaped(*ext)] * 2 + [token_shape],
        [conc_old, phase_label, y_a, y_b, x_a, x_b],
        name="ready",
    )
    pay_a, pay_b = call(
        flux_pack_x_kernel, [shaped(15, 8, 256)] * 2, [flux_own, f_a, f_b, halo_mask, made], name="flux_pack_x"
    )
    fx_a, fx_b = swap(pay_a, pay_b, "grp")
    fine_two, fine_source, fine_first, inner_mid, field = call(
        potential_inner_kernel,
        [shaped(*ext)] * 3 + [shaped(half, half, 256), shaped(*ext)],
        [flux_own, halo_mask, f_a, f_b, phi_old, yy_a, yy_b, xx_a, xx_b, weight, scale],
        [vmem(nx, 8, 256), vmem(half, 2, nx, LANES)],
        name="potential_inner",
    )
    edge = (16, nx + 2 * HALO, 256)
    edge_two, edge_source, source_mid, pay_a, pay_b = call(
        potential_edge_kernel,
        [shaped(*edge), shaped(*edge), shaped(half, half, 256), shaped(4 * half, 256), shaped(4 * half, 256)],
        [fx_a, fx_b, weight, scale, field, fine_two, fine_source, fine_first, inner_mid, conduct_mid],
        [vmem(*edge), vmem(2, 2, nx, LANES)],
        name="potential_edge",
    )
    m_a, m_b = swap(pay_a, pay_b, "dev")
    concentration, flux, stored = call(
        store_kernel,
        [shaped(nx, nx, 256), shaped(nx, nx, 256), token_shape],
        [conc_new, flux_own],
        [pltpu.SemaphoreType.DMA((8,))],
        out_specs=[FAR, FAR, WHOLE],
        name="store",
    )
    wide = (quarter, 32, 256)
    rho, load, made = call(
        coarse_ready_kernel,
        [shaped(quarter, quarter, 256), shaped(8, LANES), token_shape],
        [conduct_coarse, yy_a, yy_b],
        [vmem(*wide)] * 4,
        name="coarse_ready",
    )
    pay_a, pay_b = call(
        mid_pack_x_kernel, [shaped(3 * HALO, 8, 256)] * 2, [source_mid, m_a, m_b, made, stored], name="mid_pack_x"
    )
    mx_a, mx_b = swap(pay_a, pay_b, "grp")
    mid_two, mid_source, mid_weight, source_coarse, wide_coarse, pay_a, pay_b, sums = call(
        mid_kernel,
        [shaped(*ext_mid)] * 3
        + [shaped(quarter, 12, 256), shaped(quarter, 12, 256), shaped(72, 256), shaped(80, 256), shaped(8, 256)],
        [source_mid, conduct_mid, yy_a, yy_b, xx_a, xx_b, m_a, m_b, mx_a, mx_b, rho, load],
        [vmem(*ext_mid)] * 2 + [vmem(8, 2, half + 2 * HALO, LANES)] * 2,
        name="middle",
    )
    c_a, c_b = swap(pay_a, pay_b, "dev")
    sums = sums + c_b[72:80]
    distance = 2
    while distance < peers:
        sums = sums + exchange(sums, distance)
        distance *= 2
    (error,) = call(
        coarse_kernel,
        [shaped(8, 16, 256)],
        [source_coarse, wide_coarse, yy_a, yy_b, c_a, c_b],
        [vmem(*wide)] * 4,
        name="coarse",
    )
    fields = [mid_two, mid_source, mid_weight, fine_two, fine_source, weight]
    kept = [shaped(4, half + 2 * HALO, 256)] * 2 + [shaped(4, nx + 2 * HALO, 256)] * 2
    scratch = [vmem(*ext_mid)] * 3 + [vmem(*ext)] * 2
    scratch += [vmem(8, 2, 2, 16, LANES), vmem(half + 2 * HALO, 3, 2, 16, LANES), vmem(nx, nx, 256)]
    scratch += [pltpu.SemaphoreType.DMA((2,))]
    error, pay_a, pay_b, begun, *kept_early = call(
        finish_early_kernel,
        [shaped(8, 16, 256), shaped(2, 16, 256), shaped(2, 16, 256), shaped(nx, nx, 256)] + kept,
        [error, sums] + fields,
        scratch,
        out_specs=[WHOLE] * 3 + [FAR] + [WHOLE] * 4,
        name="finish_early",
    )
    e_a, e_b = swap(pay_a, pay_b, "grp")
    begun, zero, one, fine_one, fine_last = call(
        finish_late_kernel,
        [shaped(nx, nx, 256)] + kept,
        [error] + fields + kept_early + [begun],
        scratch,
        in_specs=[WHOLE] * 11 + [FAR],
        out_specs=[FAR] + [WHOLE] * 4,
        aliases={11: 0},
        name="finish_late",
    )
    potential = begun
    finish_args = [mid_two, mid_source, mid_weight, fine_two, edge_two, fine_source, edge_source, weight]
    finish_args += [zero, one, fine_one, fine_last]
    for second, planes in ((False, e_b), (True, e_a)):
        (potential,) = call(
            finish_edge_kernel(second),
            [shaped(nx, nx, 256)],
            [planes] + finish_args + [potential],
            [vmem(*ext_mid), vmem(*ext_mid), vmem(*ext), vmem(*ext)]
            + [vmem(2, 2, 2, 16, LANES), vmem(3, 3, 2, 16, LANES), vmem(nx, nx, 256), pltpu.SemaphoreType.DMA],
            in_specs=[WHOLE] * 13 + [FAR],
            out_specs=[FAR],
            aliases={13: 0},
            name="finish_edge_2" if second else "finish_edge_1",
        )
    return (concentration, flux, potential)


def solution(mesh):
    brick = P("grp", "dev", None)
    return jax.shard_map(
        body,
        mesh=mesh,
        in_specs=(brick, brick, brick, brick, P("grp", "dev"), brick),
        out_specs=(brick, brick, brick),
        check_vma=False,
    )
```

```python
import jax
import jax.numpy as jnp
from jax import lax
from jax.experimental import pallas as pl
from jax.experimental.pallas import tpu as pltpu
from jax.sharding import PartitionSpec as P


F32 = jnp.float32
MASS = 0.05
OMEGA = 0.8
DIFFUSION_TABLE = (1.5, 0.1, 0.4)
RATIO_TABLE = tuple(d / (1.0 + 6.0 * d) for d in DIFFUSION_TABLE)
INVERSE_TABLE = tuple(1.0 / (1.0 + 6.0 * d) for d in DIFFUSION_TABLE)
CONDUCT_TABLE = (1.0, 0.3, 0.6)
KINETIC_TABLE = (0.2, 1.0, 0.5)
SWEEPS = 4
COARSE_SWEEPS = 8
COARSE_NEAR = 8
HALO = 4
LANES = 128
VMEM_LIMIT = 28 * 1024 * 1024
VMEM_MOST = 58 * 1024 * 1024


def shaped(*shape):
    return jax.ShapeDtypeStruct(shape, F32)


WHOLE = pl.BlockSpec(memory_space=pltpu.VMEM)
FAR = pl.BlockSpec(memory_space=pltpu.HBM)


def call(kernel, outs, args, scratch=(), in_specs=None, out_specs=None, limit=VMEM_LIMIT, aliases=None, flops=10**6, name=None):
    size = sum(4 * a.size for a in args) + sum(4 * o.size for o in outs)
    return pl.pallas_call(
        kernel,
        out_shape=tuple(outs),
        in_specs=in_specs or [WHOLE] * len(args),
        out_specs=tuple(out_specs or [WHOLE] * len(outs)),
        scratch_shapes=list(scratch),
        input_output_aliases=aliases or {},
        compiler_params=pltpu.CompilerParams(vmem_limit_bytes=limit),
        cost_estimate=pl.CostEstimate(flops=flops, bytes_accessed=size, transcendentals=0),
        name=name,
    )(*args)


def vmem(*shape):
    return pltpu.VMEM(shape, F32)


def iota(shape, dim):
    return lax.broadcasted_iota(jnp.int32, shape, dim)


def pick(label, table):
    return jnp.where(label == 0, table[0], jnp.where(label == 1, table[1], table[2])).astype(F32)


def loop(low, high, body, unroll=8):
    steps = (high - low) // unroll

    def step(i, carry):
        for u in range(unroll):
            body(low + i * unroll + u)
        return carry

    if steps > 1:
        lax.fori_loop(0, steps, step, 0)
    else:
        steps = 0
    for x in range(low + steps * unroll, high):
        body(x)


def odd(axis):
    return lax.rem(lax.axis_index(axis), 2) == 1


def along_y(v):
    return pltpu.roll(v, 1, 0) + pltpu.roll(v, v.shape[0] - 1, 0)


def along_z(v):
    low, high = v[:, :LANES], v[:, LANES:]
    lane = iota(low.shape, 1)
    first, last = lane == 0, lane == LANES - 1
    low_up, high_up = pltpu.roll(low, 1, 1), pltpu.roll(high, 1, 1)
    low_down, high_down = pltpu.roll(low, LANES - 1, 1), pltpu.roll(high, LANES - 1, 1)
    low_sum = jnp.where(first, 0.0, low_up) + jnp.where(last, high_down, low_down)
    high_sum = jnp.where(first, low_up, high_up) + jnp.where(last, 0.0, high_down)
    return jnp.concatenate([low_sum, high_sum], axis=1)


def upper(shape=(8, 256)):
    return iota(shape, 0) < HALO


def twice(tile, scratch):
    for h in range(2):
        part = tile[:, h * LANES : (h + 1) * LANES]
        scratch[h, pl.ds(0, 8, stride=2), :] = part
        scratch[h, pl.ds(1, 8, stride=2), :] = part
    return jnp.concatenate([scratch[0], scratch[1]], axis=1)


def pair_rows(v, scratch):
    half = v.shape[0] // 2
    parts = []
    for h in range(2):
        scratch[h] = v[:, h * LANES : (h + 1) * LANES]
        parts.append(scratch[h, pl.ds(0, half, stride=2), :] + scratch[h, pl.ds(1, half, stride=2), :])
    return jnp.concatenate(parts, axis=1)


def either(flag, if_true, if_false):
    return jnp.where(flag, if_true, if_false)


def y_sides(r_a, r_b, at, count):
    flag = odd("dev")
    a, b = r_a[at : at + count, :], r_b[at : at + count, :]
    return either(flag, a, b), either(flag, b, a)


def x_sides(r_a, r_b, index):
    flag = odd("grp")
    a, b = r_a[index], r_b[index]
    return either(flag, a, b), either(flag, b, a)


def send_y(pay_a, pay_b, at, first, last):
    flag = odd("dev")
    n = first.shape[0]
    pay_a[at : at + n, :] = either(flag, last, first)
    pay_b[at : at + n, :] = either(flag, first, last)


def send_x(pay_a, pay_b, index, first, last):
    flag = odd("grp")
    pay_a[index] = either(flag, last, first)
    pay_b[index] = either(flag, first, last)


def halo_tile(after, before):
    parts = [after]
    if after.shape[0] < HALO:
        parts.append(jnp.zeros((2 * HALO - 2 * after.shape[0], after.shape[1]), F32))
    return jnp.concatenate(parts + [before], axis=0)


def first_pack_kernel(
    conc, label, owner, block, out_a, out_b, own_lists,
    c_first, c_last, l_first, l_last, own_owner, own_block, pay_a, pay_b, named, sems,
):
    nx = conc.shape[0]
    half = nx // 2
    lists = [pltpu.make_async_copy(owner, own_owner, sems.at[8]), pltpu.make_async_copy(block, own_block, sems.at[9])]
    reads = []
    for j in range(2):
        planes = pl.ds(half * j, half)
        for i, (ref, at, to) in enumerate(
            ((conc, 0, c_first), (conc, 28, c_last), (label, 0, l_first), (label, 28, l_last))
        ):
            reads.append(pltpu.make_async_copy(ref.at[planes, pl.ds(at, 4), :], to.at[planes], sems.at[4 * j + i]))
    for c in reads + lists:
        c.start()
    writes = []
    for j in range(2):
        for c in reads[4 * j : 4 * j + 4]:
            c.wait()
        for x in range(half * j, half * j + half):
            send_y(pay_a, pay_b, 7 * x, c_first[x], c_last[x])
            send_y(pay_a, pay_b, 7 * x + 4, l_first[x, 0:3, :].astype(F32), l_last[x, 1:4, :].astype(F32))
        rows = pl.ds(7 * half * j, 7 * half)
        for i, (pay, out) in enumerate(((pay_a, out_a), (pay_b, out_b))):
            writes.append(pltpu.make_async_copy(pay.at[rows], out.at[rows], sems.at[10 + 2 * j + i]))
            writes[-1].start()
    for c in lists:
        c.wait()
    named[...] = jnp.concatenate([own_owner[...], own_block[...], jnp.zeros((6, 256), jnp.int32)], axis=0).astype(F32)
    writes.append(pltpu.make_async_copy(named, own_lists, sems.at[14]))
    writes[-1].start()
    for c in writes:
        c.wait()


def own_kernel(conc, label, phi, named, mid, coarse, pay_a, pay_b, lists, gain, base, pairs, pairs_2):
    nx = conc.shape[0]
    half = nx // 2
    lists[...] = named[0:2, :]

    def coefficients(i):
        gain[i] = pick(label[i], RATIO_TABLE)
        base[i] = conc[i] * pick(label[i], INVERSE_TABLE)

    loop(0, nx, coefficients, 4)

    def coarsen(i):
        total = conc[2 * i] * pick(label[2 * i], CONDUCT_TABLE) + conc[2 * i + 1] * pick(label[2 * i + 1], CONDUCT_TABLE)
        mid[i] = 0.25 * pair_rows(total, pairs.at[i])

    loop(0, half, coarsen, 4)
    for i in range(half // 2):
        coarse[i] = 0.25 * pair_rows(mid[2 * i] + mid[2 * i + 1], pairs_2.at[i])
    for k in range(HALO):
        for t in range(4):
            rows = slice(8 * t, 8 * t + 8)
            send_x(pay_a, pay_b, 4 * k + t, phi[k, rows, :], phi[nx - HALO + k, rows, :])
    for k in range(MID_HALO):
        for t in range(2):
            rows = slice(8 * t, 8 * t + 8)
            send_x(pay_a, pay_b, 16 + 2 * k + t, mid[k, rows, :], mid[half - MID_HALO + k, rows, :])


def first_pack_x_kernel(conc, label, r_a, r_b, token, pay_a, pay_b):
    nx = conc.shape[0]

    def plane(ref, k, t, offset, count):
        if t < 4:
            return ref[k, 8 * t : 8 * t + 8, :].astype(F32)
        return halo_tile(*y_sides(r_a, r_b, 7 * k + offset, count))

    for t in range(5):
        for k in range(HALO):
            send_x(pay_a, pay_b, 5 * k + t, plane(conc, k, t, 0, 4), plane(conc, nx - HALO + k, t, 0, 4))
        for k in range(3):
            send_x(pay_a, pay_b, 20 + 5 * k + t, plane(label, k, t, 4, 3), plane(label, nx - 3 + k, t, 4, 3))


MID_HALO = 3


def corner_rows(n, width, reach):
    counts = [min(width, k + reach) for k in range(width)]
    counts = counts + [width] * n + counts[::-1]
    return counts, [sum(counts[:i]) for i in range(len(counts))]


def second_rows(nx):
    phi = sum(corner_rows(nx, HALO, 0)[0])
    mid = sum(corner_rows(nx // 2, MID_HALO, 1)[0])
    return phi, phi + mid, phi + mid + 64


def second_pack_kernel(phi, mid, coarse, lists, x_a, x_b, pay_a, pay_b):
    nx = phi.shape[0]
    starts = second_rows(nx)

    def put(own, width, reach, index, base):
        n = own.shape[0]
        counts, at = corner_rows(n, width, reach)
        tiles = own.shape[1] // 8
        for x in range(n):
            send_y(pay_a, pay_b, base + at[width + x], own[x, 0:width, :], own[x, 8 * tiles - width : 8 * tiles, :])
        for k in range(width):
            first_after, first_before = x_sides(x_a, x_b, index + tiles * k)
            last_after, last_before = x_sides(x_a, x_b, index + tiles * k + tiles - 1)
            for x, first, last in ((k, first_before, last_before), (width + n + k, first_after, last_after)):
                if counts[x]:
                    send_y(pay_a, pay_b, base + at[x], first[0 : counts[x]], last[8 - counts[x] : 8])

    put(phi, HALO, 0, 0, 0)
    put(mid, MID_HALO, 1, 16, starts[0])
    base = starts[1]
    for x in range(8):
        pay_a[base + 8 * x : base + 8 * x + 8, :] = coarse[x]
        pay_b[base + 8 * x : base + 8 * x + 8, :] = coarse[x]
    base = starts[2]
    pay_b[base : base + lists.shape[0], :] = lists[...]


def second_halo(r_a, r_b, n, width, reach, x, base):
    counts, at = corner_rows(n, width, reach)
    x = x - HALO + width
    if x < 0 or x >= len(counts) or not counts[x]:
        return jnp.zeros((8, 256), F32)
    return halo_tile(*y_sides(r_a, r_b, base + at[x], counts[x]))


def wide_rows(own, after_own, before_own, after, before):
    gap = jnp.zeros((6, 256), F32)
    return jnp.concatenate([own, after_own, after, gap, before, before_own], axis=0)


def sweeps_kernel(conc, label, gain_own, base_own, y_a, y_b, x_a, x_b, out, one, two, gain_far, base_far, gain_x, base_x):
    nx = conc.shape[0]

    def own(i):
        one[HALO + i, 0:32, :] = conc[i]

    loop(0, nx, own)
    for i in range(nx):
        c = halo_tile(*y_sides(y_a, y_b, 7 * i, 4))
        lab = halo_tile(*y_sides(y_a, y_b, 7 * i + 4, 3))
        one[HALO + i, 32:40, :] = c
        gain_far[i] = jnp.where(c > 0.0, pick(lab, RATIO_TABLE), 0.0)
        base_far[i] = c * pick(lab, INVERSE_TABLE)

    def put(x, rows, c, lab):
        one[x, rows, :] = c
        at = x if x < HALO else x - nx
        gain_x[at, rows, :] = jnp.where(c > 0.0, pick(lab, RATIO_TABLE), 0.0)
        base_x[at, rows, :] = c * pick(lab, INVERSE_TABLE)

    for t in range(5):
        rows = slice(8 * t, 8 * t + 8)
        for k in range(HALO):
            c_after, c_before = x_sides(x_a, x_b, 5 * k + t)
            l_after = x_sides(x_a, x_b, 20 + 5 * min(k, 2) + t)[0]
            l_before = x_sides(x_a, x_b, 20 + 5 * max(k - 1, 0) + t)[1]
            put(k, rows, c_before, l_before)
            put(HALO + nx + k, rows, c_after, l_after)

    def neighbours(old, x):
        mid = old[x]
        return (old[x - 1] + old[x + 1]) + (along_y(mid) + along_z(mid))

    fields = (one, two)
    for s in range(1, SWEEPS):
        old, new = fields[(s - 1) % 2], fields[s % 2]

        def sweep(i, old=old, new=new):
            gain = jnp.concatenate([gain_own[i], gain_far[i]], axis=0)
            base = jnp.concatenate([base_own[i], base_far[i]], axis=0)
            new[HALO + i] = base + gain * neighbours(old, HALO + i)

        loop(0, nx, sweep)
        for k in range(s, HALO):
            for x, at in ((k, k), (2 * HALO + nx - 1 - k, 2 * HALO - 1 - k)):
                new[x] = base_x[at] + gain_x[at] * neighbours(old, x)

    old = fields[(SWEEPS - 1) % 2]

    def last(i):
        out[i] = base_own[i] + gain_own[i] * neighbours(old, HALO + i)[0:32, :]

    loop(0, nx, last)


def flux_kernel(conc, label, phi, solid, flux, pay_a, pay_b):
    nx = conc.shape[0]

    def plane(i):
        drive = 0.5 * (solid[i] - phi[i])
        logc = jnp.log(conc[i])
        value = jnp.exp(drive + 0.4 * logc) - jnp.exp(0.6 * logc - drive)
        flux[i] = pick(label[i], KINETIC_TABLE) * value

    loop(0, nx, plane, 4)
    for x in range(nx):
        send_y(pay_a, pay_b, 3 * x, flux[x, 0:3, :], flux[x, 29:32, :])


def mask_kernel(flux_all, lists, far, flux, halo_mask, marked):
    nx = flux_all.shape[0]
    rows = lists.shape[0]
    pieces = [lists[i : i + 1, :] for i in range(rows)] + [far[i : i + 1, :] for i in range(far.shape[0] - rows, far.shape[0])]
    owner = jnp.concatenate(pieces[0::2], axis=1).astype(jnp.int32)
    block = jnp.concatenate(pieces[1::2], axis=1).astype(jnp.int32)
    entries = owner.shape[1]
    hit_column = (iota((64, entries), 0) == lax.rem(block, 64)).astype(jnp.bfloat16)
    reach = owner - lax.axis_index("dev") + 1
    at_row = jnp.where((reach >= 0) & (reach < 3), reach * nx + lax.shift_right_arithmetic(block, 6), -1)
    hit_row = (iota((3 * nx, entries), 0) == at_row).astype(jnp.bfloat16)
    named = lax.dot_general(hit_row, hit_column, (((1,), (1,)), ((), ())), preferred_element_type=F32)
    named = jnp.concatenate([named, jnp.zeros((3 * nx, LANES - 64), F32)], axis=1)
    for j in range(3):
        for i in range(nx):
            marked[j, i] = jnp.broadcast_to(named[j * nx + i : j * nx + i + 1, :], (8, LANES))
    is_row = lax.div(iota((32, LANES), 1), 2) == iota((32, LANES), 0)
    row, pair = iota((8, LANES), 0), lax.div(iota((8, LANES), 1), 2)
    is_after = (row < 3) & (pair == row)
    is_before = (row >= 5) & (pair == row + 24)
    spread = (lax.rem(iota((LANES, 256), 0), 2) == lax.div(iota((LANES, 256), 1), LANES)).astype(jnp.bfloat16)

    def plane(i):
        marks = jnp.where(is_row, jnp.concatenate([marked[1, i]] * 4, axis=0), 0.0)
        beyond = jnp.where(is_after, marked[2, i], jnp.where(is_before, marked[0, i], 0.0))
        marks = jnp.concatenate([marks, beyond], axis=0).astype(jnp.bfloat16)
        listed = jnp.dot(marks, spread, preferred_element_type=F32) > 0.5
        flux[i] = jnp.where(listed[0:32], flux_all[i], 0.0)
        halo_mask[i] = jnp.where(listed[32:40], 1.0, 0.0)

    loop(0, nx, plane, 16)


def store_kernel(conc, flux, conc_out, flux_out, token, sems):
    copies = []
    for i, (ref, to) in enumerate(((conc, conc_out), (flux, flux_out))):
        for j in range(4):
            rows = pl.ds(8 * j, 8)
            copies.append(pltpu.make_async_copy(ref.at[rows], to.at[rows], sems.at[4 * i + j]))
            copies[-1].start()
    token[...] = jnp.zeros(token.shape, F32)
    for c in copies:
        c.wait()


def ready_kernel(conc, label, y_a, y_b, x_a, x_b, weight, scale, token):
    nx = conc.shape[0]
    token[...] = jnp.zeros(token.shape, F32)

    def put(x, rows, c, lab):
        conduct = c * pick(lab, CONDUCT_TABLE)
        factor = OMEGA / (MASS + 6.0 * conduct)
        weight[x, rows, :] = conduct * factor
        scale[x, rows, :] = factor

    def own(i):
        put(HALO + i, slice(0, 32), conc[i], label[i])

    loop(0, nx, own, 4)
    for i in range(nx):
        c = halo_tile(*y_sides(y_a, y_b, 7 * i, 4))
        lab = halo_tile(*y_sides(y_a, y_b, 7 * i + 4, 3))
        put(HALO + i, slice(32, 40), c, lab)
    for t in range(5):
        rows = slice(8 * t, 8 * t + 8)
        for k in range(HALO):
            c_after, c_before = x_sides(x_a, x_b, 5 * k + t)
            l_after = x_sides(x_a, x_b, 20 + 5 * min(k, 2) + t)[0]
            l_before = x_sides(x_a, x_b, 20 + 5 * max(k - 1, 0) + t)[1]
            put(k, rows, c_before, l_before)
            put(HALO + nx + k, rows, c_after, l_after)


def place_phi(phi, yy_a, yy_b, xx_a, xx_b, field):
    nx = phi.shape[0]

    def own(i):
        field[HALO + i, 0:32, :] = phi[i]

    loop(0, nx, own)
    for x in range(nx + 2 * HALO):
        field[x, 32:40, :] = second_halo(yy_a, yy_b, nx, HALO, 0, x, 0)
    for t in range(4):
        for k in range(HALO):
            after, before = x_sides(xx_a, xx_b, 4 * k + t)
            field[k, 8 * t : 8 * t + 8, :] = before
            field[HALO + nx + k, 8 * t : 8 * t + 8, :] = after


def flux_pack_x_kernel(flux, r_a, r_b, mask, token, pay_a, pay_b):
    nx = flux.shape[0]

    def tile(x, t):
        if t < 4:
            return flux[x, 8 * t : 8 * t + 8, :]
        return mask[x] * halo_tile(*y_sides(r_a, r_b, 3 * x, 3))

    for k in range(3):
        for t in range(5):
            send_x(pay_a, pay_b, 5 * k + t, tile(k, t), tile(nx - 3 + k, t))


def first_sweep(field, weight, scale, x, rows, flux):
    p = field[x]
    near = (field[x - 1] + field[x + 1]) + (along_y(p) + along_z(p))
    b = scale[x, rows, :] * (MASS * p[rows, :] + flux)
    return b, 0.2 * p[rows, :] + weight[x, rows, :] * near[rows, :] + b


def potential_inner_kernel(
    flux, mask, y_a, y_b, phi, yy_a, yy_b, xx_a, xx_b, weight, scale, after_two, source, first, source_mid, field, far, pairs
):
    nx = flux.shape[0]
    place_phi(phi, yy_a, yy_b, xx_a, xx_b, field)
    for i in range(nx):
        far[i] = mask[i] * halo_tile(*y_sides(y_a, y_b, 3 * i, 3))

    def own(i):
        x = HALO + i
        f = jnp.concatenate([flux[i], far[i]], axis=0)
        source[x], first[x] = first_sweep(field, weight, scale, x, slice(0, 40), f)

    loop(0, nx, own)

    def around(values, x):
        v = values[x]
        return v, weight[x] * ((values[x - 1] + values[x + 1]) + (along_y(v) + along_z(v)))

    def sweep(x):
        v, near = around(first, x)
        after_two[x] = 0.2 * v + (source[x] + near)

    loop(HALO + 1, HALO + nx - 1, sweep)

    def remainder(x):
        v, near = around(after_two, x)
        return ((source[x] - OMEGA * v) + near)[0:32, :] / scale[x, 0:32, :]

    def coarsen(i):
        x = HALO + 2 * i
        source_mid[i] = 0.25 * pair_rows(remainder(x) + remainder(x + 1), pairs.at[i])

    loop(1, nx // 2 - 1, coarsen, 4)


def mid_factor(conduct):
    return OMEGA / (MASS + 3.0 * conduct)


def potential_edge_kernel(
    x_a, x_b, weight, scale, field, inner_two, inner_source, inner_first, inner_mid, conduct_mid,
    edge_two, edge_source, source_mid, pay_a, pay_b, first, pairs,
):
    half = source_mid.shape[0]
    nx = 2 * half
    for side, face in ((0, HALO), (1, HALO + nx)):
        base = 8 * side + HALO - face
        for k in range(3):
            x = face - 3 + k if side == 0 else face + k
            f = jnp.concatenate([x_sides(x_a, x_b, 5 * k + t)[1 - side] for t in range(5)], axis=0)
            edge_source[base + x], first[base + x] = first_sweep(field, weight, scale, x, slice(0, 40), f)

        def first_of(x, base=base):
            return inner_first[x] if HALO <= x < HALO + nx else first[base + x]

        def source_of(x, base=base):
            return inner_source[x] if HALO <= x < HALO + nx else edge_source[base + x]

        def two_of(x, base=base):
            return inner_two[x] if HALO < x < HALO + nx - 1 else edge_two[base + x]

        for x in range(face - 2, face + 1) if side == 0 else range(face - 1, face + 2):
            v = first_of(x)
            near = weight[x] * ((first_of(x - 1) + first_of(x + 1)) + (along_y(v) + along_z(v)))
            edge_two[base + x] = 0.2 * v + (source_of(x) + near)
        total = 0.0
        at = face if side == 0 else face - 2
        for x in (at, at + 1):
            v = two_of(x)
            near = weight[x] * ((two_of(x - 1) + two_of(x + 1)) + (along_y(v) + along_z(v)))
            total = total + ((source_of(x) - OMEGA * v) + near)[0:32, :] / scale[x, 0:32, :]
        at = 0 if side == 0 else half - 1
        source_mid[at] = mid_factor(conduct_mid[at]) * (0.25 * pair_rows(total, pairs.at[side]))
    for x in range(1, half - 1):
        source_mid[x] = mid_factor(conduct_mid[x]) * inner_mid[x]
    for x in range(half):
        send_y(pay_a, pay_b, 4 * x, source_mid[x, 0:4, :], source_mid[x, 12:16, :])


def mid_pack_x_kernel(field, r_a, r_b, token, token_2, pay_a, pay_b):
    n = field.shape[0]

    def tile(x, t):
        if t < 2:
            return field[x, 8 * t : 8 * t + 8, :]
        return halo_tile(*y_sides(r_a, r_b, 4 * x, 4))

    for k in range(HALO):
        for t in range(3):
            send_x(pay_a, pay_b, 3 * k + t, tile(k, t), tile(n - HALO + k, t))


def mid_kernel(
    source_own, conduct_own, yy_a, yy_b, xx_a, xx_b, y_a, y_b, x_a, x_b, rho, load,
    after_two, source, weight, coarse, conduct, pay_a, pay_b, part, scale, mid_conduct, pairs, pairs_2,
):
    n = source_own.shape[0]
    base = second_rows(2 * n)[0]

    def put(x, rows, b, k):
        factor = mid_factor(k)
        weight[x, rows, :] = k * factor
        scale[x, rows, :] = factor
        source[x, rows, :] = b
        mid_conduct[x, rows, :] = k

    def far(x):
        return second_halo(yy_a, yy_b, n, MID_HALO, 1, x, base)

    for i in range(n):
        put(HALO + i, slice(0, 16), source_own[i], conduct_own[i])
        put(HALO + i, slice(16, 24), halo_tile(*y_sides(y_a, y_b, 4 * i, 4)), far(HALO + i))
    for k in range(HALO):
        for t in range(3):
            rows = slice(8 * t, 8 * t + 8)
            b_after, b_before = x_sides(x_a, x_b, 3 * k + t)
            if t < 2:
                none = jnp.zeros((8, 256), F32)
                c_before = x_sides(xx_a, xx_b, 16 + 2 * (k - 1) + t)[1] if k > 0 else none
                c_after = x_sides(xx_a, xx_b, 16 + 2 * k + t)[0] if k < MID_HALO else none
            else:
                c_after, c_before = far(HALO + n + k), far(k)
            put(k, rows, b_before, c_before)
            put(HALO + n + k, rows, b_after, c_after)

    def around(values, x):
        v = values[x]
        return v, weight[x] * (0.25 * ((values[x - 1] + values[x + 1]) + along_y(v)) + along_z(v))

    def sweep(x):
        v, near = around(source, x)
        after_two[x] = 0.2 * v + (source[x] + near)

    loop(1, n + 2 * HALO - 1, sweep, 11)

    def remainder(x):
        v, near = around(after_two, x)
        return ((source[x] - OMEGA * v) + near) / scale[x]

    total = jnp.zeros((8, 256), F32)
    for i in range(n // 2):
        x = HALO + 2 * i
        value = 0.25 * pair_rows(remainder(x) + remainder(x + 1), pairs.at[i])
        k = 0.25 * pair_rows(mid_conduct[x] + mid_conduct[x + 1], pairs_2.at[i])
        coarse[i] = value
        conduct[i] = k
        send_y(pay_a, pay_b, 9 * i, value[1:9], jnp.concatenate([value[11:12], value[0:7]], axis=0))
        send_y(pay_a, pay_b, 9 * i + 8, k[8:9], k[11:12])
        total += rho[i] * value[0:8]
    sums = jnp.concatenate([total[:, :LANES] + total[:, LANES:], load[...]], axis=1)
    pay_b[72:80, :] = sums
    part[...] = sums


COARSE_W = 0.0625


def coarse_ready_kernel(own, r_a, r_b, rho, load, token, one, two, conduct, scale):
    token[...] = jnp.zeros(token.shape, F32)
    base = r_a.shape[0] - 64
    for x in range(8):
        after, before = y_sides(r_a, r_b, base + 8 * x, 8)
        k = jnp.concatenate([own[x], after, jnp.zeros((8, 256), F32), before], axis=0)
        conduct[x] = k
        scale[x] = OMEGA / (MASS + 2.25 * k)
        one[x] = jnp.ones(k.shape, F32)
    fields = (one, two)
    for s in range(COARSE_SWEEPS):
        old, new = fields[s % 2], fields[(s + 1) % 2]
        for x in range(8):
            near = [conduct[i] * old[i] if 0 <= i < 8 else None for i in (x - 1, x, x + 1)]
            inner = along_y(near[1])
            for other in (near[0], near[2]):
                if other is not None:
                    inner = inner + other
            new[x] = 0.2 * old[x] + scale[x] * (COARSE_W * inner + along_z(near[1]))
    last = fields[COARSE_SWEEPS % 2]
    peer, peers = lax.axis_index("dev"), lax.axis_size("dev")
    row, z = iota((8, 256), 0), iota((8, 256), 1)
    edge_y = ((row == 0) & (peer == 0)) | ((row == 7) & (peer == peers - 1))
    edge = edge_y.astype(F32) * COARSE_W + ((z == 0) | (z == 255)).astype(F32)
    total = jnp.zeros((8, 256), F32)
    for x in range(8):
        rho[x] = last[x, 0:8, :]
        total += MASS + own[x] * (edge + (COARSE_W if x in (0, 7) else 0.0))
    load[...] = total[:, :LANES] + total[:, LANES:]


def coarse_kernel(own, conduct, far_a, far_b, r_a, r_b, error, source, weight, one, two):
    base = far_a.shape[0] - 64
    for x in range(8):
        after, before = y_sides(r_a, r_b, 9 * x, 8)
        b = wide_rows(own[x, 0:8, :], own[x, 8:9, :], own[x, 11:12, :], after, before)
        last_after, last_before = y_sides(r_a, r_b, 9 * x + 8, 1)
        after, before = y_sides(far_a, far_b, base + 8 * x, 8)
        after = jnp.concatenate([after[1:8], last_after], axis=0)
        before = jnp.concatenate([last_before, before[0:7]], axis=0)
        k = wide_rows(conduct[x, 0:8, :], conduct[x, 8:9, :], conduct[x, 11:12, :], after, before)
        factor = OMEGA / (MASS + 2.25 * k)
        weight[x] = k * factor
        source[x] = factor * b
    old = source
    for s in range(1, COARSE_SWEEPS):
        new = one if s % 2 else two
        for x in range(8):
            v = old[x]
            inner = along_y(v)
            if x > 0:
                inner = inner + old[x - 1]
            if x < 7:
                inner = inner + old[x + 1]
            new[x] = 0.2 * v + (source[x] + weight[x] * (COARSE_W * inner + along_z(v)))
        old = new
    for x in range(8):
        error[x, 0:8, :] = old[x, 0:8, :]
        error[x, 8:16, :] = jnp.where(upper(), old[x, 8:16, :], old[x, 24:32, :])


def squeeze(tile):
    return jnp.where(iota((8, 256), 0) < 2, tile, pltpu.roll(tile, 4, 0))


def spread_coarse(plane, room):
    return jnp.concatenate([twice(plane[0:8], room.at[0]), twice(squeeze(plane[8:16]), room.at[1])[0:8]], axis=0)


def spread_mid(plane, room):
    parts = [twice(plane[0:8], room.at[0]), twice(plane[8:16], room.at[1]), twice(squeeze(plane[16:24]), room.at[2])[0:8]]
    return jnp.concatenate(parts, axis=0)


def smoothed(before, v, after, weight, source, w):
    inner = (before + after) + along_y(v)
    return source + (0.2 * v + weight * (w * inner + along_z(v)))


def is_early():
    return (lax.axis_index("grp") < lax.axis_size("grp") // 2) | odd("grp")


def finish_inner(error, fields, kept, out, scratch):
    mid_two, mid_source, mid_weight, fine_two, fine_source, fine_weight = fields
    zero, one, two, fine_one, fine_last, dup, dup_2, result, sems = scratch
    n = mid_two.shape[0]
    nf = fine_two.shape[0]
    for c in range(8):
        spread = spread_coarse(error[c], dup.at[c])
        for x in (2 * c + HALO, 2 * c + 1 + HALO):
            zero[x] = jnp.where(mid_weight[x] > 0.0, mid_two[x] + spread, 0.0)

    def sweep_mid(x, old, new):
        new[x] = smoothed(old[x - 1], old[x], old[x + 1], mid_weight[x], mid_source[x], 0.25)

    for x in range(HALO + 1, n - HALO - 1):
        sweep_mid(x, zero, one)
    for x in range(HALO + 2, n - HALO - 2):
        sweep_mid(x, one, two)

    def lift(m):
        spread = spread_mid(two[m], dup_2.at[m])
        x = 2 * m - HALO
        fine_one[x] = fine_two[x] + spread
        fine_one[x + 1] = fine_two[x + 1] + spread

    loop(HALO + 2, n - HALO - 2, lift, 6)

    def sweep_one(x):
        fine_last[x] = smoothed(fine_one[x - 1], fine_one[x], fine_one[x + 1], fine_weight[x], fine_source[x], 1.0)

    low, high = 2 * HALO + 1, nf - 2 * HALO - 1
    loop(low, high, sweep_one, 11)
    for field, first, to in ((zero, 0, kept[0]), (one, 1, kept[1]), (fine_one, 4, kept[2]), (fine_last, 5, kept[3])):
        for j in range(2):
            to[j] = field[HALO + first + j]
            to[2 + j] = field[field.shape[0] - HALO - 1 - first - j]
    copies = []
    low, high = low + 1, high - 1
    for j in range(2):
        mid = low + (high - low) // 2
        for x in range(low, mid) if j == 0 else range(mid, high):
            v = smoothed(fine_last[x - 1], fine_last[x], fine_last[x + 1], fine_weight[x], fine_source[x], 1.0)
            result[x - HALO] = v[0:32, :]
        rows = pl.ds(low - HALO, mid - low) if j == 0 else pl.ds(mid - HALO, high - mid)
        copies.append(pltpu.make_async_copy(result.at[rows], out.at[rows], sems.at[j]))
        copies[-1].start()
    for c in copies:
        c.wait()


def finish_early_kernel(error, sums, *rest):
    fields, (shifted, pay_a, pay_b, out), kept, scratch = rest[:6], rest[6:10], rest[10:14], rest[14:]
    resid = jnp.sum(sums[:, :LANES])
    load = jnp.sum(sums[:, LANES:])
    shift_c = jnp.full((16, 256), resid, F32) / jnp.full((16, 256), load, F32)
    for x in range(8):
        shifted[x] = error[x] + shift_c
    for k in range(2):
        send_x(pay_a, pay_b, k, shifted[k], shifted[6 + k])

    @pl.when(is_early())
    def _():
        finish_inner(shifted, fields, kept, out, scratch)


def finish_late_kernel(error, *rest):
    fields, kept_early, out, kept, scratch = rest[:6], rest[6:10], rest[11], rest[12:16], rest[16:]

    @pl.when(is_early())
    def _():
        for a, b in zip(kept_early, kept):
            b[...] = a[...]

    @pl.when(jnp.logical_not(is_early()))
    def _():
        finish_inner(error, fields, kept, out, scratch)


def finish_edge_kernel(
    x_a, x_b, mid_two, mid_source, mid_weight, fine_two, edge_two, fine_source, edge_source, fine_weight,
    zero, one, fine_one, fine_last, begun, out, zero_edge, one_edge, fine_edge, last_edge, dup, dup_2, result, sems,
):
    n = mid_two.shape[0]
    nf = fine_two.shape[0]
    nx = nf - 2 * HALO
    copies = []
    planes = x_sides(x_a, x_b, slice(0, 2))
    for side in (0, 1):
        sign = 1 if side == 0 else -1
        at = lambda k, side=side: HALO + k if side == 0 else n - HALO - 1 - k
        fine = lambda k, side=side: HALO + k if side == 0 else nf - HALO - 1 - k
        base = 8 * side + (0 if side == 0 else HALO - HALO - nx)
        for c in range(2):
            plane = planes[1 - side][c]
            spread = spread_coarse(plane, dup.at[2 * side + c])
            first = 2 * c if side == 0 else n - HALO + 2 * c
            for x in (first, first + 1):
                zero_edge[x] = jnp.where(mid_weight[x] > 0.0, mid_two[x] + spread, 0.0)

        def zero_of(k, side=side):
            return zero[2 * side + k] if k >= 0 else zero_edge[at(k)]

        def one_of(k, side=side):
            return one[2 * side + k - 1] if k >= 1 else one_edge[at(k)]

        for k in range(-2, 1):
            x = at(k)
            one_edge[x] = smoothed(zero_of(k - 1), zero_of(k), zero_of(k + 1), mid_weight[x], mid_source[x], 0.25)
        for k in range(-1, 2):
            x = at(k)
            value = smoothed(one_of(k - 1), one_of(k), one_of(k + 1), mid_weight[x], mid_source[x], 0.25)
            spread = spread_mid(value, dup_2.at[3 * side + k + 1])
            for f in (fine(2 * k), fine(2 * k + 1)):
                inside = HALO < f < nf - HALO - 1
                before = fine_two[f] if inside else edge_two[base + f]
                fine_edge[f] = before + spread

        def fine_of(k, side=side):
            return fine_one[2 * side + k - 4] if k >= 4 else fine_edge[fine(k)]

        def last_of(k, side=side):
            return fine_last[2 * side + k - 5] if k >= 5 else last_edge[fine(k)]

        for k in range(-1, 5):
            f = fine(k)
            source = fine_source[f] if HALO <= f < nf - HALO else edge_source[base + f]
            last_edge[f] = smoothed(fine_of(k - 1), fine_of(k), fine_of(k + 1), fine_weight[f], source, 1.0)
        for k in range(6):
            f = fine(k)
            v = smoothed(last_of(k - 1), last_of(k), last_of(k + 1), fine_weight[f], fine_source[f], 1.0)
            result[f - HALO] = v[0:32, :]
        rows = pl.ds(0, 6) if side == 0 else pl.ds(nx - 6, 6)
        copies.append(pltpu.make_async_copy(result.at[rows], out.at[rows], sems.at[side]))
        copies[-1].start()
    for c in copies:
        c.wait()


def both_ways(pairs):
    return pairs + [(j, i) for i, j in pairs]


def swap(pay_a, pay_b, axis):
    size = lax.axis_size(axis)
    pairs_a = [(i, i + 1) for i in range(1, size - 1, 2)]
    pairs_b = [(i, i + 1) for i in range(0, size - 1, 2)]
    return lax.ppermute(pay_a, axis, both_ways(pairs_a)), lax.ppermute(pay_b, axis, both_ways(pairs_b))


def exchange(value, distance):
    return lax.ppermute(value, "dev", [(i, i ^ distance) for i in range(lax.axis_size("dev"))])


def body(conc_old, phi_old, solid_pot, phase_label, iface_block, iface_owner):
    peers = lax.axis_size("dev")
    nx = conc_old.shape[0]
    half = nx // 2
    quarter = nx // 4
    ext = (nx + 2 * HALO, nx + 2 * HALO, 256)
    ext_mid = (half + 2 * HALO, half + 2 * HALO, 256)
    token_shape = shaped(8, LANES)

    pay_a, pay_b, own_lists = call(
        first_pack_kernel,
        [shaped(7 * nx, 256)] * 2 + [shaped(8, 256)],
        [conc_old, phase_label, iface_owner.reshape(1, -1), iface_block],
        [vmem(nx, HALO, 256)] * 2
        + [pltpu.VMEM((nx, HALO, 256), jnp.int32)] * 2
        + [pltpu.VMEM((1, 256), jnp.int32)] * 2
        + [vmem(7 * nx, 256)] * 2
        + [vmem(8, 256), pltpu.SemaphoreType.DMA((15,))],
        in_specs=[FAR] * 4,
        out_specs=[FAR] * 3,
        limit=VMEM_MOST,
        name="first_pack",
    )
    y_a, y_b = swap(pay_a, pay_b, "dev")
    conduct_mid, conduct_coarse, pay_a, pay_b, lists, gain, base = call(
        own_kernel,
        [shaped(half, half, 256), shaped(quarter, quarter, 256), shaped(22, 8, 256), shaped(22, 8, 256)]
        + [shaped(2, 256), shaped(nx, nx, 256), shaped(nx, nx, 256)],
        [conc_old, phase_label, phi_old, own_lists],
        [vmem(half, 2, nx, LANES), vmem(quarter, 2, half, LANES)],
        name="own",
    )
    xx_a, xx_b = swap(pay_a, pay_b, "grp")
    distance = peers // 2
    while distance > 1:
        lists = jnp.concatenate([lists, exchange(lists, distance)], axis=0)
        distance //= 2
    far_rows = second_rows(nx)[2]
    far_pay = call(
        second_pack_kernel,
        [shaped(far_rows, 256), shaped(far_rows + peers, 256)],
        [phi_old, conduct_mid, conduct_coarse, lists, xx_a, xx_b],
        name="second_pack",
    )
    yy_a, yy_b = swap(*far_pay, "dev")
    pay_a, pay_b = call(
        first_pack_x_kernel,
        [shaped(35, 8, 256)] * 2,
        [conc_old, phase_label, y_a, y_b, conduct_coarse],
        name="first_pack_x",
    )
    x_a, x_b = swap(pay_a, pay_b, "grp")

    (conc_new,) = call(
        sweeps_kernel,
        [shaped(nx, nx, 256)],
        [conc_old, phase_label, gain, base, y_a, y_b, x_a, x_b],
        [vmem(*ext)] * 2 + [vmem(nx, 8, 256)] * 2 + [vmem(2 * HALO, nx + 2 * HALO, 256)] * 2,
        name="sweeps",
    )
    flux_all, pay_a, pay_b = call(
        flux_kernel,
        [shaped(nx, nx, 256), shaped(3 * nx, 256), shaped(3 * nx, 256)],
        [conc_new, phase_label, phi_old, solid_pot],
        name="flux",
    )
    f_a, f_b = swap(pay_a, pay_b, "dev")
    flux_own, halo_mask = call(
        mask_kernel,
        [shaped(nx, nx, 256), shaped(nx, 8, 256)],
        [flux_all, lists, yy_b],
        [vmem(3, nx, 8, LANES)],
        name="mask",
    )
    weight, scale, made = call(
        ready_kernel,
        [shaped(*ext)] * 2 + [token_shape],
        [conc_old, phase_label, y_a, y_b, x_a, x_b],
        name="ready",
    )
    pay_a, pay_b = call(
        flux_pack_x_kernel, [shaped(15, 8, 256)] * 2, [flux_own, f_a, f_b, halo_mask, made], name="flux_pack_x"
    )
    fx_a, fx_b = swap(pay_a, pay_b, "grp")
    fine_two, fine_source, fine_first, inner_mid, field = call(
        potential_inner_kernel,
        [shaped(*ext)] * 3 + [shaped(half, half, 256), shaped(*ext)],
        [flux_own, halo_mask, f_a, f_b, phi_old, yy_a, yy_b, xx_a, xx_b, weight, scale],
        [vmem(nx, 8, 256), vmem(half, 2, nx, LANES)],
        name="potential_inner",
    )
    edge = (16, nx + 2 * HALO, 256)
    edge_two, edge_source, source_mid, pay_a, pay_b = call(
        potential_edge_kernel,
        [shaped(*edge), shaped(*edge), shaped(half, half, 256), shaped(4 * half, 256), shaped(4 * half, 256)],
        [fx_a, fx_b, weight, scale, field, fine_two, fine_source, fine_first, inner_mid, conduct_mid],
        [vmem(*edge), vmem(2, 2, nx, LANES)],
        name="potential_edge",
    )
    m_a, m_b = swap(pay_a, pay_b, "dev")
    concentration, flux, stored = call(
        store_kernel,
        [shaped(nx, nx, 256), shaped(nx, nx, 256), token_shape],
        [conc_new, flux_own],
        [pltpu.SemaphoreType.DMA((8,))],
        out_specs=[FAR, FAR, WHOLE],
        name="store",
    )
    wide = (quarter, 32, 256)
    rho, load, made = call(
        coarse_ready_kernel,
        [shaped(quarter, quarter, 256), shaped(8, LANES), token_shape],
        [conduct_coarse, yy_a, yy_b],
        [vmem(*wide)] * 4,
        name="coarse_ready",
    )
    pay_a, pay_b = call(
        mid_pack_x_kernel, [shaped(3 * HALO, 8, 256)] * 2, [source_mid, m_a, m_b, made, stored], name="mid_pack_x"
    )
    mx_a, mx_b = swap(pay_a, pay_b, "grp")
    mid_two, mid_source, mid_weight, source_coarse, wide_coarse, pay_a, pay_b, sums = call(
        mid_kernel,
        [shaped(*ext_mid)] * 3
        + [shaped(quarter, 12, 256), shaped(quarter, 12, 256), shaped(72, 256), shaped(80, 256), shaped(8, 256)],
        [source_mid, conduct_mid, yy_a, yy_b, xx_a, xx_b, m_a, m_b, mx_a, mx_b, rho, load],
        [vmem(*ext_mid)] * 2 + [vmem(8, 2, half + 2 * HALO, LANES)] * 2,
        name="middle",
    )
    c_a, c_b = swap(pay_a, pay_b, "dev")
    sums = sums + c_b[72:80]
    distance = 2
    while distance < peers:
        sums = sums + exchange(sums, distance)
        distance *= 2
    (error,) = call(
        coarse_kernel,
        [shaped(8, 16, 256)],
        [source_coarse, wide_coarse, yy_a, yy_b, c_a, c_b],
        [vmem(*wide)] * 4,
        name="coarse",
    )
    fields = [mid_two, mid_source, mid_weight, fine_two, fine_source, weight]
    kept = [shaped(4, half + 2 * HALO, 256)] * 2 + [shaped(4, nx + 2 * HALO, 256)] * 2
    scratch = [vmem(*ext_mid)] * 3 + [vmem(*ext)] * 2
    scratch += [vmem(8, 2, 2, 16, LANES), vmem(half + 2 * HALO, 3, 2, 16, LANES), vmem(nx, nx, 256)]
    scratch += [pltpu.SemaphoreType.DMA((2,))]
    error, pay_a, pay_b, begun, *kept_early = call(
        finish_early_kernel,
        [shaped(8, 16, 256), shaped(2, 16, 256), shaped(2, 16, 256), shaped(nx, nx, 256)] + kept,
        [error, sums] + fields,
        scratch,
        out_specs=[WHOLE] * 3 + [FAR] + [WHOLE] * 4,
        name="finish_early",
    )
    e_a, e_b = swap(pay_a, pay_b, "grp")
    begun, zero, one, fine_one, fine_last = call(
        finish_late_kernel,
        [shaped(nx, nx, 256)] + kept,
        [error] + fields + kept_early + [begun],
        scratch,
        in_specs=[WHOLE] * 11 + [FAR],
        out_specs=[FAR] + [WHOLE] * 4,
        aliases={11: 0},
        name="finish_late",
    )
    finish_args = [e_a, e_b, mid_two, mid_source, mid_weight, fine_two, edge_two, fine_source, edge_source, weight]
    finish_args += [zero, one, fine_one, fine_last, begun]
    (potential,) = call(
        finish_edge_kernel,
        [shaped(nx, nx, 256)],
        finish_args,
        [vmem(*ext_mid), vmem(*ext_mid), vmem(*ext), vmem(*ext)]
        + [vmem(4, 2, 2, 16, LANES), vmem(6, 3, 2, 16, LANES), vmem(nx, nx, 256)]
        + [pltpu.SemaphoreType.DMA((2,))],
        in_specs=[WHOLE] * (len(finish_args) - 1) + [FAR],
        out_specs=[FAR],
        aliases={len(finish_args) - 1: 0},
        name="finish_edge",
    )
    return (concentration, flux, potential)


def solution(mesh):
    brick = P("grp", "dev", None)
    return jax.shard_map(
        body,
        mesh=mesh,
        in_specs=(brick, brick, brick, brick, P("grp", "dev"), brick),
        out_specs=(brick, brick, brick),
        check_vma=False,
    )
```

```python
import jax
import jax.numpy as jnp
from jax import lax
from jax.experimental import pallas as pl
from jax.experimental.pallas import tpu as pltpu
from jax.sharding import PartitionSpec as P


F32 = jnp.float32
MASS = 0.05
OMEGA = 0.8
DIFFUSION_TABLE = (1.5, 0.1, 0.4)
RATIO_TABLE = tuple(d / (1.0 + 6.0 * d) for d in DIFFUSION_TABLE)
INVERSE_TABLE = tuple(1.0 / (1.0 + 6.0 * d) for d in DIFFUSION_TABLE)
CONDUCT_TABLE = (1.0, 0.3, 0.6)
KINETIC_TABLE = (0.2, 1.0, 0.5)
SWEEPS = 4
COARSE_SWEEPS = 8
COARSE_NEAR = 8
HALO = 4
LANES = 128
VMEM_LIMIT = 28 * 1024 * 1024
VMEM_MOST = 58 * 1024 * 1024


def shaped(*shape):
    return jax.ShapeDtypeStruct(shape, F32)


WHOLE = pl.BlockSpec(memory_space=pltpu.VMEM)
FAR = pl.BlockSpec(memory_space=pltpu.HBM)


def call(kernel, outs, args, scratch=(), in_specs=None, out_specs=None, limit=VMEM_LIMIT, aliases=None, flops=10**6, name=None):
    size = sum(4 * a.size for a in args) + sum(4 * o.size for o in outs)
    return pl.pallas_call(
        kernel,
        out_shape=tuple(outs),
        in_specs=in_specs or [WHOLE] * len(args),
        out_specs=tuple(out_specs or [WHOLE] * len(outs)),
        scratch_shapes=list(scratch),
        input_output_aliases=aliases or {},
        compiler_params=pltpu.CompilerParams(vmem_limit_bytes=limit),
        cost_estimate=pl.CostEstimate(flops=flops, bytes_accessed=size, transcendentals=0),
        name=name,
    )(*args)


def vmem(*shape):
    return pltpu.VMEM(shape, F32)


def iota(shape, dim):
    return lax.broadcasted_iota(jnp.int32, shape, dim)


def pick(label, table):
    return jnp.where(label == 0, table[0], jnp.where(label == 1, table[1], table[2])).astype(F32)


def loop(low, high, body, unroll=8):
    steps = (high - low) // unroll

    def step(i, carry):
        for u in range(unroll):
            body(low + i * unroll + u)
        return carry

    if steps > 1:
        lax.fori_loop(0, steps, step, 0)
    else:
        steps = 0
    for x in range(low + steps * unroll, high):
        body(x)


def odd(axis):
    return lax.rem(lax.axis_index(axis), 2) == 1


def along_y(v):
    return pltpu.roll(v, 1, 0) + pltpu.roll(v, v.shape[0] - 1, 0)


def along_z(v):
    low, high = v[:, :LANES], v[:, LANES:]
    lane = iota(low.shape, 1)
    first, last = lane == 0, lane == LANES - 1
    low_up, high_up = pltpu.roll(low, 1, 1), pltpu.roll(high, 1, 1)
    low_down, high_down = pltpu.roll(low, LANES - 1, 1), pltpu.roll(high, LANES - 1, 1)
    low_sum = jnp.where(first, 0.0, low_up) + jnp.where(last, high_down, low_down)
    high_sum = jnp.where(first, low_up, high_up) + jnp.where(last, 0.0, high_down)
    return jnp.concatenate([low_sum, high_sum], axis=1)


def upper(shape=(8, 256)):
    return iota(shape, 0) < HALO


def twice(tile, scratch):
    for h in range(2):
        part = tile[:, h * LANES : (h + 1) * LANES]
        scratch[h, pl.ds(0, 8, stride=2), :] = part
        scratch[h, pl.ds(1, 8, stride=2), :] = part
    return jnp.concatenate([scratch[0], scratch[1]], axis=1)


def pair_rows(v, scratch):
    half = v.shape[0] // 2
    parts = []
    for h in range(2):
        scratch[h] = v[:, h * LANES : (h + 1) * LANES]
        parts.append(scratch[h, pl.ds(0, half, stride=2), :] + scratch[h, pl.ds(1, half, stride=2), :])
    return jnp.concatenate(parts, axis=1)


def either(flag, if_true, if_false):
    return jnp.where(flag, if_true, if_false)


def y_sides(r_a, r_b, at, count):
    flag = odd("dev")
    a, b = r_a[at : at + count, :], r_b[at : at + count, :]
    return either(flag, a, b), either(flag, b, a)


def y_planes(r_a, r_b, index):
    flag = odd("dev")
    a, b = r_a[index], r_b[index]
    return either(flag, a, b), either(flag, b, a)


def x_sides(r_a, r_b, index):
    flag = odd("grp")
    a, b = r_a[index], r_b[index]
    return either(flag, a, b), either(flag, b, a)


def send_y(pay_a, pay_b, at, first, last):
    flag = odd("dev")
    n = first.shape[0]
    pay_a[at : at + n, :] = either(flag, last, first)
    pay_b[at : at + n, :] = either(flag, first, last)


def send_x(pay_a, pay_b, index, first, last):
    flag = odd("grp")
    pay_a[index] = either(flag, last, first)
    pay_b[index] = either(flag, first, last)


def halo_tile(after, before):
    parts = [after]
    if after.shape[0] < HALO:
        parts.append(jnp.zeros((2 * HALO - 2 * after.shape[0], after.shape[1]), F32))
    return jnp.concatenate(parts + [before], axis=0)


def first_pack_kernel(
    conc, label, owner, block, out_a, out_b, own_lists,
    c_first, c_last, l_first, l_last, own_owner, own_block, pay_a, pay_b, named, sems,
):
    nx = conc.shape[0]
    half = nx // 2
    lists = [pltpu.make_async_copy(owner, own_owner, sems.at[8]), pltpu.make_async_copy(block, own_block, sems.at[9])]
    reads = []
    for j in range(2):
        planes = pl.ds(half * j, half)
        for i, (ref, at, to) in enumerate(
            ((conc, 0, c_first), (conc, 28, c_last), (label, 0, l_first), (label, 28, l_last))
        ):
            reads.append(pltpu.make_async_copy(ref.at[planes, pl.ds(at, 4), :], to.at[planes], sems.at[4 * j + i]))
    for c in reads + lists:
        c.start()
    writes = []
    for j in range(2):
        for c in reads[4 * j : 4 * j + 4]:
            c.wait()
        for x in range(half * j, half * j + half):
            send_y(pay_a, pay_b, 7 * x, c_first[x], c_last[x])
            send_y(pay_a, pay_b, 7 * x + 4, l_first[x, 0:3, :].astype(F32), l_last[x, 1:4, :].astype(F32))
        rows = pl.ds(7 * half * j, 7 * half)
        for i, (pay, out) in enumerate(((pay_a, out_a), (pay_b, out_b))):
            writes.append(pltpu.make_async_copy(pay.at[rows], out.at[rows], sems.at[10 + 2 * j + i]))
            writes[-1].start()
    for c in lists:
        c.wait()
    named[...] = jnp.concatenate([own_owner[...], own_block[...], jnp.zeros((6, 256), jnp.int32)], axis=0).astype(F32)
    writes.append(pltpu.make_async_copy(named, own_lists, sems.at[14]))
    writes[-1].start()
    for c in writes:
        c.wait()


def own_kernel(conc, label, phi, named, mid, coarse, pay_a, pay_b, lists, gain, base, pairs, pairs_2):
    nx = conc.shape[0]
    half = nx // 2
    lists[...] = named[0:2, :]

    def coefficients(i):
        gain[i] = pick(label[i], RATIO_TABLE)
        base[i] = conc[i] * pick(label[i], INVERSE_TABLE)

    loop(0, nx, coefficients, 4)

    def coarsen(i):
        total = conc[2 * i] * pick(label[2 * i], CONDUCT_TABLE) + conc[2 * i + 1] * pick(label[2 * i + 1], CONDUCT_TABLE)
        mid[i] = 0.25 * pair_rows(total, pairs.at[i])

    loop(0, half, coarsen, 4)
    for i in range(half // 2):
        coarse[i] = 0.25 * pair_rows(mid[2 * i] + mid[2 * i + 1], pairs_2.at[i])
    for k in range(HALO):
        for t in range(4):
            rows = slice(8 * t, 8 * t + 8)
            send_x(pay_a, pay_b, 4 * k + t, phi[k, rows, :], phi[nx - HALO + k, rows, :])
    for k in range(MID_HALO):
        for t in range(2):
            rows = slice(8 * t, 8 * t + 8)
            send_x(pay_a, pay_b, 16 + 2 * k + t, mid[k, rows, :], mid[half - MID_HALO + k, rows, :])


def first_pack_x_kernel(conc, label, r_a, r_b, token, pay_a, pay_b):
    nx = conc.shape[0]

    def plane(ref, k, t, offset, count):
        if t < 4:
            return ref[k, 8 * t : 8 * t + 8, :].astype(F32)
        return halo_tile(*y_sides(r_a, r_b, 7 * k + offset, count))

    for t in range(5):
        for k in range(HALO):
            send_x(pay_a, pay_b, 5 * k + t, plane(conc, k, t, 0, 4), plane(conc, nx - HALO + k, t, 0, 4))
        for k in range(3):
            send_x(pay_a, pay_b, 20 + 5 * k + t, plane(label, k, t, 4, 3), plane(label, nx - 3 + k, t, 4, 3))


MID_HALO = 3


def corner_rows(n, width, reach):
    counts = [min(width, k + reach) for k in range(width)]
    counts = counts + [width] * n + counts[::-1]
    return counts, [sum(counts[:i]) for i in range(len(counts))]


def second_rows(nx):
    phi = sum(corner_rows(nx, HALO, 0)[0])
    mid = sum(corner_rows(nx // 2, MID_HALO, 1)[0])
    return phi, phi + mid


def second_pack_kernel(phi, mid, lists, x_a, x_b, pay_a, pay_b):
    nx = phi.shape[0]
    starts = second_rows(nx)

    def put(own, width, reach, index, base):
        n = own.shape[0]
        counts, at = corner_rows(n, width, reach)
        tiles = own.shape[1] // 8
        for x in range(n):
            send_y(pay_a, pay_b, base + at[width + x], own[x, 0:width, :], own[x, 8 * tiles - width : 8 * tiles, :])
        for k in range(width):
            first_after, first_before = x_sides(x_a, x_b, index + tiles * k)
            last_after, last_before = x_sides(x_a, x_b, index + tiles * k + tiles - 1)
            for x, first, last in ((k, first_before, last_before), (width + n + k, first_after, last_after)):
                if counts[x]:
                    send_y(pay_a, pay_b, base + at[x], first[0 : counts[x]], last[8 - counts[x] : 8])

    put(phi, HALO, 0, 0, 0)
    put(mid, MID_HALO, 1, 16, starts[0])
    base = starts[1]
    pay_b[base : base + lists.shape[0], :] = lists[...]


def second_halo(r_a, r_b, n, width, reach, x, base):
    counts, at = corner_rows(n, width, reach)
    x = x - HALO + width
    if x < 0 or x >= len(counts) or not counts[x]:
        return jnp.zeros((8, 256), F32)
    return halo_tile(*y_sides(r_a, r_b, base + at[x], counts[x]))


def wide_rows(own, after_own, before_own, after, before):
    gap = jnp.zeros((6, 256), F32)
    return jnp.concatenate([own, after_own, after, gap, before, before_own], axis=0)


def flux_plane(c, solid, phi, label):
    drive = 0.5 * (solid - phi)
    logc = jnp.log(c)
    return pick(label, KINETIC_TABLE) * (jnp.exp(drive + 0.4 * logc) - jnp.exp(0.6 * logc - drive))


def around_plane(before, v, after):
    return (before + after) + (along_y(v) + along_z(v))


def sweeps_inner_kernel(
    conc, label, phi, solid, gain, base, y_a, y_b, zero, first, second, third, gain_far, base_far, out, flux
):
    nx = conc.shape[0]

    def own(i):
        zero[i, 0:32, :] = conc[i]

    loop(0, nx, own)
    for i in range(nx):
        c = halo_tile(*y_sides(y_a, y_b, 7 * i, 4))
        lab = halo_tile(*y_sides(y_a, y_b, 7 * i + 4, 3))
        zero[i, 32:40, :] = c
        gain_far[i] = jnp.where(c > 0.0, pick(lab, RATIO_TABLE), 0.0)
        base_far[i] = c * pick(lab, INVERSE_TABLE)
    fields = (zero, first, second, third)
    for s in range(1, SWEEPS):
        old, new = fields[s - 1], fields[s]

        def sweep(i, old=old, new=new):
            g = jnp.concatenate([gain[i], gain_far[i]], axis=0)
            b = jnp.concatenate([base[i], base_far[i]], axis=0)
            new[i] = b + g * around_plane(old[i - 1], old[i], old[i + 1])

        loop(s, nx - s, sweep)

    def last(i):
        c = base[i] + gain[i] * around_plane(third[i - 1], third[i], third[i + 1])[0:32, :]
        out[i] = c
        flux[i] = flux_plane(c, solid[i], phi[i], label[i])

    loop(SWEEPS, nx - SWEEPS, last, 4)


def sweeps_edge_kernel(
    x_a, x_b, label, phi, solid, gain, base, zero, first, second, third, gain_far, base_far, out_inner, flux_inner,
    out, flux, pay_a, pay_b, zero_x, first_x, second_x, third_x,
):
    nx = out.shape[0]
    inner = (zero, first, second, third)
    edge = (zero_x, first_x, second_x, third_x)

    def copy(i):
        out[i] = out_inner[i]
        flux[i] = flux_inner[i]

    loop(SWEEPS, nx - SWEEPS, copy)
    for side in range(2):
        plane = lambda k, side=side: k if side == 0 else nx - 1 - k
        row = lambda k, side=side: 8 * side + HALO + k
        far = lambda k, index, side=side: x_sides(x_a, x_b, index)[1 - side]
        gains, bases = {}, {}
        for j in range(1, HALO + 1):
            k = HALO - j if side == 0 else j - 1
            zero_x[row(-j)] = jnp.concatenate([far(k, 5 * k + t) for t in range(5)], axis=0)
            if j < HALO:
                k = HALO - 1 - j if side == 0 else j - 1
                lab = jnp.concatenate([far(k, 20 + 5 * k + t) for t in range(5)], axis=0)
                c = zero_x[row(-j)]
                gains[-j] = jnp.where(c > 0.0, pick(lab, RATIO_TABLE), 0.0)
                bases[-j] = c * pick(lab, INVERSE_TABLE)
        for k in range(SWEEPS):
            gains[k] = jnp.concatenate([gain[plane(k)], gain_far[plane(k)]], axis=0)
            bases[k] = jnp.concatenate([base[plane(k)], base_far[plane(k)]], axis=0)
        for s in range(1, SWEEPS + 1):

            def old(k, s=s):
                return inner[s - 1][plane(k)] if k >= s - 1 else edge[s - 1][row(k)]

            for k in range(s - SWEEPS, s):
                c = bases[k] + gains[k] * around_plane(old(k - 1), old(k), old(k + 1))
                if s < SWEEPS:
                    edge[s][row(k)] = c
                else:
                    c = c[0:32, :]
                    out[plane(k)] = c
                    flux[plane(k)] = flux_plane(c, solid[plane(k)], phi[plane(k)], label[plane(k)])
    for x in range(nx):
        send_y(pay_a, pay_b, 3 * x, flux[x, 0:3, :], flux[x, 29:32, :])


def mask_kernel(flux_all, lists, far, token, flux, halo_mask, marked):
    nx = flux_all.shape[0]
    rows = lists.shape[0]
    pieces = [lists[i : i + 1, :] for i in range(rows)] + [far[i : i + 1, :] for i in range(far.shape[0] - rows, far.shape[0])]
    owner = jnp.concatenate(pieces[0::2], axis=1).astype(jnp.int32)
    block = jnp.concatenate(pieces[1::2], axis=1).astype(jnp.int32)
    entries = owner.shape[1]
    hit_column = (iota((64, entries), 0) == lax.rem(block, 64)).astype(jnp.bfloat16)
    reach = owner - lax.axis_index("dev") + 1
    at_row = jnp.where((reach >= 0) & (reach < 3), reach * nx + lax.shift_right_arithmetic(block, 6), -1)
    hit_row = (iota((3 * nx, entries), 0) == at_row).astype(jnp.bfloat16)
    named = lax.dot_general(hit_row, hit_column, (((1,), (1,)), ((), ())), preferred_element_type=F32)
    named = jnp.concatenate([named, jnp.zeros((3 * nx, LANES - 64), F32)], axis=1)
    for j in range(3):
        for i in range(nx):
            marked[j, i] = jnp.broadcast_to(named[j * nx + i : j * nx + i + 1, :], (8, LANES))
    is_row = lax.div(iota((32, LANES), 1), 2) == iota((32, LANES), 0)
    row, pair = iota((8, LANES), 0), lax.div(iota((8, LANES), 1), 2)
    is_after = (row < 3) & (pair == row)
    is_before = (row >= 5) & (pair == row + 24)
    spread = (lax.rem(iota((LANES, 256), 0), 2) == lax.div(iota((LANES, 256), 1), LANES)).astype(jnp.bfloat16)

    def plane(i):
        marks = jnp.where(is_row, jnp.concatenate([marked[1, i]] * 4, axis=0), 0.0)
        beyond = jnp.where(is_after, marked[2, i], jnp.where(is_before, marked[0, i], 0.0))
        marks = jnp.concatenate([marks, beyond], axis=0).astype(jnp.bfloat16)
        listed = jnp.dot(marks, spread, preferred_element_type=F32) > 0.5
        flux[i] = jnp.where(listed[0:32], flux_all[i], 0.0)
        halo_mask[i] = jnp.where(listed[32:40], 1.0, 0.0)

    loop(0, nx, plane, 16)


def store_kernel(conc, flux, conc_out, flux_out, token, sems):
    copies = []
    for i, (ref, to) in enumerate(((conc, conc_out), (flux, flux_out))):
        for j in range(4):
            rows = pl.ds(8 * j, 8)
            copies.append(pltpu.make_async_copy(ref.at[rows], to.at[rows], sems.at[4 * i + j]))
            copies[-1].start()
    token[...] = jnp.zeros(token.shape, F32)
    for c in copies:
        c.wait()


def ready_kernel(conc, label, y_a, y_b, x_a, x_b, weight, scale, token):
    nx = conc.shape[0]
    token[...] = jnp.zeros(token.shape, F32)

    def put(x, rows, c, lab):
        conduct = c * pick(lab, CONDUCT_TABLE)
        factor = OMEGA / (MASS + 6.0 * conduct)
        weight[x, rows, :] = conduct * factor
        scale[x, rows, :] = factor

    def own(i):
        put(HALO + i, slice(0, 32), conc[i], label[i])

    loop(0, nx, own, 4)
    for i in range(nx):
        c = halo_tile(*y_sides(y_a, y_b, 7 * i, 4))
        lab = halo_tile(*y_sides(y_a, y_b, 7 * i + 4, 3))
        put(HALO + i, slice(32, 40), c, lab)
    for t in range(5):
        rows = slice(8 * t, 8 * t + 8)
        for k in range(HALO):
            c_after, c_before = x_sides(x_a, x_b, 5 * k + t)
            l_after = x_sides(x_a, x_b, 20 + 5 * min(k, 2) + t)[0]
            l_before = x_sides(x_a, x_b, 20 + 5 * max(k - 1, 0) + t)[1]
            put(k, rows, c_before, l_before)
            put(HALO + nx + k, rows, c_after, l_after)


def place_phi(phi, yy_a, yy_b, xx_a, xx_b, field):
    nx = phi.shape[0]

    def own(i):
        field[HALO + i, 0:32, :] = phi[i]

    loop(0, nx, own)
    for x in range(nx + 2 * HALO):
        field[x, 32:40, :] = second_halo(yy_a, yy_b, nx, HALO, 0, x, 0)
    for t in range(4):
        for k in range(HALO):
            after, before = x_sides(xx_a, xx_b, 4 * k + t)
            field[k, 8 * t : 8 * t + 8, :] = before
            field[HALO + nx + k, 8 * t : 8 * t + 8, :] = after


def flux_pack_x_kernel(flux, r_a, r_b, mask, token, pay_a, pay_b):
    nx = flux.shape[0]

    def tile(x, t):
        if t < 4:
            return flux[x, 8 * t : 8 * t + 8, :]
        return mask[x] * halo_tile(*y_sides(r_a, r_b, 3 * x, 3))

    for k in range(3):
        for t in range(5):
            send_x(pay_a, pay_b, 5 * k + t, tile(k, t), tile(nx - 3 + k, t))


def first_sweep(field, weight, scale, x, rows, flux):
    p = field[x]
    near = (field[x - 1] + field[x + 1]) + (along_y(p) + along_z(p))
    b = scale[x, rows, :] * (MASS * p[rows, :] + flux)
    return b, 0.2 * p[rows, :] + weight[x, rows, :] * near[rows, :] + b


def potential_inner_kernel(
    flux, mask, y_a, y_b, phi, yy_a, yy_b, xx_a, xx_b, weight, scale, after_two, source, first, source_mid, field, far, pairs
):
    nx = flux.shape[0]
    place_phi(phi, yy_a, yy_b, xx_a, xx_b, field)
    for i in range(nx):
        far[i] = mask[i] * halo_tile(*y_sides(y_a, y_b, 3 * i, 3))

    def own(i):
        x = HALO + i
        f = jnp.concatenate([flux[i], far[i]], axis=0)
        source[x], first[x] = first_sweep(field, weight, scale, x, slice(0, 40), f)

    loop(0, nx, own)

    def around(values, x):
        v = values[x]
        return v, weight[x] * ((values[x - 1] + values[x + 1]) + (along_y(v) + along_z(v)))

    def sweep(x):
        v, near = around(first, x)
        after_two[x] = 0.2 * v + (source[x] + near)

    loop(HALO + 1, HALO + nx - 1, sweep)

    def remainder(x):
        v, near = around(after_two, x)
        return ((source[x] - OMEGA * v) + near)[0:32, :] / scale[x, 0:32, :]

    def coarsen(i):
        x = HALO + 2 * i
        source_mid[i] = 0.25 * pair_rows(remainder(x) + remainder(x + 1), pairs.at[i])

    loop(1, nx // 2 - 1, coarsen, 4)


def mid_factor(conduct):
    return OMEGA / (MASS + 3.0 * conduct)


def potential_edge_kernel(
    x_a, x_b, weight, scale, field, inner_two, inner_source, inner_first, inner_mid, conduct_mid,
    token, token_2, edge_two, edge_source, source_mid, pay_a, pay_b, first, pairs,
):
    half = source_mid.shape[0]
    nx = 2 * half
    for side, face in ((0, HALO), (1, HALO + nx)):
        base = 8 * side + HALO - face
        for k in range(3):
            x = face - 3 + k if side == 0 else face + k
            f = jnp.concatenate([x_sides(x_a, x_b, 5 * k + t)[1 - side] for t in range(5)], axis=0)
            edge_source[base + x], first[base + x] = first_sweep(field, weight, scale, x, slice(0, 40), f)

        def first_of(x, base=base):
            return inner_first[x] if HALO <= x < HALO + nx else first[base + x]

        def source_of(x, base=base):
            return inner_source[x] if HALO <= x < HALO + nx else edge_source[base + x]

        def two_of(x, base=base):
            return inner_two[x] if HALO < x < HALO + nx - 1 else edge_two[base + x]

        for x in range(face - 2, face + 1) if side == 0 else range(face - 1, face + 2):
            v = first_of(x)
            near = weight[x] * ((first_of(x - 1) + first_of(x + 1)) + (along_y(v) + along_z(v)))
            edge_two[base + x] = 0.2 * v + (source_of(x) + near)
        total = 0.0
        at = face if side == 0 else face - 2
        for x in (at, at + 1):
            v = two_of(x)
            near = weight[x] * ((two_of(x - 1) + two_of(x + 1)) + (along_y(v) + along_z(v)))
            total = total + ((source_of(x) - OMEGA * v) + near)[0:32, :] / scale[x, 0:32, :]
        at = 0 if side == 0 else half - 1
        source_mid[at] = mid_factor(conduct_mid[at]) * (0.25 * pair_rows(total, pairs.at[side]))
    for x in range(1, half - 1):
        source_mid[x] = mid_factor(conduct_mid[x]) * inner_mid[x]
    for x in range(half):
        send_y(pay_a, pay_b, 4 * x, source_mid[x, 0:4, :], source_mid[x, 12:16, :])


def mid_pack_x_kernel(field, r_a, r_b, pay_a, pay_b):
    n = field.shape[0]

    def tile(x, t):
        if t < 2:
            return field[x, 8 * t : 8 * t + 8, :]
        return halo_tile(*y_sides(r_a, r_b, 4 * x, 4))

    for k in range(HALO):
        for t in range(3):
            send_x(pay_a, pay_b, 3 * k + t, tile(k, t), tile(n - HALO + k, t))


def mid_kernel(
    source_own, conduct_own, yy_a, yy_b, xx_a, xx_b, y_a, y_b, x_a, x_b, rho, load, token,
    after_two, source, weight, coarse, conduct, pay_a, pay_b, part, scale, mid_conduct, pairs, pairs_2,
):
    n = source_own.shape[0]
    base = second_rows(2 * n)[0]

    def put(x, rows, b, k):
        factor = mid_factor(k)
        weight[x, rows, :] = k * factor
        scale[x, rows, :] = factor
        source[x, rows, :] = b
        mid_conduct[x, rows, :] = k

    def far(x):
        return second_halo(yy_a, yy_b, n, MID_HALO, 1, x, base)

    for i in range(n):
        put(HALO + i, slice(0, 16), source_own[i], conduct_own[i])
        put(HALO + i, slice(16, 24), halo_tile(*y_sides(y_a, y_b, 4 * i, 4)), far(HALO + i))
    for k in range(HALO):
        for t in range(3):
            rows = slice(8 * t, 8 * t + 8)
            b_after, b_before = x_sides(x_a, x_b, 3 * k + t)
            if t < 2:
                none = jnp.zeros((8, 256), F32)
                c_before = x_sides(xx_a, xx_b, 16 + 2 * (k - 1) + t)[1] if k > 0 else none
                c_after = x_sides(xx_a, xx_b, 16 + 2 * k + t)[0] if k < MID_HALO else none
            else:
                c_after, c_before = far(HALO + n + k), far(k)
            put(k, rows, b_before, c_before)
            put(HALO + n + k, rows, b_after, c_after)

    def around(values, x):
        v = values[x]
        return v, weight[x] * (0.25 * ((values[x - 1] + values[x + 1]) + along_y(v)) + along_z(v))

    def sweep(x):
        v, near = around(source, x)
        after_two[x] = 0.2 * v + (source[x] + near)

    loop(1, n + 2 * HALO - 1, sweep, 11)

    def remainder(x):
        v, near = around(after_two, x)
        return ((source[x] - OMEGA * v) + near) / scale[x]

    total = jnp.zeros((8, 256), F32)
    for i in range(n // 2):
        x = HALO + 2 * i
        value = 0.25 * pair_rows(remainder(x) + remainder(x + 1), pairs.at[i])
        k = 0.25 * pair_rows(mid_conduct[x] + mid_conduct[x + 1], pairs_2.at[i])
        coarse[i] = value
        conduct[i] = k
        send_y(pay_a, pay_b, 9 * i, value[1:9], jnp.concatenate([value[11:12], value[0:7]], axis=0))
        send_y(pay_a, pay_b, 9 * i + 8, k[8:9], k[11:12])
        total += rho[i] * value[0:8]
    sums = jnp.concatenate([total[:, :LANES] + total[:, LANES:], load[...]], axis=1)
    pay_b[72:80, :] = sums
    part[...] = sums


COARSE_W = 0.0625


def coarse_ready_kernel(own, r_a, r_b, rho, load, one, two, conduct, scale):
    for x in range(8):
        after, before = y_planes(r_a, r_b, x)
        k = jnp.concatenate([own[x], after, jnp.zeros((8, 256), F32), before], axis=0)
        conduct[x] = k
        scale[x] = OMEGA / (MASS + 2.25 * k)
        one[x] = jnp.ones(k.shape, F32)
    fields = (one, two)
    for s in range(COARSE_SWEEPS):
        old, new = fields[s % 2], fields[(s + 1) % 2]
        for x in range(8):
            near = [conduct[i] * old[i] if 0 <= i < 8 else None for i in (x - 1, x, x + 1)]
            inner = along_y(near[1])
            for other in (near[0], near[2]):
                if other is not None:
                    inner = inner + other
            new[x] = 0.2 * old[x] + scale[x] * (COARSE_W * inner + along_z(near[1]))
    last = fields[COARSE_SWEEPS % 2]
    peer, peers = lax.axis_index("dev"), lax.axis_size("dev")
    row, z = iota((8, 256), 0), iota((8, 256), 1)
    edge_y = ((row == 0) & (peer == 0)) | ((row == 7) & (peer == peers - 1))
    edge = edge_y.astype(F32) * COARSE_W + ((z == 0) | (z == 255)).astype(F32)
    total = jnp.zeros((8, 256), F32)
    for x in range(8):
        rho[x] = last[x, 0:8, :]
        total += MASS + own[x] * (edge + (COARSE_W if x in (0, 7) else 0.0))
    load[...] = total[:, :LANES] + total[:, LANES:]


def coarse_kernel(own, conduct, far_a, far_b, r_a, r_b, error, source, weight, one, two):
    for x in range(8):
        after, before = y_sides(r_a, r_b, 9 * x, 8)
        b = wide_rows(own[x, 0:8, :], own[x, 8:9, :], own[x, 11:12, :], after, before)
        last_after, last_before = y_sides(r_a, r_b, 9 * x + 8, 1)
        after, before = y_planes(far_a, far_b, x)
        after = jnp.concatenate([after[1:8], last_after], axis=0)
        before = jnp.concatenate([last_before, before[0:7]], axis=0)
        k = wide_rows(conduct[x, 0:8, :], conduct[x, 8:9, :], conduct[x, 11:12, :], after, before)
        factor = OMEGA / (MASS + 2.25 * k)
        weight[x] = k * factor
        source[x] = factor * b
    old = source
    for s in range(1, COARSE_SWEEPS):
        new = one if s % 2 else two
        for x in range(8):
            v = old[x]
            inner = along_y(v)
            if x > 0:
                inner = inner + old[x - 1]
            if x < 7:
                inner = inner + old[x + 1]
            new[x] = 0.2 * v + (source[x] + weight[x] * (COARSE_W * inner + along_z(v)))
        old = new
    for x in range(8):
        error[x, 0:8, :] = old[x, 0:8, :]
        error[x, 8:16, :] = jnp.where(upper(), old[x, 8:16, :], old[x, 24:32, :])


def squeeze(tile):
    return jnp.where(iota((8, 256), 0) < 2, tile, pltpu.roll(tile, 4, 0))


def spread_coarse(plane, room):
    return jnp.concatenate([twice(plane[0:8], room.at[0]), twice(squeeze(plane[8:16]), room.at[1])[0:8]], axis=0)


def spread_mid(plane, room):
    parts = [twice(plane[0:8], room.at[0]), twice(plane[8:16], room.at[1]), twice(squeeze(plane[16:24]), room.at[2])[0:8]]
    return jnp.concatenate(parts, axis=0)


def smoothed(before, v, after, weight, source, w):
    inner = (before + after) + along_y(v)
    return source + (0.2 * v + weight * (w * inner + along_z(v)))


def is_early():
    return (lax.axis_index("grp") < lax.axis_size("grp") // 2) | odd("grp")


def finish_inner(error, fields, kept, out, scratch):
    mid_two, mid_source, mid_weight, fine_two, fine_source, fine_weight = fields
    zero, one, two, fine_one, fine_last, dup, dup_2, result, sems = scratch
    n = mid_two.shape[0]
    nf = fine_two.shape[0]
    for c in range(8):
        spread = spread_coarse(error[c], dup.at[c])
        for x in (2 * c + HALO, 2 * c + 1 + HALO):
            zero[x] = jnp.where(mid_weight[x] > 0.0, mid_two[x] + spread, 0.0)

    def sweep_mid(x, old, new):
        new[x] = smoothed(old[x - 1], old[x], old[x + 1], mid_weight[x], mid_source[x], 0.25)

    for x in range(HALO + 1, n - HALO - 1):
        sweep_mid(x, zero, one)
    for x in range(HALO + 2, n - HALO - 2):
        sweep_mid(x, one, two)

    def lift(m):
        spread = spread_mid(two[m], dup_2.at[m])
        x = 2 * m - HALO
        fine_one[x] = fine_two[x] + spread
        fine_one[x + 1] = fine_two[x + 1] + spread

    loop(HALO + 2, n - HALO - 2, lift, 6)

    def sweep_one(x):
        fine_last[x] = smoothed(fine_one[x - 1], fine_one[x], fine_one[x + 1], fine_weight[x], fine_source[x], 1.0)

    low, high = 2 * HALO + 1, nf - 2 * HALO - 1
    loop(low, high, sweep_one, 11)
    for field, first, to in ((zero, 0, kept[0]), (one, 1, kept[1]), (fine_one, 4, kept[2]), (fine_last, 5, kept[3])):
        for j in range(2):
            to[j] = field[HALO + first + j]
            to[2 + j] = field[field.shape[0] - HALO - 1 - first - j]
    copies = []
    low, high = low + 1, high - 1
    for j in range(2):
        mid = low + (high - low) // 2
        for x in range(low, mid) if j == 0 else range(mid, high):
            v = smoothed(fine_last[x - 1], fine_last[x], fine_last[x + 1], fine_weight[x], fine_source[x], 1.0)
            result[x - HALO] = v[0:32, :]
        rows = pl.ds(low - HALO, mid - low) if j == 0 else pl.ds(mid - HALO, high - mid)
        copies.append(pltpu.make_async_copy(result.at[rows], out.at[rows], sems.at[j]))
        copies[-1].start()
    for c in copies:
        c.wait()


def finish_early_kernel(error, sums, *rest):
    fields, (shifted, pay_a, pay_b, out), kept, scratch = rest[:6], rest[6:10], rest[10:14], rest[14:]
    resid = jnp.sum(sums[:, :LANES])
    load = jnp.sum(sums[:, LANES:])
    shift_c = jnp.full((16, 256), resid, F32) / jnp.full((16, 256), load, F32)
    for x in range(8):
        shifted[x] = error[x] + shift_c
    for k in range(2):
        send_x(pay_a, pay_b, k, shifted[k], shifted[6 + k])

    @pl.when(is_early())
    def _():
        finish_inner(shifted, fields, kept, out, scratch)


def finish_late_kernel(error, *rest):
    fields, kept_early, out, kept, scratch = rest[:6], rest[6:10], rest[11], rest[12:16], rest[16:]

    @pl.when(is_early())
    def _():
        for a, b in zip(kept_early, kept):
            b[...] = a[...]

    @pl.when(jnp.logical_not(is_early()))
    def _():
        finish_inner(error, fields, kept, out, scratch)


def finish_edge_kernel(
    x_a, x_b, mid_two, mid_source, mid_weight, fine_two, edge_two, fine_source, edge_source, fine_weight,
    zero, one, fine_one, fine_last, begun, out, zero_edge, one_edge, fine_edge, last_edge, dup, dup_2, result, sems,
):
    n = mid_two.shape[0]
    nf = fine_two.shape[0]
    nx = nf - 2 * HALO
    copies = []
    planes = x_sides(x_a, x_b, slice(0, 2))
    for side in (0, 1):
        sign = 1 if side == 0 else -1
        at = lambda k, side=side: HALO + k if side == 0 else n - HALO - 1 - k
        fine = lambda k, side=side: HALO + k if side == 0 else nf - HALO - 1 - k
        base = 8 * side + (0 if side == 0 else HALO - HALO - nx)
        for c in range(2):
            plane = planes[1 - side][c]
            spread = spread_coarse(plane, dup.at[2 * side + c])
            first = 2 * c if side == 0 else n - HALO + 2 * c
            for x in (first, first + 1):
                zero_edge[x] = jnp.where(mid_weight[x] > 0.0, mid_two[x] + spread, 0.0)

        def zero_of(k, side=side):
            return zero[2 * side + k] if k >= 0 else zero_edge[at(k)]

        def one_of(k, side=side):
            return one[2 * side + k - 1] if k >= 1 else one_edge[at(k)]

        for k in range(-2, 1):
            x = at(k)
            one_edge[x] = smoothed(zero_of(k - 1), zero_of(k), zero_of(k + 1), mid_weight[x], mid_source[x], 0.25)
        for k in range(-1, 2):
            x = at(k)
            value = smoothed(one_of(k - 1), one_of(k), one_of(k + 1), mid_weight[x], mid_source[x], 0.25)
            spread = spread_mid(value, dup_2.at[3 * side + k + 1])
            for f in (fine(2 * k), fine(2 * k + 1)):
                inside = HALO < f < nf - HALO - 1
                before = fine_two[f] if inside else edge_two[base + f]
                fine_edge[f] = before + spread

        def fine_of(k, side=side):
            return fine_one[2 * side + k - 4] if k >= 4 else fine_edge[fine(k)]

        def last_of(k, side=side):
            return fine_last[2 * side + k - 5] if k >= 5 else last_edge[fine(k)]

        for k in range(-1, 5):
            f = fine(k)
            source = fine_source[f] if HALO <= f < nf - HALO else edge_source[base + f]
            last_edge[f] = smoothed(fine_of(k - 1), fine_of(k), fine_of(k + 1), fine_weight[f], source, 1.0)
        for k in range(6):
            f = fine(k)
            v = smoothed(last_of(k - 1), last_of(k), last_of(k + 1), fine_weight[f], fine_source[f], 1.0)
            result[f - HALO] = v[0:32, :]
        rows = pl.ds(0, 6) if side == 0 else pl.ds(nx - 6, 6)
        copies.append(pltpu.make_async_copy(result.at[rows], out.at[rows], sems.at[side]))
        copies[-1].start()
    for c in copies:
        c.wait()


def both_ways(pairs):
    return pairs + [(j, i) for i, j in pairs]


def swap(pay_a, pay_b, axis):
    size = lax.axis_size(axis)
    pairs_a = [(i, i + 1) for i in range(1, size - 1, 2)]
    pairs_b = [(i, i + 1) for i in range(0, size - 1, 2)]
    return lax.ppermute(pay_a, axis, both_ways(pairs_a)), lax.ppermute(pay_b, axis, both_ways(pairs_b))


def exchange(value, distance):
    return lax.ppermute(value, "dev", [(i, i ^ distance) for i in range(lax.axis_size("dev"))])


def body(conc_old, phi_old, solid_pot, phase_label, iface_block, iface_owner):
    peers = lax.axis_size("dev")
    nx = conc_old.shape[0]
    half = nx // 2
    quarter = nx // 4
    ext = (nx + 2 * HALO, nx + 2 * HALO, 256)
    ext_mid = (half + 2 * HALO, half + 2 * HALO, 256)
    token_shape = shaped(8, LANES)

    pay_a, pay_b, own_lists = call(
        first_pack_kernel,
        [shaped(7 * nx, 256)] * 2 + [shaped(8, 256)],
        [conc_old, phase_label, iface_owner.reshape(1, -1), iface_block],
        [vmem(nx, HALO, 256)] * 2
        + [pltpu.VMEM((nx, HALO, 256), jnp.int32)] * 2
        + [pltpu.VMEM((1, 256), jnp.int32)] * 2
        + [vmem(7 * nx, 256)] * 2
        + [vmem(8, 256), pltpu.SemaphoreType.DMA((15,))],
        in_specs=[FAR] * 4,
        out_specs=[FAR] * 3,
        limit=VMEM_MOST,
        name="first_pack",
    )
    y_a, y_b = swap(pay_a, pay_b, "dev")
    conduct_mid, conduct_coarse, pay_a, pay_b, lists, gain, base = call(
        own_kernel,
        [shaped(half, half, 256), shaped(quarter, quarter, 256), shaped(22, 8, 256), shaped(22, 8, 256)]
        + [shaped(2, 256), shaped(nx, nx, 256), shaped(nx, nx, 256)],
        [conc_old, phase_label, phi_old, own_lists],
        [vmem(half, 2, nx, LANES), vmem(quarter, 2, half, LANES)],
        name="own",
    )
    xx_a, xx_b = swap(pay_a, pay_b, "grp")
    lists = jnp.concatenate([lists] + [exchange(lists, distance) for distance in range(peers - 2, 0, -2)], axis=0)
    far_rows = second_rows(nx)[1]
    far_pay = call(
        second_pack_kernel,
        [shaped(far_rows, 256), shaped(far_rows + peers, 256)],
        [phi_old, conduct_mid, lists, xx_a, xx_b],
        name="second_pack",
    )
    yy_a, yy_b = swap(*far_pay, "dev")
    pay_a, pay_b = call(
        first_pack_x_kernel,
        [shaped(35, 8, 256)] * 2,
        [conc_old, phase_label, y_a, y_b, lists],
        name="first_pack_x",
    )
    x_a, x_b = swap(pay_a, pay_b, "grp")

    ext_y = (nx, nx + 2 * HALO, 256)
    zero, first, second, third, gain_far, base_far, conc_inner, flux_inner = call(
        sweeps_inner_kernel,
        [shaped(*ext_y)] * 4 + [shaped(nx, 8, 256)] * 2 + [shaped(nx, nx, 256)] * 2,
        [conc_old, phase_label, phi_old, solid_pot, gain, base, y_a, y_b],
        name="sweeps_inner",
    )
    edge_args = [x_a, x_b, phase_label, phi_old, solid_pot, gain, base, zero, first, second, third]
    conc_new, flux_all, pay_a, pay_b = call(
        sweeps_edge_kernel,
        [shaped(nx, nx, 256), shaped(nx, nx, 256), shaped(3 * nx, 256), shaped(3 * nx, 256)],
        edge_args + [gain_far, base_far, conc_inner, flux_inner],
        [vmem(16, nx + 2 * HALO, 256)] * 4,
        name="sweeps_edge",
    )
    f_a, f_b = swap(pay_a, pay_b, "dev")
    flux_own, halo_mask = call(
        mask_kernel,
        [shaped(nx, nx, 256), shaped(nx, 8, 256)],
        [flux_all, lists, yy_b, yy_a],
        [vmem(3, nx, 8, LANES)],
        name="mask",
    )
    weight, scale, made = call(
        ready_kernel,
        [shaped(*ext)] * 2 + [token_shape],
        [conc_old, phase_label, y_a, y_b, x_a, x_b],
        name="ready",
    )
    pay_a, pay_b = call(
        flux_pack_x_kernel, [shaped(15, 8, 256)] * 2, [flux_own, f_a, f_b, halo_mask, made], name="flux_pack_x"
    )
    fx_a, fx_b = swap(pay_a, pay_b, "grp")
    fine_two, fine_source, fine_first, inner_mid, field = call(
        potential_inner_kernel,
        [shaped(*ext)] * 3 + [shaped(half, half, 256), shaped(*ext)],
        [flux_own, halo_mask, f_a, f_b, phi_old, yy_a, yy_b, xx_a, xx_b, weight, scale],
        [vmem(nx, 8, 256), vmem(half, 2, nx, LANES)],
        name="potential_inner",
    )
    k_a, k_b = swap(conduct_coarse, conduct_coarse, "dev")
    edge = (16, nx + 2 * HALO, 256)
    edge_two, edge_source, source_mid, pay_a, pay_b = call(
        potential_edge_kernel,
        [shaped(*edge), shaped(*edge), shaped(half, half, 256), shaped(4 * half, 256), shaped(4 * half, 256)],
        [fx_a, fx_b, weight, scale, field, fine_two, fine_source, fine_first, inner_mid, conduct_mid, k_a, k_b],
        [vmem(*edge), vmem(2, 2, nx, LANES)],
        name="potential_edge",
    )
    m_a, m_b = swap(pay_a, pay_b, "dev")
    concentration, flux, stored = call(
        store_kernel,
        [shaped(nx, nx, 256), shaped(nx, nx, 256), token_shape],
        [conc_new, flux_own],
        [pltpu.SemaphoreType.DMA((8,))],
        out_specs=[FAR, FAR, WHOLE],
        name="store",
    )
    wide = (quarter, 32, 256)
    rho, load = call(
        coarse_ready_kernel,
        [shaped(quarter, quarter, 256), shaped(8, LANES)],
        [conduct_coarse, k_a, k_b],
        [vmem(*wide)] * 4,
        name="coarse_ready",
    )
    pay_a, pay_b = call(
        mid_pack_x_kernel, [shaped(3 * HALO, 8, 256)] * 2, [source_mid, m_a, m_b], name="mid_pack_x"
    )
    mx_a, mx_b = swap(pay_a, pay_b, "grp")
    mid_two, mid_source, mid_weight, source_coarse, wide_coarse, pay_a, pay_b, sums = call(
        mid_kernel,
        [shaped(*ext_mid)] * 3
        + [shaped(quarter, 12, 256), shaped(quarter, 12, 256), shaped(72, 256), shaped(80, 256), shaped(8, 256)],
        [source_mid, conduct_mid, yy_a, yy_b, xx_a, xx_b, m_a, m_b, mx_a, mx_b, rho, load, stored],
        [vmem(*ext_mid)] * 2 + [vmem(8, 2, half + 2 * HALO, LANES)] * 2,
        name="middle",
    )
    c_a, c_b = swap(pay_a, pay_b, "dev")
    sums = sums + c_b[72:80]
    distance = 2
    while distance < peers:
        sums = sums + exchange(sums, distance)
        distance *= 2
    (error,) = call(
        coarse_kernel,
        [shaped(8, 16, 256)],
        [source_coarse, wide_coarse, k_a, k_b, c_a, c_b],
        [vmem(*wide)] * 4,
        name="coarse",
    )
    fields = [mid_two, mid_source, mid_weight, fine_two, fine_source, weight]
    kept = [shaped(4, half + 2 * HALO, 256)] * 2 + [shaped(4, nx + 2 * HALO, 256)] * 2
    scratch = [vmem(*ext_mid)] * 3 + [vmem(*ext)] * 2
    scratch += [vmem(8, 2, 2, 16, LANES), vmem(half + 2 * HALO, 3, 2, 16, LANES), vmem(nx, nx, 256)]
    scratch += [pltpu.SemaphoreType.DMA((2,))]
    error, pay_a, pay_b, begun, *kept_early = call(
        finish_early_kernel,
        [shaped(8, 16, 256), shaped(2, 16, 256), shaped(2, 16, 256), shaped(nx, nx, 256)] + kept,
        [error, sums] + fields,
        scratch,
        out_specs=[WHOLE] * 3 + [FAR] + [WHOLE] * 4,
        name="finish_early",
    )
    e_a, e_b = swap(pay_a, pay_b, "grp")
    begun, zero, one, fine_one, fine_last = call(
        finish_late_kernel,
        [shaped(nx, nx, 256)] + kept,
        [error] + fields + kept_early + [begun],
        scratch,
        in_specs=[WHOLE] * 11 + [FAR],
        out_specs=[FAR] + [WHOLE] * 4,
        aliases={11: 0},
        name="finish_late",
    )
    finish_args = [e_a, e_b, mid_two, mid_source, mid_weight, fine_two, edge_two, fine_source, edge_source, weight]
    finish_args += [zero, one, fine_one, fine_last, begun]
    (potential,) = call(
        finish_edge_kernel,
        [shaped(nx, nx, 256)],
        finish_args,
        [vmem(*ext_mid), vmem(*ext_mid), vmem(*ext), vmem(*ext)]
        + [vmem(4, 2, 2, 16, LANES), vmem(6, 3, 2, 16, LANES), vmem(nx, nx, 256)]
        + [pltpu.SemaphoreType.DMA((2,))],
        in_specs=[WHOLE] * (len(finish_args) - 1) + [FAR],
        out_specs=[FAR],
        aliases={len(finish_args) - 1: 0},
        name="finish_edge",
    )
    return (concentration, flux, potential)


def solution(mesh):
    brick = P("grp", "dev", None)
    return jax.shard_map(
        body,
        mesh=mesh,
        in_specs=(brick, brick, brick, brick, P("grp", "dev"), brick),
        out_specs=(brick, brick, brick),
        check_vma=False,
    )
```

```python
import jax
import jax.numpy as jnp
from jax import lax
from jax.experimental import pallas as pl
from jax.experimental.pallas import tpu as pltpu
from jax.sharding import PartitionSpec as P


F32 = jnp.float32
MASS = 0.05
OMEGA = 0.8
DIFFUSION_TABLE = (1.5, 0.1, 0.4)
RATIO_TABLE = tuple(d / (1.0 + 6.0 * d) for d in DIFFUSION_TABLE)
INVERSE_TABLE = tuple(1.0 / (1.0 + 6.0 * d) for d in DIFFUSION_TABLE)
CONDUCT_TABLE = (1.0, 0.3, 0.6)
KINETIC_TABLE = (0.2, 1.0, 0.5)
SWEEPS = 4
COARSE_SWEEPS = 8
COARSE_NEAR = 8
HALO = 4
LANES = 128
VMEM_LIMIT = 28 * 1024 * 1024
VMEM_MOST = 58 * 1024 * 1024


def shaped(*shape):
    return jax.ShapeDtypeStruct(shape, F32)


WHOLE = pl.BlockSpec(memory_space=pltpu.VMEM)
FAR = pl.BlockSpec(memory_space=pltpu.HBM)


def call(kernel, outs, args, scratch=(), in_specs=None, out_specs=None, limit=VMEM_LIMIT, aliases=None, flops=10**6, name=None):
    size = sum(4 * a.size for a in args) + sum(4 * o.size for o in outs)
    return pl.pallas_call(
        kernel,
        out_shape=tuple(outs),
        in_specs=in_specs or [WHOLE] * len(args),
        out_specs=tuple(out_specs or [WHOLE] * len(outs)),
        scratch_shapes=list(scratch),
        input_output_aliases=aliases or {},
        compiler_params=pltpu.CompilerParams(vmem_limit_bytes=limit),
        cost_estimate=pl.CostEstimate(flops=flops, bytes_accessed=size, transcendentals=0),
        name=name,
    )(*args)


def vmem(*shape):
    return pltpu.VMEM(shape, F32)


def iota(shape, dim):
    return lax.broadcasted_iota(jnp.int32, shape, dim)


def pick(label, table):
    return jnp.where(label == 0, table[0], jnp.where(label == 1, table[1], table[2])).astype(F32)


def loop(low, high, body, unroll=8):
    steps = (high - low) // unroll

    def step(i, carry):
        for u in range(unroll):
            body(low + i * unroll + u)
        return carry

    if steps > 1:
        lax.fori_loop(0, steps, step, 0)
    else:
        steps = 0
    for x in range(low + steps * unroll, high):
        body(x)


def odd(axis):
    return lax.rem(lax.axis_index(axis), 2) == 1


def along_y(v):
    return pltpu.roll(v, 1, 0) + pltpu.roll(v, v.shape[0] - 1, 0)


def along_z(v):
    low, high = v[:, :LANES], v[:, LANES:]
    lane = iota(low.shape, 1)
    first, last = lane == 0, lane == LANES - 1
    low_up, high_up = pltpu.roll(low, 1, 1), pltpu.roll(high, 1, 1)
    low_down, high_down = pltpu.roll(low, LANES - 1, 1), pltpu.roll(high, LANES - 1, 1)
    low_sum = jnp.where(first, 0.0, low_up) + jnp.where(last, high_down, low_down)
    high_sum = jnp.where(first, low_up, high_up) + jnp.where(last, 0.0, high_down)
    return jnp.concatenate([low_sum, high_sum], axis=1)


def upper(shape=(8, 256)):
    return iota(shape, 0) < HALO


def twice(tile, scratch):
    for h in range(2):
        part = tile[:, h * LANES : (h + 1) * LANES]
        scratch[h, pl.ds(0, 8, stride=2), :] = part
        scratch[h, pl.ds(1, 8, stride=2), :] = part
    return jnp.concatenate([scratch[0], scratch[1]], axis=1)


def pair_rows(v, scratch):
    half = v.shape[0] // 2
    parts = []
    for h in range(2):
        scratch[h] = v[:, h * LANES : (h + 1) * LANES]
        parts.append(scratch[h, pl.ds(0, half, stride=2), :] + scratch[h, pl.ds(1, half, stride=2), :])
    return jnp.concatenate(parts, axis=1)


def either(flag, if_true, if_false):
    return jnp.where(flag, if_true, if_false)


def y_sides(r_a, r_b, at, count):
    flag = odd("dev")
    a, b = r_a[at : at + count, :], r_b[at : at + count, :]
    return either(flag, a, b), either(flag, b, a)


def x_sides(r_a, r_b, index):
    flag = odd("grp")
    a, b = r_a[index], r_b[index]
    return either(flag, a, b), either(flag, b, a)


def send_y(pay_a, pay_b, at, first, last):
    flag = odd("dev")
    n = first.shape[0]
    pay_a[at : at + n, :] = either(flag, last, first)
    pay_b[at : at + n, :] = either(flag, first, last)


def send_x(pay_a, pay_b, index, first, last):
    flag = odd("grp")
    pay_a[index] = either(flag, last, first)
    pay_b[index] = either(flag, first, last)


def halo_tile(after, before):
    parts = [after]
    if after.shape[0] < HALO:
        parts.append(jnp.zeros((2 * HALO - 2 * after.shape[0], after.shape[1]), F32))
    return jnp.concatenate(parts + [before], axis=0)


def first_pack_kernel(
    conc, label, owner, block, out_a, out_b, own_lists,
    c_first, c_last, l_first, l_last, own_owner, own_block, pay_a, pay_b, named, sems,
):
    nx = conc.shape[0]
    half = nx // 2
    lists = [pltpu.make_async_copy(owner, own_owner, sems.at[8]), pltpu.make_async_copy(block, own_block, sems.at[9])]
    reads = []
    for j in range(2):
        planes = pl.ds(half * j, half)
        for i, (ref, at, to) in enumerate(
            ((conc, 0, c_first), (conc, 28, c_last), (label, 0, l_first), (label, 28, l_last))
        ):
            reads.append(pltpu.make_async_copy(ref.at[planes, pl.ds(at, 4), :], to.at[planes], sems.at[4 * j + i]))
    for c in reads + lists:
        c.start()
    writes = []
    for j in range(2):
        for c in reads[4 * j : 4 * j + 4]:
            c.wait()
        for x in range(half * j, half * j + half):
            send_y(pay_a, pay_b, 7 * x, c_first[x], c_last[x])
            send_y(pay_a, pay_b, 7 * x + 4, l_first[x, 0:3, :].astype(F32), l_last[x, 1:4, :].astype(F32))
        rows = pl.ds(7 * half * j, 7 * half)
        for i, (pay, out) in enumerate(((pay_a, out_a), (pay_b, out_b))):
            writes.append(pltpu.make_async_copy(pay.at[rows], out.at[rows], sems.at[10 + 2 * j + i]))
            writes[-1].start()
    for c in lists:
        c.wait()
    named[...] = jnp.concatenate([own_owner[...], own_block[...], jnp.zeros((6, 256), jnp.int32)], axis=0).astype(F32)
    writes.append(pltpu.make_async_copy(named, own_lists, sems.at[14]))
    writes[-1].start()
    for c in writes:
        c.wait()


def own_kernel(conc, label, phi, named, mid, coarse, pay_a, pay_b, lists, gain, base, pairs, pairs_2):
    nx = conc.shape[0]
    half = nx // 2
    lists[...] = named[0:2, :]

    def coefficients(i):
        gain[i] = pick(label[i], RATIO_TABLE)
        base[i] = conc[i] * pick(label[i], INVERSE_TABLE)

    loop(0, nx, coefficients, 4)

    def coarsen(i):
        total = conc[2 * i] * pick(label[2 * i], CONDUCT_TABLE) + conc[2 * i + 1] * pick(label[2 * i + 1], CONDUCT_TABLE)
        mid[i] = 0.25 * pair_rows(total, pairs.at[i])

    loop(0, half, coarsen, 4)
    for i in range(half // 2):
        coarse[i] = 0.25 * pair_rows(mid[2 * i] + mid[2 * i + 1], pairs_2.at[i])
    for k in range(HALO):
        for t in range(4):
            rows = slice(8 * t, 8 * t + 8)
            send_x(pay_a, pay_b, 4 * k + t, phi[k, rows, :], phi[nx - HALO + k, rows, :])
    for k in range(MID_HALO):
        for t in range(2):
            rows = slice(8 * t, 8 * t + 8)
            send_x(pay_a, pay_b, 16 + 2 * k + t, mid[k, rows, :], mid[half - MID_HALO + k, rows, :])


def first_pack_x_kernel(conc, label, r_a, r_b, token, pay_a, pay_b):
    nx = conc.shape[0]

    def plane(ref, k, t, offset, count):
        if t < 4:
            return ref[k, 8 * t : 8 * t + 8, :].astype(F32)
        return halo_tile(*y_sides(r_a, r_b, 7 * k + offset, count))

    for t in range(5):
        for k in range(HALO):
            send_x(pay_a, pay_b, 5 * k + t, plane(conc, k, t, 0, 4), plane(conc, nx - HALO + k, t, 0, 4))
        for k in range(3):
            send_x(pay_a, pay_b, 20 + 5 * k + t, plane(label, k, t, 4, 3), plane(label, nx - 3 + k, t, 4, 3))


MID_HALO = 3


def corner_rows(n, width, reach):
    counts = [min(width, k + reach) for k in range(width)]
    counts = counts + [width] * n + counts[::-1]
    return counts, [sum(counts[:i]) for i in range(len(counts))]


def second_rows(nx):
    phi = sum(corner_rows(nx, HALO, 0)[0])
    mid = sum(corner_rows(nx // 2, MID_HALO, 1)[0])
    return phi, phi + mid, phi + mid + 64


def second_pack_kernel(phi, mid, coarse, lists, x_a, x_b, pay_a, pay_b):
    nx = phi.shape[0]
    starts = second_rows(nx)

    def put(own, width, reach, index, base):
        n = own.shape[0]
        counts, at = corner_rows(n, width, reach)
        tiles = own.shape[1] // 8
        for x in range(n):
            send_y(pay_a, pay_b, base + at[width + x], own[x, 0:width, :], own[x, 8 * tiles - width : 8 * tiles, :])
        for k in range(width):
            first_after, first_before = x_sides(x_a, x_b, index + tiles * k)
            last_after, last_before = x_sides(x_a, x_b, index + tiles * k + tiles - 1)
            for x, first, last in ((k, first_before, last_before), (width + n + k, first_after, last_after)):
                if counts[x]:
                    send_y(pay_a, pay_b, base + at[x], first[0 : counts[x]], last[8 - counts[x] : 8])

    put(phi, HALO, 0, 0, 0)
    put(mid, MID_HALO, 1, 16, starts[0])
    base = starts[1]
    for x in range(8):
        pay_a[base + 8 * x : base + 8 * x + 8, :] = coarse[x]
        pay_b[base + 8 * x : base + 8 * x + 8, :] = coarse[x]
    base = starts[2]
    pay_b[base : base + lists.shape[0], :] = lists[...]


def second_halo(r_a, r_b, n, width, reach, x, base):
    counts, at = corner_rows(n, width, reach)
    x = x - HALO + width
    if x < 0 or x >= len(counts) or not counts[x]:
        return jnp.zeros((8, 256), F32)
    return halo_tile(*y_sides(r_a, r_b, base + at[x], counts[x]))


def wide_rows(own, after_own, before_own, after, before):
    gap = jnp.zeros((6, 256), F32)
    return jnp.concatenate([own, after_own, after, gap, before, before_own], axis=0)


def flux_plane(c, solid, phi, label):
    drive = 0.5 * (solid - phi)
    logc = jnp.log(c)
    return pick(label, KINETIC_TABLE) * (jnp.exp(drive + 0.4 * logc) - jnp.exp(0.6 * logc - drive))


def around_plane(before, v, after):
    return (before + after) + (along_y(v) + along_z(v))


def sweeps_inner_kernel(
    conc, label, phi, solid, gain, base, y_a, y_b, zero, first, second, third, gain_far, base_far, out, flux
):
    nx = conc.shape[0]

    def own(i):
        zero[i, 0:32, :] = conc[i]

    loop(0, nx, own)
    for i in range(nx):
        c = halo_tile(*y_sides(y_a, y_b, 7 * i, 4))
        lab = halo_tile(*y_sides(y_a, y_b, 7 * i + 4, 3))
        zero[i, 32:40, :] = c
        gain_far[i] = jnp.where(c > 0.0, pick(lab, RATIO_TABLE), 0.0)
        base_far[i] = c * pick(lab, INVERSE_TABLE)
    fields = (zero, first, second, third)
    for s in range(1, SWEEPS):
        old, new = fields[s - 1], fields[s]

        def sweep(i, old=old, new=new):
            g = jnp.concatenate([gain[i], gain_far[i]], axis=0)
            b = jnp.concatenate([base[i], base_far[i]], axis=0)
            new[i] = b + g * around_plane(old[i - 1], old[i], old[i + 1])

        loop(s, nx - s, sweep)

    def last(i):
        c = base[i] + gain[i] * around_plane(third[i - 1], third[i], third[i + 1])[0:32, :]
        out[i] = c
        flux[i] = flux_plane(c, solid[i], phi[i], label[i])

    loop(SWEEPS, nx - SWEEPS, last, 4)


def sweeps_edge_kernel(
    x_a, x_b, label, phi, solid, gain, base, zero, first, second, third, gain_far, base_far, out_inner, flux_inner,
    out, flux, pay_a, pay_b, zero_x, first_x, second_x, third_x,
):
    nx = out.shape[0]
    inner = (zero, first, second, third)
    edge = (zero_x, first_x, second_x, third_x)

    def copy(i):
        out[i] = out_inner[i]
        flux[i] = flux_inner[i]

    loop(SWEEPS, nx - SWEEPS, copy)
    for side in range(2):
        plane = lambda k, side=side: k if side == 0 else nx - 1 - k
        row = lambda k, side=side: 8 * side + HALO + k
        far = lambda k, index, side=side: x_sides(x_a, x_b, index)[1 - side]
        gains, bases = {}, {}
        for j in range(1, HALO + 1):
            k = HALO - j if side == 0 else j - 1
            zero_x[row(-j)] = jnp.concatenate([far(k, 5 * k + t) for t in range(5)], axis=0)
            if j < HALO:
                k = HALO - 1 - j if side == 0 else j - 1
                lab = jnp.concatenate([far(k, 20 + 5 * k + t) for t in range(5)], axis=0)
                c = zero_x[row(-j)]
                gains[-j] = jnp.where(c > 0.0, pick(lab, RATIO_TABLE), 0.0)
                bases[-j] = c * pick(lab, INVERSE_TABLE)
        for k in range(SWEEPS):
            gains[k] = jnp.concatenate([gain[plane(k)], gain_far[plane(k)]], axis=0)
            bases[k] = jnp.concatenate([base[plane(k)], base_far[plane(k)]], axis=0)
        for s in range(1, SWEEPS + 1):

            def old(k, s=s):
                return inner[s - 1][plane(k)] if k >= s - 1 else edge[s - 1][row(k)]

            for k in range(s - SWEEPS, s):
                c = bases[k] + gains[k] * around_plane(old(k - 1), old(k), old(k + 1))
                if s < SWEEPS:
                    edge[s][row(k)] = c
                else:
                    c = c[0:32, :]
                    out[plane(k)] = c
                    flux[plane(k)] = flux_plane(c, solid[plane(k)], phi[plane(k)], label[plane(k)])
    for x in range(nx):
        send_y(pay_a, pay_b, 3 * x, flux[x, 0:3, :], flux[x, 29:32, :])


def mask_kernel(flux_all, lists, far, flux, halo_mask, marked):
    nx = flux_all.shape[0]
    rows = lists.shape[0]
    pieces = [lists[i : i + 1, :] for i in range(rows)] + [far[i : i + 1, :] for i in range(far.shape[0] - rows, far.shape[0])]
    owner = jnp.concatenate(pieces[0::2], axis=1).astype(jnp.int32)
    block = jnp.concatenate(pieces[1::2], axis=1).astype(jnp.int32)
    entries = owner.shape[1]
    hit_column = (iota((64, entries), 0) == lax.rem(block, 64)).astype(jnp.bfloat16)
    reach = owner - lax.axis_index("dev") + 1
    at_row = jnp.where((reach >= 0) & (reach < 3), reach * nx + lax.shift_right_arithmetic(block, 6), -1)
    hit_row = (iota((3 * nx, entries), 0) == at_row).astype(jnp.bfloat16)
    named = lax.dot_general(hit_row, hit_column, (((1,), (1,)), ((), ())), preferred_element_type=F32)
    named = jnp.concatenate([named, jnp.zeros((3 * nx, LANES - 64), F32)], axis=1)
    for j in range(3):
        for i in range(nx):
            marked[j, i] = jnp.broadcast_to(named[j * nx + i : j * nx + i + 1, :], (8, LANES))
    is_row = lax.div(iota((32, LANES), 1), 2) == iota((32, LANES), 0)
    row, pair = iota((8, LANES), 0), lax.div(iota((8, LANES), 1), 2)
    is_after = (row < 3) & (pair == row)
    is_before = (row >= 5) & (pair == row + 24)
    spread = (lax.rem(iota((LANES, 256), 0), 2) == lax.div(iota((LANES, 256), 1), LANES)).astype(jnp.bfloat16)

    def plane(i):
        marks = jnp.where(is_row, jnp.concatenate([marked[1, i]] * 4, axis=0), 0.0)
        beyond = jnp.where(is_after, marked[2, i], jnp.where(is_before, marked[0, i], 0.0))
        marks = jnp.concatenate([marks, beyond], axis=0).astype(jnp.bfloat16)
        listed = jnp.dot(marks, spread, preferred_element_type=F32) > 0.5
        flux[i] = jnp.where(listed[0:32], flux_all[i], 0.0)
        halo_mask[i] = jnp.where(listed[32:40], 1.0, 0.0)

    loop(0, nx, plane, 16)


def store_kernel(conc, flux, conc_out, flux_out, token, sems):
    copies = []
    for i, (ref, to) in enumerate(((conc, conc_out), (flux, flux_out))):
        for j in range(4):
            rows = pl.ds(8 * j, 8)
            copies.append(pltpu.make_async_copy(ref.at[rows], to.at[rows], sems.at[4 * i + j]))
            copies[-1].start()
    token[...] = jnp.zeros(token.shape, F32)
    for c in copies:
        c.wait()


def ready_kernel(conc, label, y_a, y_b, x_a, x_b, weight, scale, token):
    nx = conc.shape[0]
    token[...] = jnp.zeros(token.shape, F32)

    def put(x, rows, c, lab):
        conduct = c * pick(lab, CONDUCT_TABLE)
        factor = OMEGA / (MASS + 6.0 * conduct)
        weight[x, rows, :] = conduct * factor
        scale[x, rows, :] = factor

    def own(i):
        put(HALO + i, slice(0, 32), conc[i], label[i])

    loop(0, nx, own, 4)
    for i in range(nx):
        c = halo_tile(*y_sides(y_a, y_b, 7 * i, 4))
        lab = halo_tile(*y_sides(y_a, y_b, 7 * i + 4, 3))
        put(HALO + i, slice(32, 40), c, lab)
    for t in range(5):
        rows = slice(8 * t, 8 * t + 8)
        for k in range(HALO):
            c_after, c_before = x_sides(x_a, x_b, 5 * k + t)
            l_after = x_sides(x_a, x_b, 20 + 5 * min(k, 2) + t)[0]
            l_before = x_sides(x_a, x_b, 20 + 5 * max(k - 1, 0) + t)[1]
            put(k, rows, c_before, l_before)
            put(HALO + nx + k, rows, c_after, l_after)


def place_phi(phi, yy_a, yy_b, xx_a, xx_b, field):
    nx = phi.shape[0]

    def own(i):
        field[HALO + i, 0:32, :] = phi[i]

    loop(0, nx, own)
    for x in range(nx + 2 * HALO):
        field[x, 32:40, :] = second_halo(yy_a, yy_b, nx, HALO, 0, x, 0)
    for t in range(4):
        for k in range(HALO):
            after, before = x_sides(xx_a, xx_b, 4 * k + t)
            field[k, 8 * t : 8 * t + 8, :] = before
            field[HALO + nx + k, 8 * t : 8 * t + 8, :] = after


def flux_pack_x_kernel(flux, r_a, r_b, mask, token, pay_a, pay_b):
    nx = flux.shape[0]

    def tile(x, t):
        if t < 4:
            return flux[x, 8 * t : 8 * t + 8, :]
        return mask[x] * halo_tile(*y_sides(r_a, r_b, 3 * x, 3))

    for k in range(3):
        for t in range(5):
            send_x(pay_a, pay_b, 5 * k + t, tile(k, t), tile(nx - 3 + k, t))


def first_sweep(field, weight, scale, x, rows, flux):
    p = field[x]
    near = (field[x - 1] + field[x + 1]) + (along_y(p) + along_z(p))
    b = scale[x, rows, :] * (MASS * p[rows, :] + flux)
    return b, 0.2 * p[rows, :] + weight[x, rows, :] * near[rows, :] + b


def potential_inner_kernel(
    flux, mask, y_a, y_b, phi, yy_a, yy_b, xx_a, xx_b, weight, scale, after_two, source, first, source_mid, field, far, pairs
):
    nx = flux.shape[0]
    place_phi(phi, yy_a, yy_b, xx_a, xx_b, field)
    for i in range(nx):
        far[i] = mask[i] * halo_tile(*y_sides(y_a, y_b, 3 * i, 3))

    def own(i):
        x = HALO + i
        f = jnp.concatenate([flux[i], far[i]], axis=0)
        source[x], first[x] = first_sweep(field, weight, scale, x, slice(0, 40), f)

    loop(0, nx, own)

    def around(values, x):
        v = values[x]
        return v, weight[x] * ((values[x - 1] + values[x + 1]) + (along_y(v) + along_z(v)))

    def sweep(x):
        v, near = around(first, x)
        after_two[x] = 0.2 * v + (source[x] + near)

    loop(HALO + 1, HALO + nx - 1, sweep)

    def remainder(x):
        v, near = around(after_two, x)
        return ((source[x] - OMEGA * v) + near)[0:32, :] / scale[x, 0:32, :]

    def coarsen(i):
        x = HALO + 2 * i
        source_mid[i] = 0.25 * pair_rows(remainder(x) + remainder(x + 1), pairs.at[i])

    loop(1, nx // 2 - 1, coarsen, 4)


def mid_factor(conduct):
    return OMEGA / (MASS + 3.0 * conduct)


def potential_edge_kernel(
    x_a, x_b, weight, scale, field, inner_two, inner_source, inner_first, inner_mid, conduct_mid,
    edge_two, edge_source, source_mid, pay_a, pay_b, first, pairs,
):
    half = source_mid.shape[0]
    nx = 2 * half
    for side, face in ((0, HALO), (1, HALO + nx)):
        base = 8 * side + HALO - face
        for k in range(3):
            x = face - 3 + k if side == 0 else face + k
            f = jnp.concatenate([x_sides(x_a, x_b, 5 * k + t)[1 - side] for t in range(5)], axis=0)
            edge_source[base + x], first[base + x] = first_sweep(field, weight, scale, x, slice(0, 40), f)

        def first_of(x, base=base):
            return inner_first[x] if HALO <= x < HALO + nx else first[base + x]

        def source_of(x, base=base):
            return inner_source[x] if HALO <= x < HALO + nx else edge_source[base + x]

        def two_of(x, base=base):
            return inner_two[x] if HALO < x < HALO + nx - 1 else edge_two[base + x]

        for x in range(face - 2, face + 1) if side == 0 else range(face - 1, face + 2):
            v = first_of(x)
            near = weight[x] * ((first_of(x - 1) + first_of(x + 1)) + (along_y(v) + along_z(v)))
            edge_two[base + x] = 0.2 * v + (source_of(x) + near)
        total = 0.0
        at = face if side == 0 else face - 2
        for x in (at, at + 1):
            v = two_of(x)
            near = weight[x] * ((two_of(x - 1) + two_of(x + 1)) + (along_y(v) + along_z(v)))
            total = total + ((source_of(x) - OMEGA * v) + near)[0:32, :] / scale[x, 0:32, :]
        at = 0 if side == 0 else half - 1
        source_mid[at] = mid_factor(conduct_mid[at]) * (0.25 * pair_rows(total, pairs.at[side]))
    for x in range(1, half - 1):
        source_mid[x] = mid_factor(conduct_mid[x]) * inner_mid[x]
    for x in range(half):
        send_y(pay_a, pay_b, 4 * x, source_mid[x, 0:4, :], source_mid[x, 12:16, :])


def mid_pack_x_kernel(field, r_a, r_b, token, token_2, pay_a, pay_b):
    n = field.shape[0]

    def tile(x, t):
        if t < 2:
            return field[x, 8 * t : 8 * t + 8, :]
        return halo_tile(*y_sides(r_a, r_b, 4 * x, 4))

    for k in range(HALO):
        for t in range(3):
            send_x(pay_a, pay_b, 3 * k + t, tile(k, t), tile(n - HALO + k, t))


def mid_kernel(
    source_own, conduct_own, yy_a, yy_b, xx_a, xx_b, y_a, y_b, x_a, x_b, rho, load,
    after_two, source, weight, coarse, conduct, pay_a, pay_b, part, scale, mid_conduct, pairs, pairs_2,
):
    n = source_own.shape[0]
    base = second_rows(2 * n)[0]

    def put(x, rows, b, k):
        factor = mid_factor(k)
        weight[x, rows, :] = k * factor
        scale[x, rows, :] = factor
        source[x, rows, :] = b
        mid_conduct[x, rows, :] = k

    def far(x):
        return second_halo(yy_a, yy_b, n, MID_HALO, 1, x, base)

    for i in range(n):
        put(HALO + i, slice(0, 16), source_own[i], conduct_own[i])
        put(HALO + i, slice(16, 24), halo_tile(*y_sides(y_a, y_b, 4 * i, 4)), far(HALO + i))
    for k in range(HALO):
        for t in range(3):
            rows = slice(8 * t, 8 * t + 8)
            b_after, b_before = x_sides(x_a, x_b, 3 * k + t)
            if t < 2:
                none = jnp.zeros((8, 256), F32)
                c_before = x_sides(xx_a, xx_b, 16 + 2 * (k - 1) + t)[1] if k > 0 else none
                c_after = x_sides(xx_a, xx_b, 16 + 2 * k + t)[0] if k < MID_HALO else none
            else:
                c_after, c_before = far(HALO + n + k), far(k)
            put(k, rows, b_before, c_before)
            put(HALO + n + k, rows, b_after, c_after)

    def around(values, x):
        v = values[x]
        return v, weight[x] * (0.25 * ((values[x - 1] + values[x + 1]) + along_y(v)) + along_z(v))

    def sweep(x):
        v, near = around(source, x)
        after_two[x] = 0.2 * v + (source[x] + near)

    loop(1, n + 2 * HALO - 1, sweep, 11)

    def remainder(x):
        v, near = around(after_two, x)
        return ((source[x] - OMEGA * v) + near) / scale[x]

    total = jnp.zeros((8, 256), F32)
    for i in range(n // 2):
        x = HALO + 2 * i
        value = 0.25 * pair_rows(remainder(x) + remainder(x + 1), pairs.at[i])
        k = 0.25 * pair_rows(mid_conduct[x] + mid_conduct[x + 1], pairs_2.at[i])
        coarse[i] = value
        conduct[i] = k
        send_y(pay_a, pay_b, 9 * i, value[1:9], jnp.concatenate([value[11:12], value[0:7]], axis=0))
        send_y(pay_a, pay_b, 9 * i + 8, k[8:9], k[11:12])
        total += rho[i] * value[0:8]
    sums = jnp.concatenate([total[:, :LANES] + total[:, LANES:], load[...]], axis=1)
    pay_b[72:80, :] = sums
    part[...] = sums


COARSE_W = 0.0625


def coarse_ready_kernel(own, r_a, r_b, rho, load, token, one, two, conduct, scale):
    token[...] = jnp.zeros(token.shape, F32)
    base = r_a.shape[0] - 64
    for x in range(8):
        after, before = y_sides(r_a, r_b, base + 8 * x, 8)
        k = jnp.concatenate([own[x], after, jnp.zeros((8, 256), F32), before], axis=0)
        conduct[x] = k
        scale[x] = OMEGA / (MASS + 2.25 * k)
        one[x] = jnp.ones(k.shape, F32)
    fields = (one, two)
    for s in range(COARSE_SWEEPS):
        old, new = fields[s % 2], fields[(s + 1) % 2]
        for x in range(8):
            near = [conduct[i] * old[i] if 0 <= i < 8 else None for i in (x - 1, x, x + 1)]
            inner = along_y(near[1])
            for other in (near[0], near[2]):
                if other is not None:
                    inner = inner + other
            new[x] = 0.2 * old[x] + scale[x] * (COARSE_W * inner + along_z(near[1]))
    last = fields[COARSE_SWEEPS % 2]
    peer, peers = lax.axis_index("dev"), lax.axis_size("dev")
    row, z = iota((8, 256), 0), iota((8, 256), 1)
    edge_y = ((row == 0) & (peer == 0)) | ((row == 7) & (peer == peers - 1))
    edge = edge_y.astype(F32) * COARSE_W + ((z == 0) | (z == 255)).astype(F32)
    total = jnp.zeros((8, 256), F32)
    for x in range(8):
        rho[x] = last[x, 0:8, :]
        total += MASS + own[x] * (edge + (COARSE_W if x in (0, 7) else 0.0))
    load[...] = total[:, :LANES] + total[:, LANES:]


def coarse_kernel(own, conduct, far_a, far_b, r_a, r_b, error, source, weight, one, two):
    base = far_a.shape[0] - 64
    for x in range(8):
        after, before = y_sides(r_a, r_b, 9 * x, 8)
        b = wide_rows(own[x, 0:8, :], own[x, 8:9, :], own[x, 11:12, :], after, before)
        last_after, last_before = y_sides(r_a, r_b, 9 * x + 8, 1)
        after, before = y_sides(far_a, far_b, base + 8 * x, 8)
        after = jnp.concatenate([after[1:8], last_after], axis=0)
        before = jnp.concatenate([last_before, before[0:7]], axis=0)
        k = wide_rows(conduct[x, 0:8, :], conduct[x, 8:9, :], conduct[x, 11:12, :], after, before)
        factor = OMEGA / (MASS + 2.25 * k)
        weight[x] = k * factor
        source[x] = factor * b
    old = source
    for s in range(1, COARSE_SWEEPS):
        new = one if s % 2 else two
        for x in range(8):
            v = old[x]
            inner = along_y(v)
            if x > 0:
                inner = inner + old[x - 1]
            if x < 7:
                inner = inner + old[x + 1]
            new[x] = 0.2 * v + (source[x] + weight[x] * (COARSE_W * inner + along_z(v)))
        old = new
    for x in range(8):
        error[x, 0:8, :] = old[x, 0:8, :]
        error[x, 8:16, :] = jnp.where(upper(), old[x, 8:16, :], old[x, 24:32, :])


def squeeze(tile):
    return jnp.where(iota((8, 256), 0) < 2, tile, pltpu.roll(tile, 4, 0))


def spread_coarse(plane, room):
    return jnp.concatenate([twice(plane[0:8], room.at[0]), twice(squeeze(plane[8:16]), room.at[1])[0:8]], axis=0)


def spread_mid(plane, room):
    parts = [twice(plane[0:8], room.at[0]), twice(plane[8:16], room.at[1]), twice(squeeze(plane[16:24]), room.at[2])[0:8]]
    return jnp.concatenate(parts, axis=0)


def smoothed(before, v, after, weight, source, w):
    inner = (before + after) + along_y(v)
    return source + (0.2 * v + weight * (w * inner + along_z(v)))


def is_early():
    return (lax.axis_index("grp") < lax.axis_size("grp") // 2) | odd("grp")


def finish_inner(error, fields, kept, out, scratch):
    mid_two, mid_source, mid_weight, fine_two, fine_source, fine_weight = fields
    zero, one, two, fine_one, fine_last, dup, dup_2, result, sems = scratch
    n = mid_two.shape[0]
    nf = fine_two.shape[0]
    for c in range(8):
        spread = spread_coarse(error[c], dup.at[c])
        for x in (2 * c + HALO, 2 * c + 1 + HALO):
            zero[x] = jnp.where(mid_weight[x] > 0.0, mid_two[x] + spread, 0.0)

    def sweep_mid(x, old, new):
        new[x] = smoothed(old[x - 1], old[x], old[x + 1], mid_weight[x], mid_source[x], 0.25)

    for x in range(HALO + 1, n - HALO - 1):
        sweep_mid(x, zero, one)
    for x in range(HALO + 2, n - HALO - 2):
        sweep_mid(x, one, two)

    def lift(m):
        spread = spread_mid(two[m], dup_2.at[m])
        x = 2 * m - HALO
        fine_one[x] = fine_two[x] + spread
        fine_one[x + 1] = fine_two[x + 1] + spread

    loop(HALO + 2, n - HALO - 2, lift, 6)

    def sweep_one(x):
        fine_last[x] = smoothed(fine_one[x - 1], fine_one[x], fine_one[x + 1], fine_weight[x], fine_source[x], 1.0)

    low, high = 2 * HALO + 1, nf - 2 * HALO - 1
    loop(low, high, sweep_one, 11)
    for field, first, to in ((zero, 0, kept[0]), (one, 1, kept[1]), (fine_one, 4, kept[2]), (fine_last, 5, kept[3])):
        for j in range(2):
            to[j] = field[HALO + first + j]
            to[2 + j] = field[field.shape[0] - HALO - 1 - first - j]
    copies = []
    low, high = low + 1, high - 1
    for j in range(2):
        mid = low + (high - low) // 2
        for x in range(low, mid) if j == 0 else range(mid, high):
            v = smoothed(fine_last[x - 1], fine_last[x], fine_last[x + 1], fine_weight[x], fine_source[x], 1.0)
            result[x - HALO] = v[0:32, :]
        rows = pl.ds(low - HALO, mid - low) if j == 0 else pl.ds(mid - HALO, high - mid)
        copies.append(pltpu.make_async_copy(result.at[rows], out.at[rows], sems.at[j]))
        copies[-1].start()
    for c in copies:
        c.wait()


def finish_early_kernel(error, sums, *rest):
    fields, (shifted, pay_a, pay_b, out), kept, scratch = rest[:6], rest[6:10], rest[10:14], rest[14:]
    resid = jnp.sum(sums[:, :LANES])
    load = jnp.sum(sums[:, LANES:])
    shift_c = jnp.full((16, 256), resid, F32) / jnp.full((16, 256), load, F32)
    for x in range(8):
        shifted[x] = error[x] + shift_c
    for k in range(2):
        send_x(pay_a, pay_b, k, shifted[k], shifted[6 + k])

    @pl.when(is_early())
    def _():
        finish_inner(shifted, fields, kept, out, scratch)


def finish_late_kernel(error, *rest):
    fields, kept_early, out, kept, scratch = rest[:6], rest[6:10], rest[11], rest[12:16], rest[16:]

    @pl.when(is_early())
    def _():
        for a, b in zip(kept_early, kept):
            b[...] = a[...]

    @pl.when(jnp.logical_not(is_early()))
    def _():
        finish_inner(error, fields, kept, out, scratch)


def finish_edge_kernel(
    x_a, x_b, mid_two, mid_source, mid_weight, fine_two, edge_two, fine_source, edge_source, fine_weight,
    zero, one, fine_one, fine_last, begun, out, zero_edge, one_edge, fine_edge, last_edge, dup, dup_2, result, sems,
):
    n = mid_two.shape[0]
    nf = fine_two.shape[0]
    nx = nf - 2 * HALO
    copies = []
    planes = x_sides(x_a, x_b, slice(0, 2))
    for side in (0, 1):
        sign = 1 if side == 0 else -1
        at = lambda k, side=side: HALO + k if side == 0 else n - HALO - 1 - k
        fine = lambda k, side=side: HALO + k if side == 0 else nf - HALO - 1 - k
        base = 8 * side + (0 if side == 0 else HALO - HALO - nx)
        for c in range(2):
            plane = planes[1 - side][c]
            spread = spread_coarse(plane, dup.at[2 * side + c])
            first = 2 * c if side == 0 else n - HALO + 2 * c
            for x in (first, first + 1):
                zero_edge[x] = jnp.where(mid_weight[x] > 0.0, mid_two[x] + spread, 0.0)

        def zero_of(k, side=side):
            return zero[2 * side + k] if k >= 0 else zero_edge[at(k)]

        def one_of(k, side=side):
            return one[2 * side + k - 1] if k >= 1 else one_edge[at(k)]

        for k in range(-2, 1):
            x = at(k)
            one_edge[x] = smoothed(zero_of(k - 1), zero_of(k), zero_of(k + 1), mid_weight[x], mid_source[x], 0.25)
        for k in range(-1, 2):
            x = at(k)
            value = smoothed(one_of(k - 1), one_of(k), one_of(k + 1), mid_weight[x], mid_source[x], 0.25)
            spread = spread_mid(value, dup_2.at[3 * side + k + 1])
            for f in (fine(2 * k), fine(2 * k + 1)):
                inside = HALO < f < nf - HALO - 1
                before = fine_two[f] if inside else edge_two[base + f]
                fine_edge[f] = before + spread

        def fine_of(k, side=side):
            return fine_one[2 * side + k - 4] if k >= 4 else fine_edge[fine(k)]

        def last_of(k, side=side):
            return fine_last[2 * side + k - 5] if k >= 5 else last_edge[fine(k)]

        for k in range(-1, 5):
            f = fine(k)
            source = fine_source[f] if HALO <= f < nf - HALO else edge_source[base + f]
            last_edge[f] = smoothed(fine_of(k - 1), fine_of(k), fine_of(k + 1), fine_weight[f], source, 1.0)
        for k in range(6):
            f = fine(k)
            v = smoothed(last_of(k - 1), last_of(k), last_of(k + 1), fine_weight[f], fine_source[f], 1.0)
            result[f - HALO] = v[0:32, :]
        rows = pl.ds(0, 6) if side == 0 else pl.ds(nx - 6, 6)
        copies.append(pltpu.make_async_copy(result.at[rows], out.at[rows], sems.at[side]))
        copies[-1].start()
    for c in copies:
        c.wait()


def both_ways(pairs):
    return pairs + [(j, i) for i, j in pairs]


def swap(pay_a, pay_b, axis):
    size = lax.axis_size(axis)
    pairs_a = [(i, i + 1) for i in range(1, size - 1, 2)]
    pairs_b = [(i, i + 1) for i in range(0, size - 1, 2)]
    return lax.ppermute(pay_a, axis, both_ways(pairs_a)), lax.ppermute(pay_b, axis, both_ways(pairs_b))


def exchange(value, distance):
    return lax.ppermute(value, "dev", [(i, i ^ distance) for i in range(lax.axis_size("dev"))])


def body(conc_old, phi_old, solid_pot, phase_label, iface_block, iface_owner):
    peers = lax.axis_size("dev")
    nx = conc_old.shape[0]
    half = nx // 2
    quarter = nx // 4
    ext = (nx + 2 * HALO, nx + 2 * HALO, 256)
    ext_mid = (half + 2 * HALO, half + 2 * HALO, 256)
    token_shape = shaped(8, LANES)

    pay_a, pay_b, own_lists = call(
        first_pack_kernel,
        [shaped(7 * nx, 256)] * 2 + [shaped(8, 256)],
        [conc_old, phase_label, iface_owner.reshape(1, -1), iface_block],
        [vmem(nx, HALO, 256)] * 2
        + [pltpu.VMEM((nx, HALO, 256), jnp.int32)] * 2
        + [pltpu.VMEM((1, 256), jnp.int32)] * 2
        + [vmem(7 * nx, 256)] * 2
        + [vmem(8, 256), pltpu.SemaphoreType.DMA((15,))],
        in_specs=[FAR] * 4,
        out_specs=[FAR] * 3,
        limit=VMEM_MOST,
        name="first_pack",
    )
    y_a, y_b = swap(pay_a, pay_b, "dev")
    conduct_mid, conduct_coarse, pay_a, pay_b, lists, gain, base = call(
        own_kernel,
        [shaped(half, half, 256), shaped(quarter, quarter, 256), shaped(22, 8, 256), shaped(22, 8, 256)]
        + [shaped(2, 256), shaped(nx, nx, 256), shaped(nx, nx, 256)],
        [conc_old, phase_label, phi_old, own_lists],
        [vmem(half, 2, nx, LANES), vmem(quarter, 2, half, LANES)],
        name="own",
    )
    xx_a, xx_b = swap(pay_a, pay_b, "grp")
    distance = peers // 2
    while distance > 1:
        lists = jnp.concatenate([lists, exchange(lists, distance)], axis=0)
        distance //= 2
    far_rows = second_rows(nx)[2]
    far_pay = call(
        second_pack_kernel,
        [shaped(far_rows, 256), shaped(far_rows + peers, 256)],
        [phi_old, conduct_mid, conduct_coarse, lists, xx_a, xx_b],
        name="second_pack",
    )
    yy_a, yy_b = swap(*far_pay, "dev")
    pay_a, pay_b = call(
        first_pack_x_kernel,
        [shaped(35, 8, 256)] * 2,
        [conc_old, phase_label, y_a, y_b, conduct_coarse],
        name="first_pack_x",
    )
    x_a, x_b = swap(pay_a, pay_b, "grp")

    ext_y = (nx, nx + 2 * HALO, 256)
    zero, first, second, third, gain_far, base_far, conc_inner, flux_inner = call(
        sweeps_inner_kernel,
        [shaped(*ext_y)] * 4 + [shaped(nx, 8, 256)] * 2 + [shaped(nx, nx, 256)] * 2,
        [conc_old, phase_label, phi_old, solid_pot, gain, base, y_a, y_b],
        name="sweeps_inner",
    )
    edge_args = [x_a, x_b, phase_label, phi_old, solid_pot, gain, base, zero, first, second, third]
    conc_new, flux_all, pay_a, pay_b = call(
        sweeps_edge_kernel,
        [shaped(nx, nx, 256), shaped(nx, nx, 256), shaped(3 * nx, 256), shaped(3 * nx, 256)],
        edge_args + [gain_far, base_far, conc_inner, flux_inner],
        [vmem(16, nx + 2 * HALO, 256)] * 4,
        name="sweeps_edge",
    )
    f_a, f_b = swap(pay_a, pay_b, "dev")
    flux_own, halo_mask = call(
        mask_kernel,
        [shaped(nx, nx, 256), shaped(nx, 8, 256)],
        [flux_all, lists, yy_b],
        [vmem(3, nx, 8, LANES)],
        name="mask",
    )
    weight, scale, made = call(
        ready_kernel,
        [shaped(*ext)] * 2 + [token_shape],
        [conc_old, phase_label, y_a, y_b, x_a, x_b],
        name="ready",
    )
    pay_a, pay_b = call(
        flux_pack_x_kernel, [shaped(15, 8, 256)] * 2, [flux_own, f_a, f_b, halo_mask, made], name="flux_pack_x"
    )
    fx_a, fx_b = swap(pay_a, pay_b, "grp")
    fine_two, fine_source, fine_first, inner_mid, field = call(
        potential_inner_kernel,
        [shaped(*ext)] * 3 + [shaped(half, half, 256), shaped(*ext)],
        [flux_own, halo_mask, f_a, f_b, phi_old, yy_a, yy_b, xx_a, xx_b, weight, scale],
        [vmem(nx, 8, 256), vmem(half, 2, nx, LANES)],
        name="potential_inner",
    )
    edge = (16, nx + 2 * HALO, 256)
    edge_two, edge_source, source_mid, pay_a, pay_b = call(
        potential_edge_kernel,
        [shaped(*edge), shaped(*edge), shaped(half, half, 256), shaped(4 * half, 256), shaped(4 * half, 256)],
        [fx_a, fx_b, weight, scale, field, fine_two, fine_source, fine_first, inner_mid, conduct_mid],
        [vmem(*edge), vmem(2, 2, nx, LANES)],
        name="potential_edge",
    )
    m_a, m_b = swap(pay_a, pay_b, "dev")
    concentration, flux, stored = call(
        store_kernel,
        [shaped(nx, nx, 256), shaped(nx, nx, 256), token_shape],
        [conc_new, flux_own],
        [pltpu.SemaphoreType.DMA((8,))],
        out_specs=[FAR, FAR, WHOLE],
        name="store",
    )
    wide = (quarter, 32, 256)
    rho, load, made = call(
        coarse_ready_kernel,
        [shaped(quarter, quarter, 256), shaped(8, LANES), token_shape],
        [conduct_coarse, yy_a, yy_b],
        [vmem(*wide)] * 4,
        name="coarse_ready",
    )
    pay_a, pay_b = call(
        mid_pack_x_kernel, [shaped(3 * HALO, 8, 256)] * 2, [source_mid, m_a, m_b, made, stored], name="mid_pack_x"
    )
    mx_a, mx_b = swap(pay_a, pay_b, "grp")
    mid_two, mid_source, mid_weight, source_coarse, wide_coarse, pay_a, pay_b, sums = call(
        mid_kernel,
        [shaped(*ext_mid)] * 3
        + [shaped(quarter, 12, 256), shaped(quarter, 12, 256), shaped(72, 256), shaped(80, 256), shaped(8, 256)],
        [source_mid, conduct_mid, yy_a, yy_b, xx_a, xx_b, m_a, m_b, mx_a, mx_b, rho, load],
        [vmem(*ext_mid)] * 2 + [vmem(8, 2, half + 2 * HALO, LANES)] * 2,
        name="middle",
    )
    c_a, c_b = swap(pay_a, pay_b, "dev")
    sums = sums + c_b[72:80]
    distance = 2
    while distance < peers:
        sums = sums + exchange(sums, distance)
        distance *= 2
    (error,) = call(
        coarse_kernel,
        [shaped(8, 16, 256)],
        [source_coarse, wide_coarse, yy_a, yy_b, c_a, c_b],
        [vmem(*wide)] * 4,
        name="coarse",
    )
    fields = [mid_two, mid_source, mid_weight, fine_two, fine_source, weight]
    kept = [shaped(4, half + 2 * HALO, 256)] * 2 + [shaped(4, nx + 2 * HALO, 256)] * 2
    scratch = [vmem(*ext_mid)] * 3 + [vmem(*ext)] * 2
    scratch += [vmem(8, 2, 2, 16, LANES), vmem(half + 2 * HALO, 3, 2, 16, LANES), vmem(nx, nx, 256)]
    scratch += [pltpu.SemaphoreType.DMA((2,))]
    error, pay_a, pay_b, begun, *kept_early = call(
        finish_early_kernel,
        [shaped(8, 16, 256), shaped(2, 16, 256), shaped(2, 16, 256), shaped(nx, nx, 256)] + kept,
        [error, sums] + fields,
        scratch,
        out_specs=[WHOLE] * 3 + [FAR] + [WHOLE] * 4,
        name="finish_early",
    )
    e_a, e_b = swap(pay_a, pay_b, "grp")
    begun, zero, one, fine_one, fine_last = call(
        finish_late_kernel,
        [shaped(nx, nx, 256)] + kept,
        [error] + fields + kept_early + [begun],
        scratch,
        in_specs=[WHOLE] * 11 + [FAR],
        out_specs=[FAR] + [WHOLE] * 4,
        aliases={11: 0},
        name="finish_late",
    )
    finish_args = [e_a, e_b, mid_two, mid_source, mid_weight, fine_two, edge_two, fine_source, edge_source, weight]
    finish_args += [zero, one, fine_one, fine_last, begun]
    (potential,) = call(
        finish_edge_kernel,
        [shaped(nx, nx, 256)],
        finish_args,
        [vmem(*ext_mid), vmem(*ext_mid), vmem(*ext), vmem(*ext)]
        + [vmem(4, 2, 2, 16, LANES), vmem(6, 3, 2, 16, LANES), vmem(nx, nx, 256)]
        + [pltpu.SemaphoreType.DMA((2,))],
        in_specs=[WHOLE] * (len(finish_args) - 1) + [FAR],
        out_specs=[FAR],
        aliases={len(finish_args) - 1: 0},
        name="finish_edge",
    )
    return (concentration, flux, potential)


def solution(mesh):
    brick = P("grp", "dev", None)
    return jax.shard_map(
        body,
        mesh=mesh,
        in_specs=(brick, brick, brick, brick, P("grp", "dev"), brick),
        out_specs=(brick, brick, brick),
        check_vma=False,
    )
```

```python
import jax
import jax.numpy as jnp
from jax import lax
from jax.experimental import pallas as pl
from jax.experimental.pallas import tpu as pltpu
from jax.sharding import PartitionSpec as P


F32 = jnp.float32
MASS = 0.05
OMEGA = 0.8
DIFFUSION_TABLE = (1.5, 0.1, 0.4)
RATIO_TABLE = tuple(d / (1.0 + 6.0 * d) for d in DIFFUSION_TABLE)
INVERSE_TABLE = tuple(1.0 / (1.0 + 6.0 * d) for d in DIFFUSION_TABLE)
CONDUCT_TABLE = (1.0, 0.3, 0.6)
KINETIC_TABLE = (0.2, 1.0, 0.5)
SWEEPS = 4
COARSE_SWEEPS = 8
COARSE_NEAR = 8
HALO = 4
LANES = 128
VMEM_LIMIT = 28 * 1024 * 1024
VMEM_MOST = 58 * 1024 * 1024


def shaped(*shape):
    return jax.ShapeDtypeStruct(shape, F32)


WHOLE = pl.BlockSpec(memory_space=pltpu.VMEM)
FAR = pl.BlockSpec(memory_space=pltpu.HBM)


def call(kernel, outs, args, scratch=(), in_specs=None, out_specs=None, limit=VMEM_LIMIT, aliases=None, flops=10**6, name=None):
    size = sum(4 * a.size for a in args) + sum(4 * o.size for o in outs)
    return pl.pallas_call(
        kernel,
        out_shape=tuple(outs),
        in_specs=in_specs or [WHOLE] * len(args),
        out_specs=tuple(out_specs or [WHOLE] * len(outs)),
        scratch_shapes=list(scratch),
        input_output_aliases=aliases or {},
        compiler_params=pltpu.CompilerParams(vmem_limit_bytes=limit),
        cost_estimate=pl.CostEstimate(flops=flops, bytes_accessed=size, transcendentals=0),
        name=name,
    )(*args)


def vmem(*shape):
    return pltpu.VMEM(shape, F32)


def iota(shape, dim):
    return lax.broadcasted_iota(jnp.int32, shape, dim)


def pick(label, table):
    return jnp.where(label == 0, table[0], jnp.where(label == 1, table[1], table[2])).astype(F32)


def loop(low, high, body, unroll=8):
    steps = (high - low) // unroll

    def step(i, carry):
        for u in range(unroll):
            body(low + i * unroll + u)
        return carry

    if steps > 1:
        lax.fori_loop(0, steps, step, 0)
    else:
        steps = 0
    for x in range(low + steps * unroll, high):
        body(x)


def odd(axis):
    return lax.rem(lax.axis_index(axis), 2) == 1


def along_y(v):
    return pltpu.roll(v, 1, 0) + pltpu.roll(v, v.shape[0] - 1, 0)


def along_z(v):
    low, high = v[:, :LANES], v[:, LANES:]
    lane = iota(low.shape, 1)
    first, last = lane == 0, lane == LANES - 1
    low_up, high_up = pltpu.roll(low, 1, 1), pltpu.roll(high, 1, 1)
    low_down, high_down = pltpu.roll(low, LANES - 1, 1), pltpu.roll(high, LANES - 1, 1)
    low_sum = jnp.where(first, 0.0, low_up) + jnp.where(last, high_down, low_down)
    high_sum = jnp.where(first, low_up, high_up) + jnp.where(last, 0.0, high_down)
    return jnp.concatenate([low_sum, high_sum], axis=1)


def upper(shape=(8, 256)):
    return iota(shape, 0) < HALO


def twice(tile, scratch):
    for h in range(2):
        part = tile[:, h * LANES : (h + 1) * LANES]
        scratch[h, pl.ds(0, 8, stride=2), :] = part
        scratch[h, pl.ds(1, 8, stride=2), :] = part
    return jnp.concatenate([scratch[0], scratch[1]], axis=1)


def pair_rows(v, scratch):
    half = v.shape[0] // 2
    parts = []
    for h in range(2):
        scratch[h] = v[:, h * LANES : (h + 1) * LANES]
        parts.append(scratch[h, pl.ds(0, half, stride=2), :] + scratch[h, pl.ds(1, half, stride=2), :])
    return jnp.concatenate(parts, axis=1)


def either(flag, if_true, if_false):
    return jnp.where(flag, if_true, if_false)


def y_sides(r_a, r_b, at, count):
    flag = odd("dev")
    a, b = r_a[at : at + count, :], r_b[at : at + count, :]
    return either(flag, a, b), either(flag, b, a)


def x_sides(r_a, r_b, index):
    flag = odd("grp")
    a, b = r_a[index], r_b[index]
    return either(flag, a, b), either(flag, b, a)


def send_y(pay_a, pay_b, at, first, last):
    flag = odd("dev")
    n = first.shape[0]
    pay_a[at : at + n, :] = either(flag, last, first)
    pay_b[at : at + n, :] = either(flag, first, last)


def send_x(pay_a, pay_b, index, first, last):
    flag = odd("grp")
    pay_a[index] = either(flag, last, first)
    pay_b[index] = either(flag, first, last)


def halo_tile(after, before):
    parts = [after]
    if after.shape[0] < HALO:
        parts.append(jnp.zeros((2 * HALO - 2 * after.shape[0], after.shape[1]), F32))
    return jnp.concatenate(parts + [before], axis=0)


def first_pack_kernel(
    conc, label, owner, block, out_a, out_b, own_lists,
    c_first, c_last, l_first, l_last, own_owner, own_block, pay_a, pay_b, named, sems,
):
    nx = conc.shape[0]
    half = nx // 2
    lists = [pltpu.make_async_copy(owner, own_owner, sems.at[8]), pltpu.make_async_copy(block, own_block, sems.at[9])]
    reads = []
    for j in range(2):
        planes = pl.ds(half * j, half)
        for i, (ref, at, to) in enumerate(
            ((conc, 0, c_first), (conc, 28, c_last), (label, 0, l_first), (label, 28, l_last))
        ):
            reads.append(pltpu.make_async_copy(ref.at[planes, pl.ds(at, 4), :], to.at[planes], sems.at[4 * j + i]))
    for c in reads + lists:
        c.start()
    writes = []
    for j in range(2):
        for c in reads[4 * j : 4 * j + 4]:
            c.wait()
        for x in range(half * j, half * j + half):
            send_y(pay_a, pay_b, 7 * x, c_first[x], c_last[x])
            send_y(pay_a, pay_b, 7 * x + 4, l_first[x, 0:3, :].astype(F32), l_last[x, 1:4, :].astype(F32))
        rows = pl.ds(7 * half * j, 7 * half)
        for i, (pay, out) in enumerate(((pay_a, out_a), (pay_b, out_b))):
            writes.append(pltpu.make_async_copy(pay.at[rows], out.at[rows], sems.at[10 + 2 * j + i]))
            writes[-1].start()
    for c in lists:
        c.wait()
    named[...] = jnp.concatenate([own_owner[...], own_block[...], jnp.zeros((6, 256), jnp.int32)], axis=0).astype(F32)
    writes.append(pltpu.make_async_copy(named, own_lists, sems.at[14]))
    writes[-1].start()
    for c in writes:
        c.wait()


def own_kernel(conc, label, phi, named, mid, coarse, pay_a, pay_b, lists, gain, base, pairs, pairs_2):
    nx = conc.shape[0]
    half = nx // 2
    lists[...] = named[0:2, :]

    def coefficients(i):
        gain[i] = pick(label[i], RATIO_TABLE)
        base[i] = conc[i] * pick(label[i], INVERSE_TABLE)

    loop(0, nx, coefficients, 4)

    def coarsen(i):
        total = conc[2 * i] * pick(label[2 * i], CONDUCT_TABLE) + conc[2 * i + 1] * pick(label[2 * i + 1], CONDUCT_TABLE)
        mid[i] = 0.25 * pair_rows(total, pairs.at[i])

    loop(0, half, coarsen, 4)
    for i in range(half // 2):
        coarse[i] = 0.25 * pair_rows(mid[2 * i] + mid[2 * i + 1], pairs_2.at[i])
    for k in range(HALO):
        for t in range(4):
            rows = slice(8 * t, 8 * t + 8)
            send_x(pay_a, pay_b, 4 * k + t, phi[k, rows, :], phi[nx - HALO + k, rows, :])
    for k in range(MID_HALO):
        for t in range(2):
            rows = slice(8 * t, 8 * t + 8)
            send_x(pay_a, pay_b, 16 + 2 * k + t, mid[k, rows, :], mid[half - MID_HALO + k, rows, :])


def first_pack_x_kernel(conc, label, r_a, r_b, token, pay_a, pay_b):
    nx = conc.shape[0]

    def plane(ref, k, t, offset, count):
        if t < 4:
            return ref[k, 8 * t : 8 * t + 8, :].astype(F32)
        return halo_tile(*y_sides(r_a, r_b, 7 * k + offset, count))

    for t in range(5):
        for k in range(HALO):
            send_x(pay_a, pay_b, 5 * k + t, plane(conc, k, t, 0, 4), plane(conc, nx - HALO + k, t, 0, 4))
        for k in range(3):
            send_x(pay_a, pay_b, 20 + 5 * k + t, plane(label, k, t, 4, 3), plane(label, nx - 3 + k, t, 4, 3))


MID_HALO = 3


def corner_rows(n, width, reach):
    counts = [min(width, k + reach) for k in range(width)]
    counts = counts + [width] * n + counts[::-1]
    return counts, [sum(counts[:i]) for i in range(len(counts))]


def second_rows(nx):
    phi = sum(corner_rows(nx, HALO, 0)[0])
    mid = sum(corner_rows(nx // 2, MID_HALO, 1)[0])
    return phi, phi + mid, phi + mid + 64


def second_pack_kernel(phi, mid, coarse, lists, x_a, x_b, pay_a, pay_b):
    nx = phi.shape[0]
    starts = second_rows(nx)

    def put(own, width, reach, index, base):
        n = own.shape[0]
        counts, at = corner_rows(n, width, reach)
        tiles = own.shape[1] // 8
        for x in range(n):
            send_y(pay_a, pay_b, base + at[width + x], own[x, 0:width, :], own[x, 8 * tiles - width : 8 * tiles, :])
        for k in range(width):
            first_after, first_before = x_sides(x_a, x_b, index + tiles * k)
            last_after, last_before = x_sides(x_a, x_b, index + tiles * k + tiles - 1)
            for x, first, last in ((k, first_before, last_before), (width + n + k, first_after, last_after)):
                if counts[x]:
                    send_y(pay_a, pay_b, base + at[x], first[0 : counts[x]], last[8 - counts[x] : 8])

    put(phi, HALO, 0, 0, 0)
    put(mid, MID_HALO, 1, 16, starts[0])
    base = starts[1]
    for x in range(8):
        pay_a[base + 8 * x : base + 8 * x + 8, :] = coarse[x]
        pay_b[base + 8 * x : base + 8 * x + 8, :] = coarse[x]
    base = starts[2]
    pay_b[base : base + lists.shape[0], :] = lists[...]


def second_halo(r_a, r_b, n, width, reach, x, base):
    counts, at = corner_rows(n, width, reach)
    x = x - HALO + width
    if x < 0 or x >= len(counts) or not counts[x]:
        return jnp.zeros((8, 256), F32)
    return halo_tile(*y_sides(r_a, r_b, base + at[x], counts[x]))


def wide_rows(own, after_own, before_own, after, before):
    gap = jnp.zeros((6, 256), F32)
    return jnp.concatenate([own, after_own, after, gap, before, before_own], axis=0)


def flux_plane(c, solid, phi, label):
    drive = 0.5 * (solid - phi)
    logc = jnp.log(c)
    return pick(label, KINETIC_TABLE) * (jnp.exp(drive + 0.4 * logc) - jnp.exp(0.6 * logc - drive))


def around_plane(before, v, after):
    return (before + after) + (along_y(v) + along_z(v))


def sweeps_inner_kernel(
    conc, label, phi, solid, gain, base, y_a, y_b, zero, first, second, third, gain_far, base_far, out, flux
):
    nx = conc.shape[0]

    def own(i):
        zero[i, 0:32, :] = conc[i]

    loop(0, nx, own)
    for i in range(nx):
        c = halo_tile(*y_sides(y_a, y_b, 7 * i, 4))
        lab = halo_tile(*y_sides(y_a, y_b, 7 * i + 4, 3))
        zero[i, 32:40, :] = c
        gain_far[i] = jnp.where(c > 0.0, pick(lab, RATIO_TABLE), 0.0)
        base_far[i] = c * pick(lab, INVERSE_TABLE)
    fields = (zero, first, second, third)
    for s in range(1, SWEEPS):
        old, new = fields[s - 1], fields[s]

        def sweep(i, old=old, new=new):
            g = jnp.concatenate([gain[i], gain_far[i]], axis=0)
            b = jnp.concatenate([base[i], base_far[i]], axis=0)
            new[i] = b + g * around_plane(old[i - 1], old[i], old[i + 1])

        loop(s, nx - s, sweep)

    def last(i):
        c = base[i] + gain[i] * around_plane(third[i - 1], third[i], third[i + 1])[0:32, :]
        out[i] = c
        flux[i] = flux_plane(c, solid[i], phi[i], label[i])

    loop(SWEEPS, nx - SWEEPS, last, 4)


def sweeps_edge_kernel(
    x_a, x_b, label, phi, solid, gain, base, zero, first, second, third, gain_far, base_far, out_inner, flux_inner,
    out, flux, pay_a, pay_b, zero_x, first_x, second_x, third_x,
):
    nx = out.shape[0]
    inner = (zero, first, second, third)
    edge = (zero_x, first_x, second_x, third_x)

    def copy(i):
        out[i] = out_inner[i]
        flux[i] = flux_inner[i]

    loop(SWEEPS, nx - SWEEPS, copy)
    for side in range(2):
        plane = lambda k, side=side: k if side == 0 else nx - 1 - k
        row = lambda k, side=side: 8 * side + HALO + k
        far = lambda k, index, side=side: x_sides(x_a, x_b, index)[1 - side]
        gains, bases = {}, {}
        for j in range(1, HALO + 1):
            k = HALO - j if side == 0 else j - 1
            zero_x[row(-j)] = jnp.concatenate([far(k, 5 * k + t) for t in range(5)], axis=0)
            if j < HALO:
                k = HALO - 1 - j if side == 0 else j - 1
                lab = jnp.concatenate([far(k, 20 + 5 * k + t) for t in range(5)], axis=0)
                c = zero_x[row(-j)]
                gains[-j] = jnp.where(c > 0.0, pick(lab, RATIO_TABLE), 0.0)
                bases[-j] = c * pick(lab, INVERSE_TABLE)
        for k in range(SWEEPS):
            gains[k] = jnp.concatenate([gain[plane(k)], gain_far[plane(k)]], axis=0)
            bases[k] = jnp.concatenate([base[plane(k)], base_far[plane(k)]], axis=0)
        for s in range(1, SWEEPS + 1):

            def old(k, s=s):
                return inner[s - 1][plane(k)] if k >= s - 1 else edge[s - 1][row(k)]

            for k in range(s - SWEEPS, s):
                c = bases[k] + gains[k] * around_plane(old(k - 1), old(k), old(k + 1))
                if s < SWEEPS:
                    edge[s][row(k)] = c
                else:
                    c = c[0:32, :]
                    out[plane(k)] = c
                    flux[plane(k)] = flux_plane(c, solid[plane(k)], phi[plane(k)], label[plane(k)])
    for x in range(nx):
        send_y(pay_a, pay_b, 3 * x, flux[x, 0:3, :], flux[x, 29:32, :])


def mask_kernel(flux_all, lists, far, flux, halo_mask, marked):
    nx = flux_all.shape[0]
    rows = lists.shape[0]
    pieces = [lists[i : i + 1, :] for i in range(rows)] + [far[i : i + 1, :] for i in range(far.shape[0] - rows, far.shape[0])]
    owner = jnp.concatenate(pieces[0::2], axis=1).astype(jnp.int32)
    block = jnp.concatenate(pieces[1::2], axis=1).astype(jnp.int32)
    entries = owner.shape[1]
    hit_column = (iota((64, entries), 0) == lax.rem(block, 64)).astype(jnp.bfloat16)
    reach = owner - lax.axis_index("dev") + 1
    at_row = jnp.where((reach >= 0) & (reach < 3), reach * nx + lax.shift_right_arithmetic(block, 6), -1)
    hit_row = (iota((3 * nx, entries), 0) == at_row).astype(jnp.bfloat16)
    named = lax.dot_general(hit_row, hit_column, (((1,), (1,)), ((), ())), preferred_element_type=F32)
    named = jnp.concatenate([named, jnp.zeros((3 * nx, LANES - 64), F32)], axis=1)
    for j in range(3):
        for i in range(nx):
            marked[j, i] = jnp.broadcast_to(named[j * nx + i : j * nx + i + 1, :], (8, LANES))
    is_row = lax.div(iota((32, LANES), 1), 2) == iota((32, LANES), 0)
    row, pair = iota((8, LANES), 0), lax.div(iota((8, LANES), 1), 2)
    is_after = (row < 3) & (pair == row)
    is_before = (row >= 5) & (pair == row + 24)
    spread = (lax.rem(iota((LANES, 256), 0), 2) == lax.div(iota((LANES, 256), 1), LANES)).astype(jnp.bfloat16)

    def plane(i):
        marks = jnp.where(is_row, jnp.concatenate([marked[1, i]] * 4, axis=0), 0.0)
        beyond = jnp.where(is_after, marked[2, i], jnp.where(is_before, marked[0, i], 0.0))
        marks = jnp.concatenate([marks, beyond], axis=0).astype(jnp.bfloat16)
        listed = jnp.dot(marks, spread, preferred_element_type=F32) > 0.5
        flux[i] = jnp.where(listed[0:32], flux_all[i], 0.0)
        halo_mask[i] = jnp.where(listed[32:40], 1.0, 0.0)

    loop(0, nx, plane, 16)


def store_kernel(conc, flux, conc_out, flux_out, token, sems):
    copies = []
    for i, (ref, to) in enumerate(((conc, conc_out), (flux, flux_out))):
        for j in range(4):
            rows = pl.ds(8 * j, 8)
            copies.append(pltpu.make_async_copy(ref.at[rows], to.at[rows], sems.at[4 * i + j]))
            copies[-1].start()
    token[...] = jnp.zeros(token.shape, F32)
    for c in copies:
        c.wait()


def ready_kernel(conc, label, y_a, y_b, x_a, x_b, weight, scale, token):
    nx = conc.shape[0]
    token[...] = jnp.zeros(token.shape, F32)

    def put(x, rows, c, lab):
        conduct = c * pick(lab, CONDUCT_TABLE)
        factor = OMEGA / (MASS + 6.0 * conduct)
        weight[x, rows, :] = conduct * factor
        scale[x, rows, :] = factor

    def own(i):
        put(HALO + i, slice(0, 32), conc[i], label[i])

    loop(0, nx, own, 4)
    for i in range(nx):
        c = halo_tile(*y_sides(y_a, y_b, 7 * i, 4))
        lab = halo_tile(*y_sides(y_a, y_b, 7 * i + 4, 3))
        put(HALO + i, slice(32, 40), c, lab)
    for t in range(5):
        rows = slice(8 * t, 8 * t + 8)
        for k in range(HALO):
            c_after, c_before = x_sides(x_a, x_b, 5 * k + t)
            l_after = x_sides(x_a, x_b, 20 + 5 * min(k, 2) + t)[0]
            l_before = x_sides(x_a, x_b, 20 + 5 * max(k - 1, 0) + t)[1]
            put(k, rows, c_before, l_before)
            put(HALO + nx + k, rows, c_after, l_after)


def place_phi(phi, yy_a, yy_b, xx_a, xx_b, field):
    nx = phi.shape[0]

    def own(i):
        field[HALO + i, 0:32, :] = phi[i]

    loop(0, nx, own)
    for x in range(nx + 2 * HALO):
        field[x, 32:40, :] = second_halo(yy_a, yy_b, nx, HALO, 0, x, 0)
    for t in range(4):
        for k in range(HALO):
            after, before = x_sides(xx_a, xx_b, 4 * k + t)
            field[k, 8 * t : 8 * t + 8, :] = before
            field[HALO + nx + k, 8 * t : 8 * t + 8, :] = after


def flux_pack_x_kernel(flux, r_b, r_a, mask, token, pay_a, pay_b):
    nx = flux.shape[0]

    def tile(x, t):
        if t < 4:
            return flux[x, 8 * t : 8 * t + 8, :]
        return mask[x] * halo_tile(*y_sides(r_a, r_b, 3 * x, 3))

    for k in range(3):
        for t in range(5):
            send_x(pay_a, pay_b, 5 * k + t, tile(k, t), tile(nx - 3 + k, t))


def first_sweep(field, weight, scale, x, rows, flux):
    p = field[x]
    near = (field[x - 1] + field[x + 1]) + (along_y(p) + along_z(p))
    b = scale[x, rows, :] * (MASS * p[rows, :] + flux)
    return b, 0.2 * p[rows, :] + weight[x, rows, :] * near[rows, :] + b


def potential_inner_kernel(
    flux, mask, y_a, y_b, phi, yy_a, yy_b, xx_a, xx_b, weight, scale, after_two, source, first, source_mid, field, far, pairs
):
    nx = flux.shape[0]
    place_phi(phi, yy_a, yy_b, xx_a, xx_b, field)
    for i in range(nx):
        far[i] = mask[i] * halo_tile(*y_sides(y_a, y_b, 3 * i, 3))

    def own(i):
        x = HALO + i
        f = jnp.concatenate([flux[i], far[i]], axis=0)
        source[x], first[x] = first_sweep(field, weight, scale, x, slice(0, 40), f)

    loop(0, nx, own)

    def around(values, x):
        v = values[x]
        return v, weight[x] * ((values[x - 1] + values[x + 1]) + (along_y(v) + along_z(v)))

    def sweep(x):
        v, near = around(first, x)
        after_two[x] = 0.2 * v + (source[x] + near)

    loop(HALO + 1, HALO + nx - 1, sweep)

    def remainder(x):
        v, near = around(after_two, x)
        return ((source[x] - OMEGA * v) + near)[0:32, :] / scale[x, 0:32, :]

    def coarsen(i):
        x = HALO + 2 * i
        source_mid[i] = 0.25 * pair_rows(remainder(x) + remainder(x + 1), pairs.at[i])

    loop(1, nx // 2 - 1, coarsen, 4)


def mid_factor(conduct):
    return OMEGA / (MASS + 3.0 * conduct)


def potential_edge_kernel(
    x_a, x_b, weight, scale, field, inner_two, inner_source, inner_first, inner_mid, conduct_mid,
    edge_two, edge_source, source_mid, pay_a, pay_b, first, pairs,
):
    half = source_mid.shape[0]
    nx = 2 * half
    for side, face in ((0, HALO), (1, HALO + nx)):
        base = 8 * side + HALO - face
        for k in range(3):
            x = face - 3 + k if side == 0 else face + k
            f = jnp.concatenate([x_sides(x_a, x_b, 5 * k + t)[1 - side] for t in range(5)], axis=0)
            edge_source[base + x], first[base + x] = first_sweep(field, weight, scale, x, slice(0, 40), f)

        def first_of(x, base=base):
            return inner_first[x] if HALO <= x < HALO + nx else first[base + x]

        def source_of(x, base=base):
            return inner_source[x] if HALO <= x < HALO + nx else edge_source[base + x]

        def two_of(x, base=base):
            return inner_two[x] if HALO < x < HALO + nx - 1 else edge_two[base + x]

        for x in range(face - 2, face + 1) if side == 0 else range(face - 1, face + 2):
            v = first_of(x)
            near = weight[x] * ((first_of(x - 1) + first_of(x + 1)) + (along_y(v) + along_z(v)))
            edge_two[base + x] = 0.2 * v + (source_of(x) + near)
        total = 0.0
        at = face if side == 0 else face - 2
        for x in (at, at + 1):
            v = two_of(x)
            near = weight[x] * ((two_of(x - 1) + two_of(x + 1)) + (along_y(v) + along_z(v)))
            total = total + ((source_of(x) - OMEGA * v) + near)[0:32, :] / scale[x, 0:32, :]
        at = 0 if side == 0 else half - 1
        source_mid[at] = mid_factor(conduct_mid[at]) * (0.25 * pair_rows(total, pairs.at[side]))
    for x in range(1, half - 1):
        source_mid[x] = mid_factor(conduct_mid[x]) * inner_mid[x]
    for x in range(half):
        send_y(pay_a, pay_b, 4 * x, source_mid[x, 0:4, :], source_mid[x, 12:16, :])


def mid_pack_x_kernel(field, r_a, r_b, token, token_2, pay_a, pay_b):
    n = field.shape[0]

    def tile(x, t):
        if t < 2:
            return field[x, 8 * t : 8 * t + 8, :]
        return halo_tile(*y_sides(r_a, r_b, 4 * x, 4))

    for k in range(HALO):
        for t in range(3):
            send_x(pay_a, pay_b, 3 * k + t, tile(k, t), tile(n - HALO + k, t))


def mid_kernel(
    source_own, conduct_own, yy_a, yy_b, xx_a, xx_b, y_a, y_b, x_a, x_b, rho, load,
    after_two, source, weight, coarse, conduct, pay_a, pay_b, part, scale, mid_conduct, pairs, pairs_2,
):
    n = source_own.shape[0]
    base = second_rows(2 * n)[0]

    def put(x, rows, b, k):
        factor = mid_factor(k)
        weight[x, rows, :] = k * factor
        scale[x, rows, :] = factor
        source[x, rows, :] = b
        mid_conduct[x, rows, :] = k

    def far(x):
        return second_halo(yy_a, yy_b, n, MID_HALO, 1, x, base)

    for i in range(n):
        put(HALO + i, slice(0, 16), source_own[i], conduct_own[i])
        put(HALO + i, slice(16, 24), halo_tile(*y_sides(y_a, y_b, 4 * i, 4)), far(HALO + i))
    for k in range(HALO):
        for t in range(3):
            rows = slice(8 * t, 8 * t + 8)
            b_after, b_before = x_sides(x_a, x_b, 3 * k + t)
            if t < 2:
                none = jnp.zeros((8, 256), F32)
                c_before = x_sides(xx_a, xx_b, 16 + 2 * (k - 1) + t)[1] if k > 0 else none
                c_after = x_sides(xx_a, xx_b, 16 + 2 * k + t)[0] if k < MID_HALO else none
            else:
                c_after, c_before = far(HALO + n + k), far(k)
            put(k, rows, b_before, c_before)
            put(HALO + n + k, rows, b_after, c_after)

    def around(values, x):
        v = values[x]
        return v, weight[x] * (0.25 * ((values[x - 1] + values[x + 1]) + along_y(v)) + along_z(v))

    def sweep(x):
        v, near = around(source, x)
        after_two[x] = 0.2 * v + (source[x] + near)

    loop(1, n + 2 * HALO - 1, sweep, 11)

    def remainder(x):
        v, near = around(after_two, x)
        return ((source[x] - OMEGA * v) + near) / scale[x]

    total = jnp.zeros((8, 256), F32)
    for i in range(n // 2):
        x = HALO + 2 * i
        value = 0.25 * pair_rows(remainder(x) + remainder(x + 1), pairs.at[i])
        k = 0.25 * pair_rows(mid_conduct[x] + mid_conduct[x + 1], pairs_2.at[i])
        coarse[i] = value
        conduct[i] = k
        send_y(pay_a, pay_b, 9 * i, value[1:9], jnp.concatenate([value[11:12], value[0:7]], axis=0))
        send_y(pay_a, pay_b, 9 * i + 8, k[8:9], k[11:12])
        total += rho[i] * value[0:8]
    sums = jnp.concatenate([total[:, :LANES] + total[:, LANES:], load[...]], axis=1)
    pay_b[72:80, :] = sums
    part[...] = sums


COARSE_W = 0.0625


def coarse_ready_kernel(own, r_a, r_b, rho, load, token, one, two, conduct, scale):
    token[...] = jnp.zeros(token.shape, F32)
    base = r_a.shape[0] - 64
    for x in range(8):
        after, before = y_sides(r_a, r_b, base + 8 * x, 8)
        k = jnp.concatenate([own[x], after, jnp.zeros((8, 256), F32), before], axis=0)
        conduct[x] = k
        scale[x] = OMEGA / (MASS + 2.25 * k)
        one[x] = jnp.ones(k.shape, F32)
    fields = (one, two)
    for s in range(COARSE_SWEEPS):
        old, new = fields[s % 2], fields[(s + 1) % 2]
        for x in range(8):
            near = [conduct[i] * old[i] if 0 <= i < 8 else None for i in (x - 1, x, x + 1)]
            inner = along_y(near[1])
            for other in (near[0], near[2]):
                if other is not None:
                    inner = inner + other
            new[x] = 0.2 * old[x] + scale[x] * (COARSE_W * inner + along_z(near[1]))
    last = fields[COARSE_SWEEPS % 2]
    peer, peers = lax.axis_index("dev"), lax.axis_size("dev")
    row, z = iota((8, 256), 0), iota((8, 256), 1)
    edge_y = ((row == 0) & (peer == 0)) | ((row == 7) & (peer == peers - 1))
    edge = edge_y.astype(F32) * COARSE_W + ((z == 0) | (z == 255)).astype(F32)
    total = jnp.zeros((8, 256), F32)
    for x in range(8):
        rho[x] = last[x, 0:8, :]
        total += MASS + own[x] * (edge + (COARSE_W if x in (0, 7) else 0.0))
    load[...] = total[:, :LANES] + total[:, LANES:]


def coarse_kernel(own, conduct, far_a, far_b, r_a, r_b, error, source, weight, one, two):
    base = far_a.shape[0] - 64
    for x in range(8):
        after, before = y_sides(r_a, r_b, 9 * x, 8)
        b = wide_rows(own[x, 0:8, :], own[x, 8:9, :], own[x, 11:12, :], after, before)
        last_after, last_before = y_sides(r_a, r_b, 9 * x + 8, 1)
        after, before = y_sides(far_a, far_b, base + 8 * x, 8)
        after = jnp.concatenate([after[1:8], last_after], axis=0)
        before = jnp.concatenate([last_before, before[0:7]], axis=0)
        k = wide_rows(conduct[x, 0:8, :], conduct[x, 8:9, :], conduct[x, 11:12, :], after, before)
        factor = OMEGA / (MASS + 2.25 * k)
        weight[x] = k * factor
        source[x] = factor * b
    old = source
    for s in range(1, COARSE_SWEEPS):
        new = one if s % 2 else two
        for x in range(8):
            v = old[x]
            inner = along_y(v)
            if x > 0:
                inner = inner + old[x - 1]
            if x < 7:
                inner = inner + old[x + 1]
            new[x] = 0.2 * v + (source[x] + weight[x] * (COARSE_W * inner + along_z(v)))
        old = new
    for x in range(8):
        error[x, 0:8, :] = old[x, 0:8, :]
        error[x, 8:16, :] = jnp.where(upper(), old[x, 8:16, :], old[x, 24:32, :])


def squeeze(tile):
    return jnp.where(iota((8, 256), 0) < 2, tile, pltpu.roll(tile, 4, 0))


def spread_coarse(plane, room):
    return jnp.concatenate([twice(plane[0:8], room.at[0]), twice(squeeze(plane[8:16]), room.at[1])[0:8]], axis=0)


def spread_mid(plane, room):
    parts = [twice(plane[0:8], room.at[0]), twice(plane[8:16], room.at[1]), twice(squeeze(plane[16:24]), room.at[2])[0:8]]
    return jnp.concatenate(parts, axis=0)


def smoothed(before, v, after, weight, source, w):
    inner = (before + after) + along_y(v)
    return source + (0.2 * v + weight * (w * inner + along_z(v)))


def is_early():
    return (lax.axis_index("grp") < lax.axis_size("grp") // 2) | odd("grp")


def finish_inner(error, fields, kept, out, scratch):
    mid_two, mid_source, mid_weight, fine_two, fine_source, fine_weight = fields
    zero, one, two, fine_one, fine_last, dup, dup_2, result, sems = scratch
    n = mid_two.shape[0]
    nf = fine_two.shape[0]
    for c in range(8):
        spread = spread_coarse(error[c], dup.at[c])
        for x in (2 * c + HALO, 2 * c + 1 + HALO):
            zero[x] = jnp.where(mid_weight[x] > 0.0, mid_two[x] + spread, 0.0)

    def sweep_mid(x, old, new):
        new[x] = smoothed(old[x - 1], old[x], old[x + 1], mid_weight[x], mid_source[x], 0.25)

    for x in range(HALO + 1, n - HALO - 1):
        sweep_mid(x, zero, one)
    for x in range(HALO + 2, n - HALO - 2):
        sweep_mid(x, one, two)

    def lift(m):
        spread = spread_mid(two[m], dup_2.at[m])
        x = 2 * m - HALO
        fine_one[x] = fine_two[x] + spread
        fine_one[x + 1] = fine_two[x + 1] + spread

    loop(HALO + 2, n - HALO - 2, lift, 6)

    def sweep_one(x):
        fine_last[x] = smoothed(fine_one[x - 1], fine_one[x], fine_one[x + 1], fine_weight[x], fine_source[x], 1.0)

    low, high = 2 * HALO + 1, nf - 2 * HALO - 1
    loop(low, high, sweep_one, 11)
    for field, first, to in ((zero, 0, kept[0]), (one, 1, kept[1]), (fine_one, 4, kept[2]), (fine_last, 5, kept[3])):
        for j in range(2):
            to[j] = field[HALO + first + j]
            to[2 + j] = field[field.shape[0] - HALO - 1 - first - j]
    copies = []
    low, high = low + 1, high - 1
    for j in range(2):
        mid = low + (high - low) // 2
        for x in range(low, mid) if j == 0 else range(mid, high):
            v = smoothed(fine_last[x - 1], fine_last[x], fine_last[x + 1], fine_weight[x], fine_source[x], 1.0)
            result[x - HALO] = v[0:32, :]
        rows = pl.ds(low - HALO, mid - low) if j == 0 else pl.ds(mid - HALO, high - mid)
        copies.append(pltpu.make_async_copy(result.at[rows], out.at[rows], sems.at[j]))
        copies[-1].start()
    for c in copies:
        c.wait()


def finish_early_kernel(error, sums, *rest):
    fields, (shifted, pay_a, pay_b, out), kept, scratch = rest[:6], rest[6:10], rest[10:14], rest[14:]
    resid = jnp.sum(sums[:, :LANES])
    load = jnp.sum(sums[:, LANES:])
    shift_c = jnp.full((16, 256), resid, F32) / jnp.full((16, 256), load, F32)
    for x in range(8):
        shifted[x] = error[x] + shift_c
    for k in range(2):
        send_x(pay_a, pay_b, k, shifted[k], shifted[6 + k])

    @pl.when(is_early())
    def _():
        finish_inner(shifted, fields, kept, out, scratch)


def finish_late_kernel(error, *rest):
    fields, kept_early, out, kept, scratch = rest[:6], rest[6:10], rest[11], rest[12:16], rest[16:]

    @pl.when(is_early())
    def _():
        for a, b in zip(kept_early, kept):
            b[...] = a[...]

    @pl.when(jnp.logical_not(is_early()))
    def _():
        finish_inner(error, fields, kept, out, scratch)


def finish_edge_kernel(
    x_a, x_b, mid_two, mid_source, mid_weight, fine_two, edge_two, fine_source, edge_source, fine_weight,
    zero, one, fine_one, fine_last, begun, out, zero_edge, one_edge, fine_edge, last_edge, dup, dup_2, result, sems,
):
    n = mid_two.shape[0]
    nf = fine_two.shape[0]
    nx = nf - 2 * HALO
    copies = []
    planes = x_sides(x_a, x_b, slice(0, 2))
    for side in (0, 1):
        sign = 1 if side == 0 else -1
        at = lambda k, side=side: HALO + k if side == 0 else n - HALO - 1 - k
        fine = lambda k, side=side: HALO + k if side == 0 else nf - HALO - 1 - k
        base = 8 * side + (0 if side == 0 else HALO - HALO - nx)
        for c in range(2):
            plane = planes[1 - side][c]
            spread = spread_coarse(plane, dup.at[2 * side + c])
            first = 2 * c if side == 0 else n - HALO + 2 * c
            for x in (first, first + 1):
                zero_edge[x] = jnp.where(mid_weight[x] > 0.0, mid_two[x] + spread, 0.0)

        def zero_of(k, side=side):
            return zero[2 * side + k] if k >= 0 else zero_edge[at(k)]

        def one_of(k, side=side):
            return one[2 * side + k - 1] if k >= 1 else one_edge[at(k)]

        for k in range(-2, 1):
            x = at(k)
            one_edge[x] = smoothed(zero_of(k - 1), zero_of(k), zero_of(k + 1), mid_weight[x], mid_source[x], 0.25)
        for k in range(-1, 2):
            x = at(k)
            value = smoothed(one_of(k - 1), one_of(k), one_of(k + 1), mid_weight[x], mid_source[x], 0.25)
            spread = spread_mid(value, dup_2.at[3 * side + k + 1])
            for f in (fine(2 * k), fine(2 * k + 1)):
                inside = HALO < f < nf - HALO - 1
                before = fine_two[f] if inside else edge_two[base + f]
                fine_edge[f] = before + spread

        def fine_of(k, side=side):
            return fine_one[2 * side + k - 4] if k >= 4 else fine_edge[fine(k)]

        def last_of(k, side=side):
            return fine_last[2 * side + k - 5] if k >= 5 else last_edge[fine(k)]

        for k in range(-1, 5):
            f = fine(k)
            source = fine_source[f] if HALO <= f < nf - HALO else edge_source[base + f]
            last_edge[f] = smoothed(fine_of(k - 1), fine_of(k), fine_of(k + 1), fine_weight[f], source, 1.0)
        for k in range(6):
            f = fine(k)
            v = smoothed(last_of(k - 1), last_of(k), last_of(k + 1), fine_weight[f], fine_source[f], 1.0)
            result[f - HALO] = v[0:32, :]
        rows = pl.ds(0, 6) if side == 0 else pl.ds(nx - 6, 6)
        copies.append(pltpu.make_async_copy(result.at[rows], out.at[rows], sems.at[side]))
        copies[-1].start()
    for c in copies:
        c.wait()


def both_ways(pairs):
    return pairs + [(j, i) for i, j in pairs]


def swap(pay_a, pay_b, axis):
    size = lax.axis_size(axis)
    pairs_a = [(i, i + 1) for i in range(1, size - 1, 2)]
    pairs_b = [(i, i + 1) for i in range(0, size - 1, 2)]
    return lax.ppermute(pay_a, axis, both_ways(pairs_a)), lax.ppermute(pay_b, axis, both_ways(pairs_b))


def exchange(value, distance):
    return lax.ppermute(value, "dev", [(i, i ^ distance) for i in range(lax.axis_size("dev"))])


def body(conc_old, phi_old, solid_pot, phase_label, iface_block, iface_owner):
    peers = lax.axis_size("dev")
    nx = conc_old.shape[0]
    half = nx // 2
    quarter = nx // 4
    ext = (nx + 2 * HALO, nx + 2 * HALO, 256)
    ext_mid = (half + 2 * HALO, half + 2 * HALO, 256)
    token_shape = shaped(8, LANES)

    pay_a, pay_b, own_lists = call(
        first_pack_kernel,
        [shaped(7 * nx, 256)] * 2 + [shaped(8, 256)],
        [conc_old, phase_label, iface_owner.reshape(1, -1), iface_block],
        [vmem(nx, HALO, 256)] * 2
        + [pltpu.VMEM((nx, HALO, 256), jnp.int32)] * 2
        + [pltpu.VMEM((1, 256), jnp.int32)] * 2
        + [vmem(7 * nx, 256)] * 2
        + [vmem(8, 256), pltpu.SemaphoreType.DMA((15,))],
        in_specs=[FAR] * 4,
        out_specs=[FAR] * 3,
        limit=VMEM_MOST,
        name="first_pack",
    )
    y_a, y_b = swap(pay_a, pay_b, "dev")
    conduct_mid, conduct_coarse, pay_a, pay_b, lists, gain, base = call(
        own_kernel,
        [shaped(half, half, 256), shaped(quarter, quarter, 256), shaped(22, 8, 256), shaped(22, 8, 256)]
        + [shaped(2, 256), shaped(nx, nx, 256), shaped(nx, nx, 256)],
        [conc_old, phase_label, phi_old, own_lists],
        [vmem(half, 2, nx, LANES), vmem(quarter, 2, half, LANES)],
        name="own",
    )
    xx_a, xx_b = swap(pay_a, pay_b, "grp")
    distance = peers // 2
    while distance > 1:
        lists = jnp.concatenate([lists, exchange(lists, distance)], axis=0)
        distance //= 2
    far_rows = second_rows(nx)[2]
    far_pay = call(
        second_pack_kernel,
        [shaped(far_rows, 256), shaped(far_rows + peers, 256)],
        [phi_old, conduct_mid, conduct_coarse, lists, xx_a, xx_b],
        name="second_pack",
    )
    yy_a, yy_b = swap(*far_pay, "dev")
    pay_a, pay_b = call(
        first_pack_x_kernel,
        [shaped(35, 8, 256)] * 2,
        [conc_old, phase_label, y_a, y_b, conduct_coarse],
        name="first_pack_x",
    )
    x_a, x_b = swap(pay_a, pay_b, "grp")

    ext_y = (nx, nx + 2 * HALO, 256)
    zero, first, second, third, gain_far, base_far, conc_inner, flux_inner = call(
        sweeps_inner_kernel,
        [shaped(*ext_y)] * 4 + [shaped(nx, 8, 256)] * 2 + [shaped(nx, nx, 256)] * 2,
        [conc_old, phase_label, phi_old, solid_pot, gain, base, y_a, y_b],
        name="sweeps_inner",
    )
    edge_args = [x_a, x_b, phase_label, phi_old, solid_pot, gain, base, zero, first, second, third]
    conc_new, flux_all, pay_a, pay_b = call(
        sweeps_edge_kernel,
        [shaped(nx, nx, 256), shaped(nx, nx, 256), shaped(3 * nx, 256), shaped(3 * nx, 256)],
        edge_args + [gain_far, base_far, conc_inner, flux_inner],
        [vmem(16, nx + 2 * HALO, 256)] * 4,
        name="sweeps_edge",
    )
    f_a, f_b = swap(pay_a, pay_b, "dev")
    flux_own, halo_mask = call(
        mask_kernel,
        [shaped(nx, nx, 256), shaped(nx, 8, 256)],
        [flux_all, lists, yy_b],
        [vmem(3, nx, 8, LANES)],
        name="mask",
    )
    weight, scale, made = call(
        ready_kernel,
        [shaped(*ext)] * 2 + [token_shape],
        [conc_old, phase_label, y_a, y_b, x_a, x_b],
        name="ready",
    )
    pay_a, pay_b = call(
        flux_pack_x_kernel, [shaped(15, 8, 256)] * 2, [flux_own, f_b, f_a, halo_mask, made], name="flux_pack_x"
    )
    fx_a, fx_b = swap(pay_a, pay_b, "grp")
    fine_two, fine_source, fine_first, inner_mid, field = call(
        potential_inner_kernel,
        [shaped(*ext)] * 3 + [shaped(half, half, 256), shaped(*ext)],
        [flux_own, halo_mask, f_a, f_b, phi_old, yy_a, yy_b, xx_a, xx_b, weight, scale],
        [vmem(nx, 8, 256), vmem(half, 2, nx, LANES)],
        name="potential_inner",
    )
    edge = (16, nx + 2 * HALO, 256)
    edge_two, edge_source, source_mid, pay_a, pay_b = call(
        potential_edge_kernel,
        [shaped(*edge), shaped(*edge), shaped(half, half, 256), shaped(4 * half, 256), shaped(4 * half, 256)],
        [fx_a, fx_b, weight, scale, field, fine_two, fine_source, fine_first, inner_mid, conduct_mid],
        [vmem(*edge), vmem(2, 2, nx, LANES)],
        name="potential_edge",
    )
    m_a, m_b = swap(pay_a, pay_b, "dev")
    concentration, flux, stored = call(
        store_kernel,
        [shaped(nx, nx, 256), shaped(nx, nx, 256), token_shape],
        [conc_new, flux_own],
        [pltpu.SemaphoreType.DMA((8,))],
        out_specs=[FAR, FAR, WHOLE],
        name="store",
    )
    wide = (quarter, 32, 256)
    rho, load, made = call(
        coarse_ready_kernel,
        [shaped(quarter, quarter, 256), shaped(8, LANES), token_shape],
        [conduct_coarse, yy_a, yy_b],
        [vmem(*wide)] * 4,
        name="coarse_ready",
    )
    pay_a, pay_b = call(
        mid_pack_x_kernel, [shaped(3 * HALO, 8, 256)] * 2, [source_mid, m_a, m_b, made, stored], name="mid_pack_x"
    )
    mx_a, mx_b = swap(pay_a, pay_b, "grp")
    mid_two, mid_source, mid_weight, source_coarse, wide_coarse, pay_a, pay_b, sums = call(
        mid_kernel,
        [shaped(*ext_mid)] * 3
        + [shaped(quarter, 12, 256), shaped(quarter, 12, 256), shaped(72, 256), shaped(80, 256), shaped(8, 256)],
        [source_mid, conduct_mid, yy_a, yy_b, xx_a, xx_b, m_a, m_b, mx_a, mx_b, rho, load],
        [vmem(*ext_mid)] * 2 + [vmem(8, 2, half + 2 * HALO, LANES)] * 2,
        name="middle",
    )
    c_a, c_b = swap(pay_a, pay_b, "dev")
    sums = sums + c_b[72:80]
    distance = 2
    while distance < peers:
        sums = sums + exchange(sums, distance)
        distance *= 2
    (error,) = call(
        coarse_kernel,
        [shaped(8, 16, 256)],
        [source_coarse, wide_coarse, yy_a, yy_b, c_a, c_b],
        [vmem(*wide)] * 4,
        name="coarse",
    )
    fields = [mid_two, mid_source, mid_weight, fine_two, fine_source, weight]
    kept = [shaped(4, half + 2 * HALO, 256)] * 2 + [shaped(4, nx + 2 * HALO, 256)] * 2
    scratch = [vmem(*ext_mid)] * 3 + [vmem(*ext)] * 2
    scratch += [vmem(8, 2, 2, 16, LANES), vmem(half + 2 * HALO, 3, 2, 16, LANES), vmem(nx, nx, 256)]
    scratch += [pltpu.SemaphoreType.DMA((2,))]
    error, pay_a, pay_b, begun, *kept_early = call(
        finish_early_kernel,
        [shaped(8, 16, 256), shaped(2, 16, 256), shaped(2, 16, 256), shaped(nx, nx, 256)] + kept,
        [error, sums] + fields,
        scratch,
        out_specs=[WHOLE] * 3 + [FAR] + [WHOLE] * 4,
        name="finish_early",
    )
    e_a, e_b = swap(pay_a, pay_b, "grp")
    begun, zero, one, fine_one, fine_last = call(
        finish_late_kernel,
        [shaped(nx, nx, 256)] + kept,
        [error] + fields + kept_early + [begun],
        scratch,
        in_specs=[WHOLE] * 11 + [FAR],
        out_specs=[FAR] + [WHOLE] * 4,
        aliases={11: 0},
        name="finish_late",
    )
    finish_args = [e_a, e_b, mid_two, mid_source, mid_weight, fine_two, edge_two, fine_source, edge_source, weight]
    finish_args += [zero, one, fine_one, fine_last, begun]
    (potential,) = call(
        finish_edge_kernel,
        [shaped(nx, nx, 256)],
        finish_args,
        [vmem(*ext_mid), vmem(*ext_mid), vmem(*ext), vmem(*ext)]
        + [vmem(4, 2, 2, 16, LANES), vmem(6, 3, 2, 16, LANES), vmem(nx, nx, 256)]
        + [pltpu.SemaphoreType.DMA((2,))],
        in_specs=[WHOLE] * (len(finish_args) - 1) + [FAR],
        out_specs=[FAR],
        aliases={len(finish_args) - 1: 0},
        name="finish_edge",
    )
    return (concentration, flux, potential)


def solution(mesh):
    brick = P("grp", "dev", None)
    return jax.shard_map(
        body,
        mesh=mesh,
        in_specs=(brick, brick, brick, brick, P("grp", "dev"), brick),
        out_specs=(brick, brick, brick),
        check_vma=False,
    )
```

```python
import jax
import jax.numpy as jnp
from jax import lax
from jax.experimental import pallas as pl
from jax.experimental.pallas import tpu as pltpu
from jax.sharding import PartitionSpec as P


F32 = jnp.float32
MASS = 0.05
OMEGA = 0.8
DIFFUSION_TABLE = (1.5, 0.1, 0.4)
RATIO_TABLE = tuple(d / (1.0 + 6.0 * d) for d in DIFFUSION_TABLE)
INVERSE_TABLE = tuple(1.0 / (1.0 + 6.0 * d) for d in DIFFUSION_TABLE)
CONDUCT_TABLE = (1.0, 0.3, 0.6)
KINETIC_TABLE = (0.2, 1.0, 0.5)
SWEEPS = 4
COARSE_SWEEPS = 8
COARSE_NEAR = 8
HALO = 4
LANES = 128
VMEM_LIMIT = 28 * 1024 * 1024
VMEM_MOST = 58 * 1024 * 1024


def shaped(*shape):
    return jax.ShapeDtypeStruct(shape, F32)


WHOLE = pl.BlockSpec(memory_space=pltpu.VMEM)
FAR = pl.BlockSpec(memory_space=pltpu.HBM)


def call(kernel, outs, args, scratch=(), in_specs=None, out_specs=None, limit=VMEM_LIMIT, aliases=None, flops=10**6, name=None):
    size = sum(4 * a.size for a in args) + sum(4 * o.size for o in outs)
    return pl.pallas_call(
        kernel,
        out_shape=tuple(outs),
        in_specs=in_specs or [WHOLE] * len(args),
        out_specs=tuple(out_specs or [WHOLE] * len(outs)),
        scratch_shapes=list(scratch),
        input_output_aliases=aliases or {},
        compiler_params=pltpu.CompilerParams(vmem_limit_bytes=limit),
        cost_estimate=pl.CostEstimate(flops=flops, bytes_accessed=size, transcendentals=0),
        name=name,
    )(*args)


def vmem(*shape):
    return pltpu.VMEM(shape, F32)


def iota(shape, dim):
    return lax.broadcasted_iota(jnp.int32, shape, dim)


def pick(label, table):
    return jnp.where(label == 0, table[0], jnp.where(label == 1, table[1], table[2])).astype(F32)


def loop(low, high, body, unroll=8):
    steps = (high - low) // unroll

    def step(i, carry):
        for u in range(unroll):
            body(low + i * unroll + u)
        return carry

    if steps > 1:
        lax.fori_loop(0, steps, step, 0)
    else:
        steps = 0
    for x in range(low + steps * unroll, high):
        body(x)


def odd(axis):
    return lax.rem(lax.axis_index(axis), 2) == 1


def along_y(v):
    return pltpu.roll(v, 1, 0) + pltpu.roll(v, v.shape[0] - 1, 0)


def along_z(v):
    low, high = v[:, :LANES], v[:, LANES:]
    lane = iota(low.shape, 1)
    first, last = lane == 0, lane == LANES - 1
    low_up, high_up = pltpu.roll(low, 1, 1), pltpu.roll(high, 1, 1)
    low_down, high_down = pltpu.roll(low, LANES - 1, 1), pltpu.roll(high, LANES - 1, 1)
    low_sum = jnp.where(first, 0.0, low_up) + jnp.where(last, high_down, low_down)
    high_sum = jnp.where(first, low_up, high_up) + jnp.where(last, 0.0, high_down)
    return jnp.concatenate([low_sum, high_sum], axis=1)


def upper(shape=(8, 256)):
    return iota(shape, 0) < HALO


def twice(tile, scratch):
    for h in range(2):
        part = tile[:, h * LANES : (h + 1) * LANES]
        scratch[h, pl.ds(0, 8, stride=2), :] = part
        scratch[h, pl.ds(1, 8, stride=2), :] = part
    return jnp.concatenate([scratch[0], scratch[1]], axis=1)


def pair_rows(v, scratch):
    half = v.shape[0] // 2
    parts = []
    for h in range(2):
        scratch[h] = v[:, h * LANES : (h + 1) * LANES]
        parts.append(scratch[h, pl.ds(0, half, stride=2), :] + scratch[h, pl.ds(1, half, stride=2), :])
    return jnp.concatenate(parts, axis=1)


def either(flag, if_true, if_false):
    return jnp.where(flag, if_true, if_false)


def y_sides(r_a, r_b, at, count):
    flag = odd("dev")
    a, b = r_a[at : at + count, :], r_b[at : at + count, :]
    return either(flag, a, b), either(flag, b, a)


def x_sides(r_a, r_b, index):
    flag = odd("grp")
    a, b = r_a[index], r_b[index]
    return either(flag, a, b), either(flag, b, a)


def send_y(pay_a, pay_b, at, first, last):
    flag = odd("dev")
    n = first.shape[0]
    pay_a[at : at + n, :] = either(flag, last, first)
    pay_b[at : at + n, :] = either(flag, first, last)


def send_x(pay_a, pay_b, index, first, last):
    flag = odd("grp")
    pay_a[index] = either(flag, last, first)
    pay_b[index] = either(flag, first, last)


def halo_tile(after, before):
    parts = [after]
    if after.shape[0] < HALO:
        parts.append(jnp.zeros((2 * HALO - 2 * after.shape[0], after.shape[1]), F32))
    return jnp.concatenate(parts + [before], axis=0)


def first_pack_kernel(
    conc, label, owner, block, out_a, out_b, own_lists,
    c_first, c_last, l_first, l_last, own_owner, own_block, pay_a, pay_b, named, sems,
):
    nx = conc.shape[0]
    half = nx // 2
    lists = [pltpu.make_async_copy(owner, own_owner, sems.at[8]), pltpu.make_async_copy(block, own_block, sems.at[9])]
    reads = []
    for j in range(2):
        planes = pl.ds(half * j, half)
        for i, (ref, at, to) in enumerate(
            ((conc, 0, c_first), (conc, 28, c_last), (label, 0, l_first), (label, 28, l_last))
        ):
            reads.append(pltpu.make_async_copy(ref.at[planes, pl.ds(at, 4), :], to.at[planes], sems.at[4 * j + i]))
    for c in reads + lists:
        c.start()
    writes = []
    for j in range(2):
        for c in reads[4 * j : 4 * j + 4]:
            c.wait()
        for x in range(half * j, half * j + half):
            send_y(pay_a, pay_b, 7 * x, c_first[x], c_last[x])
            send_y(pay_a, pay_b, 7 * x + 4, l_first[x, 0:3, :].astype(F32), l_last[x, 1:4, :].astype(F32))
        rows = pl.ds(7 * half * j, 7 * half)
        for i, (pay, out) in enumerate(((pay_a, out_a), (pay_b, out_b))):
            writes.append(pltpu.make_async_copy(pay.at[rows], out.at[rows], sems.at[10 + 2 * j + i]))
            writes[-1].start()
    for c in lists:
        c.wait()
    named[...] = jnp.concatenate([own_owner[...], own_block[...], jnp.zeros((6, 256), jnp.int32)], axis=0).astype(F32)
    writes.append(pltpu.make_async_copy(named, own_lists, sems.at[14]))
    writes[-1].start()
    for c in writes:
        c.wait()


def own_kernel(conc, label, phi, named, mid, coarse, pay_a, pay_b, lists, gain, base, pairs, pairs_2):
    nx = conc.shape[0]
    half = nx // 2
    lists[...] = named[0:2, :]

    def coefficients(i):
        gain[i] = pick(label[i], RATIO_TABLE)
        base[i] = conc[i] * pick(label[i], INVERSE_TABLE)

    loop(0, nx, coefficients, 4)

    def coarsen(i):
        total = conc[2 * i] * pick(label[2 * i], CONDUCT_TABLE) + conc[2 * i + 1] * pick(label[2 * i + 1], CONDUCT_TABLE)
        mid[i] = 0.25 * pair_rows(total, pairs.at[i])

    loop(0, half, coarsen, 4)
    for i in range(half // 2):
        coarse[i] = 0.25 * pair_rows(mid[2 * i] + mid[2 * i + 1], pairs_2.at[i])
    for k in range(HALO):
        for t in range(4):
            rows = slice(8 * t, 8 * t + 8)
            send_x(pay_a, pay_b, 4 * k + t, phi[k, rows, :], phi[nx - HALO + k, rows, :])
    for k in range(MID_HALO):
        for t in range(2):
            rows = slice(8 * t, 8 * t + 8)
            send_x(pay_a, pay_b, 16 + 2 * k + t, mid[k, rows, :], mid[half - MID_HALO + k, rows, :])


def first_pack_x_kernel(conc, label, r_a, r_b, token, pay_a, pay_b):
    nx = conc.shape[0]

    def plane(ref, k, t, offset, count):
        if t < 4:
            return ref[k, 8 * t : 8 * t + 8, :].astype(F32)
        return halo_tile(*y_sides(r_a, r_b, 7 * k + offset, count))

    for t in range(5):
        for k in range(HALO):
            send_x(pay_a, pay_b, 5 * k + t, plane(conc, k, t, 0, 4), plane(conc, nx - HALO + k, t, 0, 4))
        for k in range(3):
            send_x(pay_a, pay_b, 20 + 5 * k + t, plane(label, k, t, 4, 3), plane(label, nx - 3 + k, t, 4, 3))


MID_HALO = 3


def corner_rows(n, width, reach):
    counts = [min(width, k + reach) for k in range(width)]
    counts = counts + [width] * n + counts[::-1]
    return counts, [sum(counts[:i]) for i in range(len(counts))]


def second_rows(nx):
    phi = sum(corner_rows(nx, HALO, 0)[0])
    mid = sum(corner_rows(nx // 2, MID_HALO, 1)[0])
    return phi, phi + mid, phi + mid + 64


def second_pack_kernel(phi, mid, coarse, lists, x_a, x_b, pay_a, pay_b):
    nx = phi.shape[0]
    starts = second_rows(nx)

    def put(own, width, reach, index, base):
        n = own.shape[0]
        counts, at = corner_rows(n, width, reach)
        tiles = own.shape[1] // 8
        for x in range(n):
            send_y(pay_a, pay_b, base + at[width + x], own[x, 0:width, :], own[x, 8 * tiles - width : 8 * tiles, :])
        for k in range(width):
            first_after, first_before = x_sides(x_a, x_b, index + tiles * k)
            last_after, last_before = x_sides(x_a, x_b, index + tiles * k + tiles - 1)
            for x, first, last in ((k, first_before, last_before), (width + n + k, first_after, last_after)):
                if counts[x]:
                    send_y(pay_a, pay_b, base + at[x], first[0 : counts[x]], last[8 - counts[x] : 8])

    put(phi, HALO, 0, 0, 0)
    put(mid, MID_HALO, 1, 16, starts[0])
    base = starts[1]
    for x in range(8):
        pay_a[base + 8 * x : base + 8 * x + 8, :] = coarse[x]
        pay_b[base + 8 * x : base + 8 * x + 8, :] = coarse[x]
    base = starts[2]
    pay_b[base : base + lists.shape[0], :] = lists[...]


def second_halo(r_a, r_b, n, width, reach, x, base):
    counts, at = corner_rows(n, width, reach)
    x = x - HALO + width
    if x < 0 or x >= len(counts) or not counts[x]:
        return jnp.zeros((8, 256), F32)
    return halo_tile(*y_sides(r_a, r_b, base + at[x], counts[x]))


def wide_rows(own, after_own, before_own, after, before):
    gap = jnp.zeros((6, 256), F32)
    return jnp.concatenate([own, after_own, after, gap, before, before_own], axis=0)


def flux_plane(c, solid, phi, label):
    drive = 0.5 * (solid - phi)
    logc = jnp.log(c)
    return pick(label, KINETIC_TABLE) * (jnp.exp(drive + 0.4 * logc) - jnp.exp(0.6 * logc - drive))


def around_plane(before, v, after):
    return (before + after) + (along_y(v) + along_z(v))


def sweeps_inner_kernel(
    conc, label, phi, solid, gain, base, y_a, y_b, zero, first, second, third, gain_far, base_far, out, flux
):
    nx = conc.shape[0]

    def own(i):
        zero[i, 0:32, :] = conc[i]

    loop(0, nx, own)
    for i in range(nx):
        c = halo_tile(*y_sides(y_a, y_b, 7 * i, 4))
        lab = halo_tile(*y_sides(y_a, y_b, 7 * i + 4, 3))
        zero[i, 32:40, :] = c
        gain_far[i] = jnp.where(c > 0.0, pick(lab, RATIO_TABLE), 0.0)
        base_far[i] = c * pick(lab, INVERSE_TABLE)
    fields = (zero, first, second, third)
    for s in range(1, SWEEPS):
        old, new = fields[s - 1], fields[s]

        def sweep(i, old=old, new=new):
            g = jnp.concatenate([gain[i], gain_far[i]], axis=0)
            b = jnp.concatenate([base[i], base_far[i]], axis=0)
            new[i] = b + g * around_plane(old[i - 1], old[i], old[i + 1])

        loop(s, nx - s, sweep)

    def last(i):
        c = base[i] + gain[i] * around_plane(third[i - 1], third[i], third[i + 1])[0:32, :]
        out[i] = c
        flux[i] = flux_plane(c, solid[i], phi[i], label[i])

    loop(SWEEPS, nx - SWEEPS, last, 4)


def sweeps_edge_kernel(
    x_a, x_b, label, phi, solid, gain, base, zero, first, second, third, gain_far, base_far, out_inner, flux_inner,
    out, flux, pay_a, pay_b, zero_x, first_x, second_x, third_x,
):
    nx = out.shape[0]
    inner = (zero, first, second, third)
    edge = (zero_x, first_x, second_x, third_x)

    def copy(i):
        out[i] = out_inner[i]
        flux[i] = flux_inner[i]

    loop(SWEEPS, nx - SWEEPS, copy)
    for side in range(2):
        plane = lambda k, side=side: k if side == 0 else nx - 1 - k
        row = lambda k, side=side: 8 * side + HALO + k
        far = lambda k, index, side=side: x_sides(x_a, x_b, index)[1 - side]
        gains, bases = {}, {}
        for j in range(1, HALO + 1):
            k = HALO - j if side == 0 else j - 1
            zero_x[row(-j)] = jnp.concatenate([far(k, 5 * k + t) for t in range(5)], axis=0)
            if j < HALO:
                k = HALO - 1 - j if side == 0 else j - 1
                lab = jnp.concatenate([far(k, 20 + 5 * k + t) for t in range(5)], axis=0)
                c = zero_x[row(-j)]
                gains[-j] = jnp.where(c > 0.0, pick(lab, RATIO_TABLE), 0.0)
                bases[-j] = c * pick(lab, INVERSE_TABLE)
        for k in range(SWEEPS):
            gains[k] = jnp.concatenate([gain[plane(k)], gain_far[plane(k)]], axis=0)
            bases[k] = jnp.concatenate([base[plane(k)], base_far[plane(k)]], axis=0)
        for s in range(1, SWEEPS + 1):

            def old(k, s=s):
                return inner[s - 1][plane(k)] if k >= s - 1 else edge[s - 1][row(k)]

            for k in range(s - SWEEPS, s):
                c = bases[k] + gains[k] * around_plane(old(k - 1), old(k), old(k + 1))
                if s < SWEEPS:
                    edge[s][row(k)] = c
                else:
                    c = c[0:32, :]
                    out[plane(k)] = c
                    flux[plane(k)] = flux_plane(c, solid[plane(k)], phi[plane(k)], label[plane(k)])
    for x in range(nx):
        send_y(pay_a, pay_b, 3 * x, flux[x, 0:3, :], flux[x, 29:32, :])


def mask_kernel(flux_all, lists, far, flux, halo_mask, marked):
    nx = flux_all.shape[0]
    rows = lists.shape[0]
    pieces = [lists[i : i + 1, :] for i in range(rows)] + [far[i : i + 1, :] for i in range(far.shape[0] - rows, far.shape[0])]
    owner = jnp.concatenate(pieces[0::2], axis=1).astype(jnp.int32)
    block = jnp.concatenate(pieces[1::2], axis=1).astype(jnp.int32)
    entries = owner.shape[1]
    hit_column = (iota((64, entries), 0) == lax.rem(block, 64)).astype(jnp.bfloat16)
    reach = owner - lax.axis_index("dev") + 1
    at_row = jnp.where((reach >= 0) & (reach < 3), reach * nx + lax.shift_right_arithmetic(block, 6), -1)
    hit_row = (iota((3 * nx, entries), 0) == at_row).astype(jnp.bfloat16)
    named = lax.dot_general(hit_row, hit_column, (((1,), (1,)), ((), ())), preferred_element_type=F32)
    named = jnp.concatenate([named, jnp.zeros((3 * nx, LANES - 64), F32)], axis=1)
    for j in range(3):
        for i in range(nx):
            marked[j, i] = jnp.broadcast_to(named[j * nx + i : j * nx + i + 1, :], (8, LANES))
    is_row = lax.div(iota((32, LANES), 1), 2) == iota((32, LANES), 0)
    row, pair = iota((8, LANES), 0), lax.div(iota((8, LANES), 1), 2)
    is_after = (row < 3) & (pair == row)
    is_before = (row >= 5) & (pair == row + 24)
    spread = (lax.rem(iota((LANES, 256), 0), 2) == lax.div(iota((LANES, 256), 1), LANES)).astype(jnp.bfloat16)

    def plane(i):
        marks = jnp.where(is_row, jnp.concatenate([marked[1, i]] * 4, axis=0), 0.0)
        beyond = jnp.where(is_after, marked[2, i], jnp.where(is_before, marked[0, i], 0.0))
        marks = jnp.concatenate([marks, beyond], axis=0).astype(jnp.bfloat16)
        listed = jnp.dot(marks, spread, preferred_element_type=F32) > 0.5
        flux[i] = jnp.where(listed[0:32], flux_all[i], 0.0)
        halo_mask[i] = jnp.where(listed[32:40], 1.0, 0.0)

    loop(0, nx, plane, 16)


def store_kernel(conc, flux, conc_out, flux_out, token, sems):
    copies = []
    for i, (ref, to) in enumerate(((conc, conc_out), (flux, flux_out))):
        for j in range(4):
            rows = pl.ds(8 * j, 8)
            copies.append(pltpu.make_async_copy(ref.at[rows], to.at[rows], sems.at[4 * i + j]))
            copies[-1].start()
    token[...] = jnp.zeros(token.shape, F32)
    for c in copies:
        c.wait()


def ready_kernel(conc, label, y_a, y_b, x_a, x_b, weight, scale, token):
    nx = conc.shape[0]
    token[...] = jnp.zeros(token.shape, F32)

    def put(x, rows, c, lab):
        conduct = c * pick(lab, CONDUCT_TABLE)
        factor = OMEGA / (MASS + 6.0 * conduct)
        weight[x, rows, :] = conduct * factor
        scale[x, rows, :] = factor

    def own(i):
        put(HALO + i, slice(0, 32), conc[i], label[i])

    loop(0, nx, own, 4)
    for i in range(nx):
        c = halo_tile(*y_sides(y_a, y_b, 7 * i, 4))
        lab = halo_tile(*y_sides(y_a, y_b, 7 * i + 4, 3))
        put(HALO + i, slice(32, 40), c, lab)
    for t in range(5):
        rows = slice(8 * t, 8 * t + 8)
        for k in range(HALO):
            c_after, c_before = x_sides(x_a, x_b, 5 * k + t)
            l_after = x_sides(x_a, x_b, 20 + 5 * min(k, 2) + t)[0]
            l_before = x_sides(x_a, x_b, 20 + 5 * max(k - 1, 0) + t)[1]
            put(k, rows, c_before, l_before)
            put(HALO + nx + k, rows, c_after, l_after)


def place_phi(phi, yy_a, yy_b, xx_a, xx_b, field):
    nx = phi.shape[0]

    def own(i):
        field[HALO + i, 0:32, :] = phi[i]

    loop(0, nx, own)
    for x in range(nx + 2 * HALO):
        field[x, 32:40, :] = second_halo(yy_a, yy_b, nx, HALO, 0, x, 0)
    for t in range(4):
        for k in range(HALO):
            after, before = x_sides(xx_a, xx_b, 4 * k + t)
            field[k, 8 * t : 8 * t + 8, :] = before
            field[HALO + nx + k, 8 * t : 8 * t + 8, :] = after


def flux_pack_x_kernel(flux, r_b, r_a, mask, token, pay_a, pay_b):
    nx = flux.shape[0]

    def tile(x, t):
        if t < 4:
            return flux[x, 8 * t : 8 * t + 8, :]
        return mask[x] * halo_tile(*y_sides(r_a, r_b, 3 * x, 3))

    for k in range(3):
        for t in range(5):
            send_x(pay_a, pay_b, 5 * k + t, tile(k, t), tile(nx - 3 + k, t))


def first_sweep(field, weight, scale, x, rows, flux):
    p = field[x]
    near = (field[x - 1] + field[x + 1]) + (along_y(p) + along_z(p))
    b = scale[x, rows, :] * (MASS * p[rows, :] + flux)
    return b, 0.2 * p[rows, :] + weight[x, rows, :] * near[rows, :] + b


def potential_inner_kernel(
    flux, mask, y_a, y_b, phi, yy_a, yy_b, xx_a, xx_b, weight, scale, after_two, source, first, source_mid, field, far, pairs
):
    nx = flux.shape[0]
    place_phi(phi, yy_a, yy_b, xx_a, xx_b, field)
    for i in range(nx):
        far[i] = mask[i] * halo_tile(*y_sides(y_a, y_b, 3 * i, 3))

    def own(i):
        x = HALO + i
        f = jnp.concatenate([flux[i], far[i]], axis=0)
        source[x], first[x] = first_sweep(field, weight, scale, x, slice(0, 40), f)

    loop(0, nx, own)

    def around(values, x):
        v = values[x]
        return v, weight[x] * ((values[x - 1] + values[x + 1]) + (along_y(v) + along_z(v)))

    def sweep(x):
        v, near = around(first, x)
        after_two[x] = 0.2 * v + (source[x] + near)

    loop(HALO + 1, HALO + nx - 1, sweep)

    def remainder(x):
        v, near = around(after_two, x)
        return ((source[x] - OMEGA * v) + near)[0:32, :] / scale[x, 0:32, :]

    def coarsen(i):
        x = HALO + 2 * i
        source_mid[i] = 0.25 * pair_rows(remainder(x) + remainder(x + 1), pairs.at[i])

    loop(1, nx // 2 - 1, coarsen, 4)


def mid_factor(conduct):
    return OMEGA / (MASS + 3.0 * conduct)


def potential_edge_kernel(
    x_a, x_b, weight, scale, field, inner_two, inner_source, inner_first, inner_mid, conduct_mid,
    edge_two, edge_source, source_mid, pay_a, pay_b, first, pairs,
):
    half = source_mid.shape[0]
    nx = 2 * half
    for side, face in ((0, HALO), (1, HALO + nx)):
        base = 8 * side + HALO - face
        for k in range(3):
            x = face - 3 + k if side == 0 else face + k
            f = jnp.concatenate([x_sides(x_a, x_b, 5 * k + t)[1 - side] for t in range(5)], axis=0)
            edge_source[base + x], first[base + x] = first_sweep(field, weight, scale, x, slice(0, 40), f)

        def first_of(x, base=base):
            return inner_first[x] if HALO <= x < HALO + nx else first[base + x]

        def source_of(x, base=base):
            return inner_source[x] if HALO <= x < HALO + nx else edge_source[base + x]

        def two_of(x, base=base):
            return inner_two[x] if HALO < x < HALO + nx - 1 else edge_two[base + x]

        for x in range(face - 2, face + 1) if side == 0 else range(face - 1, face + 2):
            v = first_of(x)
            near = weight[x] * ((first_of(x - 1) + first_of(x + 1)) + (along_y(v) + along_z(v)))
            edge_two[base + x] = 0.2 * v + (source_of(x) + near)
        total = 0.0
        at = face if side == 0 else face - 2
        for x in (at, at + 1):
            v = two_of(x)
            near = weight[x] * ((two_of(x - 1) + two_of(x + 1)) + (along_y(v) + along_z(v)))
            total = total + ((source_of(x) - OMEGA * v) + near)[0:32, :] / scale[x, 0:32, :]
        at = 0 if side == 0 else half - 1
        source_mid[at] = mid_factor(conduct_mid[at]) * (0.25 * pair_rows(total, pairs.at[side]))
    for x in range(1, half - 1):
        source_mid[x] = mid_factor(conduct_mid[x]) * inner_mid[x]
    for x in range(half):
        send_y(pay_a, pay_b, 4 * x, source_mid[x, 0:4, :], source_mid[x, 12:16, :])


def mid_pack_x_kernel(field, r_a, r_b, token, pay_a, pay_b):
    n = field.shape[0]

    def tile(x, t):
        if t < 2:
            return field[x, 8 * t : 8 * t + 8, :]
        return halo_tile(*y_sides(r_a, r_b, 4 * x, 4))

    for k in range(HALO):
        for t in range(3):
            send_x(pay_a, pay_b, 3 * k + t, tile(k, t), tile(n - HALO + k, t))


def mid_kernel(
    source_own, conduct_own, yy_a, yy_b, xx_a, xx_b, y_a, y_b, x_a, x_b, rho, load, token,
    after_two, source, weight, coarse, conduct, pay_a, pay_b, part, scale, mid_conduct, pairs, pairs_2,
):
    n = source_own.shape[0]
    base = second_rows(2 * n)[0]

    def put(x, rows, b, k):
        factor = mid_factor(k)
        weight[x, rows, :] = k * factor
        scale[x, rows, :] = factor
        source[x, rows, :] = b
        mid_conduct[x, rows, :] = k

    def far(x):
        return second_halo(yy_a, yy_b, n, MID_HALO, 1, x, base)

    for i in range(n):
        put(HALO + i, slice(0, 16), source_own[i], conduct_own[i])
        put(HALO + i, slice(16, 24), halo_tile(*y_sides(y_a, y_b, 4 * i, 4)), far(HALO + i))
    for k in range(HALO):
        for t in range(3):
            rows = slice(8 * t, 8 * t + 8)
            b_after, b_before = x_sides(x_a, x_b, 3 * k + t)
            if t < 2:
                none = jnp.zeros((8, 256), F32)
                c_before = x_sides(xx_a, xx_b, 16 + 2 * (k - 1) + t)[1] if k > 0 else none
                c_after = x_sides(xx_a, xx_b, 16 + 2 * k + t)[0] if k < MID_HALO else none
            else:
                c_after, c_before = far(HALO + n + k), far(k)
            put(k, rows, b_before, c_before)
            put(HALO + n + k, rows, b_after, c_after)

    def around(values, x):
        v = values[x]
        return v, weight[x] * (0.25 * ((values[x - 1] + values[x + 1]) + along_y(v)) + along_z(v))

    def sweep(x):
        v, near = around(source, x)
        after_two[x] = 0.2 * v + (source[x] + near)

    loop(1, n + 2 * HALO - 1, sweep, 11)

    def remainder(x):
        v, near = around(after_two, x)
        return ((source[x] - OMEGA * v) + near) / scale[x]

    total = jnp.zeros((8, 256), F32)
    for i in range(n // 2):
        x = HALO + 2 * i
        value = 0.25 * pair_rows(remainder(x) + remainder(x + 1), pairs.at[i])
        k = 0.25 * pair_rows(mid_conduct[x] + mid_conduct[x + 1], pairs_2.at[i])
        coarse[i] = value
        conduct[i] = k
        send_y(pay_a, pay_b, 9 * i, value[1:9], jnp.concatenate([value[11:12], value[0:7]], axis=0))
        send_y(pay_a, pay_b, 9 * i + 8, k[8:9], k[11:12])
        total += rho[i] * value[0:8]
    sums = jnp.concatenate([total[:, :LANES] + total[:, LANES:], load[...]], axis=1)
    pay_b[72:80, :] = sums
    part[...] = sums


COARSE_W = 0.0625


def coarse_ready_kernel(own, r_a, r_b, rho, load, token, one, two, conduct, scale):
    token[...] = jnp.zeros(token.shape, F32)
    base = r_a.shape[0] - 64
    for x in range(8):
        after, before = y_sides(r_a, r_b, base + 8 * x, 8)
        k = jnp.concatenate([own[x], after, jnp.zeros((8, 256), F32), before], axis=0)
        conduct[x] = k
        scale[x] = OMEGA / (MASS + 2.25 * k)
        one[x] = jnp.ones(k.shape, F32)
    fields = (one, two)
    for s in range(COARSE_SWEEPS):
        old, new = fields[s % 2], fields[(s + 1) % 2]
        for x in range(8):
            near = [conduct[i] * old[i] if 0 <= i < 8 else None for i in (x - 1, x, x + 1)]
            inner = along_y(near[1])
            for other in (near[0], near[2]):
                if other is not None:
                    inner = inner + other
            new[x] = 0.2 * old[x] + scale[x] * (COARSE_W * inner + along_z(near[1]))
    last = fields[COARSE_SWEEPS % 2]
    peer, peers = lax.axis_index("dev"), lax.axis_size("dev")
    row, z = iota((8, 256), 0), iota((8, 256), 1)
    edge_y = ((row == 0) & (peer == 0)) | ((row == 7) & (peer == peers - 1))
    edge = edge_y.astype(F32) * COARSE_W + ((z == 0) | (z == 255)).astype(F32)
    total = jnp.zeros((8, 256), F32)
    for x in range(8):
        rho[x] = last[x, 0:8, :]
        total += MASS + own[x] * (edge + (COARSE_W if x in (0, 7) else 0.0))
    load[...] = total[:, :LANES] + total[:, LANES:]


def coarse_kernel(own, conduct, far_a, far_b, r_a, r_b, error, source, weight, one, two):
    base = far_a.shape[0] - 64
    for x in range(8):
        after, before = y_sides(r_a, r_b, 9 * x, 8)
        b = wide_rows(own[x, 0:8, :], own[x, 8:9, :], own[x, 11:12, :], after, before)
        last_after, last_before = y_sides(r_a, r_b, 9 * x + 8, 1)
        after, before = y_sides(far_a, far_b, base + 8 * x, 8)
        after = jnp.concatenate([after[1:8], last_after], axis=0)
        before = jnp.concatenate([last_before, before[0:7]], axis=0)
        k = wide_rows(conduct[x, 0:8, :], conduct[x, 8:9, :], conduct[x, 11:12, :], after, before)
        factor = OMEGA / (MASS + 2.25 * k)
        weight[x] = k * factor
        source[x] = factor * b
    old = source
    for s in range(1, COARSE_SWEEPS):
        new = one if s % 2 else two
        for x in range(8):
            v = old[x]
            inner = along_y(v)
            if x > 0:
                inner = inner + old[x - 1]
            if x < 7:
                inner = inner + old[x + 1]
            new[x] = 0.2 * v + (source[x] + weight[x] * (COARSE_W * inner + along_z(v)))
        old = new
    for x in range(8):
        error[x, 0:8, :] = old[x, 0:8, :]
        error[x, 8:16, :] = jnp.where(upper(), old[x, 8:16, :], old[x, 24:32, :])


def squeeze(tile):
    return jnp.where(iota((8, 256), 0) < 2, tile, pltpu.roll(tile, 4, 0))


def spread_coarse(plane, room):
    return jnp.concatenate([twice(plane[0:8], room.at[0]), twice(squeeze(plane[8:16]), room.at[1])[0:8]], axis=0)


def spread_mid(plane, room):
    parts = [twice(plane[0:8], room.at[0]), twice(plane[8:16], room.at[1]), twice(squeeze(plane[16:24]), room.at[2])[0:8]]
    return jnp.concatenate(parts, axis=0)


def smoothed(before, v, after, weight, source, w):
    inner = (before + after) + along_y(v)
    return source + (0.2 * v + weight * (w * inner + along_z(v)))


def is_early():
    return (lax.axis_index("grp") < lax.axis_size("grp") // 2) | odd("grp")


def finish_inner(error, fields, kept, out, scratch):
    mid_two, mid_source, mid_weight, fine_two, fine_source, fine_weight = fields
    zero, one, two, fine_one, fine_last, dup, dup_2, result, sems = scratch
    n = mid_two.shape[0]
    nf = fine_two.shape[0]
    for c in range(8):
        spread = spread_coarse(error[c], dup.at[c])
        for x in (2 * c + HALO, 2 * c + 1 + HALO):
            zero[x] = jnp.where(mid_weight[x] > 0.0, mid_two[x] + spread, 0.0)

    def sweep_mid(x, old, new):
        new[x] = smoothed(old[x - 1], old[x], old[x + 1], mid_weight[x], mid_source[x], 0.25)

    for x in range(HALO + 1, n - HALO - 1):
        sweep_mid(x, zero, one)
    for x in range(HALO + 2, n - HALO - 2):
        sweep_mid(x, one, two)

    def lift(m):
        spread = spread_mid(two[m], dup_2.at[m])
        x = 2 * m - HALO
        fine_one[x] = fine_two[x] + spread
        fine_one[x + 1] = fine_two[x + 1] + spread

    loop(HALO + 2, n - HALO - 2, lift, 6)

    def sweep_one(x):
        fine_last[x] = smoothed(fine_one[x - 1], fine_one[x], fine_one[x + 1], fine_weight[x], fine_source[x], 1.0)

    low, high = 2 * HALO + 1, nf - 2 * HALO - 1
    loop(low, high, sweep_one, 11)
    for field, first, to in ((zero, 0, kept[0]), (one, 1, kept[1]), (fine_one, 4, kept[2]), (fine_last, 5, kept[3])):
        for j in range(2):
            to[j] = field[HALO + first + j]
            to[2 + j] = field[field.shape[0] - HALO - 1 - first - j]
    copies = []
    low, high = low + 1, high - 1
    for j in range(2):
        mid = low + (high - low) // 2
        for x in range(low, mid) if j == 0 else range(mid, high):
            v = smoothed(fine_last[x - 1], fine_last[x], fine_last[x + 1], fine_weight[x], fine_source[x], 1.0)
            result[x - HALO] = v[0:32, :]
        rows = pl.ds(low - HALO, mid - low) if j == 0 else pl.ds(mid - HALO, high - mid)
        copies.append(pltpu.make_async_copy(result.at[rows], out.at[rows], sems.at[j]))
        copies[-1].start()
    for c in copies:
        c.wait()


def finish_early_kernel(error, sums, *rest):
    fields, (shifted, pay_a, pay_b, out), kept, scratch = rest[:6], rest[6:10], rest[10:14], rest[14:]
    resid = jnp.sum(sums[:, :LANES])
    load = jnp.sum(sums[:, LANES:])
    shift_c = jnp.full((16, 256), resid, F32) / jnp.full((16, 256), load, F32)
    for x in range(8):
        shifted[x] = error[x] + shift_c
    for k in range(2):
        send_x(pay_a, pay_b, k, shifted[k], shifted[6 + k])

    @pl.when(is_early())
    def _():
        finish_inner(shifted, fields, kept, out, scratch)


def finish_late_kernel(error, *rest):
    fields, kept_early, out, kept, scratch = rest[:6], rest[6:10], rest[11], rest[12:16], rest[16:]

    @pl.when(is_early())
    def _():
        for a, b in zip(kept_early, kept):
            b[...] = a[...]

    @pl.when(jnp.logical_not(is_early()))
    def _():
        finish_inner(error, fields, kept, out, scratch)


def finish_edge_kernel(
    x_a, x_b, mid_two, mid_source, mid_weight, fine_two, edge_two, fine_source, edge_source, fine_weight,
    zero, one, fine_one, fine_last, begun, out, zero_edge, one_edge, fine_edge, last_edge, dup, dup_2, result, sems,
):
    n = mid_two.shape[0]
    nf = fine_two.shape[0]
    nx = nf - 2 * HALO
    copies = []
    planes = x_sides(x_a, x_b, slice(0, 2))
    for side in (0, 1):
        sign = 1 if side == 0 else -1
        at = lambda k, side=side: HALO + k if side == 0 else n - HALO - 1 - k
        fine = lambda k, side=side: HALO + k if side == 0 else nf - HALO - 1 - k
        base = 8 * side + (0 if side == 0 else HALO - HALO - nx)
        for c in range(2):
            plane = planes[1 - side][c]
            spread = spread_coarse(plane, dup.at[2 * side + c])
            first = 2 * c if side == 0 else n - HALO + 2 * c
            for x in (first, first + 1):
                zero_edge[x] = jnp.where(mid_weight[x] > 0.0, mid_two[x] + spread, 0.0)

        def zero_of(k, side=side):
            return zero[2 * side + k] if k >= 0 else zero_edge[at(k)]

        def one_of(k, side=side):
            return one[2 * side + k - 1] if k >= 1 else one_edge[at(k)]

        for k in range(-2, 1):
            x = at(k)
            one_edge[x] = smoothed(zero_of(k - 1), zero_of(k), zero_of(k + 1), mid_weight[x], mid_source[x], 0.25)
        for k in range(-1, 2):
            x = at(k)
            value = smoothed(one_of(k - 1), one_of(k), one_of(k + 1), mid_weight[x], mid_source[x], 0.25)
            spread = spread_mid(value, dup_2.at[3 * side + k + 1])
            for f in (fine(2 * k), fine(2 * k + 1)):
                inside = HALO < f < nf - HALO - 1
                before = fine_two[f] if inside else edge_two[base + f]
                fine_edge[f] = before + spread

        def fine_of(k, side=side):
            return fine_one[2 * side + k - 4] if k >= 4 else fine_edge[fine(k)]

        def last_of(k, side=side):
            return fine_last[2 * side + k - 5] if k >= 5 else last_edge[fine(k)]

        for k in range(-1, 5):
            f = fine(k)
            source = fine_source[f] if HALO <= f < nf - HALO else edge_source[base + f]
            last_edge[f] = smoothed(fine_of(k - 1), fine_of(k), fine_of(k + 1), fine_weight[f], source, 1.0)
        for k in range(6):
            f = fine(k)
            v = smoothed(last_of(k - 1), last_of(k), last_of(k + 1), fine_weight[f], fine_source[f], 1.0)
            result[f - HALO] = v[0:32, :]
        rows = pl.ds(0, 6) if side == 0 else pl.ds(nx - 6, 6)
        copies.append(pltpu.make_async_copy(result.at[rows], out.at[rows], sems.at[side]))
        copies[-1].start()
    for c in copies:
        c.wait()


def both_ways(pairs):
    return pairs + [(j, i) for i, j in pairs]


def swap(pay_a, pay_b, axis):
    size = lax.axis_size(axis)
    pairs_a = [(i, i + 1) for i in range(1, size - 1, 2)]
    pairs_b = [(i, i + 1) for i in range(0, size - 1, 2)]
    return lax.ppermute(pay_a, axis, both_ways(pairs_a)), lax.ppermute(pay_b, axis, both_ways(pairs_b))


def exchange(value, distance):
    return lax.ppermute(value, "dev", [(i, i ^ distance) for i in range(lax.axis_size("dev"))])


def body(conc_old, phi_old, solid_pot, phase_label, iface_block, iface_owner):
    peers = lax.axis_size("dev")
    nx = conc_old.shape[0]
    half = nx // 2
    quarter = nx // 4
    ext = (nx + 2 * HALO, nx + 2 * HALO, 256)
    ext_mid = (half + 2 * HALO, half + 2 * HALO, 256)
    token_shape = shaped(8, LANES)

    pay_a, pay_b, own_lists = call(
        first_pack_kernel,
        [shaped(7 * nx, 256)] * 2 + [shaped(8, 256)],
        [conc_old, phase_label, iface_owner.reshape(1, -1), iface_block],
        [vmem(nx, HALO, 256)] * 2
        + [pltpu.VMEM((nx, HALO, 256), jnp.int32)] * 2
        + [pltpu.VMEM((1, 256), jnp.int32)] * 2
        + [vmem(7 * nx, 256)] * 2
        + [vmem(8, 256), pltpu.SemaphoreType.DMA((15,))],
        in_specs=[FAR] * 4,
        out_specs=[FAR] * 3,
        limit=VMEM_MOST,
        name="first_pack",
    )
    y_a, y_b = swap(pay_a, pay_b, "dev")
    conduct_mid, conduct_coarse, pay_a, pay_b, lists, gain, base = call(
        own_kernel,
        [shaped(half, half, 256), shaped(quarter, quarter, 256), shaped(22, 8, 256), shaped(22, 8, 256)]
        + [shaped(2, 256), shaped(nx, nx, 256), shaped(nx, nx, 256)],
        [conc_old, phase_label, phi_old, own_lists],
        [vmem(half, 2, nx, LANES), vmem(quarter, 2, half, LANES)],
        name="own",
    )
    xx_a, xx_b = swap(pay_a, pay_b, "grp")
    distance = peers // 2
    while distance > 1:
        lists = jnp.concatenate([lists, exchange(lists, distance)], axis=0)
        distance //= 2
    far_rows = second_rows(nx)[2]
    far_pay = call(
        second_pack_kernel,
        [shaped(far_rows, 256), shaped(far_rows + peers, 256)],
        [phi_old, conduct_mid, conduct_coarse, lists, xx_a, xx_b],
        name="second_pack",
    )
    yy_a, yy_b = swap(*far_pay, "dev")
    pay_a, pay_b = call(
        first_pack_x_kernel,
        [shaped(35, 8, 256)] * 2,
        [conc_old, phase_label, y_a, y_b, conduct_coarse],
        name="first_pack_x",
    )
    x_a, x_b = swap(pay_a, pay_b, "grp")

    ext_y = (nx, nx + 2 * HALO, 256)
    zero, first, second, third, gain_far, base_far, conc_inner, flux_inner = call(
        sweeps_inner_kernel,
        [shaped(*ext_y)] * 4 + [shaped(nx, 8, 256)] * 2 + [shaped(nx, nx, 256)] * 2,
        [conc_old, phase_label, phi_old, solid_pot, gain, base, y_a, y_b],
        name="sweeps_inner",
    )
    edge_args = [x_a, x_b, phase_label, phi_old, solid_pot, gain, base, zero, first, second, third]
    conc_new, flux_all, pay_a, pay_b = call(
        sweeps_edge_kernel,
        [shaped(nx, nx, 256), shaped(nx, nx, 256), shaped(3 * nx, 256), shaped(3 * nx, 256)],
        edge_args + [gain_far, base_far, conc_inner, flux_inner],
        [vmem(16, nx + 2 * HALO, 256)] * 4,
        name="sweeps_edge",
    )
    f_a, f_b = swap(pay_a, pay_b, "dev")
    flux_own, halo_mask = call(
        mask_kernel,
        [shaped(nx, nx, 256), shaped(nx, 8, 256)],
        [flux_all, lists, yy_b],
        [vmem(3, nx, 8, LANES)],
        name="mask",
    )
    weight, scale, made = call(
        ready_kernel,
        [shaped(*ext)] * 2 + [token_shape],
        [conc_old, phase_label, y_a, y_b, x_a, x_b],
        name="ready",
    )
    pay_a, pay_b = call(
        flux_pack_x_kernel, [shaped(15, 8, 256)] * 2, [flux_own, f_b, f_a, halo_mask, made], name="flux_pack_x"
    )
    fx_a, fx_b = swap(pay_a, pay_b, "grp")
    fine_two, fine_source, fine_first, inner_mid, field = call(
        potential_inner_kernel,
        [shaped(*ext)] * 3 + [shaped(half, half, 256), shaped(*ext)],
        [flux_own, halo_mask, f_a, f_b, phi_old, yy_a, yy_b, xx_a, xx_b, weight, scale],
        [vmem(nx, 8, 256), vmem(half, 2, nx, LANES)],
        name="potential_inner",
    )
    edge = (16, nx + 2 * HALO, 256)
    edge_two, edge_source, source_mid, pay_a, pay_b = call(
        potential_edge_kernel,
        [shaped(*edge), shaped(*edge), shaped(half, half, 256), shaped(4 * half, 256), shaped(4 * half, 256)],
        [fx_a, fx_b, weight, scale, field, fine_two, fine_source, fine_first, inner_mid, conduct_mid],
        [vmem(*edge), vmem(2, 2, nx, LANES)],
        name="potential_edge",
    )
    m_a, m_b = swap(pay_a, pay_b, "dev")
    concentration, flux, stored = call(
        store_kernel,
        [shaped(nx, nx, 256), shaped(nx, nx, 256), token_shape],
        [conc_new, flux_own],
        [pltpu.SemaphoreType.DMA((8,))],
        out_specs=[FAR, FAR, WHOLE],
        name="store",
    )
    wide = (quarter, 32, 256)
    rho, load, made = call(
        coarse_ready_kernel,
        [shaped(quarter, quarter, 256), shaped(8, LANES), token_shape],
        [conduct_coarse, yy_a, yy_b],
        [vmem(*wide)] * 4,
        name="coarse_ready",
    )
    pay_a, pay_b = call(
        mid_pack_x_kernel, [shaped(3 * HALO, 8, 256)] * 2, [source_mid, m_a, m_b, made], name="mid_pack_x"
    )
    mx_a, mx_b = swap(pay_a, pay_b, "grp")
    mid_two, mid_source, mid_weight, source_coarse, wide_coarse, pay_a, pay_b, sums = call(
        mid_kernel,
        [shaped(*ext_mid)] * 3
        + [shaped(quarter, 12, 256), shaped(quarter, 12, 256), shaped(72, 256), shaped(80, 256), shaped(8, 256)],
        [source_mid, conduct_mid, yy_a, yy_b, xx_a, xx_b, m_a, m_b, mx_a, mx_b, rho, load, stored],
        [vmem(*ext_mid)] * 2 + [vmem(8, 2, half + 2 * HALO, LANES)] * 2,
        name="middle",
    )
    c_a, c_b = swap(pay_a, pay_b, "dev")
    sums = sums + c_b[72:80]
    distance = 2
    while distance < peers:
        sums = sums + exchange(sums, distance)
        distance *= 2
    (error,) = call(
        coarse_kernel,
        [shaped(8, 16, 256)],
        [source_coarse, wide_coarse, yy_a, yy_b, c_a, c_b],
        [vmem(*wide)] * 4,
        name="coarse",
    )
    fields = [mid_two, mid_source, mid_weight, fine_two, fine_source, weight]
    kept = [shaped(4, half + 2 * HALO, 256)] * 2 + [shaped(4, nx + 2 * HALO, 256)] * 2
    scratch = [vmem(*ext_mid)] * 3 + [vmem(*ext)] * 2
    scratch += [vmem(8, 2, 2, 16, LANES), vmem(half + 2 * HALO, 3, 2, 16, LANES), vmem(nx, nx, 256)]
    scratch += [pltpu.SemaphoreType.DMA((2,))]
    error, pay_a, pay_b, begun, *kept_early = call(
        finish_early_kernel,
        [shaped(8, 16, 256), shaped(2, 16, 256), shaped(2, 16, 256), shaped(nx, nx, 256)] + kept,
        [error, sums] + fields,
        scratch,
        out_specs=[WHOLE] * 3 + [FAR] + [WHOLE] * 4,
        name="finish_early",
    )
    e_a, e_b = swap(pay_a, pay_b, "grp")
    begun, zero, one, fine_one, fine_last = call(
        finish_late_kernel,
        [shaped(nx, nx, 256)] + kept,
        [error] + fields + kept_early + [begun],
        scratch,
        in_specs=[WHOLE] * 11 + [FAR],
        out_specs=[FAR] + [WHOLE] * 4,
        aliases={11: 0},
        name="finish_late",
    )
    finish_args = [e_a, e_b, mid_two, mid_source, mid_weight, fine_two, edge_two, fine_source, edge_source, weight]
    finish_args += [zero, one, fine_one, fine_last, begun]
    (potential,) = call(
        finish_edge_kernel,
        [shaped(nx, nx, 256)],
        finish_args,
        [vmem(*ext_mid), vmem(*ext_mid), vmem(*ext), vmem(*ext)]
        + [vmem(4, 2, 2, 16, LANES), vmem(6, 3, 2, 16, LANES), vmem(nx, nx, 256)]
        + [pltpu.SemaphoreType.DMA((2,))],
        in_specs=[WHOLE] * (len(finish_args) - 1) + [FAR],
        out_specs=[FAR],
        aliases={len(finish_args) - 1: 0},
        name="finish_edge",
    )
    return (concentration, flux, potential)


def solution(mesh):
    brick = P("grp", "dev", None)
    return jax.shard_map(
        body,
        mesh=mesh,
        in_specs=(brick, brick, brick, brick, P("grp", "dev"), brick),
        out_specs=(brick, brick, brick),
        check_vma=False,
    )
```
